32 devices in a mesh: train: 4 (over y, x), roll: 8 (over z, core).
Axes of the slice: x: 2, y: 2, z: 4, core: 2. Of those that a mesh axis runs over, the one named last changes fastest.
Arguments:
- master_gate: float32 [4, 2048, 7168], P(None, 'roll', 'train'), may hold values from -1 to 1
- master_up: float32 [4, 2048, 7168], P(None, 'roll', 'train'), may hold values from -1 to 1
- master_down: float32 [4, 2048, 7168], P(None, 'roll', 'train'), may hold values from -1 to 1
- tokens: bfloat16 [512, 7168], P('roll'), may hold values from -6 to 6
- expert_ids: int32 [512, 2], P('roll'), may hold values from 0 to 3, all different within a row; in each aligned block of 64 rows (0 to 63, 64 to 127, ...) at most 32 rows name the same one
- gate_weights: float32 [512, 2], P('roll'), may hold values from 0.2 to 1
- placement: int32 [8], replicated, may hold values from 0 to 3, as said below
Outputs:
- slot_gate: bfloat16 [8, 16, 128, 7168], P('roll', None, 'train')
- slot_up: bfloat16 [8, 16, 128, 7168], P('roll', None, 'train')
- slot_down: bfloat16 [8, 16, 128, 7168], P('roll', None, 'train')
- mixed_out: bfloat16 [512, 7168], P('roll', 'train')
The draws below stay inside these ranges and needn't reach their ends.
Inputs may be any that keep to these rules, and one draw needn't show every extreme that they name: `expert_ids`: the 2 experts of a row differ. In each aligned block of 64 rows (the rows of one index of roll) no expert is named by more than 32 rows, a bound that some block reaches. `placement`: every expert of the window is held by exactly two owners.
All inputs are finite; a program needn't handle non-finite values. Where the reference program divides by a largest or mean magnitude, that divisor is 1e-20 or more.
Results may differ from the reference program's by a relative error of at most 0.0093.
Values may be sent and summed in bfloat16 or wider, within the bound.
No kernel may reach another device: no remote copies, remote signals or barrier semaphores. Data moves between devices by JAX's collectives and lax.ppermute only.
A program may use at most 256 MiB of HBM per device.

```python
import math
import jax
import jax.numpy as jnp
import numpy as np
from jax import lax

D = 7168
FF = 2048
BLOCK = 128
TOP = 2
TOK_DEV = 64
MOST = 32
EXPERTS = 4
OWNERS = 8
TOKENS = 512


def apply_scales(key, raw_field, spread, fan_in):
    key_row, key_col = jax.random.split(key)
    row_scale = jnp.exp(jax.random.uniform(key_row, (EXPERTS, FF, 1), jnp.float32, -spread, spread))
    col_scale = jnp.exp(jax.random.uniform(key_col, (EXPERTS, 1, D), jnp.float32, -spread, spread))
    divisor = math.sinh(2.0 * spread) / (2.0 * spread) * math.sqrt(fan_in)
    return jnp.clip(raw_field * row_scale * col_scale / divisor, -1.0, 1.0)


def draw_master_gate(key, part):
    key = jax.random.fold_in(key, 11)
    key_field, key_scale = jax.random.split(key)
    raw_field = jnp.clip(jax.random.normal(key_field, (EXPERTS, FF, D), jnp.float32), -4.0, 4.0)
    return apply_scales(key_scale, raw_field, 1.15, D)


def draw_master_up(key, part):
    key = jax.random.fold_in(key, 12)
    key_field, key_scale = jax.random.split(key)
    raw_field = jnp.clip(jax.random.normal(key_field, (EXPERTS, FF, D), jnp.float32), -4.0, 4.0)
    return apply_scales(key_scale, raw_field, 1.15, D)


def draw_master_down(key, part):
    key = jax.random.fold_in(key, 13)
    key_field, key_scale = jax.random.split(key)
    raw_field = jnp.clip(jax.random.normal(key_field, (EXPERTS, FF, D), jnp.float32), -4.0, 4.0)
    return apply_scales(key_scale, raw_field, 1.15, FF)


def draw_placement(key, part):
    key = jax.random.fold_in(key, 31)
    listed = jnp.concatenate((jnp.arange(EXPERTS, dtype=jnp.int32), jnp.arange(EXPERTS, dtype=jnp.int32)))
    return listed[jax.random.permutation(key, OWNERS)]


def levels(rng, shape, cuts, smallest, top_value):
    loudness, own = 1.0, jax.random.fold_in(rng, 6)
    for position, shards_of in cuts:
        draws = jnp.exp(jax.random.uniform(jax.random.fold_in(own, position), (shards_of,), jnp.float32, smallest / len(cuts), top_value / len(cuts)))
        loudness = loudness * jnp.repeat(draws, shape[position] // shards_of).reshape([-1 if axis == position else 1 for axis in range(len(shape))])
    return loudness


def assign_block(key, own, number, rows, count, top, most, lean):
    ranking = jax.random.permutation(key, count)
    crowded, common = portions_of(count, rows * top, most, lean, True), portions_of(count, rows * top, most, lean, False)
    places = jnp.arange(count)

    def named(tallies, turn):
        used = int((tallies > 0).sum())
        fixed = max(1, used // 4)
        passed = fixed + (places - fixed + turn * (used - fixed)) % max(1, count - fixed)
        return jnp.zeros((count,), jnp.int32).at[ranking[jnp.where(places < fixed, places, passed)]].set(jnp.asarray(tallies, jnp.int32))

    tallies = jnp.where(number % 4 == 0, named(crowded, number // 4), named(common, number - number // 4 - 1))
    mixed = jax.random.permutation(jax.random.fold_in(own, 3), count)
    source_of, taker = mixed[0:count // 2 * 2:2], mixed[1:count // 2 * 2:2]
    room = jnp.minimum(tallies[source_of] - 1, most - tallies[taker]) // 2
    room = jnp.where((source_of == ranking[0]) | (taker == ranking[0]) | (tallies[taker] == 0), 0, jnp.maximum(room, 0))
    passed = jax.random.randint(jax.random.fold_in(own, 4), (count // 2,), 0, 1 << 20) % (room + 1)
    tallies = tallies.at[source_of].add(-passed).at[taker].add(passed)
    members = jnp.searchsorted(jnp.cumsum(tallies), jnp.arange(rows * top), side="right").astype(jnp.int32)
    listing = members.reshape(top, rows).T
    listing = listing[jax.random.permutation(jax.random.fold_in(own, 1), rows)]
    turn = jax.random.randint(jax.random.fold_in(own, 2), (rows, 1), 0, top)
    return jnp.take_along_axis(listing, (jnp.arange(top)[None, :] + turn) % top, axis=1)


def portions_of(number_of, total, limit, lean, full):
    weights = [(1 << 20) // math.isqrt(standing ** lean) + 1 for standing in range(1, number_of + 1)]
    largest = limit if full else min(limit, max(-(-total // number_of), total * weights[0] // sum(weights)))
    least = 1 if total - largest >= number_of - 1 else 0
    given, rest = [largest] + [least] * (number_of - 1), total - largest - least * (number_of - 1)
    while rest > 0:
        movable = [i for i in range(1, number_of) if given[i] < largest] or [i for i in range(1, number_of) if given[i] < limit]
        pool, remaining = sum([weights[i] for i in movable]), rest
        for i in movable:
            addition = min(limit - given[i], max(1, remaining * weights[i] // pool), rest)
            given[i] = given[i] + addition
            rest = rest - addition
    return np.array(given)


def scatter_about(rng, shape, width, reach, cuts=(), kind=jnp.bfloat16):
    loudness = levels(rng, shape, cuts, -0.22, 0.18) if cuts else 1.0
    entries = jax.random.normal(rng, shape, jnp.float32) * width * loudness
    return jnp.minimum(jnp.maximum(entries, -reach), reach).astype(kind)


def setup_inputs(seed: int = 0) -> dict:
    seeds = jax.random.split(jax.random.key(seed), 8)
    master_gate = draw_master_gate(jax.random.fold_in(seeds[7], 71), 0)
    master_up = draw_master_up(jax.random.fold_in(seeds[7], 71), 0)
    master_down = draw_master_down(jax.random.fold_in(seeds[7], 71), 0)
    tokens = scatter_about(seeds[3], (TOKENS, D), 1.0, 6.0, ((0, 8),))
    expert_ids_keys = jax.random.split(jax.random.fold_in(seeds[4], 1), TOKENS // TOK_DEV)
    expert_ids_turns = jax.random.permutation(jax.random.fold_in(seeds[4], 3), TOKENS // TOK_DEV)
    expert_ids = jax.vmap(lambda own, number: assign_block(jax.random.fold_in(seeds[4], 2), own, number, TOK_DEV, EXPERTS, TOP, MOST, 2))(expert_ids_keys, expert_ids_turns).reshape((TOKENS, TOP))
    gate_weights = jnp.clip(0.2 + 0.8 * jax.random.uniform(seeds[5], (TOKENS, TOP), jnp.float32) ** levels(seeds[5], (TOKENS, TOP), ((0, 8),), -0.2, 0.2), 0.2, 1.0)
    placement = draw_placement(jax.random.fold_in(seeds[7], 71), 0)
    return {"master_gate": master_gate, "master_up": master_up, "master_down": master_down, "tokens": tokens, "expert_ids": expert_ids, "gate_weights": gate_weights, "placement": placement}


def quantize_blocks(master):
    blocks = master.reshape(EXPERTS, FF // BLOCK, BLOCK, D // BLOCK, BLOCK)
    block_scale = jnp.max(jnp.abs(blocks), axis=(2, 4)).astype(jnp.bfloat16)
    quantized = (blocks / block_scale.astype(jnp.float32)[:, :, None, :, None]).astype(jnp.bfloat16)
    return quantized, block_scale


def dequantize_blocks(quantized, block_scale):
    restored = quantized.astype(jnp.float32) * block_scale.astype(jnp.float32)[:, :, None, :, None]
    return restored.astype(jnp.bfloat16).reshape(EXPERTS, FF, D)


def reference(master_gate, master_up, master_down, tokens, expert_ids, gate_weights, placement):
    slots = []
    restored_all = []
    for master in (master_gate, master_up, master_down):
        quantized, block_scale = quantize_blocks(master)
        slots.append(quantized.reshape(EXPERTS, FF // BLOCK, BLOCK, D)[placement])
        restored_all.append(dequantize_blocks(quantized, block_scale))
    dequant_gate, dequant_up, dequant_down = restored_all

    def add_expert(expert, total):
        weight_gate = dequant_gate[expert]
        weight_up = dequant_up[expert]
        weight_down = dequant_down[expert]
        pre_gate = lax.dot_general(tokens, weight_gate, (((1,), (1,)), ((), ())), preferred_element_type=jnp.float32)
        pre_up = lax.dot_general(tokens, weight_up, (((1,), (1,)), ((), ())), preferred_element_type=jnp.float32)
        hidden = (jax.nn.silu(pre_gate) * pre_up).astype(jnp.bfloat16)
        expert_out = jnp.dot(hidden, weight_down, preferred_element_type=jnp.float32).astype(jnp.bfloat16)
        token_weight = jnp.sum(jnp.where(expert_ids == expert, gate_weights, jnp.zeros_like(gate_weights)), axis=1)
        return total + token_weight[:, None] * expert_out.astype(jnp.float32)

    total = lax.fori_loop(0, EXPERTS, add_expert, jnp.zeros((TOKENS, D), jnp.float32))
    return (slots[0], slots[1], slots[2], total.astype(jnp.bfloat16))
```

```python
import functools

import jax
import jax.numpy as jnp
from jax import lax
from jax.experimental import pallas as pl
from jax.experimental.pallas import tpu as pltpu
from jax.sharding import PartitionSpec as P

BLOCK = 128
CORES = 2
VMEM_BYTES = 48 * 1024 * 1024


def any_spec():
    return pl.BlockSpec(memory_space=pl.ANY)


def smem_spec():
    return pl.BlockSpec(memory_space=pltpu.SMEM)


def quantize_kernel(trains, x_ref, q_ref, d_ref):
    rows = BLOCK // trains
    features = x_ref.shape[-1]
    for col in range(features // BLOCK):
        cols = slice(col * BLOCK, (col + 1) * BLOCK)
        block = x_ref[0, :, cols]
        peak = jnp.max(jnp.max(jnp.abs(block), axis=0, keepdims=True), axis=1, keepdims=True)
        scale = peak.astype(jnp.bfloat16).astype(jnp.float32)
        quant = (block * (1.0 / scale)).astype(jnp.bfloat16)
        q_ref[:, 0, 0, :, cols] = quant.reshape(trains, rows, BLOCK)
        d_ref[0, 0, :, cols] = (quant.astype(jnp.float32) * scale).astype(jnp.bfloat16)


def quantize(master, first, count, trains):
    experts, _, features = master.shape
    rows = BLOCK // trains
    return pl.pallas_call(
        functools.partial(quantize_kernel, trains),
        grid=(experts, count),
        in_specs=[pl.BlockSpec((1, BLOCK, features), lambda e, b: (e, first + b, 0))],
        out_specs=[
            pl.BlockSpec((trains, 1, 1, rows, features), lambda e, b: (0, e, b, 0, 0)),
            pl.BlockSpec((1, 1, BLOCK, features), lambda e, b: (e, b, 0, 0)),
        ],
        out_shape=[
            jax.ShapeDtypeStruct((trains, experts, count, rows, features), jnp.bfloat16),
            jax.ShapeDtypeStruct((experts, count, BLOCK, features), jnp.bfloat16),
        ],
        compiler_params=pltpu.CompilerParams(vmem_limit_bytes=VMEM_BYTES),
        cost_estimate=pl.CostEstimate(
            flops=8 * experts * count * BLOCK * features,
            bytes_accessed=8 * experts * count * BLOCK * features,
            transcendentals=0,
        ),
        name="quantize",
    )(master)


def gather_kernel(picks, plan_ref, x_ref, *refs):
    outs, sem = refs[:-1], refs[-1]
    copies = []
    for out, places in zip(outs, picks):
        for slot, place in enumerate(places):
            copies.append(
                pltpu.make_async_copy(
                    x_ref.at[:, plan_ref[place]], out.at[slot], sem.at[len(copies)]
                )
            )
    for copy in copies:
        copy.start()
    for copy in copies:
        copy.wait()


def gather_pieces(plan, x, picks):
    trains, _, count, rows, features = x.shape
    total = sum(len(places) for places in picks)
    piece = trains * count * rows * features
    return pl.pallas_call(
        functools.partial(gather_kernel, picks),
        in_specs=[smem_spec(), any_spec()],
        out_specs=[any_spec()] * len(picks),
        out_shape=[
            jax.ShapeDtypeStruct((len(places), trains, count, rows, features), x.dtype)
            for places in picks
        ],
        scratch_shapes=[pltpu.SemaphoreType.DMA((total,))],
        cost_estimate=pl.CostEstimate(
            flops=0, bytes_accessed=4 * total * piece, transcendentals=0
        ),
        name="gather_pieces",
    )(plan, x)


def pick_kernel(choices, plan_ref, *refs):
    cands, out, sem = refs[:-2], refs[-2], refs[-1]
    for cand, slot, side, place, wanted in choices:
        hit = (plan_ref[side[0]] == side[1]) & (plan_ref[place] == wanted)

        @pl.when(hit)
        def _():
            pltpu.make_async_copy(cands[cand].at[slot], out, sem).start()

    pltpu.make_async_copy(cands[0].at[0], out, sem).wait()


def pick_piece(plan, cands, choices):
    shape = cands[0].shape[1:]
    size = 1
    for dim in shape:
        size *= dim
    return pl.pallas_call(
        functools.partial(pick_kernel, choices),
        in_specs=[smem_spec()] + [any_spec()] * len(cands),
        out_specs=any_spec(),
        out_shape=jax.ShapeDtypeStruct(shape, cands[0].dtype),
        scratch_shapes=[pltpu.SemaphoreType.DMA],
        cost_estimate=pl.CostEstimate(flops=0, bytes_accessed=4 * size, transcendentals=0),
        name="pick_piece",
    )(plan, *cands)


def place_kernel(layout, plan_ref, *refs):
    own, other, sources, first, count, blocks, n_in, aliased = layout
    cands = refs[: n_in]
    out, sem = refs[n_in + aliased], refs[n_in + aliased + 1]
    trains, _, _, features = cands[own[0][0][0]].shape[-4:]

    def target(source, part):
        start = source * blocks + first
        return out.at[pl.ds(start, count), :, pl.ds(part * features, features)]

    waits = []
    for offset, choices in enumerate(own):
        source = plan_ref[sources[offset][0]]
        for cand, slot, tests in choices:
            hit = None
            for place, wanted in tests:
                test = plan_ref[place] == wanted
                hit = test if hit is None else hit & test
            piece = cands[cand]

            def go(piece=piece, slot=slot, source=source, offset=offset):
                for part in range(trains):
                    if isinstance(slot, str):
                        expert = plan_ref[int(slot)]
                        view = piece.at[part, expert]
                    else:
                        view = piece.at[slot, part]
                    pltpu.make_async_copy(
                        view, target(source, part), sem.at[2 * offset, part]
                    ).start()

            if hit is None:
                go()
            else:
                pl.when(hit)(go)
        source_other = plan_ref[sources[offset][1]]
        for part in range(trains):
            pltpu.make_async_copy(
                cands[other[offset]].at[part], target(source_other, part), sem.at[2 * offset + 1, part]
            ).start()
        waits.append(offset)
    for offset in waits:
        for part in range(trains):
            piece = cands[other[offset]].at[part]
            for side in range(2):
                pltpu.make_async_copy(
                    piece, target(0, part), sem.at[2 * offset + side, part]
                ).wait()


def place_chunk(plan, cands, own, other, sources, first, blocks, out):
    trains, count, rows, features = cands[other[0]].shape
    offsets = len(own)
    aliased = out is not None
    layout = (own, other, sources, first, count, blocks, len(cands), int(aliased))
    shape = (2 * offsets * blocks, rows, trains * features)
    operands = list(cands) + ([out] if aliased else [])
    return pl.pallas_call(
        functools.partial(place_kernel, layout),
        in_specs=[smem_spec()] + [any_spec()] * len(operands),
        out_specs=any_spec(),
        out_shape=jax.ShapeDtypeStruct(shape, jnp.bfloat16),
        scratch_shapes=[pltpu.SemaphoreType.DMA((2 * offsets, trains))],
        input_output_aliases={len(operands): 0} if aliased else {},
        cost_estimate=pl.CostEstimate(
            flops=0,
            bytes_accessed=8 * offsets * trains * count * rows * features,
            transcendentals=0,
        ),
        name="place_chunk",
    )(plan, *operands)


def make_plan(placement, experts, owners):
    chips = owners // CORES
    me = lax.axis_index("roll")
    chip, core = me // CORES, me % CORES
    expert_range = jnp.arange(experts, dtype=jnp.int32)
    owner_chip = jnp.arange(owners, dtype=jnp.int32) // CORES
    held = placement[None, :] == expert_range[:, None]
    last = jnp.max(jnp.where(held, owner_chip[None, :], -1), axis=1)
    first = jnp.min(jnp.where(held, owner_chip[None, :], chips), axis=1)

    def ranks(key):
        ahead = (key[None, :] > key[:, None]) | (
            (key[None, :] == key[:, None]) & (expert_range[None, :] < expert_range[:, None])
        )
        return jnp.sum(ahead.astype(jnp.int32), axis=1)

    rank_up, rank_down = ranks(last), ranks(-first)
    order_up = jnp.sum(
        jnp.where(rank_up[:, None] == expert_range[None, :], expert_range[:, None], 0), axis=0
    )
    order_down = jnp.sum(
        jnp.where(rank_down[:, None] == expert_range[None, :], expert_range[:, None], 0), axis=0
    )
    own = jnp.sum(jnp.where(jnp.arange(owners) == me, placement, 0))
    mate = jnp.sum(jnp.where(jnp.arange(owners) == chip * CORES + 1 - core, placement, 0))

    def at(table, expert):
        return jnp.sum(jnp.where(expert_range == expert, table, 0))

    scalars = [own, mate, at(rank_up, own), at(rank_up, mate), at(rank_down, own), at(rank_down, mate)]
    names = ["own", "mate", "up_own", "up_mate", "down_own", "down_mate"]
    for offset in range(chips):
        source = (chip + chips - offset) % chips
        scalars += [
            (chip >= offset).astype(jnp.int32),
            source * CORES + core,
            source * CORES + 1 - core,
        ]
        names += [f"side{offset}", f"from{offset}", f"mate_from{offset}"]
    places = {name: 2 * experts + i for i, name in enumerate(names)}
    plan = jnp.concatenate(
        (order_up, order_down, jnp.stack([s.astype(jnp.int32) for s in scalars]))
    ).astype(jnp.int32)
    return plan, places


def slot_links(experts, chips, tight):
    caps = [min(experts, CORES * (chips - 1 - link)) for link in range(chips - 1)]
    if tight:
        middle = chips // 2 - 1
        caps = [min(cap, experts - 1) if link >= middle else cap for link, cap in enumerate(caps)]
    return [sum(1 for cap in caps if slot < cap) for slot in range(experts)]


def slot_groups(experts, chips, tight):
    links = slot_links(experts, chips, tight)
    groups = []
    for slot in range(experts):
        if groups and links[groups[-1][0]] == links[slot]:
            groups[-1].append(slot)
        else:
            groups.append([slot])
    return [(slots, links[slots[0]]) for slots in groups]


def hop(piece, links, step, chips, up):
    pairs = []
    for link in range(step - 1, links):
        for core in range(CORES):
            if up:
                pairs.append((link * CORES + core, (link + 1) * CORES + core))
            else:
                pairs.append(
                    ((chips - 1 - link) * CORES + core, (chips - 2 - link) * CORES + core)
                )
    return lax.ppermute(piece, "roll", pairs)


def swap_cores(piece, chips):
    pairs = []
    for chip in range(chips):
        for core in range(CORES):
            pairs.append((chip * CORES + core, chip * CORES + 1 - core))
    return lax.ppermute(piece, "roll", pairs)


def hand_off(plan, places, x, chips, tight):
    experts = x.shape[1]
    groups = slot_groups(experts, chips, tight)
    picks = [[slot for slot in slots] for slots, _ in groups]
    picks += [[experts + slot for slot in slots] for slots, _ in groups]
    picks += [[places["mate"]]]
    gathered = gather_pieces(plan, x, tuple(tuple(p) for p in picks))
    n = len(groups)
    mate_piece = gathered[2 * n][0]
    moved = {}
    now = {True: list(gathered[:n]), False: list(gathered[n : 2 * n])}
    for step in range(1, chips):
        for up in (True, False):
            for g, (slots, links) in enumerate(groups):
                if links >= step:
                    now[up][g] = hop(now[up][g], links, step, chips, up)
                    moved[up, step, g] = now[up][g]
    cands = [x]
    own = [[(0, str(places["own"]), ())]]
    other = [swap_cores(mate_piece, chips)]
    for offset in range(1, chips):
        here, choices_mate, choices_own = [], [], []
        for up, step in ((True, offset), (False, chips - offset)):
            for g, (slots, links) in enumerate(groups):
                if links < step:
                    continue
                here.append(moved[up, step, g])
                for i, slot in enumerate(slots):
                    side = (places[f"side{offset}"], int(up))
                    kind = "up" if up else "down"
                    choices_mate.append((len(here) - 1, i, side, places[f"{kind}_mate"], slot))
                    choices_own.append(
                        (len(cands) + len(here) - 1, i, (side, (places[f"{kind}_own"], slot)))
                    )
        other.append(swap_cores(pick_piece(plan, here, choices_mate), chips))
        cands += here
        own.append(choices_own)
    base = len(cands)
    cands += other
    sources = [(places[f"from{o}"], places[f"mate_from{o}"]) for o in range(chips)]
    return cands, own, [base + o for o in range(chips)], sources


def select_experts(pre, onehot):
    tokens, top, experts = onehot.shape
    pre = pre.reshape(tokens, experts, -1)
    total = jnp.zeros((tokens, top, pre.shape[2]), jnp.float32)
    for expert in range(experts):
        total = total + jnp.where(onehot[:, :, expert, None], pre[:, None, expert], 0.0)
    return total


def per_device(master_gate, master_up, master_down, tokens, expert_ids, gate_weights, placement):
    trains = lax.axis_size("train")
    owners = lax.axis_size("roll")
    chips = owners // CORES
    experts, hidden_rows, features = master_gate.shape
    blocks = hidden_rows // BLOCK
    chunks = []
    for m in range(3):
        for b in range(blocks):
            chunks.append((m, b, 1))
    plan, places = make_plan(placement, experts, owners)

    masters = (master_gate, master_up, master_down)
    dequant = [[], [], []]
    outs = [None, None, None]
    for m, first, count in chunks:
        quant, restored = quantize(masters[m], first, count, trains)
        dequant[m].append(restored)
        x = lax.all_to_all(quant, "train", split_axis=0, concat_axis=0, tiled=True)
        cands, own, other, sources = hand_off(plan, places, x, chips, False)
        outs[m] = place_chunk(plan, cands, own, other, sources, first, blocks, outs[m])

    train_me = lax.axis_index("train")
    mine = lax.dynamic_slice_in_dim(tokens, train_me * features, features, axis=1)
    every = lax.all_gather(mine, "roll", axis=0, tiled=True)
    ids = lax.all_gather(expert_ids, "roll", axis=0, tiled=True)
    weights = lax.all_gather(gate_weights, "roll", axis=0, tiled=True)
    onehot = ids[:, :, None] == jnp.arange(experts, dtype=jnp.int32)
    parts = []
    for m in range(2):
        for restored in dequant[m]:
            flat = restored.reshape(-1, features)
            pre = lax.dot_general(
                every, flat, (((1,), (1,)), ((), ())), preferred_element_type=jnp.float32
            )
            parts.append(select_experts(pre, onehot))
    pre = jnp.concatenate(parts, axis=2)
    pre = lax.psum_scatter(pre, "train", scatter_dimension=0, tiled=True)
    hidden = (jax.nn.silu(pre[:, :, :hidden_rows]) * pre[:, :, hidden_rows:]).astype(jnp.bfloat16)
    hidden = lax.all_gather(hidden, "train", axis=0, tiled=True)
    mixed = jnp.zeros((every.shape[0], features), jnp.float32)
    down = jnp.concatenate(dequant[2], axis=1) if len(dequant[2]) > 1 else dequant[2][0]
    for expert in range(experts):
        mask = onehot[:, :, expert]
        routed = jnp.sum(jnp.where(mask[:, :, None], hidden, jnp.zeros((), hidden.dtype)), axis=1)
        weight = jnp.sum(jnp.where(mask, weights, 0.0), axis=1)
        value = jnp.dot(
            routed, down[expert].reshape(hidden_rows, features), preferred_element_type=jnp.float32
        )
        mixed = mixed + weight[:, None] * value
    mixed = lax.psum_scatter(mixed, "roll", scatter_dimension=0, tiled=True).astype(jnp.bfloat16)
    return (outs[0][None], outs[1][None], outs[2][None], mixed)


def solution(mesh):
    in_specs = (
        P(None, "roll", "train"),
        P(None, "roll", "train"),
        P(None, "roll", "train"),
        P("roll", None),
        P("roll", None),
        P("roll", None),
        P(),
    )
    out_specs = (
        P("roll", None, "train", None),
        P("roll", None, "train", None),
        P("roll", None, "train", None),
        P("roll", "train"),
    )
    return jax.shard_map(
        per_device, mesh=mesh, in_specs=in_specs, out_specs=out_specs, check_vma=False
    )
```

```python
import functools

import jax
import jax.numpy as jnp
from jax import lax
from jax.experimental import pallas as pl
from jax.experimental.pallas import tpu as pltpu
from jax.sharding import PartitionSpec as P

BLOCK = 128
CORES = 2
VMEM_BYTES = 48 * 1024 * 1024


def any_spec():
    return pl.BlockSpec(memory_space=pl.ANY)


def smem_spec():
    return pl.BlockSpec(memory_space=pltpu.SMEM)


def quantize_kernel(trains, x_ref, q_ref, d_ref):
    rows = BLOCK // trains
    features = x_ref.shape[-1]
    for col in range(features // BLOCK):
        cols = slice(col * BLOCK, (col + 1) * BLOCK)
        block = x_ref[0, :, cols]
        peak = jnp.max(jnp.max(jnp.abs(block), axis=0, keepdims=True), axis=1, keepdims=True)
        scale = peak.astype(jnp.bfloat16).astype(jnp.float32)
        quant = (block * (1.0 / scale)).astype(jnp.bfloat16)
        q_ref[:, 0, 0, :, cols] = quant.reshape(trains, rows, BLOCK)
        d_ref[0, 0, :, cols] = (quant.astype(jnp.float32) * scale).astype(jnp.bfloat16)


def quantize(master, first, count, trains):
    experts, _, features = master.shape
    rows = BLOCK // trains
    return pl.pallas_call(
        functools.partial(quantize_kernel, trains),
        grid=(experts, count),
        in_specs=[pl.BlockSpec((1, BLOCK, features), lambda e, b: (e, first + b, 0))],
        out_specs=[
            pl.BlockSpec((trains, 1, 1, rows, features), lambda e, b: (0, e, b, 0, 0)),
            pl.BlockSpec((1, 1, BLOCK, features), lambda e, b: (e, b, 0, 0)),
        ],
        out_shape=[
            jax.ShapeDtypeStruct((trains, experts, count, rows, features), jnp.bfloat16),
            jax.ShapeDtypeStruct((experts, count, BLOCK, features), jnp.bfloat16),
        ],
        compiler_params=pltpu.CompilerParams(vmem_limit_bytes=VMEM_BYTES),
        cost_estimate=pl.CostEstimate(
            flops=8 * experts * count * BLOCK * features,
            bytes_accessed=8 * experts * count * BLOCK * features,
            transcendentals=0,
        ),
        name="quantize",
    )(master)


def gather_kernel(picks, plan_ref, x_ref, *refs):
    outs, (held, sem_in, sem_out) = refs[:-3], refs[-3:]
    loads, stores = [], []
    for out, places in zip(outs, picks):
        for slot, place in enumerate(places):
            n = len(loads)
            loads.append(
                pltpu.make_async_copy(x_ref.at[:, plan_ref[place]], held.at[n], sem_in.at[n])
            )
            stores.append(pltpu.make_async_copy(held.at[n], out.at[slot], sem_out.at[n]))
    for load in loads:
        load.start()
    for load, store in zip(loads, stores):
        load.wait()
        store.start()
    for store in stores:
        store.wait()


def gather_pieces(plan, x, picks):
    trains, _, count, rows, features = x.shape
    total = sum(len(places) for places in picks)
    piece = trains * count * rows * features
    return pl.pallas_call(
        functools.partial(gather_kernel, picks),
        in_specs=[smem_spec(), any_spec()],
        out_specs=[any_spec()] * len(picks),
        out_shape=[
            jax.ShapeDtypeStruct((len(places), trains, count, rows, features), x.dtype)
            for places in picks
        ],
        scratch_shapes=[
            pltpu.VMEM((total, trains, count, rows, features), x.dtype),
            pltpu.SemaphoreType.DMA((total,)),
            pltpu.SemaphoreType.DMA((total,)),
        ],
        compiler_params=pltpu.CompilerParams(vmem_limit_bytes=VMEM_BYTES),
        cost_estimate=pl.CostEstimate(
            flops=0, bytes_accessed=4 * total * piece, transcendentals=0
        ),
        name="gather_pieces",
    )(plan, x)


def pick_kernel(choices, plan_ref, *refs):
    cands, (out, held, sem) = refs[:-3], refs[-3:]
    for cand, slot, side, place, wanted in choices:
        hit = (plan_ref[side[0]] == side[1]) & (plan_ref[place] == wanted)

        @pl.when(hit)
        def _():
            pltpu.make_async_copy(cands[cand].at[slot], held, sem.at[0]).start()

    pltpu.make_async_copy(cands[0].at[0], held, sem.at[0]).wait()
    store = pltpu.make_async_copy(held, out, sem.at[1])
    store.start()
    store.wait()


def pick_piece(plan, cands, choices):
    shape = cands[0].shape[1:]
    size = 1
    for dim in shape:
        size *= dim
    return pl.pallas_call(
        functools.partial(pick_kernel, choices),
        in_specs=[smem_spec()] + [any_spec()] * len(cands),
        out_specs=any_spec(),
        out_shape=jax.ShapeDtypeStruct(shape, cands[0].dtype),
        scratch_shapes=[
            pltpu.VMEM(shape, cands[0].dtype),
            pltpu.SemaphoreType.DMA((2,)),
        ],
        compiler_params=pltpu.CompilerParams(vmem_limit_bytes=VMEM_BYTES),
        cost_estimate=pl.CostEstimate(flops=0, bytes_accessed=4 * size, transcendentals=0),
        name="pick_piece",
    )(plan, *cands)


def place_kernel(layout, plan_ref, *refs):
    own, other, sources, first, count, blocks, n_in, aliased = layout
    cands = refs[:n_in]
    out, held, sem_in, sem_out = refs[n_in + aliased :]
    trains, _, _, features = cands[other[0]].shape

    for offset, choices in enumerate(own):
        for cand, slot, tests in choices:
            hit = None
            for place, wanted in tests:
                test = plan_ref[place] == wanted
                hit = test if hit is None else hit & test
            if isinstance(slot, str):
                view = cands[cand].at[:, plan_ref[int(slot)]]
            else:
                view = cands[cand].at[slot]

            def go(view=view, offset=offset):
                pltpu.make_async_copy(view, held.at[2 * offset], sem_in.at[2 * offset]).start()

            if hit is None:
                go()
            else:
                pl.when(hit)(go)
        pltpu.make_async_copy(
            cands[other[offset]], held.at[2 * offset + 1], sem_in.at[2 * offset + 1]
        ).start()
    stores = []
    for offset in range(len(own)):
        for side in range(2):
            n = 2 * offset + side
            pltpu.make_async_copy(cands[other[0]], held.at[n], sem_in.at[n]).wait()
            start = plan_ref[sources[offset][side]] * blocks + first
            for part in range(trains):
                store = pltpu.make_async_copy(
                    held.at[n, part],
                    out.at[pl.ds(start, count), :, pl.ds(part * features, features)],
                    sem_out.at[n, part],
                )
                store.start()
                stores.append(store)
    for store in stores:
        store.wait()


def place_chunk(plan, cands, own, other, sources, first, blocks, out):
    trains, count, rows, features = cands[other[0]].shape
    offsets = len(own)
    aliased = out is not None
    layout = (own, other, sources, first, count, blocks, len(cands), int(aliased))
    shape = (2 * offsets * blocks, rows, trains * features)
    operands = list(cands) + ([out] if aliased else [])
    return pl.pallas_call(
        functools.partial(place_kernel, layout),
        in_specs=[smem_spec()] + [any_spec()] * len(operands),
        out_specs=any_spec(),
        out_shape=jax.ShapeDtypeStruct(shape, jnp.bfloat16),
        scratch_shapes=[
            pltpu.VMEM((2 * offsets, trains, count, rows, features), jnp.bfloat16),
            pltpu.SemaphoreType.DMA((2 * offsets,)),
            pltpu.SemaphoreType.DMA((2 * offsets, trains)),
        ],
        input_output_aliases={len(operands): 0} if aliased else {},
        compiler_params=pltpu.CompilerParams(vmem_limit_bytes=VMEM_BYTES),
        cost_estimate=pl.CostEstimate(
            flops=0,
            bytes_accessed=8 * offsets * trains * count * rows * features,
            transcendentals=0,
        ),
        name="place_chunk",
    )(plan, *operands)


def make_plan(placement, experts, owners):
    chips = owners // CORES
    me = lax.axis_index("roll")
    chip, core = me // CORES, me % CORES
    expert_range = jnp.arange(experts, dtype=jnp.int32)
    owner_chip = jnp.arange(owners, dtype=jnp.int32) // CORES
    held = placement[None, :] == expert_range[:, None]
    last = jnp.max(jnp.where(held, owner_chip[None, :], -1), axis=1)
    first = jnp.min(jnp.where(held, owner_chip[None, :], chips), axis=1)

    def ranks(key):
        ahead = (key[None, :] > key[:, None]) | (
            (key[None, :] == key[:, None]) & (expert_range[None, :] < expert_range[:, None])
        )
        return jnp.sum(ahead.astype(jnp.int32), axis=1)

    rank_up, rank_down = ranks(last), ranks(-first)
    order_up = jnp.sum(
        jnp.where(rank_up[:, None] == expert_range[None, :], expert_range[:, None], 0), axis=0
    )
    order_down = jnp.sum(
        jnp.where(rank_down[:, None] == expert_range[None, :], expert_range[:, None], 0), axis=0
    )
    own = jnp.sum(jnp.where(jnp.arange(owners) == me, placement, 0))
    mate = jnp.sum(jnp.where(jnp.arange(owners) == chip * CORES + 1 - core, placement, 0))

    def at(table, expert):
        return jnp.sum(jnp.where(expert_range == expert, table, 0))

    scalars = [own, mate, at(rank_up, own), at(rank_up, mate), at(rank_down, own), at(rank_down, mate)]
    names = ["own", "mate", "up_own", "up_mate", "down_own", "down_mate"]
    for offset in range(chips):
        source = (chip + chips - offset) % chips
        scalars += [
            (chip >= offset).astype(jnp.int32),
            source * CORES + core,
            source * CORES + 1 - core,
        ]
        names += [f"side{offset}", f"from{offset}", f"mate_from{offset}"]
    places = {name: 2 * experts + i for i, name in enumerate(names)}
    plan = jnp.concatenate(
        (order_up, order_down, jnp.stack([s.astype(jnp.int32) for s in scalars]))
    ).astype(jnp.int32)
    return plan, places


def slot_links(experts, chips, tight):
    caps = [min(experts, CORES * (chips - 1 - link)) for link in range(chips - 1)]
    if tight:
        middle = chips // 2 - 1
        caps = [min(cap, experts - 1) if link >= middle else cap for link, cap in enumerate(caps)]
    return [sum(1 for cap in caps if slot < cap) for slot in range(experts)]


def slot_groups(experts, chips, tight):
    links = slot_links(experts, chips, tight)
    groups = []
    for slot in range(experts):
        if groups and links[groups[-1][0]] == links[slot]:
            groups[-1].append(slot)
        else:
            groups.append([slot])
    return [(slots, links[slots[0]]) for slots in groups]


def hop(piece, links, step, chips, up):
    pairs = []
    for link in range(step - 1, links):
        for core in range(CORES):
            if up:
                pairs.append((link * CORES + core, (link + 1) * CORES + core))
            else:
                pairs.append(
                    ((chips - 1 - link) * CORES + core, (chips - 2 - link) * CORES + core)
                )
    return lax.ppermute(piece, "roll", pairs)


def swap_cores(piece, chips):
    pairs = []
    for chip in range(chips):
        for core in range(CORES):
            pairs.append((chip * CORES + core, chip * CORES + 1 - core))
    return lax.ppermute(piece, "roll", pairs)


def hand_off(plan, places, x, chips, tight):
    experts = x.shape[1]
    groups = slot_groups(experts, chips, tight)
    picks = [[slot for slot in slots] for slots, _ in groups]
    picks += [[experts + slot for slot in slots] for slots, _ in groups]
    picks += [[places["mate"]]]
    gathered = gather_pieces(plan, x, tuple(tuple(p) for p in picks))
    n = len(groups)
    mate_piece = gathered[2 * n][0]
    moved = {}
    now = {True: list(gathered[:n]), False: list(gathered[n : 2 * n])}
    for step in range(1, chips):
        for up in (True, False):
            for g, (slots, links) in enumerate(groups):
                if links >= step:
                    now[up][g] = hop(now[up][g], links, step, chips, up)
                    moved[up, step, g] = now[up][g]
    cands = [x]
    own = [[(0, str(places["own"]), ())]]
    other = [swap_cores(mate_piece, chips)]
    for offset in range(1, chips):
        here, choices_mate, choices_own = [], [], []
        for up, step in ((True, offset), (False, chips - offset)):
            for g, (slots, links) in enumerate(groups):
                if links < step:
                    continue
                here.append(moved[up, step, g])
                for i, slot in enumerate(slots):
                    side = (places[f"side{offset}"], int(up))
                    kind = "up" if up else "down"
                    choices_mate.append((len(here) - 1, i, side, places[f"{kind}_mate"], slot))
                    choices_own.append(
                        (len(cands) + len(here) - 1, i, (side, (places[f"{kind}_own"], slot)))
                    )
        other.append(swap_cores(pick_piece(plan, here, choices_mate), chips))
        cands += here
        own.append(choices_own)
    base = len(cands)
    cands += other
    sources = [(places[f"from{o}"], places[f"mate_from{o}"]) for o in range(chips)]
    return cands, own, [base + o for o in range(chips)], sources


def select_experts(pre, onehot):
    tokens, top, experts = onehot.shape
    pre = pre.reshape(tokens, experts, -1)
    total = jnp.zeros((tokens, top, pre.shape[2]), jnp.float32)
    for expert in range(experts):
        total = total + jnp.where(onehot[:, :, expert, None], pre[:, None, expert], 0.0)
    return total


def per_device(master_gate, master_up, master_down, tokens, expert_ids, gate_weights, placement):
    trains = lax.axis_size("train")
    owners = lax.axis_size("roll")
    chips = owners // CORES
    experts, hidden_rows, features = master_gate.shape
    blocks = hidden_rows // BLOCK
    chunks = []
    for m in range(3):
        for b in range(blocks):
            chunks.append((m, b, 1))
    plan, places = make_plan(placement, experts, owners)

    masters = (master_gate, master_up, master_down)
    dequant = [[], [], []]
    outs = [None, None, None]
    for m, first, count in chunks:
        quant, restored = quantize(masters[m], first, count, trains)
        dequant[m].append(restored)
        x = lax.all_to_all(quant, "train", split_axis=0, concat_axis=0, tiled=True)
        cands, own, other, sources = hand_off(plan, places, x, chips, False)
        outs[m] = place_chunk(plan, cands, own, other, sources, first, blocks, outs[m])

    train_me = lax.axis_index("train")
    mine = lax.dynamic_slice_in_dim(tokens, train_me * features, features, axis=1)
    every = lax.all_gather(mine, "roll", axis=0, tiled=True)
    ids = lax.all_gather(expert_ids, "roll", axis=0, tiled=True)
    weights = lax.all_gather(gate_weights, "roll", axis=0, tiled=True)
    onehot = ids[:, :, None] == jnp.arange(experts, dtype=jnp.int32)
    parts = []
    for m in range(2):
        for restored in dequant[m]:
            flat = restored.reshape(-1, features)
            pre = lax.dot_general(
                every, flat, (((1,), (1,)), ((), ())), preferred_element_type=jnp.float32
            )
            parts.append(select_experts(pre, onehot))
    pre = jnp.concatenate(parts, axis=2)
    pre = lax.psum_scatter(pre, "train", scatter_dimension=0, tiled=True)
    hidden = (jax.nn.silu(pre[:, :, :hidden_rows]) * pre[:, :, hidden_rows:]).astype(jnp.bfloat16)
    hidden = lax.all_gather(hidden, "train", axis=0, tiled=True)
    mixed = jnp.zeros((every.shape[0], features), jnp.float32)
    down = jnp.concatenate(dequant[2], axis=1) if len(dequant[2]) > 1 else dequant[2][0]
    for expert in range(experts):
        mask = onehot[:, :, expert]
        routed = jnp.sum(jnp.where(mask[:, :, None], hidden, jnp.zeros((), hidden.dtype)), axis=1)
        weight = jnp.sum(jnp.where(mask, weights, 0.0), axis=1)
        value = jnp.dot(
            routed, down[expert].reshape(hidden_rows, features), preferred_element_type=jnp.float32
        )
        mixed = mixed + weight[:, None] * value
    mixed = lax.psum_scatter(mixed, "roll", scatter_dimension=0, tiled=True).astype(jnp.bfloat16)
    return (outs[0][None], outs[1][None], outs[2][None], mixed)


def solution(mesh):
    in_specs = (
        P(None, "roll", "train"),
        P(None, "roll", "train"),
        P(None, "roll", "train"),
        P("roll", None),
        P("roll", None),
        P("roll", None),
        P(),
    )
    out_specs = (
        P("roll", None, "train", None),
        P("roll", None, "train", None),
        P("roll", None, "train", None),
        P("roll", "train"),
    )
    return jax.shard_map(
        per_device, mesh=mesh, in_specs=in_specs, out_specs=out_specs, check_vma=False
    )
```

```python
import functools

import jax
import jax.numpy as jnp
from jax import lax
from jax.experimental import pallas as pl
from jax.experimental.pallas import tpu as pltpu
from jax.sharding import PartitionSpec as P

BLOCK = 128
CORES = 2
VMEM_BYTES = 48 * 1024 * 1024


def any_spec():
    return pl.BlockSpec(memory_space=pl.ANY)


def smem_spec():
    return pl.BlockSpec(memory_space=pltpu.SMEM)


def quantize_kernel(trains, x_ref, *refs):
    q_ref, d_ref = refs[-2:]
    rows = BLOCK // trains
    features = x_ref.shape[-1]
    for col in range(features // BLOCK):
        cols = slice(col * BLOCK, (col + 1) * BLOCK)
        block = x_ref[0, :, cols]
        peak = jnp.max(jnp.max(jnp.abs(block), axis=0, keepdims=True), axis=1, keepdims=True)
        scale = peak.astype(jnp.bfloat16).astype(jnp.float32)
        quant = (block * (1.0 / scale)).astype(jnp.bfloat16)
        q_ref[:, 0, 0, :, cols] = quant.reshape(trains, rows, BLOCK)
        d_ref[0, 0, :, cols] = (quant.astype(jnp.float32) * scale).astype(jnp.bfloat16)


def quantize(master, first, count, trains, after=()):
    experts, _, features = master.shape
    rows = BLOCK // trains
    return pl.pallas_call(
        functools.partial(quantize_kernel, trains),
        grid=(experts, count),
        in_specs=[pl.BlockSpec((1, BLOCK, features), lambda e, b: (e, first + b, 0))]
        + [any_spec()] * len(after),
        out_specs=[
            pl.BlockSpec((trains, 1, 1, rows, features), lambda e, b: (0, e, b, 0, 0)),
            pl.BlockSpec((1, 1, BLOCK, features), lambda e, b: (e, b, 0, 0)),
        ],
        out_shape=[
            jax.ShapeDtypeStruct((trains, experts, count, rows, features), jnp.bfloat16),
            jax.ShapeDtypeStruct((experts, count, BLOCK, features), jnp.bfloat16),
        ],
        compiler_params=pltpu.CompilerParams(vmem_limit_bytes=VMEM_BYTES),
        cost_estimate=pl.CostEstimate(
            flops=8 * experts * count * BLOCK * features,
            bytes_accessed=8 * experts * count * BLOCK * features,
            transcendentals=0,
        ),
        name="quantize",
    )(master, *after)


def start_choice(plan_ref, arrays, choice, target, sem):
    tests, array, (kind, n) = choice
    ref = arrays[array]
    if kind == "is":
        view = ref.at[n]
    elif kind == "at":
        view = ref.at[plan_ref[n]]
    else:
        view = ref.at[:, plan_ref[n]]
    hit = None
    for place, value in tests:
        test = plan_ref[place] == value
        hit = test if hit is None else hit & test

    def go():
        pltpu.make_async_copy(view, target, sem).start()

    if hit is None:
        go()
    else:
        pl.when(hit)(go)


def pack_kernel(pieces, n_in, plan_ref, *refs):
    arrays = refs[:n_in]
    out, held, sem_in, sem_out = refs[-4:]
    for n, choices in enumerate(pieces):
        for choice in choices:
            start_choice(plan_ref, arrays, choice, held.at[n], sem_in.at[n])
    for n in range(len(pieces)):
        pltpu.make_async_copy(held.at[n], held.at[n], sem_in.at[n]).wait()
        pltpu.make_async_copy(held.at[n], out.at[n], sem_out.at[n]).start()
    for n in range(len(pieces)):
        pltpu.make_async_copy(held.at[n], out.at[n], sem_out.at[n]).wait()


class Arrays:
    def __init__(self):
        self.items = []

    def add(self, array):
        for n, item in enumerate(self.items):
            if item is array:
                return n
        self.items.append(array)
        return len(self.items) - 1


def number_choices(pieces, arrays):
    return [[(tests, arrays.add(a), index) for tests, a, index in choices] for choices in pieces]


def pack(plan, shape, pieces, after=()):
    arrays = Arrays()
    pieces = number_choices(pieces, arrays)
    n_in = len(arrays.items)
    size = len(pieces)
    for dim in shape:
        size *= dim
    operands = arrays.items + list(after)
    return pl.pallas_call(
        functools.partial(pack_kernel, pieces, n_in),
        in_specs=[smem_spec()] + [any_spec()] * len(operands),
        out_specs=any_spec(),
        out_shape=jax.ShapeDtypeStruct((len(pieces),) + shape, jnp.bfloat16),
        scratch_shapes=[
            pltpu.VMEM((len(pieces),) + shape, jnp.bfloat16),
            pltpu.SemaphoreType.DMA((len(pieces),)),
            pltpu.SemaphoreType.DMA((len(pieces),)),
        ],
        compiler_params=pltpu.CompilerParams(vmem_limit_bytes=VMEM_BYTES),
        cost_estimate=pl.CostEstimate(flops=0, bytes_accessed=4 * size, transcendentals=0),
        name="pack",
    )(plan, *operands)


def place_kernel(pieces, sources, first, blocks, n_in, plan_ref, *refs):
    arrays = refs[:n_in]
    out, held, sem_in, sem_out = refs[-4:]
    trains, count, _, features = held.shape[1:]
    for n, choices in enumerate(pieces):
        for choice in choices:
            start_choice(plan_ref, arrays, choice, held.at[n], sem_in.at[n])
    stores = []
    for n in range(len(pieces)):
        pltpu.make_async_copy(held.at[n], held.at[n], sem_in.at[n]).wait()
        start = plan_ref[sources[n]] * blocks + first
        for part in range(trains):
            store = pltpu.make_async_copy(
                held.at[n, part],
                out.at[pl.ds(start, count), :, pl.ds(part * features, features)],
                sem_out.at[n, part],
            )
            store.start()
            stores.append(store)
    for store in stores:
        store.wait()


def place_pieces(plan, shape, owners, pieces, sources, first, blocks, out):
    trains, count, rows, features = shape
    arrays = Arrays()
    pieces = number_choices(pieces, arrays)
    n_in = len(arrays.items)
    operands = arrays.items + ([] if out is None else [out])
    return pl.pallas_call(
        functools.partial(place_kernel, pieces, sources, first, blocks, n_in),
        in_specs=[smem_spec()] + [any_spec()] * len(operands),
        out_specs=any_spec(),
        out_shape=jax.ShapeDtypeStruct((owners * blocks, rows, trains * features), jnp.bfloat16),
        scratch_shapes=[
            pltpu.VMEM((len(pieces),) + shape, jnp.bfloat16),
            pltpu.SemaphoreType.DMA((len(pieces),)),
            pltpu.SemaphoreType.DMA((len(pieces), trains)),
        ],
        input_output_aliases={} if out is None else {len(operands): 0},
        compiler_params=pltpu.CompilerParams(vmem_limit_bytes=VMEM_BYTES),
        cost_estimate=pl.CostEstimate(
            flops=0,
            bytes_accessed=4 * len(pieces) * trains * count * rows * features,
            transcendentals=0,
        ),
        name="place_pieces",
    )(plan, *operands)


def count_distinct(placement, experts, owners):
    expert_range = jnp.arange(experts, dtype=jnp.int32)
    half = owners // 2
    held = placement[None, :] == expert_range[:, None]
    sides = [jnp.any(held[:, :half], axis=1), jnp.any(held[:, half:], axis=1)]
    return jnp.maximum(*[jnp.sum(side.astype(jnp.int32)) for side in sides])


def make_plan(placement, experts, owners, cap):
    me = lax.axis_index("roll")
    chip, core = me // CORES, me % CORES
    side = chip // 2
    inner = ((chip == 1) | (chip == 2)).astype(jnp.int32)
    expert_range = jnp.arange(experts, dtype=jnp.int32)
    owner_range = jnp.arange(owners, dtype=jnp.int32)
    owner_side = owner_range // (owners // 2)

    def ranks(on_side):
        held = (placement[None, :] == expert_range[:, None]) & (owner_side == on_side)[None, :]
        need = jnp.any(held, axis=1).astype(jnp.int32)
        ahead = (need[None, :] > need[:, None]) | (
            (need[None, :] == need[:, None]) & (expert_range[None, :] < expert_range[:, None])
        )
        return jnp.sum(ahead.astype(jnp.int32), axis=1)

    here, there = ranks(side), ranks(1 - side)
    send = jnp.sum(
        jnp.where(there[:, None] == expert_range[None, :], expert_range[:, None], 0), axis=0
    )

    def expert_of(owner):
        return jnp.sum(jnp.where(owner_range == owner, placement, 0))

    def rank_of(table, expert):
        return jnp.sum(jnp.where(expert_range == expert, table, 0))

    outer = 3 * side
    own, mate = expert_of(me), expert_of(chip * CORES + 1 - core)
    out0, out1 = expert_of(outer * CORES), expert_of(outer * CORES + 1)
    chip_of = [chip, 1 + 4 * side - chip, 2 - side, 3 - 3 * side]
    entries = {
        "inner": inner,
        "core": core,
        "own": own,
        "mate": mate,
        "out0": out0,
        "out1": out1,
        "here_own": jnp.minimum(rank_of(here, own), cap - 1),
        "here_mate": jnp.minimum(rank_of(here, mate), cap - 1),
        "here_out0": jnp.minimum(rank_of(here, out0), cap - 1),
        "here_out1": jnp.minimum(rank_of(here, out1), cap - 1),
        "there_own": rank_of(there, own),
        "there_mate": rank_of(there, mate),
    }
    for n, source in enumerate(chip_of):
        entries[f"from_own{n}"] = source * CORES + core
        entries[f"from_mate{n}"] = source * CORES + 1 - core
    places = {name: experts + n for n, name in enumerate(entries)}
    for slot in range(experts):
        places[f"send{slot}"] = slot
    plan = jnp.concatenate((send, jnp.stack([v.astype(jnp.int32) for v in entries.values()])))
    return plan, places


def line_schedule(chunks, experts, cap):
    head = min(2, chunks)
    middle = [("own", c) for c in range(head)]
    middle += [("far", c) for c in range(chunks)]
    middle += [("own", c) for c in range(head, chunks)]
    inwards = [[("far", c, s) for s in range(cap)] for c in range(chunks)]
    rest = [("near", c, s) for c in range(chunks) for s in range(cap, experts)]
    inwards += [rest[i : i + cap] for i in range(0, len(rest), cap)]
    fresh = [("x", c, i) for c in range(chunks) for i in range(CORES)]
    relayed = [(n + 2, (kind, c, i)) for n, (kind, c) in enumerate(middle) for i in range(CORES)]
    outwards = []
    n = 0
    while fresh or relayed or n < max(len(middle), len(inwards)):
        now = []
        while relayed and relayed[0][0] <= n and len(now) < cap:
            now.append(relayed.pop(0)[1])
        while fresh and fresh[0][1] <= n and len(now) < cap:
            now.append(fresh.pop(0))
        outwards.append(now)
        n += 1
    return middle, inwards, outwards


def link_pairs(chip_pairs, swap_chips=()):
    pairs = []
    for core in range(CORES):
        for a, b in chip_pairs:
            pairs.append((a * CORES + core, b * CORES + core))
        for chip in swap_chips:
            pairs.append((chip * CORES + core, chip * CORES + 1 - core))
    return pairs


def line_exchange(masters, placement, trains, owners, cap):
    experts, hidden_rows, features = masters[0].shape
    blocks = hidden_rows // BLOCK
    shape = (trains, 1, BLOCK // trains, features)
    plan, places = make_plan(placement, experts, owners, cap)
    chunks = [(m, b) for m in range(3) for b in range(blocks)]
    middle, inwards, outwards = line_schedule(len(chunks), experts, cap)
    rounds = len(outwards)
    edge_pairs = link_pairs([(0, 1), (1, 0), (2, 3), (3, 2)])
    middle_pairs = link_pairs([(1, 2), (2, 1)], swap_chips=(0, 3))
    swap_pairs = link_pairs([], swap_chips=range(4))
    is_inner, is_outer = (places["inner"], 1), (places["inner"], 0)

    xs, dequant = {}, [[], [], []]
    got_edge, got_middle, where = {}, {}, {}
    sent_edge = {}

    def prepare(c, after):
        m, b = chunks[c]
        quant, restored = quantize(masters[m], b, 1, trains, after)
        dequant[m].append(restored)
        xs[c] = lax.all_to_all(quant, "train", split_axis=0, concat_axis=0, tiled=True)

    def arrived(c, who):
        own = who == "own"
        pieces = [[((), xs[c], ("expert", places[who]))]]
        near = []
        for slot in range(experts):
            key = ("far", c, slot) if slot < cap else ("near", c, slot)
            n, i = where[key]
            near.append(((is_inner, (places[f"there_{who}"], slot)), got_edge[n], ("is", i)))
        pieces.append(near)
        pieces.append([((is_inner,), got_middle["own", c], ("at", places[f"here_{who}"]))])
        pieces.append([((is_inner,), got_middle["far", c], ("at", places[f"here_{who}"]))])
        for position, kind in ((1, "x"), (2, "own"), (3, "far")):
            for core in range(CORES):
                n, i = where["out", kind, c, core if own else 1 - core]
                pieces[position].append(
                    ((is_outer, (places["core"], core)), got_edge[n], ("is", i))
                )
        return pieces

    outs = [None, None, None]
    done = set()

    def finish(c):
        m, b = chunks[c]
        swapped = lax.ppermute(pack(plan, shape, arrived(c, "mate")), "roll", swap_pairs)
        pieces = arrived(c, "own") + [[((), swapped, ("is", n))] for n in range(4)]
        sources = [places[f"from_own{n}"] for n in range(4)]
        sources += [places[f"from_mate{n}"] for n in range(4)]
        outs[m] = place_pieces(plan, shape, owners, pieces, sources, b, blocks, outs[m])

    ready_in = {}
    for n, pieces in enumerate(inwards):
        for piece in pieces:
            ready_in[piece[1]] = max(ready_in.get(piece[1], 0), n)
    for n, pieces in enumerate(outwards):
        for piece in pieces:
            ready_in[piece[1]] = max(ready_in.get(piece[1], 0), n)

    for n in range(rounds):
        if n < len(chunks) and n not in xs:
            prepare(n, (sent_edge[n - 2],) if n >= 2 else ())
        ins = inwards[n] if n < len(inwards) else []
        outs_now = outwards[n]
        width = max(len(ins), len(outs_now))
        pieces = []
        for i in range(width):
            choices = []
            if i < len(outs_now):
                kind, c, core = outs_now[i]
                where["out", kind, c, core] = (n, i)
                if kind == "x":
                    choices.append(((is_inner,), xs[c], ("expert", places[f"out{core}"])))
                else:
                    choices.append(
                        ((is_inner,), got_middle[kind, c], ("at", places[f"here_out{core}"]))
                    )
            else:
                choices.append(((is_inner,), xs[min(n, len(chunks) - 1)], ("expert", places["own"])))
            if i < len(ins):
                kind, c, slot = ins[i]
                where[kind, c, slot] = (n, i)
                choices.append(((is_outer,), xs[c], ("expert", places[f"send{slot}"])))
            else:
                choices.append(((is_outer,), xs[min(n, len(chunks) - 1)], ("expert", places["own"])))
            pieces.append(choices)
        if width:
            after = (got_edge[n - 2],) if n >= 2 else ()
            sent_edge[n] = pack(plan, shape, pieces, after)
            got_edge[n] = lax.ppermute(sent_edge[n], "roll", edge_pairs)
        if n < len(middle):
            kind, c = middle[n]
            if kind == "own":
                pieces = [[((), xs[c], ("expert", places[f"send{s}"]))] for s in range(cap)]
                after = (got_middle[middle[n - 2]],) if n >= 2 else ()
                going = pack(plan, shape, pieces, after)
            else:
                going = got_edge[where["far", c, 0][0]]
            got_middle[kind, c] = lax.ppermute(going, "roll", middle_pairs)
        for c in range(len(chunks)):
            if c in ready_in and ready_in[c] == n - 1:
                finish(c)
                done.add(c)
    for c in range(len(chunks)):
        if c not in done:
            finish(c)
    return outs, dequant


def direct_exchange(masters, placement, trains, owners):
    experts, hidden_rows, features = masters[0].shape
    blocks = hidden_rows // BLOCK
    rows = BLOCK // trains
    outs, dequant = [], []
    for master in masters:
        quant, restored = quantize(master, 0, blocks, trains)
        dequant.append([restored])
        x = lax.all_to_all(quant, "train", split_axis=0, concat_axis=0, tiled=True)
        x = jnp.transpose(x, (1, 2, 3, 0, 4)).reshape(experts, blocks, rows, trains * features)
        picked = jnp.take(x, placement, axis=0)
        got = lax.all_to_all(picked, "roll", split_axis=0, concat_axis=0, tiled=True)
        outs.append(got.reshape(owners * blocks, rows, trains * features))
    return outs, dequant


def select_experts(pre, onehot):
    tokens, top, experts = onehot.shape
    pre = pre.reshape(tokens, experts, -1)
    total = jnp.zeros((tokens, top, pre.shape[2]), jnp.float32)
    for expert in range(experts):
        total = total + jnp.where(onehot[:, :, expert, None], pre[:, None, expert], 0.0)
    return total


def gather_tokens(tokens, expert_ids, gate_weights, features):
    mine = lax.dynamic_slice_in_dim(tokens, lax.axis_index("train") * features, features, axis=1)
    top = expert_ids.shape[1]
    high = lax.reduce_precision(gate_weights, 8, 7)
    middle = lax.reduce_precision(gate_weights - high, 8, 7)
    low = gate_weights - high - middle
    beside = jnp.concatenate((expert_ids.astype(jnp.float32), high, middle, low), axis=1)
    beside = jnp.pad(beside, ((0, 0), (0, BLOCK - 4 * top))).astype(jnp.bfloat16)
    every = lax.all_gather(jnp.concatenate((mine, beside), axis=1), "roll", axis=0, tiled=True)
    side = every[:, features : features + 4 * top].astype(jnp.float32)
    ids = side[:, :top].astype(jnp.int32)
    weights = side[:, top : 2 * top] + side[:, 2 * top : 3 * top] + side[:, 3 * top :]
    return every[:, :features], ids, weights


def decode_step(tokens, ids, weights, dequant, experts):
    features = tokens.shape[1]
    onehot = ids[:, :, None] == jnp.arange(experts, dtype=jnp.int32)
    parts = []
    for m in range(2):
        for restored in dequant[m]:
            flat = restored.reshape(-1, features)
            pre = lax.dot_general(
                tokens, flat, (((1,), (1,)), ((), ())), preferred_element_type=jnp.float32
            )
            parts.append(select_experts(pre, onehot))
    pre = lax.psum(jnp.concatenate(parts, axis=2), "train")
    hidden_rows = pre.shape[2] // 2
    hidden = (jax.nn.silu(pre[:, :, :hidden_rows]) * pre[:, :, hidden_rows:]).astype(jnp.bfloat16)
    down = jnp.concatenate(dequant[2], axis=1) if len(dequant[2]) > 1 else dequant[2][0]
    mixed = jnp.zeros((tokens.shape[0], features), jnp.float32)
    for expert in range(experts):
        mask = onehot[:, :, expert]
        routed = jnp.sum(jnp.where(mask[:, :, None], hidden, jnp.zeros((), hidden.dtype)), axis=1)
        weight = jnp.sum(jnp.where(mask, weights, 0.0), axis=1)
        value = jnp.dot(
            routed, down[expert].reshape(hidden_rows, features), preferred_element_type=jnp.float32
        )
        mixed = mixed + weight[:, None] * value
    return lax.psum_scatter(mixed, "roll", scatter_dimension=0, tiled=True).astype(jnp.bfloat16)


def per_device(master_gate, master_up, master_down, tokens, expert_ids, gate_weights, placement):
    trains = lax.axis_size("train")
    owners = lax.axis_size("roll")
    experts, _, features = master_gate.shape
    masters = (master_gate, master_up, master_down)
    routed = gather_tokens(tokens, expert_ids, gate_weights, features)

    def run(exchange, masters, placement, routed):
        outs, dequant = exchange(masters, placement)
        return tuple(outs) + (decode_step(*routed, dequant, experts),)

    if owners // CORES == 4:
        most = min(experts, owners // 2)
        branches = []
        for cap in (most - 1, most):
            def exchange(masters, placement, cap=cap):
                return line_exchange(masters, placement, trains, owners, cap)

            branches.append(functools.partial(run, exchange))
        tight = count_distinct(placement, experts, owners) <= most - 1
        outs = lax.cond(tight, branches[0], branches[1], masters, placement, routed)
    else:
        def exchange(masters, placement):
            return direct_exchange(masters, placement, trains, owners)

        outs = run(exchange, masters, placement, routed)
    return tuple(out[None] for out in outs[:3]) + (outs[3],)


def solution(mesh):
    in_specs = (
        P(None, "roll", "train"),
        P(None, "roll", "train"),
        P(None, "roll", "train"),
        P("roll", None),
        P("roll", None),
        P("roll", None),
        P(),
    )
    out_specs = (
        P("roll", None, "train", None),
        P("roll", None, "train", None),
        P("roll", None, "train", None),
        P("roll", "train"),
    )
    return jax.shard_map(
        per_device, mesh=mesh, in_specs=in_specs, out_specs=out_specs, check_vma=False
    )
```

```python
import functools

import jax
import jax.numpy as jnp
from jax import lax
from jax.experimental import pallas as pl
from jax.experimental.pallas import tpu as pltpu
from jax.sharding import PartitionSpec as P

BLOCK = 128
CORES = 2
VMEM_BYTES = 48 * 1024 * 1024


def any_spec():
    return pl.BlockSpec(memory_space=pl.ANY)


def smem_spec():
    return pl.BlockSpec(memory_space=pltpu.SMEM)


def quantize_kernel(trains, x_ref, *refs):
    q_ref, d_ref = refs[-2:]
    rows = BLOCK // trains
    features = x_ref.shape[-1]
    for col in range(features // BLOCK):
        cols = slice(col * BLOCK, (col + 1) * BLOCK)
        block = x_ref[0, :, cols]
        peak = jnp.max(jnp.max(jnp.abs(block), axis=0, keepdims=True), axis=1, keepdims=True)
        scale = peak.astype(jnp.bfloat16).astype(jnp.float32)
        quant = (block * (1.0 / scale)).astype(jnp.bfloat16)
        q_ref[:, 0, 0, :, cols] = quant.reshape(trains, rows, BLOCK)
        d_ref[0, 0, :, cols] = (quant.astype(jnp.float32) * scale).astype(jnp.bfloat16)


def quantize(master, first, count, trains, after=()):
    experts, _, features = master.shape
    rows = BLOCK // trains
    return pl.pallas_call(
        functools.partial(quantize_kernel, trains),
        grid=(experts, count),
        in_specs=[pl.BlockSpec((1, BLOCK, features), lambda e, b: (e, first + b, 0))]
        + [any_spec()] * len(after),
        out_specs=[
            pl.BlockSpec((trains, 1, 1, rows, features), lambda e, b: (0, e, b, 0, 0)),
            pl.BlockSpec((1, 1, BLOCK, features), lambda e, b: (e, b, 0, 0)),
        ],
        out_shape=[
            jax.ShapeDtypeStruct((trains, experts, count, rows, features), jnp.bfloat16),
            jax.ShapeDtypeStruct((experts, count, BLOCK, features), jnp.bfloat16),
        ],
        compiler_params=pltpu.CompilerParams(vmem_limit_bytes=VMEM_BYTES),
        cost_estimate=pl.CostEstimate(
            flops=8 * experts * count * BLOCK * features,
            bytes_accessed=8 * experts * count * BLOCK * features,
            transcendentals=0,
        ),
        name="quantize",
    )(master, *after)


def start_choice(plan_ref, arrays, choice, target, sem):
    tests, array, (kind, n) = choice
    ref = arrays[array]
    if kind == "is":
        view = ref.at[n]
    elif kind == "at":
        view = ref.at[plan_ref[n]]
    else:
        view = ref.at[:, plan_ref[n]]
    hit = None
    for place, value in tests:
        test = plan_ref[place] == value
        hit = test if hit is None else hit & test

    def go():
        pltpu.make_async_copy(view, target, sem).start()

    if hit is None:
        go()
    else:
        pl.when(hit)(go)


def pack_kernel(pieces, n_in, plan_ref, *refs):
    arrays = refs[:n_in]
    out, held, sem_in, sem_out = refs[-4:]
    for n, choices in enumerate(pieces):
        for choice in choices:
            start_choice(plan_ref, arrays, choice, held.at[n], sem_in.at[n])
    for n in range(len(pieces)):
        pltpu.make_async_copy(held.at[n], held.at[n], sem_in.at[n]).wait()
        pltpu.make_async_copy(held.at[n], out.at[n], sem_out.at[n]).start()
    for n in range(len(pieces)):
        pltpu.make_async_copy(held.at[n], out.at[n], sem_out.at[n]).wait()


class Arrays:
    def __init__(self):
        self.items = []

    def add(self, array):
        for n, item in enumerate(self.items):
            if item is array:
                return n
        self.items.append(array)
        return len(self.items) - 1


def number_choices(pieces, arrays):
    return [[(tests, arrays.add(a), index) for tests, a, index in choices] for choices in pieces]


def pack(plan, shape, pieces, after=()):
    arrays = Arrays()
    pieces = number_choices(pieces, arrays)
    n_in = len(arrays.items)
    size = len(pieces)
    for dim in shape:
        size *= dim
    operands = arrays.items + list(after)
    return pl.pallas_call(
        functools.partial(pack_kernel, pieces, n_in),
        in_specs=[smem_spec()] + [any_spec()] * len(operands),
        out_specs=any_spec(),
        out_shape=jax.ShapeDtypeStruct((len(pieces),) + shape, jnp.bfloat16),
        scratch_shapes=[
            pltpu.VMEM((len(pieces),) + shape, jnp.bfloat16),
            pltpu.SemaphoreType.DMA((len(pieces),)),
            pltpu.SemaphoreType.DMA((len(pieces),)),
        ],
        compiler_params=pltpu.CompilerParams(vmem_limit_bytes=VMEM_BYTES),
        cost_estimate=pl.CostEstimate(flops=0, bytes_accessed=4 * size, transcendentals=0),
        name="pack",
    )(plan, *operands)


def place_kernel(pieces, sources, first, blocks, n_in, plan_ref, *refs):
    arrays = refs[:n_in]
    out, mark, held, sem_in, sem_out = refs[-5:]
    trains, count, _, features = held.shape[1:]
    for n, choices in enumerate(pieces):
        for choice in choices:
            start_choice(plan_ref, arrays, choice, held.at[n], sem_in.at[n])
    mark[...] = jnp.zeros_like(mark)
    stores = []
    for n in range(len(pieces)):
        pltpu.make_async_copy(held.at[n], held.at[n], sem_in.at[n]).wait()
        start = plan_ref[sources[n]] * blocks + first
        for part in range(trains):
            store = pltpu.make_async_copy(
                held.at[n, part],
                out.at[pl.ds(start, count), :, pl.ds(part * features, features)],
                sem_out.at[n, part],
            )
            store.start()
            stores.append(store)
    for store in stores:
        store.wait()


def place_pieces(plan, shape, owners, pieces, sources, first, blocks, out, after=()):
    trains, count, rows, features = shape
    arrays = Arrays()
    pieces = number_choices(pieces, arrays)
    n_in = len(arrays.items)
    operands = arrays.items + list(after) + ([] if out is None else [out])
    return pl.pallas_call(
        functools.partial(place_kernel, pieces, sources, first, blocks, n_in),
        in_specs=[smem_spec()] + [any_spec()] * len(operands),
        out_specs=[any_spec(), pl.BlockSpec(memory_space=pltpu.VMEM)],
        out_shape=[
            jax.ShapeDtypeStruct((owners * blocks, rows, trains * features), jnp.bfloat16),
            jax.ShapeDtypeStruct((8, BLOCK), jnp.float32),
        ],
        scratch_shapes=[
            pltpu.VMEM((len(pieces),) + shape, jnp.bfloat16),
            pltpu.SemaphoreType.DMA((len(pieces),)),
            pltpu.SemaphoreType.DMA((len(pieces), trains)),
        ],
        input_output_aliases={} if out is None else {len(operands): 0},
        compiler_params=pltpu.CompilerParams(vmem_limit_bytes=VMEM_BYTES),
        cost_estimate=pl.CostEstimate(
            flops=0,
            bytes_accessed=4 * len(pieces) * trains * count * rows * features,
            transcendentals=0,
        ),
        name="place_pieces",
    )(plan, *operands)


def count_distinct(placement, experts, owners):
    expert_range = jnp.arange(experts, dtype=jnp.int32)
    half = owners // 2
    held = placement[None, :] == expert_range[:, None]
    sides = [jnp.any(held[:, :half], axis=1), jnp.any(held[:, half:], axis=1)]
    return jnp.maximum(*[jnp.sum(side.astype(jnp.int32)) for side in sides])


def make_plan(placement, experts, owners):
    me = lax.axis_index("roll")
    chip, core = me // CORES, me % CORES
    side = chip // 2
    inner = ((chip == 1) | (chip == 2)).astype(jnp.int32)
    expert_range = jnp.arange(experts, dtype=jnp.int32)
    owner_range = jnp.arange(owners, dtype=jnp.int32)
    owner_side = owner_range // (owners // 2)

    def ranks(on_side):
        held = (placement[None, :] == expert_range[:, None]) & (owner_side == on_side)[None, :]
        need = jnp.any(held, axis=1).astype(jnp.int32)
        ahead = (need[None, :] > need[:, None]) | (
            (need[None, :] == need[:, None]) & (expert_range[None, :] < expert_range[:, None])
        )
        return jnp.sum(ahead.astype(jnp.int32), axis=1)

    here, there = ranks(side), ranks(1 - side)
    send = jnp.sum(
        jnp.where(there[:, None] == expert_range[None, :], expert_range[:, None], 0), axis=0
    )

    def expert_of(owner):
        return jnp.sum(jnp.where(owner_range == owner, placement, 0))

    def rank_of(table, expert):
        return jnp.sum(jnp.where(expert_range == expert, table, 0))

    outer = 3 * side
    own, mate = expert_of(me), expert_of(chip * CORES + 1 - core)
    out0, out1 = expert_of(outer * CORES), expert_of(outer * CORES + 1)
    chip_of = [chip, 1 + 4 * side - chip, 2 - side, 3 - 3 * side]
    entries = {
        "inner": inner,
        "core": core,
        "own": own,
        "mate": mate,
        "out0": out0,
        "out1": out1,
        "here_own": rank_of(here, own),
        "here_mate": rank_of(here, mate),
        "here_out0": rank_of(here, out0),
        "here_out1": rank_of(here, out1),
        "there_own": rank_of(there, own),
        "there_mate": rank_of(there, mate),
    }
    for n, source in enumerate(chip_of):
        entries[f"from_own{n}"] = source * CORES + core
        entries[f"from_mate{n}"] = source * CORES + 1 - core
    places = {name: experts + n for n, name in enumerate(entries)}
    for slot in range(experts):
        places[f"send{slot}"] = slot
    plan = jnp.concatenate((send, jnp.stack([v.astype(jnp.int32) for v in entries.values()])))
    return plan, places


def line_schedule(chunks, experts, cap):
    head = min(2, chunks)
    middle = [("own", c) for c in range(head)]
    middle += [("far", c) for c in range(chunks)]
    middle += [("own", c) for c in range(head, chunks)]
    inwards = [[("far", c, s) for s in range(cap)] for c in range(chunks)]
    rest = [("near", c, s) for c in range(chunks) for s in range(cap, experts)]
    inwards += [rest[i : i + cap] for i in range(0, len(rest), cap)]
    fresh = [("x", c, i) for c in range(chunks) for i in range(CORES)]
    relayed = [(n + 2, (kind, c, i)) for n, (kind, c) in enumerate(middle) for i in range(CORES)]
    outwards = []
    n = 0
    while fresh or relayed or n < max(len(middle), len(inwards)):
        now = []
        while relayed and relayed[0][0] <= n and len(now) < cap:
            now.append(relayed.pop(0)[1])
        while fresh and fresh[0][1] <= n and len(now) < cap:
            now.append(fresh.pop(0))
        outwards.append(now)
        n += 1
    return middle, inwards, outwards


def link_pairs(chip_pairs, swap_chips=(), cross=False):
    pairs = []
    for core in range(CORES):
        for a, b in chip_pairs:
            pairs.append((a * CORES + core, b * CORES + (1 - core if cross else core)))
        for chip in swap_chips:
            pairs.append((chip * CORES + core, chip * CORES + 1 - core))
    return pairs


EDGES = ((0, 1), (1, 0), (2, 3), (3, 2))


def line_exchange(masters, begun, plan, places, routed, trains, owners, cap):
    experts, hidden_rows, features = masters[0].shape
    blocks = hidden_rows // BLOCK
    shape = (trains, 1, BLOCK // trains, features)
    chunks = [(m, b) for m in range(3) for b in range(blocks)]
    middle, inwards, outwards = line_schedule(len(chunks), experts, cap)
    rounds = len(outwards)
    edge_pairs = link_pairs(EDGES)
    cross_pairs = link_pairs(EDGES, cross=True)
    middle_pairs = link_pairs([(1, 2), (2, 1)], swap_chips=(0, 3))
    swap_pairs = link_pairs([], swap_chips=range(4))
    is_inner, is_outer = (places["inner"], 1), (places["inner"], 0)
    on_core = [(places["core"], core) for core in range(CORES)]
    xs, dequant = {}, {}
    got_edge, got_middle, where = {}, {}, {}
    last = [begun[0][0]]

    def packed(pieces):
        last[0] = pack(plan, shape, pieces, (last[0],))
        return last[0]

    def exchange_train(c, quant):
        xs[c] = lax.all_to_all(quant, "train", split_axis=0, concat_axis=0, tiled=True)

    def prepare(c):
        m, b = chunks[c]
        quant, dequant[c] = quantize(masters[m], b, 1, trains, (last[0],))
        last[0] = quant
        exchange_train(c, quant)

    xs[0], dequant[0] = begun[0]
    quant, dequant[1] = begun[1]
    exchange_train(1, quant)

    crossed = [n >= len(middle) for n in range(rounds)]
    ready = {(c, 0): 0 for c in range(len(chunks))}
    ready_to_swap = dict(ready)

    def note(c, position, n, swap=True):
        ready[c, position] = max(ready.get((c, position), 0), n)
        if swap:
            ready_to_swap[c, position] = max(ready_to_swap.get((c, position), 0), n)

    for n, (kind, c) in enumerate(middle):
        note(c, 2 if kind == "own" else 3, n)
    for n, pieces in enumerate(inwards):
        for _, c, _ in pieces:
            note(c, 1, n)
    for n, pieces in enumerate(outwards):
        for kind, c, _ in pieces:
            note(c, {"x": 1, "own": 2, "far": 3}[kind], n, not crossed[n])

    def find(c, position, who):
        own = who == "own"
        if position == 0:
            return [((), xs[c], ("expert", places[who]))]
        choices = []
        if position == 1:
            for slot in range(experts):
                n, i = where["far" if slot < cap else "near", c, slot]
                test = (places[f"there_{who}"], slot)
                choices.append(((is_inner, test), got_edge[n], ("is", i)))
        else:
            got = got_middle["own" if position == 2 else "far", c]
            choices.append(((is_inner,), got, ("at", places[f"here_{who}"])))
        kind = {1: "x", 2: "own", 3: "far"}[position]
        for core in range(CORES):
            n, i = where["out", kind, c, core if own else 1 - core]
            if not crossed[n]:
                choices.append(((is_outer, on_core[core]), got_edge[n], ("is", i)))
        return choices

    def find_crossed(c, position, which):
        kind = {1: "x", 2: "own", 3: "far"}.get(position)
        n = where["out", kind, c, 0][0] if kind else 0
        return [((is_outer,), got_edge[n][which], ("is", 0))] if crossed[n] else []

    groups = []
    for c in range(len(chunks)):
        early = [p for p in range(4) if ready[c, p] < rounds - 4]
        late = [p for p in range(4) if p not in early]
        for positions in (early, late):
            if positions:
                groups.append((max(ready_to_swap[c, p] for p in positions), c, positions))
    groups.sort(key=lambda group: group[0])
    swapped, outs = {}, [None, None, None]

    def swap(group):
        _, c, positions = group
        pieces = []
        for p in positions:
            choices = find(c, p, "mate")
            if find_crossed(c, p, 0):
                choices.append(((is_outer,), xs[c], ("expert", places["own"])))
            pieces.append(choices)
        swapped[c, tuple(positions)] = lax.ppermute(packed(pieces), "roll", swap_pairs)

    def place(group):
        _, c, positions = group
        m, b = chunks[c]
        got = swapped[c, tuple(positions)]
        pieces = [find(c, p, "own") + find_crossed(c, p, 0) for p in positions]
        for n, p in enumerate(positions):
            crossing = find_crossed(c, p, 1)
            pieces.append([((is_inner,) if crossing else (), got, ("is", n))] + crossing)
        sources = [places[f"from_own{p}"] for p in positions]
        sources += [places[f"from_mate{p}"] for p in positions]
        outs[m], last[0] = place_pieces(
            plan, shape, owners, pieces, sources, b, blocks, outs[m], (last[0],)
        )

    tokens, ids, weights = routed
    state = {"pre": None}
    ups = 2 * blocks

    def decode(n):
        if n < ups:
            state["pre"] = pre_activations(
                tokens, ids, dequant[n], state["pre"], n, ups, (last[0],)
            )
            last[0] = state["pre"]
        if n == ups - 1:
            state["sum"] = lax.psum(state["pre"], "train")
        if n == ups + 3:
            down = [dequant[c] for c in range(ups, len(chunks))]
            last[0] = mix_experts(state["sum"], ids, weights, down, (last[0],))
            state["out"] = lax.psum_scatter(last[0], "roll", scatter_dimension=0, tiled=True)

    to_swap, to_place = list(groups), []
    for n in range(max(rounds, ups + 4)):
        if n < rounds:
            ins = inwards[n] if n < len(inwards) else []
            outs_now = outwards[n]
            spare = xs[min(n, len(chunks) - 1)]
            pieces = []
            for i in range(max(len(ins), len(outs_now))):
                choices = [((is_inner,), spare, ("expert", places["own"]))]
                if i < len(outs_now):
                    kind, c, core = outs_now[i]
                    where["out", kind, c, core] = (n, i)
                    if kind == "x":
                        choices = [((is_inner,), xs[c], ("expert", places[f"out{core}"]))]
                    else:
                        got, index = got_middle[kind, c], ("at", places[f"here_out{core}"])
                        choices = [((is_inner,), got, index)]
                if i < len(ins):
                    kind, c, slot = ins[i]
                    where[kind, c, slot] = (n, i)
                    choices.append(((is_outer,), xs[c], ("expert", places[f"send{slot}"])))
                else:
                    choices.append(((is_outer,), spare, ("expert", places["own"])))
                pieces.append(choices)
            if crossed[n]:
                got = []
                kind, c, _ = outs_now[0]
                for pairs, names in (
                    (edge_pairs, ("here_out0", "here_out1")),
                    (cross_pairs, ("here_out1", "here_out0")),
                ):
                    choices = [
                        ((is_inner, on_core[core]), got_middle[kind, c], ("at", places[names[core]]))
                        for core in range(CORES)
                    ]
                    choices.append(((is_outer,), spare, ("expert", places["own"])))
                    got.append(lax.ppermute(packed([choices]), "roll", pairs))
                got_edge[n] = got
            elif pieces:
                got_edge[n] = lax.ppermute(packed(pieces), "roll", edge_pairs)
            if n < len(middle):
                kind, c = middle[n]
                if kind == "own":
                    pieces = [[((), xs[c], ("expert", places[f"send{s}"]))] for s in range(cap)]
                    going = packed(pieces)
                else:
                    going = got_edge[where["far", c, 0][0]]
                got_middle[kind, c] = lax.ppermute(going, "roll", middle_pairs)
        if n + 2 < len(chunks):
            prepare(n + 2)
        decode(n)
        for group in list(to_place):
            if max(ready[group[1], p] for p in group[2]) <= n - 2:
                place(group)
                to_place.remove(group)
        while to_swap and to_swap[0][0] <= n - 2:
            to_place.append(to_swap.pop(0))
            swap(to_place[-1])
    for group in to_swap:
        swap(group)
    for group in to_place + to_swap:
        place(group)
    return tuple(outs) + (state["out"].astype(jnp.bfloat16),)


def direct_exchange(masters, placement, trains, owners):
    experts, hidden_rows, features = masters[0].shape
    blocks = hidden_rows // BLOCK
    rows = BLOCK // trains
    outs, dequant = [], []
    for master in masters:
        quant, restored = quantize(master, 0, blocks, trains)
        dequant.append([restored])
        x = lax.all_to_all(quant, "train", split_axis=0, concat_axis=0, tiled=True)
        x = jnp.transpose(x, (1, 2, 3, 0, 4)).reshape(experts, blocks, rows, trains * features)
        picked = jnp.take(x, placement, axis=0)
        got = lax.all_to_all(picked, "roll", split_axis=0, concat_axis=0, tiled=True)
        outs.append(got.reshape(owners * blocks, rows, trains * features))
    return outs, dequant


def pre_activation_kernel(experts, top, tok_ref, ids_ref, w_ref, *refs):
    out_ref = refs[-1]
    features = tok_ref.shape[1]
    weights = w_ref[...].reshape(experts * BLOCK, features)
    pre = lax.dot_general(
        tok_ref[...], weights, (((1,), (1,)), ((), ())), preferred_element_type=jnp.float32
    )
    for k in range(top):
        total = jnp.zeros((pre.shape[0], BLOCK), jnp.float32)
        for expert in range(experts):
            part = pre[:, expert * BLOCK : (expert + 1) * BLOCK]
            total = total + jnp.where(ids_ref[:, k : k + 1] == expert, part, 0.0)
        out_ref[:, k * BLOCK : (k + 1) * BLOCK] = total


def pre_activations(tokens, ids, restored, out, column, columns, after=()):
    count, features = tokens.shape
    experts, top = restored.shape[0], ids.shape[1]
    tile = min(count, 2 * BLOCK)
    operands = [tokens, ids, restored] + list(after) + ([] if out is None else [out])
    return pl.pallas_call(
        functools.partial(pre_activation_kernel, experts, top),
        grid=(count // tile,),
        in_specs=[
            pl.BlockSpec((tile, features), lambda i: (i, 0)),
            pl.BlockSpec((tile, top), lambda i: (i, 0)),
            pl.BlockSpec(restored.shape, lambda i: (0, 0, 0, 0)),
        ]
        + [any_spec()] * (len(operands) - 3),
        out_specs=pl.BlockSpec((tile, top * BLOCK), lambda i: (i, column)),
        out_shape=jax.ShapeDtypeStruct((count, columns * top * BLOCK), jnp.float32),
        input_output_aliases={} if out is None else {len(operands) - 1: 0},
        compiler_params=pltpu.CompilerParams(vmem_limit_bytes=VMEM_BYTES),
        cost_estimate=pl.CostEstimate(
            flops=2 * count * features * experts * BLOCK,
            bytes_accessed=2 * features * (count + experts * BLOCK),
            transcendentals=0,
        ),
        name="pre_activations",
    )(*operands)


def mix_kernel(experts, top, blocks, pre_ref, ids_ref, weights_ref, *refs):
    downs, out_ref = refs[:blocks], refs[-1]
    width = top * BLOCK
    hidden = {}
    for b in range(blocks):
        for k in range(top):
            start = b * width + k * BLOCK
            gate = pre_ref[:, start : start + BLOCK]
            up = pre_ref[:, blocks * width + start : blocks * width + start + BLOCK]
            value = gate / (1.0 + jnp.exp(-gate)) * up
            hidden[b, k] = value.astype(jnp.bfloat16).astype(jnp.float32)
    total = jnp.zeros(out_ref.shape, jnp.float32)
    for expert in range(experts):
        weight = jnp.zeros((out_ref.shape[0], 1), jnp.float32)
        for k in range(top):
            weight = weight + jnp.where(
                ids_ref[:, k : k + 1] == expert, weights_ref[:, k : k + 1], 0.0
            )
        value = jnp.zeros(out_ref.shape, jnp.float32)
        for b in range(blocks):
            routed = jnp.zeros((out_ref.shape[0], BLOCK), jnp.float32)
            for k in range(top):
                routed = routed + jnp.where(ids_ref[:, k : k + 1] == expert, hidden[b, k], 0.0)
            value = value + jnp.dot(
                routed.astype(jnp.bfloat16), downs[b][expert, 0], preferred_element_type=jnp.float32
            )
        total = total + weight * value
    out_ref[...] = total


def mix_experts(pre, ids, weights, downs, after=()):
    count, top = ids.shape
    experts, _, _, features = downs[0].shape
    blocks = len(downs)
    tile = min(count, BLOCK)
    operands = [pre, ids, weights] + list(downs) + list(after)
    return pl.pallas_call(
        functools.partial(mix_kernel, experts, top, blocks),
        grid=(count // tile,),
        in_specs=[
            pl.BlockSpec((tile, pre.shape[1]), lambda i: (i, 0)),
            pl.BlockSpec((tile, top), lambda i: (i, 0)),
            pl.BlockSpec((tile, top), lambda i: (i, 0)),
        ]
        + [pl.BlockSpec(down.shape, lambda i: (0, 0, 0, 0)) for down in downs]
        + [any_spec()] * len(after),
        out_specs=pl.BlockSpec((tile, features), lambda i: (i, 0)),
        out_shape=jax.ShapeDtypeStruct((count, features), jnp.float32),
        compiler_params=pltpu.CompilerParams(vmem_limit_bytes=VMEM_BYTES),
        cost_estimate=pl.CostEstimate(
            flops=2 * count * features * experts * blocks * BLOCK,
            bytes_accessed=4 * count * features + 2 * experts * blocks * BLOCK * features,
            transcendentals=0,
        ),
        name="mix_experts",
    )(*operands)


def gather_tokens(tokens, expert_ids, gate_weights, features):
    mine = lax.dynamic_slice_in_dim(tokens, lax.axis_index("train") * features, features, axis=1)
    top = expert_ids.shape[1]
    high = lax.reduce_precision(gate_weights, 8, 7)
    middle = lax.reduce_precision(gate_weights - high, 8, 7)
    low = gate_weights - high - middle
    beside = jnp.concatenate((expert_ids.astype(jnp.float32), high, middle, low), axis=1)
    beside = jnp.pad(beside, ((0, 0), (0, BLOCK - 4 * top))).astype(jnp.bfloat16)
    every = lax.all_gather(jnp.concatenate((mine, beside), axis=1), "roll", axis=0, tiled=True)
    side = every[:, features : features + 4 * top].astype(jnp.float32)
    ids = side[:, :top].astype(jnp.int32)
    weights = side[:, top : 2 * top] + side[:, 2 * top : 3 * top] + side[:, 3 * top :]
    return every[:, :features], ids, weights


def per_device(master_gate, master_up, master_down, tokens, expert_ids, gate_weights, placement):
    trains = lax.axis_size("train")
    owners = lax.axis_size("roll")
    experts, hidden_rows, features = master_gate.shape
    blocks = hidden_rows // BLOCK
    masters = (master_gate, master_up, master_down)
    if owners // CORES == 4:
        chunks = [(m, b) for m in range(3) for b in range(blocks)]
        begun = [quantize(masters[m], b, 1, trains) for m, b in chunks[:2]]
        first = lax.all_to_all(begun[0][0], "train", split_axis=0, concat_axis=0, tiled=True)
        begun = ((first, begun[0][1]), tuple(begun[1]))
        routed = gather_tokens(tokens, expert_ids, gate_weights, features)
        plan, places = make_plan(placement, experts, owners)
        most = min(experts, owners // 2)

        def branch(cap, masters, begun, plan, routed):
            return line_exchange(masters, begun, plan, places, routed, trains, owners, cap)

        tight = count_distinct(placement, experts, owners) <= most - 1
        outs = lax.cond(
            tight,
            functools.partial(branch, most - 1),
            functools.partial(branch, most),
            masters,
            begun,
            plan,
            routed,
        )
    else:
        routed = gather_tokens(tokens, expert_ids, gate_weights, features)
        outs, dequant = direct_exchange(masters, placement, trains, owners)
        tokens, ids, weights = routed
        pre = None
        for n in range(2 * blocks):
            m, b = n // blocks, n % blocks
            pre = pre_activations(
                tokens, ids, dequant[m][0][:, b : b + 1], pre, n, 2 * blocks
            )
        pre = lax.psum(pre, "train")
        downs = [dequant[2][0][:, b : b + 1] for b in range(blocks)]
        mixed = mix_experts(pre, ids, weights, downs)
        mixed = lax.psum_scatter(mixed, "roll", scatter_dimension=0, tiled=True)
        outs = tuple(outs) + (mixed.astype(jnp.bfloat16),)
    return tuple(out[None] for out in outs[:3]) + (outs[3],)


def solution(mesh):
    in_specs = (
        P(None, "roll", "train"),
        P(None, "roll", "train"),
        P(None, "roll", "train"),
        P("roll", None),
        P("roll", None),
        P("roll", None),
        P(),
    )
    out_specs = (
        P("roll", None, "train", None),
        P("roll", None, "train", None),
        P("roll", None, "train", None),
        P("roll", "train"),
    )
    return jax.shard_map(
        per_device, mesh=mesh, in_specs=in_specs, out_specs=out_specs, check_vma=False
    )
```

```python
import functools

import jax
import jax.numpy as jnp
from jax import lax
from jax.experimental import pallas as pl
from jax.experimental.pallas import tpu as pltpu
from jax.sharding import PartitionSpec as P

BLOCK = 128
CORES = 2
VMEM_BYTES = 48 * 1024 * 1024
LIGHT = pl.CostEstimate(flops=1, bytes_accessed=1, transcendentals=0)


def any_spec():
    return pl.BlockSpec(memory_space=pl.ANY)


def smem_spec():
    return pl.BlockSpec(memory_space=pltpu.SMEM)


def quantize_kernel(trains, x_ref, *refs):
    q_ref, d_ref = refs[-2:]
    rows = BLOCK // trains
    features = x_ref.shape[-1]
    for col in range(features // BLOCK):
        cols = slice(col * BLOCK, (col + 1) * BLOCK)
        block = x_ref[0, :, cols]
        peak = jnp.max(jnp.max(jnp.abs(block), axis=0, keepdims=True), axis=1, keepdims=True)
        scale = peak.astype(jnp.bfloat16).astype(jnp.float32)
        quant = (block * (1.0 / scale)).astype(jnp.bfloat16)
        q_ref[:, 0, 0, :, cols] = quant.reshape(trains, rows, BLOCK)
        d_ref[0, 0, :, cols] = (quant.astype(jnp.float32) * scale).astype(jnp.bfloat16)


def quantize(master, first, count, trains, after=()):
    experts, _, features = master.shape
    rows = BLOCK // trains
    return pl.pallas_call(
        functools.partial(quantize_kernel, trains),
        grid=(experts, count),
        in_specs=[pl.BlockSpec((1, BLOCK, features), lambda e, b: (e, first + b, 0))]
        + [any_spec()] * len(after),
        out_specs=[
            pl.BlockSpec((trains, 1, 1, rows, features), lambda e, b: (0, e, b, 0, 0)),
            pl.BlockSpec((1, 1, BLOCK, features), lambda e, b: (e, b, 0, 0)),
        ],
        out_shape=[
            jax.ShapeDtypeStruct((trains, experts, count, rows, features), jnp.bfloat16),
            jax.ShapeDtypeStruct((experts, count, BLOCK, features), jnp.bfloat16),
        ],
        compiler_params=pltpu.CompilerParams(vmem_limit_bytes=VMEM_BYTES),
        cost_estimate=LIGHT,
        name="quantize",
    )(master, *after)


def start_choice(plan_ref, arrays, choice, target, sem):
    tests, array, (kind, n) = choice
    ref = arrays[array]
    if kind == "is":
        view = ref.at[n]
    elif kind == "at":
        view = ref.at[plan_ref[n]]
    else:
        view = ref.at[:, plan_ref[n]]
    hit = None
    for place, value in tests:
        test = plan_ref[place] == value
        hit = test if hit is None else hit & test

    def go():
        pltpu.make_async_copy(view, target, sem).start()

    if hit is None:
        go()
    else:
        pl.when(hit)(go)


def pack_kernel(pieces, n_in, plan_ref, *refs):
    arrays = refs[:n_in]
    out, held, sem_in, sem_out = refs[-4:]
    for n, choices in enumerate(pieces):
        for choice in choices:
            start_choice(plan_ref, arrays, choice, held.at[n], sem_in.at[n])
    for n in range(len(pieces)):
        pltpu.make_async_copy(held.at[n], held.at[n], sem_in.at[n]).wait()
        pltpu.make_async_copy(held.at[n], out.at[n], sem_out.at[n]).start()
    for n in range(len(pieces)):
        pltpu.make_async_copy(held.at[n], out.at[n], sem_out.at[n]).wait()


class Arrays:
    def __init__(self):
        self.items = []

    def add(self, array):
        for n, item in enumerate(self.items):
            if item is array:
                return n
        self.items.append(array)
        return len(self.items) - 1


def number_choices(pieces, arrays):
    return [[(tests, arrays.add(a), index) for tests, a, index in choices] for choices in pieces]


def pack(plan, shape, pieces, after=()):
    arrays = Arrays()
    pieces = number_choices(pieces, arrays)
    n_in = len(arrays.items)
    size = len(pieces)
    for dim in shape:
        size *= dim
    operands = arrays.items + list(after)
    return pl.pallas_call(
        functools.partial(pack_kernel, pieces, n_in),
        in_specs=[smem_spec()] + [any_spec()] * len(operands),
        out_specs=any_spec(),
        out_shape=jax.ShapeDtypeStruct((len(pieces),) + shape, jnp.bfloat16),
        scratch_shapes=[
            pltpu.VMEM((len(pieces),) + shape, jnp.bfloat16),
            pltpu.SemaphoreType.DMA((len(pieces),)),
            pltpu.SemaphoreType.DMA((len(pieces),)),
        ],
        compiler_params=pltpu.CompilerParams(vmem_limit_bytes=VMEM_BYTES),
        cost_estimate=LIGHT,
        name="pack",
    )(plan, *operands)


def place_kernel(pieces, sources, first, blocks, n_in, plan_ref, *refs):
    arrays = refs[:n_in]
    out, mark, held, sem_in, sem_out = refs[-5:]
    trains, count, _, features = held.shape[1:]
    for n, choices in enumerate(pieces):
        for choice in choices:
            start_choice(plan_ref, arrays, choice, held.at[n], sem_in.at[n])
    mark[...] = jnp.zeros_like(mark)
    stores = []
    for n in range(len(pieces)):
        pltpu.make_async_copy(held.at[n], held.at[n], sem_in.at[n]).wait()
        start = plan_ref[sources[n]] * blocks + first
        for part in range(trains):
            store = pltpu.make_async_copy(
                held.at[n, part],
                out.at[pl.ds(start, count), :, pl.ds(part * features, features)],
                sem_out.at[n, part],
            )
            store.start()
            stores.append(store)
    for store in stores:
        store.wait()


def place_pieces(plan, shape, owners, pieces, sources, first, blocks, out, after=()):
    trains, count, rows, features = shape
    arrays = Arrays()
    pieces = number_choices(pieces, arrays)
    n_in = len(arrays.items)
    operands = arrays.items + list(after) + ([] if out is None else [out])
    return pl.pallas_call(
        functools.partial(place_kernel, pieces, sources, first, blocks, n_in),
        in_specs=[smem_spec()] + [any_spec()] * len(operands),
        out_specs=[any_spec(), pl.BlockSpec(memory_space=pltpu.VMEM)],
        out_shape=[
            jax.ShapeDtypeStruct((owners * blocks, rows, trains * features), jnp.bfloat16),
            jax.ShapeDtypeStruct((8, BLOCK), jnp.float32),
        ],
        scratch_shapes=[
            pltpu.VMEM((len(pieces),) + shape, jnp.bfloat16),
            pltpu.SemaphoreType.DMA((len(pieces),)),
            pltpu.SemaphoreType.DMA((len(pieces), trains)),
        ],
        input_output_aliases={} if out is None else {len(operands): 0},
        compiler_params=pltpu.CompilerParams(vmem_limit_bytes=VMEM_BYTES),
        cost_estimate=LIGHT,
        name="place_pieces",
    )(plan, *operands)


def count_distinct(placement, experts, owners):
    expert_range = jnp.arange(experts, dtype=jnp.int32)
    half = owners // 2
    held = placement[None, :] == expert_range[:, None]
    sides = [jnp.any(held[:, :half], axis=1), jnp.any(held[:, half:], axis=1)]
    return jnp.maximum(*[jnp.sum(side.astype(jnp.int32)) for side in sides])


def make_plan(placement, experts, owners):
    me = lax.axis_index("roll")
    chip, core = me // CORES, me % CORES
    side = chip // 2
    inner = ((chip == 1) | (chip == 2)).astype(jnp.int32)
    expert_range = jnp.arange(experts, dtype=jnp.int32)
    owner_range = jnp.arange(owners, dtype=jnp.int32)
    owner_side = owner_range // (owners // 2)

    def ranks(on_side):
        held = (placement[None, :] == expert_range[:, None]) & (owner_side == on_side)[None, :]
        need = jnp.any(held, axis=1).astype(jnp.int32)
        ahead = (need[None, :] > need[:, None]) | (
            (need[None, :] == need[:, None]) & (expert_range[None, :] < expert_range[:, None])
        )
        return jnp.sum(ahead.astype(jnp.int32), axis=1)

    here, there = ranks(side), ranks(1 - side)
    send = jnp.sum(
        jnp.where(there[:, None] == expert_range[None, :], expert_range[:, None], 0), axis=0
    )

    def expert_of(owner):
        return jnp.sum(jnp.where(owner_range == owner, placement, 0))

    def rank_of(table, expert):
        return jnp.sum(jnp.where(expert_range == expert, table, 0))

    outer = 3 * side
    own, mate = expert_of(me), expert_of(chip * CORES + 1 - core)
    out0, out1 = expert_of(outer * CORES), expert_of(outer * CORES + 1)
    chip_of = [chip, 1 + 4 * side - chip, 2 - side, 3 - 3 * side]
    entries = {
        "inner": inner,
        "core": core,
        "own": own,
        "mate": mate,
        "out0": out0,
        "out1": out1,
        "here_own": rank_of(here, own),
        "here_mate": rank_of(here, mate),
        "here_out0": rank_of(here, out0),
        "here_out1": rank_of(here, out1),
        "there_own": rank_of(there, own),
        "there_mate": rank_of(there, mate),
    }
    for n, source in enumerate(chip_of):
        entries[f"from_own{n}"] = source * CORES + core
        entries[f"from_mate{n}"] = source * CORES + 1 - core
    places = {name: experts + n for n, name in enumerate(entries)}
    for slot in range(experts):
        places[f"send{slot}"] = slot
    plan = jnp.concatenate((send, jnp.stack([v.astype(jnp.int32) for v in entries.values()])))
    return plan, places


def line_schedule(chunks, experts, cap):
    head = min(2, chunks)
    middle = [("own", c) for c in range(head)]
    middle += [("far", c) for c in range(chunks)]
    middle += [("own", c) for c in range(head, chunks)]
    inwards = [[("far", c, s) for s in range(cap)] for c in range(chunks)]
    rest = [("near", c, s) for c in range(chunks) for s in range(cap, experts)]
    inwards += [rest[i : i + cap] for i in range(0, len(rest), cap)]
    fresh = [("x", c, i) for c in range(chunks) for i in range(CORES)]
    relayed = [(n + 2, (kind, c, i)) for n, (kind, c) in enumerate(middle) for i in range(CORES)]
    outwards = []
    n = 0
    while fresh or relayed or n < max(len(middle), len(inwards)):
        now = []
        while relayed and relayed[0][0] <= n and len(now) < cap:
            now.append(relayed.pop(0)[1])
        while fresh and fresh[0][1] <= n and len(now) < cap:
            now.append(fresh.pop(0))
        outwards.append(now)
        n += 1
    return middle, inwards, outwards


def link_pairs(chip_pairs, swap_chips=(), cross=False):
    pairs = []
    for core in range(CORES):
        for a, b in chip_pairs:
            pairs.append((a * CORES + core, b * CORES + (1 - core if cross else core)))
        for chip in swap_chips:
            pairs.append((chip * CORES + core, chip * CORES + 1 - core))
    return pairs


EDGES = ((0, 1), (1, 0), (2, 3), (3, 2))


def line_exchange(masters, begun, plan, places, routed, trains, owners, cap):
    experts, hidden_rows, features = masters[0].shape
    blocks = hidden_rows // BLOCK
    shape = (trains, 1, BLOCK // trains, features)
    chunks = [(m, b) for m in range(3) for b in range(blocks)]
    middle, inwards, outwards = line_schedule(len(chunks), experts, cap)
    rounds = len(outwards)
    edge_pairs = link_pairs(EDGES)
    cross_pairs = link_pairs(EDGES, cross=True)
    middle_pairs = link_pairs([(1, 2), (2, 1)], swap_chips=(0, 3))
    swap_pairs = link_pairs([], swap_chips=range(4))
    is_inner, is_outer = (places["inner"], 1), (places["inner"], 0)
    on_core = [(places["core"], core) for core in range(CORES)]
    xs, dequant = {}, {}
    got_edge, got_middle, where = {}, {}, {}
    last = [begun[0][0]]

    def packed(pieces):
        last[0] = pack(plan, shape, pieces, (last[0],))
        return last[0]

    def exchange_train(c, quant):
        xs[c] = lax.all_to_all(quant, "train", split_axis=0, concat_axis=0, tiled=True)

    def prepare(c):
        m, b = chunks[c]
        quant, dequant[c] = quantize(masters[m], b, 1, trains, (last[0],))
        last[0] = quant
        exchange_train(c, quant)

    xs[0], dequant[0] = begun[0]
    quant, dequant[1] = begun[1]
    exchange_train(1, quant)

    crossed = [n >= len(middle) for n in range(rounds)]
    ready = {(c, 0): 0 for c in range(len(chunks))}
    ready_to_swap = dict(ready)

    def note(c, position, n, swap=True):
        ready[c, position] = max(ready.get((c, position), 0), n)
        if swap:
            ready_to_swap[c, position] = max(ready_to_swap.get((c, position), 0), n)

    for n, (kind, c) in enumerate(middle):
        note(c, 2 if kind == "own" else 3, n)
    for n, pieces in enumerate(inwards):
        for _, c, _ in pieces:
            note(c, 1, n)
    for n, pieces in enumerate(outwards):
        for kind, c, _ in pieces:
            note(c, {"x": 1, "own": 2, "far": 3}[kind], n, not crossed[n])

    def find(c, position, who):
        own = who == "own"
        if position == 0:
            return [((), xs[c], ("expert", places[who]))]
        choices = []
        if position == 1:
            for slot in range(experts):
                n, i = where["far" if slot < cap else "near", c, slot]
                test = (places[f"there_{who}"], slot)
                choices.append(((is_inner, test), got_edge[n], ("is", i)))
        else:
            got = got_middle["own" if position == 2 else "far", c]
            choices.append(((is_inner,), got, ("at", places[f"here_{who}"])))
        kind = {1: "x", 2: "own", 3: "far"}[position]
        for core in range(CORES):
            n, i = where["out", kind, c, core if own else 1 - core]
            if not crossed[n]:
                choices.append(((is_outer, on_core[core]), got_edge[n], ("is", i)))
        return choices

    def find_crossed(c, position, which):
        kind = {1: "x", 2: "own", 3: "far"}.get(position)
        n = where["out", kind, c, 0][0] if kind else 0
        return [((is_outer,), got_edge[n][which], ("is", 0))] if crossed[n] else []

    groups = []
    for c in range(len(chunks)):
        early = [p for p in range(4) if ready[c, p] < rounds - 4]
        late = [p for p in range(4) if p not in early]
        for positions in (early, late):
            if positions:
                groups.append((max(ready_to_swap[c, p] for p in positions), c, positions))
    groups.sort(key=lambda group: group[0])
    swapped, outs = {}, [None, None, None]

    def swap(group):
        _, c, positions = group
        pieces = []
        for p in positions:
            choices = find(c, p, "mate")
            if find_crossed(c, p, 0):
                choices.append(((is_outer,), xs[c], ("expert", places["own"])))
            pieces.append(choices)
        swapped[c, tuple(positions)] = lax.ppermute(packed(pieces), "roll", swap_pairs)

    def place(group):
        _, c, positions = group
        m, b = chunks[c]
        got = swapped[c, tuple(positions)]
        pieces = [find(c, p, "own") + find_crossed(c, p, 0) for p in positions]
        for n, p in enumerate(positions):
            crossing = find_crossed(c, p, 1)
            pieces.append([((is_inner,) if crossing else (), got, ("is", n))] + crossing)
        sources = [places[f"from_own{p}"] for p in positions]
        sources += [places[f"from_mate{p}"] for p in positions]
        outs[m], last[0] = place_pieces(
            plan, shape, owners, pieces, sources, b, blocks, outs[m], (last[0],)
        )

    tokens, ids, weights = routed
    state = {"pre": None}
    ups = 2 * blocks

    def decode(n):
        if n < ups:
            state["pre"] = pre_activations(
                tokens, ids, dequant[n], state["pre"], n, ups, (last[0],)
            )
            last[0] = state["pre"]
        if n == ups - 1:
            state["sum"] = lax.psum(state["pre"], "train")
        if n == ups + 3:
            down = [dequant[c] for c in range(ups, len(chunks))]
            last[0] = mix_experts(state["sum"], ids, weights, down, (last[0],))
            state["out"] = lax.psum_scatter(last[0], "roll", scatter_dimension=0, tiled=True)

    to_swap, to_place = list(groups), []
    for n in range(max(rounds, ups + 4)):
        if n < rounds:
            ins = inwards[n] if n < len(inwards) else []
            outs_now = outwards[n]
            spare = xs[min(n, len(chunks) - 1)]
            pieces = []
            for i in range(max(len(ins), len(outs_now))):
                choices = [((is_inner,), spare, ("expert", places["own"]))]
                if i < len(outs_now):
                    kind, c, core = outs_now[i]
                    where["out", kind, c, core] = (n, i)
                    if kind == "x":
                        choices = [((is_inner,), xs[c], ("expert", places[f"out{core}"]))]
                    else:
                        got, index = got_middle[kind, c], ("at", places[f"here_out{core}"])
                        choices = [((is_inner,), got, index)]
                if i < len(ins):
                    kind, c, slot = ins[i]
                    where[kind, c, slot] = (n, i)
                    choices.append(((is_outer,), xs[c], ("expert", places[f"send{slot}"])))
                else:
                    choices.append(((is_outer,), spare, ("expert", places["own"])))
                pieces.append(choices)
            if crossed[n]:
                got = []
                kind, c, _ = outs_now[0]
                for pairs, names in (
                    (edge_pairs, ("here_out0", "here_out1")),
                    (cross_pairs, ("here_out1", "here_out0")),
                ):
                    choices = [
                        ((is_inner, on_core[core]), got_middle[kind, c], ("at", places[names[core]]))
                        for core in range(CORES)
                    ]
                    choices.append(((is_outer,), spare, ("expert", places["own"])))
                    got.append(lax.ppermute(packed([choices]), "roll", pairs))
                got_edge[n] = got
            elif pieces:
                got_edge[n] = lax.ppermute(packed(pieces), "roll", edge_pairs)
            if n < len(middle):
                kind, c = middle[n]
                if kind == "own":
                    pieces = [[((), xs[c], ("expert", places[f"send{s}"]))] for s in range(cap)]
                    going = packed(pieces)
                else:
                    going = got_edge[where["far", c, 0][0]]
                got_middle[kind, c] = lax.ppermute(going, "roll", middle_pairs)
        if n + 2 < len(chunks):
            prepare(n + 2)
        decode(n)
        for group in list(to_place):
            if max(ready[group[1], p] for p in group[2]) <= n - 2:
                place(group)
                to_place.remove(group)
        while to_swap and to_swap[0][0] <= n - 2:
            to_place.append(to_swap.pop(0))
            swap(to_place[-1])
    for group in to_swap:
        swap(group)
    for group in to_place + to_swap:
        place(group)
    return tuple(outs) + (state["out"].astype(jnp.bfloat16),)


def direct_exchange(masters, placement, trains, owners):
    experts, hidden_rows, features = masters[0].shape
    blocks = hidden_rows // BLOCK
    rows = BLOCK // trains
    outs, dequant = [], []
    for master in masters:
        quant, restored = quantize(master, 0, blocks, trains)
        dequant.append([restored])
        x = lax.all_to_all(quant, "train", split_axis=0, concat_axis=0, tiled=True)
        x = jnp.transpose(x, (1, 2, 3, 0, 4)).reshape(experts, blocks, rows, trains * features)
        picked = jnp.take(x, placement, axis=0)
        got = lax.all_to_all(picked, "roll", split_axis=0, concat_axis=0, tiled=True)
        outs.append(got.reshape(owners * blocks, rows, trains * features))
    return outs, dequant


def pre_activation_kernel(experts, top, tok_ref, ids_ref, w_ref, *refs):
    out_ref = refs[-1]
    features = tok_ref.shape[1]
    weights = w_ref[...].reshape(experts * BLOCK, features)
    pre = lax.dot_general(
        tok_ref[...], weights, (((1,), (1,)), ((), ())), preferred_element_type=jnp.float32
    )
    for k in range(top):
        total = jnp.zeros((pre.shape[0], BLOCK), jnp.float32)
        for expert in range(experts):
            part = pre[:, expert * BLOCK : (expert + 1) * BLOCK]
            total = total + jnp.where(ids_ref[:, k : k + 1] == expert, part, 0.0)
        out_ref[:, k * BLOCK : (k + 1) * BLOCK] = total


def pre_activations(tokens, ids, restored, out, column, columns, after=()):
    count, features = tokens.shape
    experts, top = restored.shape[0], ids.shape[1]
    tile = min(count, 2 * BLOCK)
    operands = [tokens, ids, restored] + list(after) + ([] if out is None else [out])
    return pl.pallas_call(
        functools.partial(pre_activation_kernel, experts, top),
        grid=(count // tile,),
        in_specs=[
            pl.BlockSpec((tile, features), lambda i: (i, 0)),
            pl.BlockSpec((tile, top), lambda i: (i, 0)),
            pl.BlockSpec(restored.shape, lambda i: (0, 0, 0, 0)),
        ]
        + [any_spec()] * (len(operands) - 3),
        out_specs=pl.BlockSpec((tile, top * BLOCK), lambda i: (i, column)),
        out_shape=jax.ShapeDtypeStruct((count, columns * top * BLOCK), jnp.float32),
        input_output_aliases={} if out is None else {len(operands) - 1: 0},
        compiler_params=pltpu.CompilerParams(vmem_limit_bytes=VMEM_BYTES),
        cost_estimate=LIGHT,
        name="pre_activations",
    )(*operands)


def mix_kernel(experts, top, blocks, pre_ref, ids_ref, weights_ref, *refs):
    downs, out_ref = refs[:blocks], refs[-1]
    width = top * BLOCK
    hidden = {}
    for b in range(blocks):
        for k in range(top):
            start = b * width + k * BLOCK
            gate = pre_ref[:, start : start + BLOCK]
            up = pre_ref[:, blocks * width + start : blocks * width + start + BLOCK]
            value = gate / (1.0 + jnp.exp(-gate)) * up
            hidden[b, k] = value.astype(jnp.bfloat16).astype(jnp.float32)
    total = jnp.zeros(out_ref.shape, jnp.float32)
    for expert in range(experts):
        weight = jnp.zeros((out_ref.shape[0], 1), jnp.float32)
        for k in range(top):
            weight = weight + jnp.where(
                ids_ref[:, k : k + 1] == expert, weights_ref[:, k : k + 1], 0.0
            )
        value = jnp.zeros(out_ref.shape, jnp.float32)
        for b in range(blocks):
            routed = jnp.zeros((out_ref.shape[0], BLOCK), jnp.float32)
            for k in range(top):
                routed = routed + jnp.where(ids_ref[:, k : k + 1] == expert, hidden[b, k], 0.0)
            value = value + jnp.dot(
                routed.astype(jnp.bfloat16), downs[b][expert, 0], preferred_element_type=jnp.float32
            )
        total = total + weight * value
    out_ref[...] = total


def mix_experts(pre, ids, weights, downs, after=()):
    count, top = ids.shape
    experts, _, _, features = downs[0].shape
    blocks = len(downs)
    tile = min(count, BLOCK)
    operands = [pre, ids, weights] + list(downs) + list(after)
    return pl.pallas_call(
        functools.partial(mix_kernel, experts, top, blocks),
        grid=(count // tile,),
        in_specs=[
            pl.BlockSpec((tile, pre.shape[1]), lambda i: (i, 0)),
            pl.BlockSpec((tile, top), lambda i: (i, 0)),
            pl.BlockSpec((tile, top), lambda i: (i, 0)),
        ]
        + [pl.BlockSpec(down.shape, lambda i: (0, 0, 0, 0)) for down in downs]
        + [any_spec()] * len(after),
        out_specs=pl.BlockSpec((tile, features), lambda i: (i, 0)),
        out_shape=jax.ShapeDtypeStruct((count, features), jnp.float32),
        compiler_params=pltpu.CompilerParams(vmem_limit_bytes=VMEM_BYTES),
        cost_estimate=LIGHT,
        name="mix_experts",
    )(*operands)


def gather_tokens(tokens, expert_ids, gate_weights, features):
    mine = lax.dynamic_slice_in_dim(tokens, lax.axis_index("train") * features, features, axis=1)
    top = expert_ids.shape[1]
    high = lax.reduce_precision(gate_weights, 8, 7)
    middle = lax.reduce_precision(gate_weights - high, 8, 7)
    low = gate_weights - high - middle
    beside = jnp.concatenate((expert_ids.astype(jnp.float32), high, middle, low), axis=1)
    beside = jnp.pad(beside, ((0, 0), (0, BLOCK - 4 * top))).astype(jnp.bfloat16)
    every = lax.all_gather(jnp.concatenate((mine, beside), axis=1), "roll", axis=0, tiled=True)
    side = every[:, features : features + 4 * top].astype(jnp.float32)
    ids = side[:, :top].astype(jnp.int32)
    weights = side[:, top : 2 * top] + side[:, 2 * top : 3 * top] + side[:, 3 * top :]
    return every[:, :features], ids, weights


def per_device(master_gate, master_up, master_down, tokens, expert_ids, gate_weights, placement):
    trains = lax.axis_size("train")
    owners = lax.axis_size("roll")
    experts, hidden_rows, features = master_gate.shape
    blocks = hidden_rows // BLOCK
    masters = (master_gate, master_up, master_down)
    if owners // CORES == 4:
        chunks = [(m, b) for m in range(3) for b in range(blocks)]
        begun = [quantize(masters[m], b, 1, trains) for m, b in chunks[:2]]
        first = lax.all_to_all(begun[0][0], "train", split_axis=0, concat_axis=0, tiled=True)
        begun = ((first, begun[0][1]), tuple(begun[1]))
        routed = gather_tokens(tokens, expert_ids, gate_weights, features)
        plan, places = make_plan(placement, experts, owners)
        most = min(experts, owners // 2)

        def branch(cap, masters, begun, plan, routed):
            return line_exchange(masters, begun, plan, places, routed, trains, owners, cap)

        tight = count_distinct(placement, experts, owners) <= most - 1
        outs = lax.cond(
            tight,
            functools.partial(branch, most - 1),
            functools.partial(branch, most),
            masters,
            begun,
            plan,
            routed,
        )
    else:
        routed = gather_tokens(tokens, expert_ids, gate_weights, features)
        outs, dequant = direct_exchange(masters, placement, trains, owners)
        tokens, ids, weights = routed
        pre = None
        for n in range(2 * blocks):
            m, b = n // blocks, n % blocks
            pre = pre_activations(
                tokens, ids, dequant[m][0][:, b : b + 1], pre, n, 2 * blocks
            )
        pre = lax.psum(pre, "train")
        downs = [dequant[2][0][:, b : b + 1] for b in range(blocks)]
        mixed = mix_experts(pre, ids, weights, downs)
        mixed = lax.psum_scatter(mixed, "roll", scatter_dimension=0, tiled=True)
        outs = tuple(outs) + (mixed.astype(jnp.bfloat16),)
    return tuple(out[None] for out in outs[:3]) + (outs[3],)


def solution(mesh):
    in_specs = (
        P(None, "roll", "train"),
        P(None, "roll", "train"),
        P(None, "roll", "train"),
        P("roll", None),
        P("roll", None),
        P("roll", None),
        P(),
    )
    out_specs = (
        P("roll", None, "train", None),
        P("roll", None, "train", None),
        P("roll", None, "train", None),
        P("roll", "train"),
    )
    return jax.shard_map(
        per_device, mesh=mesh, in_specs=in_specs, out_specs=out_specs, check_vma=False
    )
```

```python
import functools

import jax
import jax.numpy as jnp
from jax import lax
from jax.experimental import pallas as pl
from jax.experimental.pallas import tpu as pltpu
from jax.sharding import PartitionSpec as P

BLOCK = 128
CORES = 2
VMEM_BYTES = 48 * 1024 * 1024
LIGHT = pl.CostEstimate(flops=1, bytes_accessed=1, transcendentals=0)


def any_spec():
    return pl.BlockSpec(memory_space=pl.ANY)


def smem_spec():
    return pl.BlockSpec(memory_space=pltpu.SMEM)


def quantize_kernel(trains, x_ref, *refs):
    q_ref, d_ref = refs[-2:]
    rows = BLOCK // trains
    features = x_ref.shape[-1]
    for col in range(features // BLOCK):
        cols = slice(col * BLOCK, (col + 1) * BLOCK)
        block = x_ref[0, :, cols]
        peak = jnp.max(jnp.max(jnp.abs(block), axis=0, keepdims=True), axis=1, keepdims=True)
        scale = peak.astype(jnp.bfloat16).astype(jnp.float32)
        quant = (block * (1.0 / scale)).astype(jnp.bfloat16)
        q_ref[:, 0, 0, :, cols] = quant.reshape(trains, rows, BLOCK)
        d_ref[0, 0, :, cols] = (quant.astype(jnp.float32) * scale).astype(jnp.bfloat16)


def quantize(master, trains, slots, base, into=None, after=()):
    experts, hidden_rows, features = master.shape
    blocks = hidden_rows // BLOCK
    rows = BLOCK // trains
    operands = [master] + list(after) + ([] if into is None else [into])
    return pl.pallas_call(
        functools.partial(quantize_kernel, trains),
        grid=(experts, blocks),
        in_specs=[pl.BlockSpec((1, BLOCK, features), lambda e, b: (e, b, 0))]
        + [any_spec()] * (len(operands) - 1),
        out_specs=[
            pl.BlockSpec((trains, 1, 1, rows, features), lambda e, b: (0, base + e, b, 0, 0)),
            pl.BlockSpec((1, 1, BLOCK, features), lambda e, b: (e, b, 0, 0)),
        ],
        out_shape=[
            jax.ShapeDtypeStruct((trains, slots, blocks, rows, features), jnp.bfloat16),
            jax.ShapeDtypeStruct((experts, blocks, BLOCK, features), jnp.bfloat16),
        ],
        input_output_aliases={} if into is None else {len(operands) - 1: 0},
        compiler_params=pltpu.CompilerParams(vmem_limit_bytes=VMEM_BYTES),
        cost_estimate=LIGHT,
        name="quantize",
    )(*operands)


def start_choice(plan_ref, arrays, choice, target, sem):
    tests, array, (kind, n, *more) = choice
    ref = arrays[array]
    if kind == "is":
        view = ref.at[n]
    elif kind == "at":
        view = ref.at[plan_ref[n]]
    else:
        view = ref.at[:, plan_ref[n] + more[0], pl.ds(more[1], 1)]
    hit = None
    for place, value in tests:
        test = plan_ref[place] == value
        hit = test if hit is None else hit & test

    def go():
        pltpu.make_async_copy(view, target, sem).start()

    if hit is None:
        go()
    else:
        pl.when(hit)(go)


def pack_kernel(pieces, n_in, plan_ref, *refs):
    arrays = refs[:n_in]
    out, held, sem_in, sem_out = refs[-4:]
    for n, choices in enumerate(pieces):
        for choice in choices:
            start_choice(plan_ref, arrays, choice, held.at[n], sem_in.at[n])
    for n in range(len(pieces)):
        pltpu.make_async_copy(held.at[n], held.at[n], sem_in.at[n]).wait()
        pltpu.make_async_copy(held.at[n], out.at[n], sem_out.at[n]).start()
    for n in range(len(pieces)):
        pltpu.make_async_copy(held.at[n], out.at[n], sem_out.at[n]).wait()


class Arrays:
    def __init__(self):
        self.items = []

    def add(self, array):
        for n, item in enumerate(self.items):
            if item is array:
                return n
        self.items.append(array)
        return len(self.items) - 1


def number_choices(pieces, arrays):
    return [[(tests, arrays.add(a), index) for tests, a, index in choices] for choices in pieces]


def pack(plan, shape, pieces, after=()):
    arrays = Arrays()
    pieces = number_choices(pieces, arrays)
    n_in = len(arrays.items)
    size = len(pieces)
    for dim in shape:
        size *= dim
    operands = arrays.items + list(after)
    return pl.pallas_call(
        functools.partial(pack_kernel, pieces, n_in),
        in_specs=[smem_spec()] + [any_spec()] * len(operands),
        out_specs=any_spec(),
        out_shape=jax.ShapeDtypeStruct((len(pieces),) + shape, jnp.bfloat16),
        scratch_shapes=[
            pltpu.VMEM((len(pieces),) + shape, jnp.bfloat16),
            pltpu.SemaphoreType.DMA((len(pieces),)),
            pltpu.SemaphoreType.DMA((len(pieces),)),
        ],
        compiler_params=pltpu.CompilerParams(vmem_limit_bytes=VMEM_BYTES),
        cost_estimate=LIGHT,
        name="pack",
    )(plan, *operands)


def place_kernel(pieces, sources, first, blocks, n_in, plan_ref, *refs):
    arrays = refs[:n_in]
    out, mark, held, sem_in, sem_out = refs[-5:]
    trains, count, _, features = held.shape[1:]
    for n, choices in enumerate(pieces):
        for choice in choices:
            start_choice(plan_ref, arrays, choice, held.at[n], sem_in.at[n])
    mark[...] = jnp.zeros_like(mark)
    stores = []
    for n in range(len(pieces)):
        pltpu.make_async_copy(held.at[n], held.at[n], sem_in.at[n]).wait()
        start = plan_ref[sources[n]] * blocks + first
        for part in range(trains):
            store = pltpu.make_async_copy(
                held.at[n, part],
                out.at[pl.ds(start, count), :, pl.ds(part * features, features)],
                sem_out.at[n, part],
            )
            store.start()
            stores.append(store)
    for store in stores:
        store.wait()


def place_pieces(plan, shape, owners, pieces, sources, first, blocks, out, after=()):
    trains, count, rows, features = shape
    arrays = Arrays()
    pieces = number_choices(pieces, arrays)
    n_in = len(arrays.items)
    operands = arrays.items + list(after) + ([] if out is None else [out])
    return pl.pallas_call(
        functools.partial(place_kernel, pieces, sources, first, blocks, n_in),
        in_specs=[smem_spec()] + [any_spec()] * len(operands),
        out_specs=[any_spec(), pl.BlockSpec(memory_space=pltpu.VMEM)],
        out_shape=[
            jax.ShapeDtypeStruct((owners * blocks, rows, trains * features), jnp.bfloat16),
            jax.ShapeDtypeStruct((8, BLOCK), jnp.float32),
        ],
        scratch_shapes=[
            pltpu.VMEM((len(pieces),) + shape, jnp.bfloat16),
            pltpu.SemaphoreType.DMA((len(pieces),)),
            pltpu.SemaphoreType.DMA((len(pieces), trains)),
        ],
        input_output_aliases={} if out is None else {len(operands): 0},
        compiler_params=pltpu.CompilerParams(vmem_limit_bytes=VMEM_BYTES),
        cost_estimate=LIGHT,
        name="place_pieces",
    )(plan, *operands)


def count_distinct(placement, experts, owners):
    expert_range = jnp.arange(experts, dtype=jnp.int32)
    half = owners // 2
    held = placement[None, :] == expert_range[:, None]
    sides = [jnp.any(held[:, :half], axis=1), jnp.any(held[:, half:], axis=1)]
    return jnp.maximum(*[jnp.sum(side.astype(jnp.int32)) for side in sides])


def make_plan(placement, experts, owners):
    me = lax.axis_index("roll")
    chip, core = me // CORES, me % CORES
    side = chip // 2
    inner = ((chip == 1) | (chip == 2)).astype(jnp.int32)
    expert_range = jnp.arange(experts, dtype=jnp.int32)
    owner_range = jnp.arange(owners, dtype=jnp.int32)
    owner_side = owner_range // (owners // 2)

    def ranks(on_side):
        held = (placement[None, :] == expert_range[:, None]) & (owner_side == on_side)[None, :]
        need = jnp.any(held, axis=1).astype(jnp.int32)
        ahead = (need[None, :] > need[:, None]) | (
            (need[None, :] == need[:, None]) & (expert_range[None, :] < expert_range[:, None])
        )
        return jnp.sum(ahead.astype(jnp.int32), axis=1)

    here, there = ranks(side), ranks(1 - side)
    send = jnp.sum(
        jnp.where(there[:, None] == expert_range[None, :], expert_range[:, None], 0), axis=0
    )

    def expert_of(owner):
        return jnp.sum(jnp.where(owner_range == owner, placement, 0))

    def rank_of(table, expert):
        return jnp.sum(jnp.where(expert_range == expert, table, 0))

    outer = 3 * side
    own, mate = expert_of(me), expert_of(chip * CORES + 1 - core)
    out0, out1 = expert_of(outer * CORES), expert_of(outer * CORES + 1)
    chip_of = [chip, 1 + 4 * side - chip, 2 - side, 3 - 3 * side]
    entries = {
        "inner": inner,
        "core": core,
        "chip": chip,
        "side": side,
        "own": own,
        "mate": mate,
        "out0": out0,
        "out1": out1,
        "here_own": rank_of(here, own),
        "here_mate": rank_of(here, mate),
        "here_out0": rank_of(here, out0),
        "here_out1": rank_of(here, out1),
        "there_own": rank_of(there, own),
        "there_mate": rank_of(there, mate),
    }
    for n, source in enumerate(chip_of):
        entries[f"from_own{n}"] = source * CORES + core
        entries[f"from_mate{n}"] = source * CORES + 1 - core
    places = {name: experts + n for n, name in enumerate(entries)}
    for slot in range(experts):
        places[f"send{slot}"] = slot
    plan = jnp.concatenate((send, jnp.stack([v.astype(jnp.int32) for v in entries.values()])))
    return plan, places


def line_schedule(opens, experts, cap, ride_from):
    chunks = range(len(opens))
    own, far = list(chunks), list(chunks)
    fresh = [("x", c, i) for c in chunks for i in range(CORES)]
    near = [("near", c, s) for c in chunks for s in range(cap, experts)]
    middle, inwards, outwards = [], [], []
    arrived, relayed, ride_due = [], [], {"in": ride_from}
    n = 0
    while own or arrived or far or near or fresh or relayed or ride_due:
        across, ins, outs = [], [], []
        if arrived and arrived[0][0] <= n:
            c = arrived.pop(0)[1]
            across = [("far", c, s) for s in range(cap)]
        elif own and opens[own[0]] <= n:
            c = own.pop(0)
            across = [("own", c, s) for s in range(cap)]
        if across:
            relayed += [(n + 2, (across[0][0], c, i)) for i in range(CORES)]
        if ride_due.get("across", n + 1) <= n and (not across or across[0][0] == "own"):
            across.append(("ride", 0, 0))
            del ride_due["across"]
            ride_due["out"] = n + 2
        if far and opens[far[0]] <= n:
            c = far.pop(0)
            ins = [("far", c, s) for s in range(cap)]
            arrived.append((n + 2, c))
        else:
            if ride_due.get("in", n + 1) <= n:
                ins = [("ride", 0, 0), ("ride", 0, 1)]
                del ride_due["in"]
                ride_due["across"] = n + 2
            while near and opens[near[0][1]] <= n and len(ins) < cap:
                ins.append(near.pop(0))
        while relayed and relayed[0][0] <= n and len(outs) < cap:
            outs.append(relayed.pop(0)[1])
        if ride_due.get("out", n + 1) <= n and len(outs) < cap:
            outs.append(("ride", 0, 0))
            del ride_due["out"]
        while fresh and opens[fresh[0][1]] <= n and len(outs) < cap:
            outs.append(fresh.pop(0))
        middle.append(across)
        inwards.append(ins)
        outwards.append(outs)
        n += 1
    return middle, inwards, outwards


def link_pairs(chip_pairs, swap_chips=(), cross=False):
    pairs = []
    for core in range(CORES):
        for a, b in chip_pairs:
            pairs.append((a * CORES + core, b * CORES + (1 - core if cross else core)))
        for chip in swap_chips:
            pairs.append((chip * CORES + core, chip * CORES + 1 - core))
    return pairs


EDGES = ((0, 1), (1, 0), (2, 3), (3, 2))


def line_exchange(x_first, quant_rest, pre, down, plan, places, ids, weights, shapes, cap):
    experts, blocks, trains, owners = shapes
    features = x_first.shape[-1]
    rows = BLOCK // trains
    shape = (trains, 1, rows, features)
    chunks = [(m, b) for m in range(3) for b in range(blocks)]
    count = len(chunks)
    opens = [0 if m == 0 else 3 for m, _ in chunks]
    middle, inwards, outwards = line_schedule(opens, experts, cap, 7)
    rounds = len(outwards)
    last_across = max(n for n in range(rounds) if middle[n])
    edge_pairs = link_pairs(EDGES)
    cross_pairs = link_pairs(EDGES, cross=True)
    middle_pairs = link_pairs([(1, 2), (2, 1)], swap_chips=(0, 3))
    swap_pairs = link_pairs([], swap_chips=range(4))
    is_inner, is_outer = (places["inner"], 1), (places["inner"], 0)
    on_core = [(places["core"], core) for core in range(CORES)]
    got_edge, got_middle, where = {}, {}, {}
    last = [x_first]

    x_rest = lax.all_to_all(quant_rest, "train", split_axis=0, concat_axis=0, tiled=True)

    def local(c, name):
        m, b = chunks[c]
        if m == 0:
            return x_first, ("expert", places[name], 0, b)
        return x_rest, ("expert", places[name], (m - 1) * experts, b)

    def packed(pieces, after=()):
        last[0] = pack(plan, shape, pieces, [last[0]] + list(after))
        return last[0]

    crossed = [n > last_across for n in range(rounds)]
    ready = {(c, 0): opens[c] for c in range(count)}
    ready_to_swap = dict(ready)

    def note(c, position, n, swap=True):
        ready[c, position] = max(ready.get((c, position), 0), n)
        if swap:
            ready_to_swap[c, position] = max(ready_to_swap.get((c, position), 0), n)

    from_kind = {"x": 1, "own": 2, "far": 3}
    kind_of = {position: kind for kind, position in from_kind.items()}
    for n in range(rounds):
        for i, piece in enumerate(middle[n]):
            where[("across",) + piece] = (n, i)
            if piece[0] != "ride":
                note(piece[1], 2 if piece[0] == "own" else 3, n)
        for i, piece in enumerate(inwards[n]):
            where[("in",) + piece] = (n, i)
            if piece[0] != "ride":
                note(piece[1], 1, n)
        for i, piece in enumerate(outwards[n]):
            where[("out",) + piece] = (n, i)
            if piece[0] != "ride":
                note(piece[1], from_kind[piece[0]], n, not crossed[n])

    def across(kind, c):
        return got_middle[where["across", kind, c, 0][0]]

    def find(c, position, who):
        if position == 0:
            return [((),) + local(c, who)]
        choices = []
        if position == 1:
            for slot in range(experts):
                n, i = where["in", "far" if slot < cap else "near", c, slot]
                test = (places[f"there_{who}"], slot)
                choices.append(((is_inner, test), got_edge[n], ("is", i)))
        else:
            got = across(kind_of[position], c)
            choices.append(((is_inner,), got, ("at", places[f"here_{who}"])))
        for core in range(CORES):
            n, i = where["out", kind_of[position], c, core if who == "own" else 1 - core]
            if not crossed[n]:
                choices.append(((is_outer, on_core[core]), got_edge[n], ("is", i)))
        return choices

    def find_crossed(c, position, which):
        if position == 0:
            return []
        n = where["out", kind_of[position], c, 0][0]
        return [((is_outer,), got_edge[n][which], ("is", 0))] if crossed[n] else []

    groups = []
    for c in range(count):
        early = [p for p in range(4) if ready[c, p] < rounds - 4]
        late = [p for p in range(4) if p not in early]
        for positions in (early, late):
            if positions:
                groups.append((max(ready_to_swap[c, p] for p in positions), c, positions))
    groups.sort(key=lambda group: group[0])
    swapped, outs = {}, [None, None, None]

    def swap(group):
        _, c, positions = group
        pieces = []
        for p in positions:
            choices = find(c, p, "mate")
            if find_crossed(c, p, 0):
                choices.append(((is_outer,),) + local(c, "own"))
            pieces.append(choices)
        swapped[c, tuple(positions)] = lax.ppermute(packed(pieces), "roll", swap_pairs)

    def place(group):
        _, c, positions = group
        m, b = chunks[c]
        got = swapped[c, tuple(positions)]
        pieces = [find(c, p, "own") + find_crossed(c, p, 0) for p in positions]
        for n, p in enumerate(positions):
            crossing = find_crossed(c, p, 1)
            pieces.append([((is_inner,) if crossing else (), got, ("is", n))] + crossing)
        sources = [places[f"from_own{p}"] for p in positions]
        sources += [places[f"from_mate{p}"] for p in positions]
        outs[m], last[0] = place_pieces(
            plan, shape, owners, pieces, sources, b, blocks, outs[m], (last[0],)
        )

    ride = {}
    summed = lax.psum(pre, "train")

    def ride_mix():
        ride["keep"], going = mix_experts(summed, ids, weights, down, plan, places, (last[0],))
        last[0] = ride["keep"]
        going = going.reshape((-1,) + shape)
        ride["swapped"] = lax.ppermute(going, "roll", swap_pairs)

    def ride_cores():
        got = ride["swapped"].reshape(-1, features)
        ride["sums"], going = sum_cores(plan, places, ride["keep"], got, (last[0],))
        last[0] = ride["sums"]
        ride["in"] = going.reshape((-1,) + shape)

    def ride_in():
        n, i = where["in", "ride", 0, 0]
        got = got_edge[n].reshape(-1, BLOCK, features)
        ride["inner"], going = sum_inwards(plan, places, ride["sums"], got, i, (last[0],))
        last[0] = ride["inner"]
        ride["across"] = going.reshape((-1,) + shape)

    def ride_across():
        n, i = where["across", "ride", 0, 0]
        got = got_middle[n].reshape(-1, BLOCK, features)
        ride["final"], going = sum_across(
            plan, places, ride["sums"], ride["inner"], got, i, (last[0],)
        )
        last[0] = ride["final"]
        ride["out"] = going.reshape((-1,) + shape)

    def ride_out():
        n, i = where["out", "ride", 0, 0]
        got = got_edge[n].reshape(-1, BLOCK, features)
        ride["mixed"] = sum_outwards(
            plan, places, ride["sums"], ride["final"], got, i, (last[0],)
        )
        last[0] = ride["mixed"]

    to_swap, to_place = list(groups), []
    for n in range(rounds):
        spare = lambda name: local(0, name)
        if middle[n]:
            if where.get(("across", "ride", 0, 0), (-1,))[0] == n:
                ride_in()
            pieces = []
            for kind, c, slot in middle[n]:
                if kind == "own":
                    pieces.append([((),) + local(c, f"send{slot}")])
                elif kind == "ride":
                    pieces.append([((), ride["across"], ("is", 0))])
                else:
                    m, i = where["in", kind, c, slot]
                    pieces.append([((), got_edge[m], ("is", i))])
            after = [got_middle[n - 2]] if n - 2 in got_middle else []
            got_middle[n] = lax.ppermute(packed(pieces, after), "roll", middle_pairs)
        if where["out", "ride", 0, 0][0] == n:
            ride_across()
        if crossed[n]:
            got = []
            kind, c, _ = outwards[n][0]
            for pairs, names in (
                (edge_pairs, ("here_out0", "here_out1")),
                (cross_pairs, ("here_out1", "here_out0")),
            ):
                choices = [
                    ((is_inner, on_core[core]), across(kind, c), ("at", places[names[core]]))
                    for core in range(CORES)
                ]
                choices.append(((is_outer,),) + spare("own"))
                got.append(lax.ppermute(packed([choices]), "roll", pairs))
            got_edge[n] = got
        else:
            pieces = []
            for i in range(max(len(inwards[n]), len(outwards[n]))):
                choices = [((is_inner,),) + spare("own"), ((is_outer,),) + spare("own")]
                if i < len(outwards[n]):
                    kind, c, core = outwards[n][i]
                    if kind == "x":
                        choices[0] = ((is_inner,),) + local(c, f"out{core}")
                    elif kind == "ride":
                        choices[0] = ((is_inner,), ride["out"], ("is", 0))
                    else:
                        index = ("at", places[f"here_out{core}"])
                        choices[0] = ((is_inner,), across(kind, c), index)
                if i < len(inwards[n]):
                    kind, c, slot = inwards[n][i]
                    if kind == "ride":
                        choices[1] = ((is_outer,), ride["in"], ("is", slot))
                    else:
                        choices[1] = ((is_outer,),) + local(c, f"send{slot}")
                pieces.append(choices)
            if pieces:
                after = [got_edge[n - 2]] if n - 2 in got_edge else []
                got_edge[n] = lax.ppermute(packed(pieces, after), "roll", edge_pairs)
        if n == 4:
            ride_mix()
        if n == 6:
            ride_cores()
        if n == where["out", "ride", 0, 0][0] + 2:
            ride_out()
        for group in list(to_place):
            if max(ready[group[1], p] for p in group[2]) <= n - 2:
                place(group)
                to_place.remove(group)
        while to_swap and to_swap[0][0] <= n - 2:
            to_place.append(to_swap.pop(0))
            swap(to_place[-1])
    if "mixed" not in ride:
        ride_out()
    for group in to_swap:
        swap(group)
    for group in to_place + to_swap:
        place(group)
    return tuple(outs) + (ride["mixed"],)


def direct_exchange(quants, placement, trains, owners):
    outs = []
    for quant in quants:
        _, experts, blocks, rows, features = quant.shape
        x = lax.all_to_all(quant, "train", split_axis=0, concat_axis=0, tiled=True)
        x = jnp.transpose(x, (1, 2, 3, 0, 4)).reshape(experts, blocks, rows, trains * features)
        picked = jnp.take(x, placement, axis=0)
        got = lax.all_to_all(picked, "roll", split_axis=0, concat_axis=0, tiled=True)
        outs.append(got.reshape(owners * blocks, rows, trains * features))
    return outs


def pre_activation_kernel(experts, top, tok_ref, ids_ref, w_ref, *refs):
    out_ref = refs[-1]
    features = tok_ref.shape[1]
    weights = w_ref[...].reshape(experts * BLOCK, features)
    pre = lax.dot_general(
        tok_ref[...], weights, (((1,), (1,)), ((), ())), preferred_element_type=jnp.float32
    )
    for k in range(top):
        total = jnp.zeros((pre.shape[0], BLOCK), jnp.float32)
        for expert in range(experts):
            part = pre[:, expert * BLOCK : (expert + 1) * BLOCK]
            total = total + jnp.where(ids_ref[:, k : k + 1] == expert, part, 0.0)
        out_ref[:, k * BLOCK : (k + 1) * BLOCK] = total


def pre_activations(tokens, ids, restored, block, out, column, columns, after=()):
    count, features = tokens.shape
    experts, top = restored.shape[0], ids.shape[1]
    tile = min(count, 2 * BLOCK)
    operands = [tokens, ids, restored] + list(after) + ([] if out is None else [out])
    return pl.pallas_call(
        functools.partial(pre_activation_kernel, experts, top),
        grid=(count // tile,),
        in_specs=[
            pl.BlockSpec((tile, features), lambda i: (i, 0)),
            pl.BlockSpec((tile, top), lambda i: (i, 0)),
            pl.BlockSpec((experts, 1, BLOCK, features), lambda i: (0, block, 0, 0)),
        ]
        + [any_spec()] * (len(operands) - 3),
        out_specs=pl.BlockSpec((tile, top * BLOCK), lambda i: (i, column)),
        out_shape=jax.ShapeDtypeStruct((count, columns * top * BLOCK), jnp.float32),
        input_output_aliases={} if out is None else {len(operands) - 1: 0},
        compiler_params=pltpu.CompilerParams(vmem_limit_bytes=VMEM_BYTES),
        cost_estimate=LIGHT,
        name="pre_activations",
    )(*operands)


def mix_rows(experts, top, blocks, pre_ref, ids_ref, weights_ref, down_ref):
    width = top * BLOCK
    count, features = ids_ref.shape[0], down_ref.shape[-1]
    hidden = {}
    for b in range(blocks):
        for k in range(top):
            start = b * width + k * BLOCK
            gate = pre_ref[:, start : start + BLOCK]
            up = pre_ref[:, blocks * width + start : blocks * width + start + BLOCK]
            value = gate / (1.0 + jnp.exp(-gate)) * up
            hidden[b, k] = value.astype(jnp.bfloat16).astype(jnp.float32)
    total = jnp.zeros((count, features), jnp.float32)
    for expert in range(experts):
        weight = jnp.zeros((count, 1), jnp.float32)
        for k in range(top):
            weight = weight + jnp.where(
                ids_ref[:, k : k + 1] == expert, weights_ref[:, k : k + 1], 0.0
            )
        value = jnp.zeros((count, features), jnp.float32)
        for b in range(blocks):
            routed = jnp.zeros((count, BLOCK), jnp.float32)
            for k in range(top):
                routed = routed + jnp.where(ids_ref[:, k : k + 1] == expert, hidden[b, k], 0.0)
            value = value + jnp.dot(
                routed.astype(jnp.bfloat16), down_ref[expert, b], preferred_element_type=jnp.float32
            )
        total = total + weight * value
    return total


def mix_kernel(sizes, pre_ref, ids_ref, weights_ref, down_ref, out_ref):
    out_ref[...] = mix_rows(*sizes, pre_ref, ids_ref, weights_ref, down_ref)


def mix_split_kernel(sizes, core, pre_ref, ids_ref, weights_ref, down_ref, plan_ref, *refs):
    keep_ref, send_ref = refs[-2:]
    total = mix_rows(*sizes, pre_ref, ids_ref, weights_ref, down_ref)
    half = total.shape[0] // CORES
    first = plan_ref[core] == 0
    keep_ref[0] = jnp.where(first, total[:half], total[half:])
    send_ref[...] = jnp.where(first, total[half:], total[:half]).astype(send_ref.dtype)


def mix_specs(pre, ids, down, tile):
    return [
        pl.BlockSpec((tile, pre.shape[1]), lambda i: (i, 0)),
        pl.BlockSpec((tile, ids.shape[1]), lambda i: (i, 0)),
        pl.BlockSpec((tile, ids.shape[1]), lambda i: (i, 0)),
        pl.BlockSpec(down.shape, lambda i: (0, 0, 0, 0)),
    ]


def mix_experts(pre, ids, weights, down, plan=None, places=None, after=()):
    count, top = ids.shape
    experts, blocks, _, features = down.shape
    sizes = (experts, top, blocks)
    tile = min(count, BLOCK)
    params = pltpu.CompilerParams(vmem_limit_bytes=VMEM_BYTES)
    if plan is None:
        return pl.pallas_call(
            functools.partial(mix_kernel, sizes),
            grid=(count // tile,),
            in_specs=mix_specs(pre, ids, down, tile),
            out_specs=pl.BlockSpec((tile, features), lambda i: (i, 0)),
            out_shape=jax.ShapeDtypeStruct((count, features), jnp.float32),
            compiler_params=params,
            cost_estimate=LIGHT,
            name="mix_experts",
        )(pre, ids, weights, down)
    half = tile // CORES
    return pl.pallas_call(
        functools.partial(mix_split_kernel, sizes, places["core"]),
        grid=(count // tile,),
        in_specs=mix_specs(pre, ids, down, tile) + [smem_spec()] + [any_spec()] * len(after),
        out_specs=[
            pl.BlockSpec((1, half, features), lambda i: (i, 0, 0)),
            pl.BlockSpec((half, features), lambda i: (i, 0)),
        ],
        out_shape=[
            jax.ShapeDtypeStruct((count // tile, half, features), jnp.float32),
            jax.ShapeDtypeStruct((count // CORES, features), jnp.bfloat16),
        ],
        compiler_params=params,
        cost_estimate=LIGHT,
        name="mix_experts",
    )(pre, ids, weights, down, plan, *after)


def sum_call(kernel, name, out_shape, plan, arrays, piece, after):
    vmem = pl.BlockSpec(memory_space=pltpu.VMEM)
    operands = [plan] + list(arrays)
    specs = [smem_spec()] + [vmem] * len(arrays)
    if piece is not None:
        array, first, number = piece
        operands += [array] * number
        for n in range(number):
            specs.append(
                pl.BlockSpec((1,) + array.shape[1:], lambda i, n=n: (first + n, 0, 0))
            )
    return pl.pallas_call(
        kernel,
        grid=(1,),
        in_specs=specs + [any_spec()] * len(after),
        out_specs=[vmem] * len(out_shape) if isinstance(out_shape, list) else vmem,
        out_shape=out_shape,
        compiler_params=pltpu.CompilerParams(vmem_limit_bytes=VMEM_BYTES),
        cost_estimate=LIGHT,
        name=name,
    )(*operands, *after)


def sum_cores_kernel(places, plan_ref, keep_ref, got_ref, *refs):
    sums_ref, send_ref = refs[-2:]
    chips, tokens, features = keep_ref.shape
    for chip in range(chips):
        rows = slice(chip * tokens, (chip + 1) * tokens)
        sums_ref[chip] = keep_ref[chip] + got_ref[rows, :].astype(jnp.float32)
    side, chip = plan_ref[places["side"]], plan_ref[places["chip"]]
    for n in range(2):
        send_ref[n * tokens : (n + 1) * tokens, :] = sums_ref[2 * (1 - side) + n].astype(
            send_ref.dtype
        )
    partner = sums_ref[1 + 4 * side - chip].astype(send_ref.dtype)
    for n in range(2, 4):
        send_ref[n * tokens : (n + 1) * tokens, :] = partner


def sum_cores(plan, places, keep, got, after=()):
    _, tokens, features = keep.shape
    out_shape = [
        jax.ShapeDtypeStruct(keep.shape, jnp.float32),
        jax.ShapeDtypeStruct((4 * tokens, features), jnp.bfloat16),
    ]
    kernel = functools.partial(sum_cores_kernel, places)
    return sum_call(kernel, "sum_cores", out_shape, plan, [keep, got], None, after)


def sum_inwards_kernel(places, plan_ref, sums_ref, over_ref, here_ref, *refs):
    inner_ref, send_ref = refs[-2:]
    tokens = inner_ref.shape[0]
    side, chip = plan_ref[places["side"]], plan_ref[places["chip"]]
    for n in range(2):
        rows = slice(n * tokens, (n + 1) * tokens)
        total = sums_ref[2 * (1 - side) + n] + over_ref[0, rows, :].astype(jnp.float32)
        send_ref[rows, :] = total.astype(send_ref.dtype)
    inner_ref[...] = sums_ref[chip] + here_ref[0, :tokens, :].astype(jnp.float32)


def sum_inwards(plan, places, sums, got, first, after=()):
    _, tokens, features = sums.shape
    out_shape = [
        jax.ShapeDtypeStruct((tokens, features), jnp.float32),
        jax.ShapeDtypeStruct((2 * tokens, features), jnp.bfloat16),
    ]
    kernel = functools.partial(sum_inwards_kernel, places)
    return sum_call(kernel, "sum_inwards", out_shape, plan, [sums], (got, first, 2), after)


def sum_across_kernel(places, plan_ref, sums_ref, inner_ref, got_ref, *refs):
    final_ref, send_ref = refs[-2:]
    tokens = inner_ref.shape[0]
    side, chip = plan_ref[places["side"]], plan_ref[places["chip"]]
    place = chip - 2 * side
    low = got_ref[0, :tokens, :].astype(jnp.float32)
    high = got_ref[0, tokens:, :].astype(jnp.float32)
    final_ref[...] = inner_ref[...] + jnp.where(place == 0, low, high)
    total = sums_ref[1 + 4 * side - chip] + jnp.where(place == 0, high, low)
    for n in range(2):
        send_ref[n * tokens : (n + 1) * tokens, :] = total.astype(send_ref.dtype)


def sum_across(plan, places, sums, inner, got, first, after=()):
    _, tokens, features = sums.shape
    out_shape = [
        jax.ShapeDtypeStruct((tokens, features), jnp.float32),
        jax.ShapeDtypeStruct((2 * tokens, features), jnp.bfloat16),
    ]
    kernel = functools.partial(sum_across_kernel, places)
    return sum_call(kernel, "sum_across", out_shape, plan, [sums, inner], (got, first, 1), after)


def sum_outwards_kernel(places, plan_ref, sums_ref, final_ref, got_ref, *refs):
    out_ref = refs[-1]
    tokens = final_ref.shape[0]
    outer = sums_ref[plan_ref[places["chip"]]] + got_ref[0, :tokens, :].astype(jnp.float32)
    out_ref[...] = jnp.where(plan_ref[places["inner"]] == 1, final_ref[...], outer).astype(
        out_ref.dtype
    )


def sum_outwards(plan, places, sums, final, got, first, after=()):
    out_shape = jax.ShapeDtypeStruct(final.shape, jnp.bfloat16)
    kernel = functools.partial(sum_outwards_kernel, places)
    return sum_call(kernel, "sum_outwards", out_shape, plan, [sums, final], (got, first, 1), after)


def gather_tokens(tokens, expert_ids, gate_weights, features):
    mine = lax.dynamic_slice_in_dim(tokens, lax.axis_index("train") * features, features, axis=1)
    top = expert_ids.shape[1]
    high = lax.reduce_precision(gate_weights, 8, 7)
    middle = lax.reduce_precision(gate_weights - high, 8, 7)
    low = gate_weights - high - middle
    beside = jnp.concatenate((expert_ids.astype(jnp.float32), high, middle, low), axis=1)
    beside = jnp.pad(beside, ((0, 0), (0, BLOCK - 4 * top))).astype(jnp.bfloat16)
    every = lax.all_gather(jnp.concatenate((mine, beside), axis=1), "roll", axis=0, tiled=True)
    side = every[:, features : features + 4 * top].astype(jnp.float32)
    ids = side[:, :top].astype(jnp.int32)
    weights = side[:, top : 2 * top] + side[:, 2 * top : 3 * top] + side[:, 3 * top :]
    return every[:, :features], ids, weights


def per_device(master_gate, master_up, master_down, tokens, expert_ids, gate_weights, placement):
    trains = lax.axis_size("train")
    owners = lax.axis_size("roll")
    experts, hidden_rows, features = master_gate.shape
    blocks = hidden_rows // BLOCK
    in_line = owners // CORES == 4 and CORES * tokens.shape[0] == BLOCK
    quant, gate = quantize(master_gate, trains, experts, 0)
    if in_line:
        first = lax.all_to_all(quant, "train", split_axis=0, concat_axis=0, tiled=True)
        rest, up = quantize(master_up, trains, 2 * experts, 0, None, (quant,))
        rest, down = quantize(master_down, trains, 2 * experts, experts, rest)
    else:
        quant_up, up = quantize(master_up, trains, experts, 0)
        quant_down, down = quantize(master_down, trains, experts, 0)
    every, ids, weights = gather_tokens(tokens, expert_ids, gate_weights, features)
    pre = None
    for n in range(2 * blocks):
        restored = (gate, up)[n // blocks]
        pre = pre_activations(
            every, ids, restored, n % blocks, pre, n, 2 * blocks, (down,) if n == 0 else ()
        )
    if in_line:
        plan, places = make_plan(placement, experts, owners)
        most = min(experts, owners // 2)
        shapes = (experts, blocks, trains, owners)

        def branch(cap, first, rest, pre, down, plan, ids, weights):
            return line_exchange(first, rest, pre, down, plan, places, ids, weights, shapes, cap)

        tight = count_distinct(placement, experts, owners) <= most - 1
        outs = lax.cond(
            tight,
            functools.partial(branch, most - 1),
            functools.partial(branch, most),
            first,
            rest,
            pre,
            down,
            plan,
            ids,
            weights,
        )
    else:
        outs = direct_exchange((quant, quant_up, quant_down), placement, trains, owners)
        mixed = mix_experts(lax.psum(pre, "train"), ids, weights, down)
        mixed = lax.psum_scatter(mixed, "roll", scatter_dimension=0, tiled=True)
        outs = tuple(outs) + (mixed.astype(jnp.bfloat16),)
    return tuple(out[None] for out in outs[:3]) + (outs[3],)


def solution(mesh):
    in_specs = (
        P(None, "roll", "train"),
        P(None, "roll", "train"),
        P(None, "roll", "train"),
        P("roll", None),
        P("roll", None),
        P("roll", None),
        P(),
    )
    out_specs = (
        P("roll", None, "train", None),
        P("roll", None, "train", None),
        P("roll", None, "train", None),
        P("roll", "train"),
    )
    return jax.shard_map(
        per_device, mesh=mesh, in_specs=in_specs, out_specs=out_specs, check_vma=False
    )
```

```python
import functools

import jax
import jax.numpy as jnp
from jax import lax
from jax.experimental import pallas as pl
from jax.experimental.pallas import tpu as pltpu
from jax.sharding import PartitionSpec as P

BLOCK = 128
CORES = 2
VMEM_BYTES = 48 * 1024 * 1024
LIGHT = pl.CostEstimate(flops=1, bytes_accessed=1, transcendentals=0)


def any_spec():
    return pl.BlockSpec(memory_space=pl.ANY)


def smem_spec():
    return pl.BlockSpec(memory_space=pltpu.SMEM)


def quantize_kernel(trains, x_ref, *refs):
    q_ref, d_ref = refs[-2:]
    rows = BLOCK // trains
    features = x_ref.shape[-1]
    for col in range(features // BLOCK):
        cols = slice(col * BLOCK, (col + 1) * BLOCK)
        block = x_ref[0, :, cols]
        peak = jnp.max(jnp.max(jnp.abs(block), axis=0, keepdims=True), axis=1, keepdims=True)
        scale = peak.astype(jnp.bfloat16).astype(jnp.float32)
        quant = (block * (1.0 / scale)).astype(jnp.bfloat16)
        q_ref[:, 0, 0, :, cols] = quant.reshape(trains, rows, BLOCK)
        d_ref[0, 0, :, cols] = (quant.astype(jnp.float32) * scale).astype(jnp.bfloat16)


def quantize(master, first, blocks, trains, slots, base=0, into=None, after=()):
    experts, _, features = master.shape
    rows = BLOCK // trains
    operands = [master] + list(after) + ([] if into is None else [into])
    return pl.pallas_call(
        functools.partial(quantize_kernel, trains),
        grid=(experts, blocks),
        in_specs=[pl.BlockSpec((1, BLOCK, features), lambda e, b: (e, first + b, 0))]
        + [any_spec()] * (len(operands) - 1),
        out_specs=[
            pl.BlockSpec((trains, 1, 1, rows, features), lambda e, b: (0, base + e, b, 0, 0)),
            pl.BlockSpec((1, 1, BLOCK, features), lambda e, b: (e, b, 0, 0)),
        ],
        out_shape=[
            jax.ShapeDtypeStruct((trains, slots, blocks, rows, features), jnp.bfloat16),
            jax.ShapeDtypeStruct((experts, blocks, BLOCK, features), jnp.bfloat16),
        ],
        input_output_aliases={} if into is None else {len(operands) - 1: 0},
        compiler_params=pltpu.CompilerParams(vmem_limit_bytes=VMEM_BYTES),
        cost_estimate=LIGHT,
        name="quantize",
    )(*operands)


def start_choice(plan_ref, arrays, choice, target, sem):
    tests, array, (kind, n, *more) = choice
    ref = arrays[array]
    if kind == "is":
        view = ref.at[n]
    elif kind == "at":
        view = ref.at[plan_ref[n]]
    else:
        view = ref.at[:, plan_ref[n] + more[0], pl.ds(more[1], 1)]
    hit = None
    for place, value in tests:
        test = plan_ref[place] == value
        hit = test if hit is None else hit & test

    def go():
        pltpu.make_async_copy(view, target, sem).start()

    if hit is None:
        go()
    else:
        pl.when(hit)(go)


def pack_kernel(pieces, n_in, plan_ref, *refs):
    arrays = refs[:n_in]
    out, held, sem_in, sem_out = refs[-4:]
    for n, choices in enumerate(pieces):
        for choice in choices:
            start_choice(plan_ref, arrays, choice, held.at[n], sem_in.at[n])
    for n in range(len(pieces)):
        pltpu.make_async_copy(held.at[n], held.at[n], sem_in.at[n]).wait()
        pltpu.make_async_copy(held.at[n], out.at[n], sem_out.at[n]).start()
    for n in range(len(pieces)):
        pltpu.make_async_copy(held.at[n], out.at[n], sem_out.at[n]).wait()


class Arrays:
    def __init__(self):
        self.items = []

    def add(self, array):
        for n, item in enumerate(self.items):
            if item is array:
                return n
        self.items.append(array)
        return len(self.items) - 1


def number_choices(pieces, arrays):
    return [[(tests, arrays.add(a), index) for tests, a, index in choices] for choices in pieces]


def pack(plan, shape, pieces, after=()):
    arrays = Arrays()
    pieces = number_choices(pieces, arrays)
    n_in = len(arrays.items)
    size = len(pieces)
    for dim in shape:
        size *= dim
    operands = arrays.items + list(after)
    return pl.pallas_call(
        functools.partial(pack_kernel, pieces, n_in),
        in_specs=[smem_spec()] + [any_spec()] * len(operands),
        out_specs=any_spec(),
        out_shape=jax.ShapeDtypeStruct((len(pieces),) + shape, jnp.bfloat16),
        scratch_shapes=[
            pltpu.VMEM((len(pieces),) + shape, jnp.bfloat16),
            pltpu.SemaphoreType.DMA((len(pieces),)),
            pltpu.SemaphoreType.DMA((len(pieces),)),
        ],
        compiler_params=pltpu.CompilerParams(vmem_limit_bytes=VMEM_BYTES),
        cost_estimate=LIGHT,
        name="pack",
    )(plan, *operands)


def place_kernel(pieces, sources, first, blocks, n_in, plan_ref, *refs):
    arrays = refs[:n_in]
    out, mark, held, sem_in, sem_out = refs[-5:]
    trains, count, _, features = held.shape[1:]
    for n, choices in enumerate(pieces):
        for choice in choices:
            start_choice(plan_ref, arrays, choice, held.at[n], sem_in.at[n])
    mark[...] = jnp.zeros_like(mark)
    stores = []
    for n in range(len(pieces)):
        pltpu.make_async_copy(held.at[n], held.at[n], sem_in.at[n]).wait()
        start = plan_ref[sources[n]] * blocks + first
        for part in range(trains):
            store = pltpu.make_async_copy(
                held.at[n, part],
                out.at[pl.ds(start, count), :, pl.ds(part * features, features)],
                sem_out.at[n, part],
            )
            store.start()
            stores.append(store)
    for store in stores:
        store.wait()


def place_pieces(plan, shape, owners, pieces, sources, first, blocks, out, after=()):
    trains, count, rows, features = shape
    arrays = Arrays()
    pieces = number_choices(pieces, arrays)
    n_in = len(arrays.items)
    operands = arrays.items + list(after) + ([] if out is None else [out])
    return pl.pallas_call(
        functools.partial(place_kernel, pieces, sources, first, blocks, n_in),
        in_specs=[smem_spec()] + [any_spec()] * len(operands),
        out_specs=[any_spec(), pl.BlockSpec(memory_space=pltpu.VMEM)],
        out_shape=[
            jax.ShapeDtypeStruct((owners * blocks, rows, trains * features), jnp.bfloat16),
            jax.ShapeDtypeStruct((8, BLOCK), jnp.float32),
        ],
        scratch_shapes=[
            pltpu.VMEM((len(pieces),) + shape, jnp.bfloat16),
            pltpu.SemaphoreType.DMA((len(pieces),)),
            pltpu.SemaphoreType.DMA((len(pieces), trains)),
        ],
        input_output_aliases={} if out is None else {len(operands): 0},
        compiler_params=pltpu.CompilerParams(vmem_limit_bytes=VMEM_BYTES),
        cost_estimate=LIGHT,
        name="place_pieces",
    )(plan, *operands)


def plan_places(experts):
    names = [f"send{slot}" for slot in range(experts)]
    names += ["inner", "core", "chip", "side", "own", "mate", "out0", "out1", "most"]
    names += [f"{list_}_{who}" for list_ in ("here", "there") for who in ("own", "mate", "out0", "out1")]
    names += [f"from_{who}{n}" for who in ("own", "mate") for n in range(4)]
    return {name: n for n, name in enumerate(names)}


def plan_kernel(experts, owners, places, me_ref, placement_ref, out_ref):
    me = me_ref[0]
    chip, core = lax.div(me, CORES), lax.rem(me, CORES)
    side = lax.div(chip, 2)
    half = owners // 2
    needs, ranks = [], []
    for s in range(2):
        need = []
        for e in range(experts):
            found = jnp.int32(0)
            for o in range(s * half, (s + 1) * half):
                found = jnp.where(placement_ref[o] == e, 1, found)
            need.append(found)
        rank = []
        for e in range(experts):
            total = jnp.int32(0)
            for other in range(experts):
                if other != e:
                    ahead = need[other] >= need[e] if other < e else need[other] > need[e]
                    total = total + jnp.where(ahead, 1, 0)
            rank.append(total)
        needs.append(sum(need))
        ranks.append(rank)
    here = [jnp.where(side == 0, a, b) for a, b in zip(*ranks)]
    there = [jnp.where(side == 0, b, a) for a, b in zip(*ranks)]
    outer = 3 * side
    values = {
        "inner": jnp.where((chip == 1) | (chip == 2), 1, 0),
        "core": core,
        "chip": chip,
        "side": side,
        "own": placement_ref[me],
        "mate": placement_ref[chip * CORES + 1 - core],
        "out0": placement_ref[outer * CORES],
        "out1": placement_ref[outer * CORES + 1],
        "most": jnp.maximum(*needs),
    }
    for slot in range(experts):
        values[f"send{slot}"] = sum(jnp.where(there[e] == slot, e, 0) for e in range(experts))
    for who in ("own", "mate", "out0", "out1"):
        for list_, rank in (("here", here), ("there", there)):
            values[f"{list_}_{who}"] = sum(
                jnp.where(values[who] == e, rank[e], 0) for e in range(experts)
            )
    for n, source in enumerate((chip, 1 + 4 * side - chip, 2 - side, 3 - 3 * side)):
        values[f"from_own{n}"] = source * CORES + core
        values[f"from_mate{n}"] = source * CORES + 1 - core
    for name, n in places.items():
        out_ref[n] = values[name]


def make_plan(placement, experts, owners, after=()):
    places = plan_places(experts)
    me = jnp.reshape(lax.axis_index("roll"), (1,)).astype(jnp.int32)
    plan = pl.pallas_call(
        lambda *refs: plan_kernel(experts, owners, places, refs[0], refs[1], refs[-1]),
        in_specs=[smem_spec(), smem_spec()] + [any_spec()] * len(after),
        out_specs=smem_spec(),
        out_shape=jax.ShapeDtypeStruct((len(places),), jnp.int32),
        cost_estimate=LIGHT,
        name="plan",
    )(me, placement, *after)
    return plan, places


def line_schedule(opens, experts, cap, ride_from):
    chunks = range(len(opens))
    own, far = list(chunks), list(chunks)
    fresh = [("x", c, i) for c in chunks for i in range(CORES)]
    near = [("near", c, s) for c in chunks for s in range(cap, experts)]
    middle, inwards, outwards = [], [], []
    arrived, relayed, ride_due = [], [], {"in": ride_from}
    n = 0
    while own or arrived or far or near or fresh or relayed or ride_due:
        across, ins, outs = [], [], []
        if arrived and arrived[0][0] <= n:
            c = arrived.pop(0)[1]
            across = [("far", c, s) for s in range(cap)]
        elif own and opens[own[0]] <= n:
            c = own.pop(0)
            across = [("own", c, s) for s in range(cap)]
        if across:
            relayed += [(n + 2, (across[0][0], c, i)) for i in range(CORES)]
        if ride_due.get("across", n + 1) <= n and (not across or across[0][0] == "own"):
            across.append(("ride", 0, 0))
            del ride_due["across"]
            ride_due["out"] = n + 2
        if far and opens[far[0]] <= n:
            c = far.pop(0)
            ins = [("far", c, s) for s in range(cap)]
            arrived.append((n + 2, c))
        else:
            if ride_due.get("in", n + 1) <= n:
                ins = [("ride", 0, 0), ("ride", 0, 1)]
                del ride_due["in"]
                ride_due["across"] = n + 2
            while near and opens[near[0][1]] <= n and len(ins) < cap:
                ins.append(near.pop(0))
        while relayed and relayed[0][0] <= n and len(outs) < cap:
            outs.append(relayed.pop(0)[1])
        if ride_due.get("out", n + 1) <= n and len(outs) < cap:
            outs.append(("ride", 0, 0))
            del ride_due["out"]
        while fresh and opens[fresh[0][1]] <= n and len(outs) < cap:
            outs.append(fresh.pop(0))
        middle.append(across)
        inwards.append(ins)
        outwards.append(outs)
        n += 1
    return middle, inwards, outwards


def link_pairs(chip_pairs, swap_chips=()):
    pairs = []
    for core in range(CORES):
        for a, b in chip_pairs:
            pairs.append((a * CORES + core, b * CORES + core))
        for chip in swap_chips:
            pairs.append((chip * CORES + core, chip * CORES + 1 - core))
    return pairs


EDGES = ((0, 1), (1, 0), (2, 3), (3, 2))


def line_exchange(x_first, quants, dequant, plan, places, routed, shapes, cap):
    experts, blocks, trains, owners = shapes
    features = x_first.shape[-1]
    rows = BLOCK // trains
    shape = (trains, 1, rows, features)
    chunks = [(m, b) for m in range(3) for b in range(blocks)]
    count = len(chunks)
    opens = [0 if c == 0 else 1 if m == 0 else 4 for c, (m, _) in enumerate(chunks)]
    ride_from = 8
    middle, inwards, outwards = line_schedule(opens, experts, cap, ride_from)
    rounds = len(outwards)
    edge_pairs = link_pairs(EDGES)
    middle_pairs = link_pairs([(1, 2), (2, 1)], swap_chips=(0, 3))
    swap_pairs = link_pairs([], swap_chips=range(4))
    is_inner, is_outer = (places["inner"], 1), (places["inner"], 0)
    on_core = [(places["core"], core) for core in range(CORES)]
    got_edge, got_middle, where = {}, {}, {}
    last = [x_first]

    xs = [x_first] + [
        lax.all_to_all(quant, "train", split_axis=0, concat_axis=0, tiled=True) for quant in quants
    ]

    def local(c, name):
        m, b = chunks[c]
        if c == 0:
            return xs[0], ("expert", places[name], 0, 0)
        if m == 0:
            return xs[1], ("expert", places[name], 0, b - 1)
        return xs[-1], ("expert", places[name], (m - 1) * experts, b)

    def packed(pieces, after=()):
        last[0] = pack(plan, shape, pieces, [last[0]] + list(after))
        return last[0]

    ready = {(c, 0): opens[c] for c in range(count)}

    def note(c, position, n):
        ready[c, position] = max(ready.get((c, position), 0), n)

    from_kind = {"x": 1, "own": 2, "far": 3}
    kind_of = {position: kind for kind, position in from_kind.items()}
    for n in range(rounds):
        for i, piece in enumerate(middle[n]):
            where[("across",) + piece] = (n, i)
            if piece[0] != "ride":
                note(piece[1], 2 if piece[0] == "own" else 3, n)
        for i, piece in enumerate(inwards[n]):
            where[("in",) + piece] = (n, i)
            if piece[0] != "ride":
                note(piece[1], 1, n)
        for i, piece in enumerate(outwards[n]):
            where[("out",) + piece] = (n, i)
            if piece[0] != "ride":
                note(piece[1], from_kind[piece[0]], n)

    def across(kind, c):
        return got_middle[where["across", kind, c, 0][0]]

    def find(c, position, who):
        if position == 0:
            return [((),) + local(c, who)]
        choices = []
        if position == 1:
            for slot in range(experts):
                n, i = where["in", "far" if slot < cap else "near", c, slot]
                test = (places[f"there_{who}"], slot)
                choices.append(((is_inner, test), got_edge[n], ("is", i)))
        else:
            got = across(kind_of[position], c)
            choices.append(((is_inner,), got, ("at", places[f"here_{who}"])))
        for core in range(CORES):
            n, i = where["out", kind_of[position], c, core if who == "own" else 1 - core]
            choices.append(((is_outer, on_core[core]), got_edge[n], ("is", i)))
        return choices

    groups = []
    for c in range(count):
        early = [p for p in range(4) if ready[c, p] < rounds - 4]
        late = [p for p in range(4) if p not in early]
        for positions in (early[:2], early[2:], late):
            if positions:
                groups.append((max(ready[c, p] for p in positions), c, positions))
    groups.sort(key=lambda group: group[0])
    swapped, swap_round, outs = {}, {}, [None, None, None]

    def swap(group, n):
        _, c, positions = group
        pieces = [find(c, p, "mate") for p in positions]
        swap_round[c, positions[0]] = n
        swapped[c, positions[0]] = lax.ppermute(packed(pieces), "roll", swap_pairs)

    def place(group):
        _, c, positions = group
        m, b = chunks[c]
        got = swapped[c, positions[0]]
        pieces = [find(c, p, "own") for p in positions]
        pieces += [[((), got, ("is", n))] for n in range(len(positions))]
        sources = [places[f"from_own{p}"] for p in positions]
        sources += [places[f"from_mate{p}"] for p in positions]
        outs[m], last[0] = place_pieces(
            plan, shape, owners, pieces, sources, b, blocks, outs[m], (last[0],)
        )

    ride = {}
    tokens, ids, weights = routed
    ups, down = dequant[:-1], dequant[-1]

    def ride_first():
        pre, columns = None, 2 * blocks
        for restored in ups:
            for b in range(restored.shape[1]):
                column = 0 if pre is None else column + 1
                pre = pre_activations(tokens, ids, restored, b, pre, column, columns, (last[0],))
                last[0] = pre
        ride["pre"] = lax.psum(pre, "train")
    def ride_mix():
        ride["keep"], going = mix_experts(
            ride["pre"], ids, weights, down, plan, places, (last[0],)
        )
        last[0] = ride["keep"]
        going = going.reshape((-1,) + shape)
        ride["swapped"] = lax.ppermute(going, "roll", swap_pairs)

    def ride_cores():
        got = ride["swapped"].reshape(-1, features)
        ride["sums"], going = sum_cores(plan, places, ride["keep"], got, (last[0],))
        last[0] = ride["sums"]
        ride["in"] = going.reshape((-1,) + shape)

    def ride_in():
        n, i = where["in", "ride", 0, 0]
        got = got_edge[n].reshape(-1, BLOCK, features)
        ride["inner"], going = sum_inwards(plan, places, ride["sums"], got, i, (last[0],))
        last[0] = ride["inner"]
        ride["across"] = going.reshape((-1,) + shape)

    def ride_across():
        n, i = where["across", "ride", 0, 0]
        got = got_middle[n].reshape(-1, BLOCK, features)
        ride["final"], going = sum_across(
            plan, places, ride["sums"], ride["inner"], got, i, (last[0],)
        )
        last[0] = ride["final"]
        ride["out"] = going.reshape((-1,) + shape)

    def ride_out():
        n, i = where["out", "ride", 0, 0]
        got = got_edge[n].reshape(-1, BLOCK, features)
        ride["mixed"] = sum_outwards(
            plan, places, ride["sums"], ride["final"], got, i, (last[0],)
        )
        last[0] = ride["mixed"]

    to_swap, to_place = list(groups), []
    spare = local(0, "own")
    for n in range(rounds):
        while to_swap and to_swap[0][0] <= n - 2:
            to_place.append(to_swap.pop(0))
            swap(to_place[-1], n)
        if middle[n]:
            if where.get(("across", "ride", 0, 0), (-1,))[0] == n:
                ride_in()
            pieces = []
            for kind, c, slot in middle[n]:
                if kind == "own":
                    pieces.append([((),) + local(c, f"send{slot}")])
                elif kind == "ride":
                    pieces.append([((), ride["across"], ("is", 0))])
                else:
                    m, i = where["in", kind, c, slot]
                    pieces.append([((), got_edge[m], ("is", i))])
            after = [got_middle[n - 2]] if n - 2 in got_middle else []
            got_middle[n] = lax.ppermute(packed(pieces, after), "roll", middle_pairs)
        if where["out", "ride", 0, 0][0] == n:
            ride_across()
        pieces = []
        for i in range(max(len(inwards[n]), len(outwards[n]))):
            choices = [((is_inner,),) + spare, ((is_outer,),) + spare]
            if i < len(outwards[n]):
                kind, c, core = outwards[n][i]
                if kind == "x":
                    choices[0] = ((is_inner,),) + local(c, f"out{core}")
                elif kind == "ride":
                    choices[0] = ((is_inner,), ride["out"], ("is", 0))
                else:
                    index = ("at", places[f"here_out{core}"])
                    choices[0] = ((is_inner,), across(kind, c), index)
            if i < len(inwards[n]):
                kind, c, slot = inwards[n][i]
                if kind == "ride":
                    choices[1] = ((is_outer,), ride["in"], ("is", slot))
                else:
                    choices[1] = ((is_outer,),) + local(c, f"send{slot}")
            pieces.append(choices)
        if pieces:
            after = [got_edge[n - 2]] if n - 2 in got_edge else []
            got_edge[n] = lax.ppermute(packed(pieces, after), "roll", edge_pairs)
        if n == 0:
            ride_first()
        if n == ride_from - 3:
            ride_mix()
        if n == ride_from - 1:
            ride_cores()
        if n == where["out", "ride", 0, 0][0] + 2:
            ride_out()
        for group in list(to_place):
            if swap_round[group[1], group[2][0]] <= n - 2:
                place(group)
                to_place.remove(group)
    if "mixed" not in ride:
        ride_out()
    for group in to_swap:
        swap(group, rounds)
    for group in to_place + to_swap:
        place(group)
    return tuple(outs) + (ride["mixed"],)


def direct_exchange(quants, placement, trains, owners):
    outs = []
    for quant in quants:
        _, experts, blocks, rows, features = quant.shape
        x = lax.all_to_all(quant, "train", split_axis=0, concat_axis=0, tiled=True)
        x = jnp.transpose(x, (1, 2, 3, 0, 4)).reshape(experts, blocks, rows, trains * features)
        picked = jnp.take(x, placement, axis=0)
        got = lax.all_to_all(picked, "roll", split_axis=0, concat_axis=0, tiled=True)
        outs.append(got.reshape(owners * blocks, rows, trains * features))
    return outs


def pre_activation_kernel(experts, top, tok_ref, ids_ref, w_ref, *refs):
    out_ref = refs[-1]
    features = tok_ref.shape[1]
    weights = w_ref[...].reshape(experts * BLOCK, features)
    pre = lax.dot_general(
        tok_ref[...], weights, (((1,), (1,)), ((), ())), preferred_element_type=jnp.float32
    )
    for k in range(top):
        total = jnp.zeros((pre.shape[0], BLOCK), jnp.float32)
        for expert in range(experts):
            part = pre[:, expert * BLOCK : (expert + 1) * BLOCK]
            total = total + jnp.where(ids_ref[:, k : k + 1] == expert, part, 0.0)
        out_ref[:, k * BLOCK : (k + 1) * BLOCK] = total


def pre_activations(tokens, ids, restored, block, out, column, columns, after=()):
    count, features = tokens.shape
    experts, top = restored.shape[0], ids.shape[1]
    tile = min(count, 2 * BLOCK)
    operands = [tokens, ids, restored] + list(after) + ([] if out is None else [out])
    return pl.pallas_call(
        functools.partial(pre_activation_kernel, experts, top),
        grid=(count // tile,),
        in_specs=[
            pl.BlockSpec((tile, features), lambda i: (i, 0)),
            pl.BlockSpec((tile, top), lambda i: (i, 0)),
            pl.BlockSpec((experts, 1, BLOCK, features), lambda i: (0, block, 0, 0)),
        ]
        + [any_spec()] * (len(operands) - 3),
        out_specs=pl.BlockSpec((tile, top * BLOCK), lambda i: (i, column)),
        out_shape=jax.ShapeDtypeStruct((count, columns * top * BLOCK), jnp.float32),
        input_output_aliases={} if out is None else {len(operands) - 1: 0},
        compiler_params=pltpu.CompilerParams(vmem_limit_bytes=VMEM_BYTES),
        cost_estimate=LIGHT,
        name="pre_activations",
    )(*operands)


def mix_rows(experts, top, blocks, pre_ref, ids_ref, weights_ref, down_ref):
    width = top * BLOCK
    count, features = ids_ref.shape[0], down_ref.shape[-1]
    hidden = {}
    for b in range(blocks):
        for k in range(top):
            start = b * width + k * BLOCK
            gate = pre_ref[:, start : start + BLOCK]
            up = pre_ref[:, blocks * width + start : blocks * width + start + BLOCK]
            value = gate / (1.0 + jnp.exp(-gate)) * up
            hidden[b, k] = value.astype(jnp.bfloat16).astype(jnp.float32)
    total = jnp.zeros((count, features), jnp.float32)
    for expert in range(experts):
        weight = jnp.zeros((count, 1), jnp.float32)
        for k in range(top):
            weight = weight + jnp.where(
                ids_ref[:, k : k + 1] == expert, weights_ref[:, k : k + 1], 0.0
            )
        value = jnp.zeros((count, features), jnp.float32)
        for b in range(blocks):
            routed = jnp.zeros((count, BLOCK), jnp.float32)
            for k in range(top):
                routed = routed + jnp.where(ids_ref[:, k : k + 1] == expert, hidden[b, k], 0.0)
            value = value + jnp.dot(
                routed.astype(jnp.bfloat16), down_ref[expert, b], preferred_element_type=jnp.float32
            )
        total = total + weight * value
    return total


def mix_kernel(sizes, pre_ref, ids_ref, weights_ref, down_ref, out_ref):
    out_ref[...] = mix_rows(*sizes, pre_ref, ids_ref, weights_ref, down_ref)


def mix_split_kernel(sizes, core, pre_ref, ids_ref, weights_ref, down_ref, plan_ref, *refs):
    keep_ref, send_ref = refs[-2:]
    total = mix_rows(*sizes, pre_ref, ids_ref, weights_ref, down_ref)
    half = total.shape[0] // CORES
    first = plan_ref[core] == 0
    keep_ref[0] = jnp.where(first, total[:half], total[half:])
    send_ref[...] = jnp.where(first, total[half:], total[:half]).astype(send_ref.dtype)


def mix_specs(pre, ids, down, tile):
    return [
        pl.BlockSpec((tile, pre.shape[1]), lambda i: (i, 0)),
        pl.BlockSpec((tile, ids.shape[1]), lambda i: (i, 0)),
        pl.BlockSpec((tile, ids.shape[1]), lambda i: (i, 0)),
        pl.BlockSpec(down.shape, lambda i: (0, 0, 0, 0)),
    ]


def mix_experts(pre, ids, weights, down, plan=None, places=None, after=()):
    count, top = ids.shape
    experts, blocks, _, features = down.shape
    sizes = (experts, top, blocks)
    tile = min(count, BLOCK)
    params = pltpu.CompilerParams(vmem_limit_bytes=VMEM_BYTES)
    if plan is None:
        return pl.pallas_call(
            functools.partial(mix_kernel, sizes),
            grid=(count // tile,),
            in_specs=mix_specs(pre, ids, down, tile),
            out_specs=pl.BlockSpec((tile, features), lambda i: (i, 0)),
            out_shape=jax.ShapeDtypeStruct((count, features), jnp.float32),
            compiler_params=params,
            cost_estimate=LIGHT,
            name="mix_experts",
        )(pre, ids, weights, down)
    half = tile // CORES
    return pl.pallas_call(
        functools.partial(mix_split_kernel, sizes, places["core"]),
        grid=(count // tile,),
        in_specs=mix_specs(pre, ids, down, tile) + [smem_spec()] + [any_spec()] * len(after),
        out_specs=[
            pl.BlockSpec((1, half, features), lambda i: (i, 0, 0)),
            pl.BlockSpec((half, features), lambda i: (i, 0)),
        ],
        out_shape=[
            jax.ShapeDtypeStruct((count // tile, half, features), jnp.float32),
            jax.ShapeDtypeStruct((count // CORES, features), jnp.bfloat16),
        ],
        compiler_params=params,
        cost_estimate=LIGHT,
        name="mix_experts",
    )(pre, ids, weights, down, plan, *after)


def sum_call(kernel, name, out_shape, plan, arrays, piece, after):
    vmem = pl.BlockSpec(memory_space=pltpu.VMEM)
    operands = [plan] + list(arrays)
    specs = [smem_spec()] + [vmem] * len(arrays)
    if piece is not None:
        array, first, number = piece
        operands += [array] * number
        for n in range(number):
            specs.append(
                pl.BlockSpec((1,) + array.shape[1:], lambda i, n=n: (first + n, 0, 0))
            )
    return pl.pallas_call(
        kernel,
        grid=(1,),
        in_specs=specs + [any_spec()] * len(after),
        out_specs=[vmem] * len(out_shape) if isinstance(out_shape, list) else vmem,
        out_shape=out_shape,
        compiler_params=pltpu.CompilerParams(vmem_limit_bytes=VMEM_BYTES),
        cost_estimate=LIGHT,
        name=name,
    )(*operands, *after)


def sum_cores_kernel(places, plan_ref, keep_ref, got_ref, *refs):
    sums_ref, send_ref = refs[-2:]
    chips, tokens, features = keep_ref.shape
    for chip in range(chips):
        rows = slice(chip * tokens, (chip + 1) * tokens)
        sums_ref[chip] = keep_ref[chip] + got_ref[rows, :].astype(jnp.float32)
    side, chip = plan_ref[places["side"]], plan_ref[places["chip"]]
    for n in range(2):
        send_ref[n * tokens : (n + 1) * tokens, :] = sums_ref[2 * (1 - side) + n].astype(
            send_ref.dtype
        )
    partner = sums_ref[1 + 4 * side - chip].astype(send_ref.dtype)
    for n in range(2, 4):
        send_ref[n * tokens : (n + 1) * tokens, :] = partner


def sum_cores(plan, places, keep, got, after=()):
    _, tokens, features = keep.shape
    out_shape = [
        jax.ShapeDtypeStruct(keep.shape, jnp.float32),
        jax.ShapeDtypeStruct((4 * tokens, features), jnp.bfloat16),
    ]
    kernel = functools.partial(sum_cores_kernel, places)
    return sum_call(kernel, "sum_cores", out_shape, plan, [keep, got], None, after)


def sum_inwards_kernel(places, plan_ref, sums_ref, over_ref, here_ref, *refs):
    inner_ref, send_ref = refs[-2:]
    tokens = inner_ref.shape[0]
    side, chip = plan_ref[places["side"]], plan_ref[places["chip"]]
    for n in range(2):
        rows = slice(n * tokens, (n + 1) * tokens)
        total = sums_ref[2 * (1 - side) + n] + over_ref[0, rows, :].astype(jnp.float32)
        send_ref[rows, :] = total.astype(send_ref.dtype)
    inner_ref[...] = sums_ref[chip] + here_ref[0, :tokens, :].astype(jnp.float32)


def sum_inwards(plan, places, sums, got, first, after=()):
    _, tokens, features = sums.shape
    out_shape = [
        jax.ShapeDtypeStruct((tokens, features), jnp.float32),
        jax.ShapeDtypeStruct((2 * tokens, features), jnp.bfloat16),
    ]
    kernel = functools.partial(sum_inwards_kernel, places)
    return sum_call(kernel, "sum_inwards", out_shape, plan, [sums], (got, first, 2), after)


def sum_across_kernel(places, plan_ref, sums_ref, inner_ref, got_ref, *refs):
    final_ref, send_ref = refs[-2:]
    tokens = inner_ref.shape[0]
    side, chip = plan_ref[places["side"]], plan_ref[places["chip"]]
    place = chip - 2 * side
    low = got_ref[0, :tokens, :].astype(jnp.float32)
    high = got_ref[0, tokens:, :].astype(jnp.float32)
    final_ref[...] = inner_ref[...] + jnp.where(place == 0, low, high)
    total = sums_ref[1 + 4 * side - chip] + jnp.where(place == 0, high, low)
    for n in range(2):
        send_ref[n * tokens : (n + 1) * tokens, :] = total.astype(send_ref.dtype)


def sum_across(plan, places, sums, inner, got, first, after=()):
    _, tokens, features = sums.shape
    out_shape = [
        jax.ShapeDtypeStruct((tokens, features), jnp.float32),
        jax.ShapeDtypeStruct((2 * tokens, features), jnp.bfloat16),
    ]
    kernel = functools.partial(sum_across_kernel, places)
    return sum_call(kernel, "sum_across", out_shape, plan, [sums, inner], (got, first, 1), after)


def sum_outwards_kernel(places, plan_ref, sums_ref, final_ref, got_ref, *refs):
    out_ref = refs[-1]
    tokens = final_ref.shape[0]
    outer = sums_ref[plan_ref[places["chip"]]] + got_ref[0, :tokens, :].astype(jnp.float32)
    out_ref[...] = jnp.where(plan_ref[places["inner"]] == 1, final_ref[...], outer).astype(
        out_ref.dtype
    )


def sum_outwards(plan, places, sums, final, got, first, after=()):
    out_shape = jax.ShapeDtypeStruct(final.shape, jnp.bfloat16)
    kernel = functools.partial(sum_outwards_kernel, places)
    return sum_call(kernel, "sum_outwards", out_shape, plan, [sums, final], (got, first, 1), after)


def gather_tokens(tokens, expert_ids, gate_weights, features):
    mine = lax.dynamic_slice_in_dim(tokens, lax.axis_index("train") * features, features, axis=1)
    top = expert_ids.shape[1]
    high = lax.reduce_precision(gate_weights, 8, 7)
    middle = lax.reduce_precision(gate_weights - high, 8, 7)
    low = gate_weights - high - middle
    beside = jnp.concatenate((expert_ids.astype(jnp.float32), high, middle, low), axis=1)
    beside = jnp.pad(beside, ((0, 0), (0, BLOCK - 4 * top))).astype(jnp.bfloat16)
    every = lax.all_gather(jnp.concatenate((mine, beside), axis=1), "roll", axis=0, tiled=True)
    side = every[:, features : features + 4 * top].astype(jnp.float32)
    ids = side[:, :top].astype(jnp.int32)
    weights = side[:, top : 2 * top] + side[:, 2 * top : 3 * top] + side[:, 3 * top :]
    return every[:, :features], ids, weights


def per_device(master_gate, master_up, master_down, tokens, expert_ids, gate_weights, placement):
    trains = lax.axis_size("train")
    owners = lax.axis_size("roll")
    experts, hidden_rows, features = master_gate.shape
    blocks = hidden_rows // BLOCK
    if owners // CORES == 4 and CORES * tokens.shape[0] == BLOCK:
        quant, gate = quantize(master_gate, 0, 1, trains, experts)
        x_first = lax.all_to_all(quant, "train", split_axis=0, concat_axis=0, tiled=True)
        plan, places = make_plan(placement, experts, owners, (quant,))
        quants, dequant, after = [], [gate], plan
        if blocks > 1:
            after, gate = quantize(master_gate, 1, blocks - 1, trains, experts, 0, None, (plan,))
            quants.append(after)
            dequant.append(gate)
        rest, up = quantize(master_up, 0, blocks, trains, 2 * experts, 0, None, (after,))
        rest, down = quantize(master_down, 0, blocks, trains, 2 * experts, experts, rest)
        quants.append(rest)
        dequant += [up, down]
        routed = gather_tokens(tokens, expert_ids, gate_weights, features)
        most = min(experts, owners // 2)
        shapes = (experts, blocks, trains, owners)

        def branch(cap, x_first, quants, dequant, plan, routed):
            return line_exchange(x_first, quants, dequant, plan, places, routed, shapes, cap)

        outs = lax.cond(
            plan[places["most"]] <= most - 1,
            functools.partial(branch, most - 1),
            functools.partial(branch, most),
            x_first,
            quants,
            dequant,
            plan,
            routed,
        )
    else:
        masters = (master_gate, master_up, master_down)
        quants, dequant = zip(*[quantize(w, 0, blocks, trains, experts) for w in masters])
        every, ids, weights = gather_tokens(tokens, expert_ids, gate_weights, features)
        outs = direct_exchange(quants, placement, trains, owners)
        pre = None
        for n in range(2 * blocks):
            restored = dequant[n // blocks]
            pre = pre_activations(every, ids, restored, n % blocks, pre, n, 2 * blocks)
        mixed = mix_experts(lax.psum(pre, "train"), ids, weights, dequant[2])
        mixed = lax.psum_scatter(mixed, "roll", scatter_dimension=0, tiled=True)
        outs = tuple(outs) + (mixed.astype(jnp.bfloat16),)
    return tuple(out[None] for out in outs[:3]) + (outs[3],)


def solution(mesh):
    in_specs = (
        P(None, "roll", "train"),
        P(None, "roll", "train"),
        P(None, "roll", "train"),
        P("roll", None),
        P("roll", None),
        P("roll", None),
        P(),
    )
    out_specs = (
        P("roll", None, "train", None),
        P("roll", None, "train", None),
        P("roll", None, "train", None),
        P("roll", "train"),
    )
    return jax.shard_map(
        per_device, mesh=mesh, in_specs=in_specs, out_specs=out_specs, check_vma=False
    )
```

```python
import functools

import jax
import jax.numpy as jnp
from jax import lax
from jax.experimental import pallas as pl
from jax.experimental.pallas import tpu as pltpu
from jax.sharding import PartitionSpec as P

BLOCK = 128
CORES = 2
VMEM_BYTES = 48 * 1024 * 1024
LIGHT = pl.CostEstimate(flops=1, bytes_accessed=1, transcendentals=0)


def any_spec():
    return pl.BlockSpec(memory_space=pl.ANY)


def smem_spec():
    return pl.BlockSpec(memory_space=pltpu.SMEM)


def quantize_kernel(trains, x_ref, *refs):
    q_ref, d_ref = refs[-2:]
    rows = BLOCK // trains
    features = x_ref.shape[-1]
    for col in range(features // BLOCK):
        cols = slice(col * BLOCK, (col + 1) * BLOCK)
        block = x_ref[0, :, cols]
        peak = jnp.max(jnp.max(jnp.abs(block), axis=0, keepdims=True), axis=1, keepdims=True)
        scale = peak.astype(jnp.bfloat16).astype(jnp.float32)
        quant = (block * (1.0 / scale)).astype(jnp.bfloat16)
        q_ref[:, 0, 0, :, cols] = quant.reshape(trains, rows, BLOCK)
        d_ref[0, 0, :, cols] = (quant.astype(jnp.float32) * scale).astype(jnp.bfloat16)


def quantize(master, first, blocks, trains, slots, base=0, into=None, after=()):
    experts, _, features = master.shape
    rows = BLOCK // trains
    operands = [master] + list(after) + ([] if into is None else [into])
    return pl.pallas_call(
        functools.partial(quantize_kernel, trains),
        grid=(experts, blocks),
        in_specs=[pl.BlockSpec((1, BLOCK, features), lambda e, b: (e, first + b, 0))]
        + [any_spec()] * (len(operands) - 1),
        out_specs=[
            pl.BlockSpec((trains, 1, 1, rows, features), lambda e, b: (0, base + e, b, 0, 0)),
            pl.BlockSpec((1, 1, BLOCK, features), lambda e, b: (e, b, 0, 0)),
        ],
        out_shape=[
            jax.ShapeDtypeStruct((trains, slots, blocks, rows, features), jnp.bfloat16),
            jax.ShapeDtypeStruct((experts, blocks, BLOCK, features), jnp.bfloat16),
        ],
        input_output_aliases={} if into is None else {len(operands) - 1: 0},
        compiler_params=pltpu.CompilerParams(vmem_limit_bytes=VMEM_BYTES),
        cost_estimate=LIGHT,
        name="quantize",
    )(*operands)


def start_choice(plan_ref, arrays, choice, target, sem):
    tests, array, (kind, n, *more) = choice
    ref = arrays[array]
    if kind == "is":
        view = ref.at[n]
    elif kind == "at":
        view = ref.at[plan_ref[n]]
    else:
        view = ref.at[:, plan_ref[n] + more[0], pl.ds(more[1], 1)]
    hit = None
    for place, value in tests:
        test = plan_ref[place] == value
        hit = test if hit is None else hit & test

    def go():
        pltpu.make_async_copy(view, target, sem).start()

    if hit is None:
        go()
    else:
        pl.when(hit)(go)


def pack_kernel(pieces, n_in, plan_ref, *refs):
    arrays = refs[:n_in]
    out, held, sem_in, sem_out = refs[-4:]
    for n, choices in enumerate(pieces):
        for choice in choices:
            start_choice(plan_ref, arrays, choice, held.at[n], sem_in.at[n])
    for n in range(len(pieces)):
        pltpu.make_async_copy(held.at[n], held.at[n], sem_in.at[n]).wait()
        pltpu.make_async_copy(held.at[n], out.at[n], sem_out.at[n]).start()
    for n in range(len(pieces)):
        pltpu.make_async_copy(held.at[n], out.at[n], sem_out.at[n]).wait()


class Arrays:
    def __init__(self):
        self.items = []

    def add(self, array):
        for n, item in enumerate(self.items):
            if item is array:
                return n
        self.items.append(array)
        return len(self.items) - 1


def number_choices(pieces, arrays):
    return [[(tests, arrays.add(a), index) for tests, a, index in choices] for choices in pieces]


def pack(plan, shape, pieces, after=()):
    arrays = Arrays()
    pieces = number_choices(pieces, arrays)
    n_in = len(arrays.items)
    size = len(pieces)
    for dim in shape:
        size *= dim
    operands = arrays.items + list(after)
    return pl.pallas_call(
        functools.partial(pack_kernel, pieces, n_in),
        in_specs=[smem_spec()] + [any_spec()] * len(operands),
        out_specs=any_spec(),
        out_shape=jax.ShapeDtypeStruct((len(pieces),) + shape, jnp.bfloat16),
        scratch_shapes=[
            pltpu.VMEM((len(pieces),) + shape, jnp.bfloat16),
            pltpu.SemaphoreType.DMA((len(pieces),)),
            pltpu.SemaphoreType.DMA((len(pieces),)),
        ],
        compiler_params=pltpu.CompilerParams(vmem_limit_bytes=VMEM_BYTES),
        cost_estimate=LIGHT,
        name="pack",
    )(plan, *operands)


def place_kernel(pieces, sources, first, blocks, n_in, plan_ref, *refs):
    arrays = refs[:n_in]
    out, mark, held, sem_in, sem_out = refs[-5:]
    trains, count, _, features = held.shape[1:]
    for n, choices in enumerate(pieces):
        for choice in choices:
            start_choice(plan_ref, arrays, choice, held.at[n], sem_in.at[n])
    mark[...] = jnp.zeros_like(mark)
    stores = []
    for n in range(len(pieces)):
        pltpu.make_async_copy(held.at[n], held.at[n], sem_in.at[n]).wait()
        start = plan_ref[sources[n]] * blocks + first
        for part in range(trains):
            store = pltpu.make_async_copy(
                held.at[n, part],
                out.at[pl.ds(start, count), :, pl.ds(part * features, features)],
                sem_out.at[n, part],
            )
            store.start()
            stores.append(store)
    for store in stores:
        store.wait()


def place_pieces(plan, shape, owners, pieces, sources, first, blocks, out, after=()):
    trains, count, rows, features = shape
    arrays = Arrays()
    pieces = number_choices(pieces, arrays)
    n_in = len(arrays.items)
    operands = arrays.items + list(after) + ([] if out is None else [out])
    return pl.pallas_call(
        functools.partial(place_kernel, pieces, sources, first, blocks, n_in),
        in_specs=[smem_spec()] + [any_spec()] * len(operands),
        out_specs=[any_spec(), pl.BlockSpec(memory_space=pltpu.VMEM)],
        out_shape=[
            jax.ShapeDtypeStruct((owners * blocks, rows, trains * features), jnp.bfloat16),
            jax.ShapeDtypeStruct((8, BLOCK), jnp.float32),
        ],
        scratch_shapes=[
            pltpu.VMEM((len(pieces),) + shape, jnp.bfloat16),
            pltpu.SemaphoreType.DMA((len(pieces),)),
            pltpu.SemaphoreType.DMA((len(pieces), trains)),
        ],
        input_output_aliases={} if out is None else {len(operands): 0},
        compiler_params=pltpu.CompilerParams(vmem_limit_bytes=VMEM_BYTES),
        cost_estimate=LIGHT,
        name="place_pieces",
    )(plan, *operands)


def plan_places(experts):
    names = [f"send{slot}" for slot in range(experts)]
    names += ["inner", "core", "chip", "side", "own", "mate", "out0", "out1", "most"]
    names += [f"{list_}_{who}" for list_ in ("here", "there") for who in ("own", "mate", "out0", "out1")]
    names += [f"from_{who}{n}" for who in ("own", "mate") for n in range(4)]
    return {name: n for n, name in enumerate(names)}


def plan_kernel(experts, owners, places, me_ref, placement_ref, out_ref):
    me = me_ref[0]
    chip, core = lax.div(me, CORES), lax.rem(me, CORES)
    side = lax.div(chip, 2)
    half = owners // 2
    needs, ranks = [], []
    for s in range(2):
        need = []
        for e in range(experts):
            found = jnp.int32(0)
            for o in range(s * half, (s + 1) * half):
                found = jnp.where(placement_ref[o] == e, 1, found)
            need.append(found)
        rank = []
        for e in range(experts):
            total = jnp.int32(0)
            for other in range(experts):
                if other != e:
                    ahead = need[other] >= need[e] if other < e else need[other] > need[e]
                    total = total + jnp.where(ahead, 1, 0)
            rank.append(total)
        needs.append(sum(need))
        ranks.append(rank)
    here = [jnp.where(side == 0, a, b) for a, b in zip(*ranks)]
    there = [jnp.where(side == 0, b, a) for a, b in zip(*ranks)]
    outer = 3 * side
    values = {
        "inner": jnp.where((chip == 1) | (chip == 2), 1, 0),
        "core": core,
        "chip": chip,
        "side": side,
        "own": placement_ref[me],
        "mate": placement_ref[chip * CORES + 1 - core],
        "out0": placement_ref[outer * CORES],
        "out1": placement_ref[outer * CORES + 1],
        "most": jnp.maximum(*needs),
    }
    for slot in range(experts):
        values[f"send{slot}"] = sum(jnp.where(there[e] == slot, e, 0) for e in range(experts))
    for who in ("own", "mate", "out0", "out1"):
        for list_, rank in (("here", here), ("there", there)):
            values[f"{list_}_{who}"] = sum(
                jnp.where(values[who] == e, rank[e], 0) for e in range(experts)
            )
    for n, source in enumerate((chip, 1 + 4 * side - chip, 2 - side, 3 - 3 * side)):
        values[f"from_own{n}"] = source * CORES + core
        values[f"from_mate{n}"] = source * CORES + 1 - core
    for name, n in places.items():
        out_ref[n] = values[name]


def make_plan(placement, experts, owners, after=()):
    places = plan_places(experts)
    me = jnp.reshape(lax.axis_index("roll"), (1,)).astype(jnp.int32)
    plan = pl.pallas_call(
        lambda *refs: plan_kernel(experts, owners, places, refs[0], refs[1], refs[-1]),
        in_specs=[smem_spec(), smem_spec()] + [any_spec()] * len(after),
        out_specs=smem_spec(),
        out_shape=jax.ShapeDtypeStruct((len(places),), jnp.int32),
        cost_estimate=LIGHT,
        name="plan",
    )(me, placement, *after)
    return plan, places


def line_schedule(opens, experts, cap, ride_from):
    chunks = range(len(opens))
    own, far = list(chunks), list(chunks)
    fresh = [("x", c, i) for c in chunks for i in range(CORES)]
    near = [("near", c, s) for c in chunks for s in range(cap, experts)]
    middle, inwards, outwards = [], [], []
    arrived, relayed, ride_due = [], [], {"in": ride_from}
    n = 0
    while own or arrived or far or near or fresh or relayed or ride_due:
        across, ins, outs = [], [], []
        if arrived and arrived[0][0] <= n:
            c = arrived.pop(0)[1]
            across = [("far", c, s) for s in range(cap)]
        elif own and opens[own[0]] <= n:
            c = own.pop(0)
            across = [("own", c, s) for s in range(cap)]
        if across:
            relayed += [(n + 2, (across[0][0], c, i)) for i in range(CORES)]
        if ride_due.get("across", n + 1) <= n and (not across or across[0][0] == "own"):
            across.append(("ride", 0, 0))
            del ride_due["across"]
            ride_due["out"] = n + 2
        if far and opens[far[0]] <= n:
            c = far.pop(0)
            ins = [("far", c, s) for s in range(cap)]
            arrived.append((n + 2, c))
        else:
            if ride_due.get("in", n + 1) <= n:
                ins = [("ride", 0, 0), ("ride", 0, 1)]
                del ride_due["in"]
                ride_due["across"] = n + 2
            while near and opens[near[0][1]] <= n and len(ins) < cap:
                ins.append(near.pop(0))
        while relayed and relayed[0][0] <= n and len(outs) < cap:
            outs.append(relayed.pop(0)[1])
        if ride_due.get("out", n + 1) <= n and len(outs) < cap:
            outs.append(("ride", 0, 0))
            del ride_due["out"]
        while fresh and opens[fresh[0][1]] <= n and len(outs) < cap:
            outs.append(fresh.pop(0))
        middle.append(across)
        inwards.append(ins)
        outwards.append(outs)
        n += 1
    return middle, inwards, outwards


def link_pairs(chip_pairs, swap_chips=()):
    pairs = []
    for core in range(CORES):
        for a, b in chip_pairs:
            pairs.append((a * CORES + core, b * CORES + core))
        for chip in swap_chips:
            pairs.append((chip * CORES + core, chip * CORES + 1 - core))
    return pairs


EDGES = ((0, 1), (1, 0), (2, 3), (3, 2))


def line_exchange(x_first, quant_rest, dequant, plan, places, routed, shapes, cap):
    experts, blocks, trains, owners = shapes
    features = x_first.shape[-1]
    rows = BLOCK // trains
    shape = (trains, 1, rows, features)
    chunks = [(m, b) for m in range(3) for b in range(blocks)]
    count = len(chunks)
    opens = [0 if m == 0 else 4 for m, _ in chunks]
    ride_from = 8
    middle, inwards, outwards = line_schedule(opens, experts, cap, ride_from)
    rounds = len(outwards)
    edge_pairs = link_pairs(EDGES)
    middle_pairs = link_pairs([(1, 2), (2, 1)], swap_chips=(0, 3))
    swap_pairs = link_pairs([], swap_chips=range(4))
    is_inner, is_outer = (places["inner"], 1), (places["inner"], 0)
    on_core = [(places["core"], core) for core in range(CORES)]
    got_edge, got_middle, where = {}, {}, {}
    last = [x_first]

    x_rest = lax.all_to_all(quant_rest, "train", split_axis=0, concat_axis=0, tiled=True)

    def local(c, name):
        m, b = chunks[c]
        if m == 0:
            return x_first, ("expert", places[name], 0, b)
        return x_rest, ("expert", places[name], (m - 1) * experts, b)

    def packed(pieces, after=()):
        last[0] = pack(plan, shape, pieces, [last[0]] + list(after))
        return last[0]

    ready = {(c, 0): opens[c] for c in range(count)}

    def note(c, position, n):
        ready[c, position] = max(ready.get((c, position), 0), n)

    from_kind = {"x": 1, "own": 2, "far": 3}
    kind_of = {position: kind for kind, position in from_kind.items()}
    for n in range(rounds):
        for i, piece in enumerate(middle[n]):
            where[("across",) + piece] = (n, i)
            if piece[0] != "ride":
                note(piece[1], 2 if piece[0] == "own" else 3, n)
        for i, piece in enumerate(inwards[n]):
            where[("in",) + piece] = (n, i)
            if piece[0] != "ride":
                note(piece[1], 1, n)
        for i, piece in enumerate(outwards[n]):
            where[("out",) + piece] = (n, i)
            if piece[0] != "ride":
                note(piece[1], from_kind[piece[0]], n)

    def across(kind, c):
        return got_middle[where["across", kind, c, 0][0]]

    def find(c, position, who):
        if position == 0:
            return [((),) + local(c, who)]
        choices = []
        if position == 1:
            for slot in range(experts):
                n, i = where["in", "far" if slot < cap else "near", c, slot]
                test = (places[f"there_{who}"], slot)
                choices.append(((is_inner, test), got_edge[n], ("is", i)))
        else:
            got = across(kind_of[position], c)
            choices.append(((is_inner,), got, ("at", places[f"here_{who}"])))
        for core in range(CORES):
            n, i = where["out", kind_of[position], c, core if who == "own" else 1 - core]
            choices.append(((is_outer, on_core[core]), got_edge[n], ("is", i)))
        return choices

    to_swap = sorted((ready[c, p], c, p) for c in range(count) for p in range(4))
    to_place = []
    outs = [None, None, None]

    def swap(n, by):
        taken = []
        while to_swap and to_swap[0][0] <= by and len(taken) < 3:
            taken.append(to_swap.pop(0))
        if taken:
            got = lax.ppermute(
                packed([find(c, p, "mate") for _, c, p in taken]), "roll", swap_pairs
            )
            to_place.append((n, got, [(c, p) for _, c, p in taken]))
        return bool(taken)

    def place(got, taken):
        for c in sorted({c for c, _ in taken}):
            m, b = chunks[c]
            here = [(i, p) for i, (other, p) in enumerate(taken) if other == c]
            pieces = [find(c, p, "own") for _, p in here]
            pieces += [[((), got, ("is", i))] for i, _ in here]
            sources = [places[f"from_own{p}"] for _, p in here]
            sources += [places[f"from_mate{p}"] for _, p in here]
            outs[m], last[0] = place_pieces(
                plan, shape, owners, pieces, sources, b, blocks, outs[m], (last[0],)
            )

    ride = {}
    tokens, ids, weights = routed
    ups, down = dequant[:-1], dequant[-1]

    def ride_first():
        pre, columns = None, 2 * blocks
        for restored in ups:
            for b in range(restored.shape[1]):
                column = 0 if pre is None else column + 1
                pre = pre_activations(tokens, ids, restored, b, pre, column, columns, (last[0],))
                last[0] = pre
        ride["pre"] = lax.psum(pre, "train")
    def ride_mix():
        ride["keep"], going = mix_experts(
            ride["pre"], ids, weights, down, plan, places, (last[0],)
        )
        last[0] = ride["keep"]
        going = going.reshape((-1,) + shape)
        ride["swapped"] = lax.ppermute(going, "roll", swap_pairs)

    def ride_cores():
        got = ride["swapped"].reshape(-1, features)
        ride["sums"], going = sum_cores(plan, places, ride["keep"], got, (last[0],))
        last[0] = ride["sums"]
        ride["in"] = going.reshape((-1,) + shape)

    def ride_in():
        n, i = where["in", "ride", 0, 0]
        got = got_edge[n].reshape(-1, BLOCK, features)
        ride["inner"], going = sum_inwards(plan, places, ride["sums"], got, i, (last[0],))
        last[0] = ride["inner"]
        ride["across"] = going.reshape((-1,) + shape)

    def ride_across():
        n, i = where["across", "ride", 0, 0]
        got = got_middle[n].reshape(-1, BLOCK, features)
        ride["final"], going = sum_across(
            plan, places, ride["sums"], ride["inner"], got, i, (last[0],)
        )
        last[0] = ride["final"]
        ride["out"] = going.reshape((-1,) + shape)

    def ride_out():
        n, i = where["out", "ride", 0, 0]
        got = got_edge[n].reshape(-1, BLOCK, features)
        ride["mixed"] = sum_outwards(
            plan, places, ride["sums"], ride["final"], got, i, (last[0],)
        )
        last[0] = ride["mixed"]

    spare = local(0, "own")
    for n in range(rounds):
        swap(n, n - 2)
        if middle[n]:
            if where.get(("across", "ride", 0, 0), (-1,))[0] == n:
                ride_in()
            pieces = []
            for kind, c, slot in middle[n]:
                if kind == "own":
                    pieces.append([((),) + local(c, f"send{slot}")])
                elif kind == "ride":
                    pieces.append([((), ride["across"], ("is", 0))])
                else:
                    m, i = where["in", kind, c, slot]
                    pieces.append([((), got_edge[m], ("is", i))])
            after = [got_middle[n - 2]] if n - 2 in got_middle else []
            got_middle[n] = lax.ppermute(packed(pieces, after), "roll", middle_pairs)
        if where["out", "ride", 0, 0][0] == n:
            ride_across()
        pieces = []
        for i in range(max(len(inwards[n]), len(outwards[n]))):
            choices = [((is_inner,),) + spare, ((is_outer,),) + spare]
            if i < len(outwards[n]):
                kind, c, core = outwards[n][i]
                if kind == "x":
                    choices[0] = ((is_inner,),) + local(c, f"out{core}")
                elif kind == "ride":
                    choices[0] = ((is_inner,), ride["out"], ("is", 0))
                else:
                    index = ("at", places[f"here_out{core}"])
                    choices[0] = ((is_inner,), across(kind, c), index)
            if i < len(inwards[n]):
                kind, c, slot = inwards[n][i]
                if kind == "ride":
                    choices[1] = ((is_outer,), ride["in"], ("is", slot))
                else:
                    choices[1] = ((is_outer,),) + local(c, f"send{slot}")
            pieces.append(choices)
        if pieces:
            after = [got_edge[n - 2]] if n - 2 in got_edge else []
            got_edge[n] = lax.ppermute(packed(pieces, after), "roll", edge_pairs)
        if n == 0:
            ride_first()
        if n == ride_from - 3:
            ride_mix()
        if n == ride_from - 1:
            ride_cores()
        if n == where["out", "ride", 0, 0][0] + 2:
            ride_out()
        while to_place and to_place[0][0] <= n - 2:
            place(*to_place.pop(0)[1:])
    while to_swap:
        swap(rounds, to_swap[0][0])
    if "mixed" not in ride:
        ride_out()
    for _, got, taken in to_place:
        place(got, taken)
    return tuple(outs) + (ride["mixed"],)


def direct_exchange(quants, placement, trains, owners):
    outs = []
    for quant in quants:
        _, experts, blocks, rows, features = quant.shape
        x = lax.all_to_all(quant, "train", split_axis=0, concat_axis=0, tiled=True)
        x = jnp.transpose(x, (1, 2, 3, 0, 4)).reshape(experts, blocks, rows, trains * features)
        picked = jnp.take(x, placement, axis=0)
        got = lax.all_to_all(picked, "roll", split_axis=0, concat_axis=0, tiled=True)
        outs.append(got.reshape(owners * blocks, rows, trains * features))
    return outs


def pre_activation_kernel(experts, top, tok_ref, ids_ref, w_ref, *refs):
    out_ref = refs[-1]
    features = tok_ref.shape[1]
    weights = w_ref[...].reshape(experts * BLOCK, features)
    pre = lax.dot_general(
        tok_ref[...], weights, (((1,), (1,)), ((), ())), preferred_element_type=jnp.float32
    )
    for k in range(top):
        total = jnp.zeros((pre.shape[0], BLOCK), jnp.float32)
        for expert in range(experts):
            part = pre[:, expert * BLOCK : (expert + 1) * BLOCK]
            total = total + jnp.where(ids_ref[:, k : k + 1] == expert, part, 0.0)
        out_ref[:, k * BLOCK : (k + 1) * BLOCK] = total


def pre_activations(tokens, ids, restored, block, out, column, columns, after=()):
    count, features = tokens.shape
    experts, top = restored.shape[0], ids.shape[1]
    tile = min(count, 2 * BLOCK)
    operands = [tokens, ids, restored] + list(after) + ([] if out is None else [out])
    return pl.pallas_call(
        functools.partial(pre_activation_kernel, experts, top),
        grid=(count // tile,),
        in_specs=[
            pl.BlockSpec((tile, features), lambda i: (i, 0)),
            pl.BlockSpec((tile, top), lambda i: (i, 0)),
            pl.BlockSpec((experts, 1, BLOCK, features), lambda i: (0, block, 0, 0)),
        ]
        + [any_spec()] * (len(operands) - 3),
        out_specs=pl.BlockSpec((tile, top * BLOCK), lambda i: (i, column)),
        out_shape=jax.ShapeDtypeStruct((count, columns * top * BLOCK), jnp.float32),
        input_output_aliases={} if out is None else {len(operands) - 1: 0},
        compiler_params=pltpu.CompilerParams(vmem_limit_bytes=VMEM_BYTES),
        cost_estimate=LIGHT,
        name="pre_activations",
    )(*operands)


def mix_rows(experts, top, blocks, pre_ref, ids_ref, weights_ref, down_ref):
    width = top * BLOCK
    count, features = ids_ref.shape[0], down_ref.shape[-1]
    hidden = {}
    for b in range(blocks):
        for k in range(top):
            start = b * width + k * BLOCK
            gate = pre_ref[:, start : start + BLOCK]
            up = pre_ref[:, blocks * width + start : blocks * width + start + BLOCK]
            value = gate / (1.0 + jnp.exp(-gate)) * up
            hidden[b, k] = value.astype(jnp.bfloat16).astype(jnp.float32)
    total = jnp.zeros((count, features), jnp.float32)
    for expert in range(experts):
        weight = jnp.zeros((count, 1), jnp.float32)
        for k in range(top):
            weight = weight + jnp.where(
                ids_ref[:, k : k + 1] == expert, weights_ref[:, k : k + 1], 0.0
            )
        value = jnp.zeros((count, features), jnp.float32)
        for b in range(blocks):
            routed = jnp.zeros((count, BLOCK), jnp.float32)
            for k in range(top):
                routed = routed + jnp.where(ids_ref[:, k : k + 1] == expert, hidden[b, k], 0.0)
            value = value + jnp.dot(
                routed.astype(jnp.bfloat16), down_ref[expert, b], preferred_element_type=jnp.float32
            )
        total = total + weight * value
    return total


def mix_kernel(sizes, pre_ref, ids_ref, weights_ref, down_ref, out_ref):
    out_ref[...] = mix_rows(*sizes, pre_ref, ids_ref, weights_ref, down_ref)


def mix_split_kernel(sizes, core, pre_ref, ids_ref, weights_ref, down_ref, plan_ref, *refs):
    keep_ref, send_ref = refs[-2:]
    total = mix_rows(*sizes, pre_ref, ids_ref, weights_ref, down_ref)
    half = total.shape[0] // CORES
    first = plan_ref[core] == 0
    keep_ref[0] = jnp.where(first, total[:half], total[half:])
    send_ref[...] = jnp.where(first, total[half:], total[:half]).astype(send_ref.dtype)


def mix_specs(pre, ids, down, tile):
    return [
        pl.BlockSpec((tile, pre.shape[1]), lambda i: (i, 0)),
        pl.BlockSpec((tile, ids.shape[1]), lambda i: (i, 0)),
        pl.BlockSpec((tile, ids.shape[1]), lambda i: (i, 0)),
        pl.BlockSpec(down.shape, lambda i: (0, 0, 0, 0)),
    ]


def mix_experts(pre, ids, weights, down, plan=None, places=None, after=()):
    count, top = ids.shape
    experts, blocks, _, features = down.shape
    sizes = (experts, top, blocks)
    tile = min(count, BLOCK)
    params = pltpu.CompilerParams(vmem_limit_bytes=VMEM_BYTES)
    if plan is None:
        return pl.pallas_call(
            functools.partial(mix_kernel, sizes),
            grid=(count // tile,),
            in_specs=mix_specs(pre, ids, down, tile),
            out_specs=pl.BlockSpec((tile, features), lambda i: (i, 0)),
            out_shape=jax.ShapeDtypeStruct((count, features), jnp.float32),
            compiler_params=params,
            cost_estimate=LIGHT,
            name="mix_experts",
        )(pre, ids, weights, down)
    half = tile // CORES
    return pl.pallas_call(
        functools.partial(mix_split_kernel, sizes, places["core"]),
        grid=(count // tile,),
        in_specs=mix_specs(pre, ids, down, tile) + [smem_spec()] + [any_spec()] * len(after),
        out_specs=[
            pl.BlockSpec((1, half, features), lambda i: (i, 0, 0)),
            pl.BlockSpec((half, features), lambda i: (i, 0)),
        ],
        out_shape=[
            jax.ShapeDtypeStruct((count // tile, half, features), jnp.float32),
            jax.ShapeDtypeStruct((count // CORES, features), jnp.bfloat16),
        ],
        compiler_params=params,
        cost_estimate=LIGHT,
        name="mix_experts",
    )(pre, ids, weights, down, plan, *after)


def sum_call(kernel, name, out_shape, plan, arrays, piece, after):
    vmem = pl.BlockSpec(memory_space=pltpu.VMEM)
    operands = [plan] + list(arrays)
    specs = [smem_spec()] + [vmem] * len(arrays)
    if piece is not None:
        array, first, number = piece
        operands += [array] * number
        for n in range(number):
            specs.append(
                pl.BlockSpec((1,) + array.shape[1:], lambda i, n=n: (first + n, 0, 0))
            )
    return pl.pallas_call(
        kernel,
        grid=(1,),
        in_specs=specs + [any_spec()] * len(after),
        out_specs=[vmem] * len(out_shape) if isinstance(out_shape, list) else vmem,
        out_shape=out_shape,
        compiler_params=pltpu.CompilerParams(vmem_limit_bytes=VMEM_BYTES),
        cost_estimate=LIGHT,
        name=name,
    )(*operands, *after)


def sum_cores_kernel(places, plan_ref, keep_ref, got_ref, *refs):
    sums_ref, send_ref = refs[-2:]
    chips, tokens, features = keep_ref.shape
    for chip in range(chips):
        rows = slice(chip * tokens, (chip + 1) * tokens)
        sums_ref[chip] = keep_ref[chip] + got_ref[rows, :].astype(jnp.float32)
    side, chip = plan_ref[places["side"]], plan_ref[places["chip"]]
    for n in range(2):
        send_ref[n * tokens : (n + 1) * tokens, :] = sums_ref[2 * (1 - side) + n].astype(
            send_ref.dtype
        )
    partner = sums_ref[1 + 4 * side - chip].astype(send_ref.dtype)
    for n in range(2, 4):
        send_ref[n * tokens : (n + 1) * tokens, :] = partner


def sum_cores(plan, places, keep, got, after=()):
    _, tokens, features = keep.shape
    out_shape = [
        jax.ShapeDtypeStruct(keep.shape, jnp.float32),
        jax.ShapeDtypeStruct((4 * tokens, features), jnp.bfloat16),
    ]
    kernel = functools.partial(sum_cores_kernel, places)
    return sum_call(kernel, "sum_cores", out_shape, plan, [keep, got], None, after)


def sum_inwards_kernel(places, plan_ref, sums_ref, over_ref, here_ref, *refs):
    inner_ref, send_ref = refs[-2:]
    tokens = inner_ref.shape[0]
    side, chip = plan_ref[places["side"]], plan_ref[places["chip"]]
    for n in range(2):
        rows = slice(n * tokens, (n + 1) * tokens)
        total = sums_ref[2 * (1 - side) + n] + over_ref[0, rows, :].astype(jnp.float32)
        send_ref[rows, :] = total.astype(send_ref.dtype)
    inner_ref[...] = sums_ref[chip] + here_ref[0, :tokens, :].astype(jnp.float32)


def sum_inwards(plan, places, sums, got, first, after=()):
    _, tokens, features = sums.shape
    out_shape = [
        jax.ShapeDtypeStruct((tokens, features), jnp.float32),
        jax.ShapeDtypeStruct((2 * tokens, features), jnp.bfloat16),
    ]
    kernel = functools.partial(sum_inwards_kernel, places)
    return sum_call(kernel, "sum_inwards", out_shape, plan, [sums], (got, first, 2), after)


def sum_across_kernel(places, plan_ref, sums_ref, inner_ref, got_ref, *refs):
    final_ref, send_ref = refs[-2:]
    tokens = inner_ref.shape[0]
    side, chip = plan_ref[places["side"]], plan_ref[places["chip"]]
    place = chip - 2 * side
    low = got_ref[0, :tokens, :].astype(jnp.float32)
    high = got_ref[0, tokens:, :].astype(jnp.float32)
    final_ref[...] = inner_ref[...] + jnp.where(place == 0, low, high)
    total = sums_ref[1 + 4 * side - chip] + jnp.where(place == 0, high, low)
    for n in range(2):
        send_ref[n * tokens : (n + 1) * tokens, :] = total.astype(send_ref.dtype)


def sum_across(plan, places, sums, inner, got, first, after=()):
    _, tokens, features = sums.shape
    out_shape = [
        jax.ShapeDtypeStruct((tokens, features), jnp.float32),
        jax.ShapeDtypeStruct((2 * tokens, features), jnp.bfloat16),
    ]
    kernel = functools.partial(sum_across_kernel, places)
    return sum_call(kernel, "sum_across", out_shape, plan, [sums, inner], (got, first, 1), after)


def sum_outwards_kernel(places, plan_ref, sums_ref, final_ref, got_ref, *refs):
    out_ref = refs[-1]
    tokens = final_ref.shape[0]
    outer = sums_ref[plan_ref[places["chip"]]] + got_ref[0, :tokens, :].astype(jnp.float32)
    out_ref[...] = jnp.where(plan_ref[places["inner"]] == 1, final_ref[...], outer).astype(
        out_ref.dtype
    )


def sum_outwards(plan, places, sums, final, got, first, after=()):
    out_shape = jax.ShapeDtypeStruct(final.shape, jnp.bfloat16)
    kernel = functools.partial(sum_outwards_kernel, places)
    return sum_call(kernel, "sum_outwards", out_shape, plan, [sums, final], (got, first, 1), after)


def gather_tokens(tokens, expert_ids, gate_weights, features):
    mine = lax.dynamic_slice_in_dim(tokens, lax.axis_index("train") * features, features, axis=1)
    top = expert_ids.shape[1]
    high = lax.reduce_precision(gate_weights, 8, 7)
    middle = lax.reduce_precision(gate_weights - high, 8, 7)
    low = gate_weights - high - middle
    beside = jnp.concatenate((expert_ids.astype(jnp.float32), high, middle, low), axis=1)
    beside = jnp.pad(beside, ((0, 0), (0, BLOCK - 4 * top))).astype(jnp.bfloat16)
    every = lax.all_gather(jnp.concatenate((mine, beside), axis=1), "roll", axis=0, tiled=True)
    side = every[:, features : features + 4 * top].astype(jnp.float32)
    ids = side[:, :top].astype(jnp.int32)
    weights = side[:, top : 2 * top] + side[:, 2 * top : 3 * top] + side[:, 3 * top :]
    return every[:, :features], ids, weights


def per_device(master_gate, master_up, master_down, tokens, expert_ids, gate_weights, placement):
    trains = lax.axis_size("train")
    owners = lax.axis_size("roll")
    experts, hidden_rows, features = master_gate.shape
    blocks = hidden_rows // BLOCK
    if owners // CORES == 4 and CORES * tokens.shape[0] == BLOCK:
        quant, gate = quantize(master_gate, 0, blocks, trains, experts)
        x_first = lax.all_to_all(quant, "train", split_axis=0, concat_axis=0, tiled=True)
        plan, places = make_plan(placement, experts, owners, (quant,))
        rest, up = quantize(master_up, 0, blocks, trains, 2 * experts, 0, None, (plan,))
        rest, down = quantize(master_down, 0, blocks, trains, 2 * experts, experts, rest)
        dequant = (gate, up, down)
        routed = gather_tokens(tokens, expert_ids, gate_weights, features)
        most = min(experts, owners // 2)
        shapes = (experts, blocks, trains, owners)

        def branch(cap, x_first, rest, dequant, plan, routed):
            return line_exchange(x_first, rest, dequant, plan, places, routed, shapes, cap)

        outs = lax.cond(
            plan[places["most"]] <= most - 1,
            functools.partial(branch, most - 1),
            functools.partial(branch, most),
            x_first,
            rest,
            dequant,
            plan,
            routed,
        )
    else:
        masters = (master_gate, master_up, master_down)
        quants, dequant = zip(*[quantize(w, 0, blocks, trains, experts) for w in masters])
        every, ids, weights = gather_tokens(tokens, expert_ids, gate_weights, features)
        outs = direct_exchange(quants, placement, trains, owners)
        pre = None
        for n in range(2 * blocks):
            restored = dequant[n // blocks]
            pre = pre_activations(every, ids, restored, n % blocks, pre, n, 2 * blocks)
        mixed = mix_experts(lax.psum(pre, "train"), ids, weights, dequant[2])
        mixed = lax.psum_scatter(mixed, "roll", scatter_dimension=0, tiled=True)
        outs = tuple(outs) + (mixed.astype(jnp.bfloat16),)
    return tuple(out[None] for out in outs[:3]) + (outs[3],)


def solution(mesh):
    in_specs = (
        P(None, "roll", "train"),
        P(None, "roll", "train"),
        P(None, "roll", "train"),
        P("roll", None),
        P("roll", None),
        P("roll", None),
        P(),
    )
    out_specs = (
        P("roll", None, "train", None),
        P("roll", None, "train", None),
        P("roll", None, "train", None),
        P("roll", "train"),
    )
    return jax.shard_map(
        per_device, mesh=mesh, in_specs=in_specs, out_specs=out_specs, check_vma=False
    )
```

```python
import functools

import jax
import jax.numpy as jnp
from jax import lax
from jax.experimental import pallas as pl
from jax.experimental.pallas import tpu as pltpu
from jax.sharding import PartitionSpec as P

BLOCK = 128
CORES = 2
VMEM_BYTES = 48 * 1024 * 1024
LIGHT = pl.CostEstimate(flops=1, bytes_accessed=1, transcendentals=0)


def any_spec():
    return pl.BlockSpec(memory_space=pl.ANY)


def smem_spec():
    return pl.BlockSpec(memory_space=pltpu.SMEM)


def quantize_kernel(trains, x_ref, *refs):
    q_ref, d_ref = refs[-2:]
    rows = BLOCK // trains
    features = x_ref.shape[-1]
    for col in range(features // BLOCK):
        cols = slice(col * BLOCK, (col + 1) * BLOCK)
        block = x_ref[0, :, cols]
        peak = jnp.max(jnp.max(jnp.abs(block), axis=0, keepdims=True), axis=1, keepdims=True)
        scale = peak.astype(jnp.bfloat16).astype(jnp.float32)
        quant = (block * (1.0 / scale)).astype(jnp.bfloat16)
        q_ref[:, 0, 0, :, cols] = quant.reshape(trains, rows, BLOCK)
        d_ref[0, 0, :, cols] = (quant.astype(jnp.float32) * scale).astype(jnp.bfloat16)


def quantize(master, first, blocks, trains, slots, base=0, into=None, after=()):
    experts, _, features = master.shape
    rows = BLOCK // trains
    operands = [master] + list(after) + ([] if into is None else [into])
    return pl.pallas_call(
        functools.partial(quantize_kernel, trains),
        grid=(experts, blocks),
        in_specs=[pl.BlockSpec((1, BLOCK, features), lambda e, b: (e, first + b, 0))]
        + [any_spec()] * (len(operands) - 1),
        out_specs=[
            pl.BlockSpec((trains, 1, 1, rows, features), lambda e, b: (0, base + e, b, 0, 0)),
            pl.BlockSpec((1, 1, BLOCK, features), lambda e, b: (e, b, 0, 0)),
        ],
        out_shape=[
            jax.ShapeDtypeStruct((trains, slots, blocks, rows, features), jnp.bfloat16),
            jax.ShapeDtypeStruct((experts, blocks, BLOCK, features), jnp.bfloat16),
        ],
        input_output_aliases={} if into is None else {len(operands) - 1: 0},
        compiler_params=pltpu.CompilerParams(vmem_limit_bytes=VMEM_BYTES),
        cost_estimate=LIGHT,
        name="quantize",
    )(*operands)


def start_choice(plan_ref, arrays, choice, target, sem):
    tests, array, (kind, n, *more) = choice
    ref = arrays[array]
    if kind == "is":
        view = ref.at[n]
    elif kind == "at":
        view = ref.at[plan_ref[n]]
    else:
        view = ref.at[:, plan_ref[n] + more[0], pl.ds(more[1], 1)]
    hit = None
    for place, value in tests:
        test = plan_ref[place] == value
        hit = test if hit is None else hit & test

    def go():
        pltpu.make_async_copy(view, target, sem).start()

    if hit is None:
        go()
    else:
        pl.when(hit)(go)


def pack_kernel(pieces, n_in, plan_ref, *refs):
    arrays = refs[:n_in]
    out, held, sem_in, sem_out = refs[-4:]
    for n, choices in enumerate(pieces):
        for choice in choices:
            start_choice(plan_ref, arrays, choice, held.at[n], sem_in.at[n])
    for n in range(len(pieces)):
        pltpu.make_async_copy(held.at[n], held.at[n], sem_in.at[n]).wait()
        pltpu.make_async_copy(held.at[n], out.at[n], sem_out.at[n]).start()
    for n in range(len(pieces)):
        pltpu.make_async_copy(held.at[n], out.at[n], sem_out.at[n]).wait()


class Arrays:
    def __init__(self):
        self.items = []

    def add(self, array):
        for n, item in enumerate(self.items):
            if item is array:
                return n
        self.items.append(array)
        return len(self.items) - 1


def number_choices(pieces, arrays):
    return [[(tests, arrays.add(a), index) for tests, a, index in choices] for choices in pieces]


def pack(plan, shape, pieces, after=()):
    arrays = Arrays()
    pieces = number_choices(pieces, arrays)
    n_in = len(arrays.items)
    size = len(pieces)
    for dim in shape:
        size *= dim
    operands = arrays.items + list(after)
    return pl.pallas_call(
        functools.partial(pack_kernel, pieces, n_in),
        in_specs=[smem_spec()] + [any_spec()] * len(operands),
        out_specs=any_spec(),
        out_shape=jax.ShapeDtypeStruct((len(pieces),) + shape, jnp.bfloat16),
        scratch_shapes=[
            pltpu.VMEM((len(pieces),) + shape, jnp.bfloat16),
            pltpu.SemaphoreType.DMA((len(pieces),)),
            pltpu.SemaphoreType.DMA((len(pieces),)),
        ],
        compiler_params=pltpu.CompilerParams(vmem_limit_bytes=VMEM_BYTES),
        cost_estimate=LIGHT,
        name="pack",
    )(plan, *operands)


def place_kernel(pieces, sources, first, blocks, n_in, plan_ref, *refs):
    arrays = refs[:n_in]
    out, mark, held, sem_in, sem_out = refs[-5:]
    trains, count, _, features = held.shape[1:]
    for n, choices in enumerate(pieces):
        for choice in choices:
            start_choice(plan_ref, arrays, choice, held.at[n], sem_in.at[n])
    mark[...] = jnp.zeros_like(mark)
    stores = []
    for n in range(len(pieces)):
        pltpu.make_async_copy(held.at[n], held.at[n], sem_in.at[n]).wait()
        start = plan_ref[sources[n]] * blocks + first
        for part in range(trains):
            store = pltpu.make_async_copy(
                held.at[n, part],
                out.at[pl.ds(start, count), :, pl.ds(part * features, features)],
                sem_out.at[n, part],
            )
            store.start()
            stores.append(store)
    for store in stores:
        store.wait()


def place_pieces(plan, shape, owners, pieces, sources, first, blocks, out, after=()):
    trains, count, rows, features = shape
    arrays = Arrays()
    pieces = number_choices(pieces, arrays)
    n_in = len(arrays.items)
    operands = arrays.items + list(after) + ([] if out is None else [out])
    return pl.pallas_call(
        functools.partial(place_kernel, pieces, sources, first, blocks, n_in),
        in_specs=[smem_spec()] + [any_spec()] * len(operands),
        out_specs=[any_spec(), pl.BlockSpec(memory_space=pltpu.VMEM)],
        out_shape=[
            jax.ShapeDtypeStruct((owners * blocks, rows, trains * features), jnp.bfloat16),
            jax.ShapeDtypeStruct((8, BLOCK), jnp.float32),
        ],
        scratch_shapes=[
            pltpu.VMEM((len(pieces),) + shape, jnp.bfloat16),
            pltpu.SemaphoreType.DMA((len(pieces),)),
            pltpu.SemaphoreType.DMA((len(pieces), trains)),
        ],
        input_output_aliases={} if out is None else {len(operands): 0},
        compiler_params=pltpu.CompilerParams(vmem_limit_bytes=VMEM_BYTES),
        cost_estimate=LIGHT,
        name="place_pieces",
    )(plan, *operands)


def plan_places(experts):
    names = [f"send{slot}" for slot in range(experts)]
    names += ["inner", "core", "chip", "side", "own", "mate", "out0", "out1", "most"]
    names += [f"{list_}_{who}" for list_ in ("here", "there") for who in ("own", "mate", "out0", "out1")]
    names += [f"from_{who}{n}" for who in ("own", "mate") for n in range(4)]
    return {name: n for n, name in enumerate(names)}


def plan_kernel(experts, owners, places, me_ref, placement_ref, out_ref):
    me = me_ref[0]
    chip, core = lax.div(me, CORES), lax.rem(me, CORES)
    side = lax.div(chip, 2)
    half = owners // 2
    needs, ranks = [], []
    for s in range(2):
        need = []
        for e in range(experts):
            found = jnp.int32(0)
            for o in range(s * half, (s + 1) * half):
                found = jnp.where(placement_ref[o] == e, 1, found)
            need.append(found)
        rank = []
        for e in range(experts):
            total = jnp.int32(0)
            for other in range(experts):
                if other != e:
                    ahead = need[other] >= need[e] if other < e else need[other] > need[e]
                    total = total + jnp.where(ahead, 1, 0)
            rank.append(total)
        needs.append(sum(need))
        ranks.append(rank)
    here = [jnp.where(side == 0, a, b) for a, b in zip(*ranks)]
    there = [jnp.where(side == 0, b, a) for a, b in zip(*ranks)]
    outer = 3 * side
    values = {
        "inner": jnp.where((chip == 1) | (chip == 2), 1, 0),
        "core": core,
        "chip": chip,
        "side": side,
        "own": placement_ref[me],
        "mate": placement_ref[chip * CORES + 1 - core],
        "out0": placement_ref[outer * CORES],
        "out1": placement_ref[outer * CORES + 1],
        "most": jnp.maximum(*needs),
    }
    for slot in range(experts):
        values[f"send{slot}"] = sum(jnp.where(there[e] == slot, e, 0) for e in range(experts))
    for who in ("own", "mate", "out0", "out1"):
        for list_, rank in (("here", here), ("there", there)):
            values[f"{list_}_{who}"] = sum(
                jnp.where(values[who] == e, rank[e], 0) for e in range(experts)
            )
    for n, source in enumerate((chip, 1 + 4 * side - chip, 2 - side, 3 - 3 * side)):
        values[f"from_own{n}"] = source * CORES + core
        values[f"from_mate{n}"] = source * CORES + 1 - core
    for name, n in places.items():
        out_ref[n] = values[name]


def make_plan(placement, experts, owners, after=()):
    places = plan_places(experts)
    me = jnp.reshape(lax.axis_index("roll"), (1,)).astype(jnp.int32)
    plan = pl.pallas_call(
        lambda *refs: plan_kernel(experts, owners, places, refs[0], refs[1], refs[-1]),
        in_specs=[smem_spec(), smem_spec()] + [any_spec()] * len(after),
        out_specs=smem_spec(),
        out_shape=jax.ShapeDtypeStruct((len(places),), jnp.int32),
        cost_estimate=LIGHT,
        name="plan",
    )(me, placement, *after)
    return plan, places


def line_schedule(opens, experts, cap, ride_from):
    chunks = range(len(opens))
    own, far = list(chunks), list(chunks)
    fresh = [("x", c, i) for c in chunks for i in range(CORES)]
    near = [("near", c, s) for c in chunks for s in range(cap, experts)]
    middle, inwards, outwards = [], [], []
    arrived, relayed, ride_due = [], [], {"in": ride_from}
    n = 0
    while own or arrived or far or near or fresh or relayed or ride_due:
        across, ins, outs = [], [], []
        if arrived and arrived[0][0] <= n:
            c = arrived.pop(0)[1]
            across = [("far", c, s) for s in range(cap)]
        elif own and opens[own[0]] <= n:
            c = own.pop(0)
            across = [("own", c, s) for s in range(cap)]
        if across:
            relayed += [(n + 2, (across[0][0], c, i)) for i in range(CORES)]
        if ride_due.get("across", n + 1) <= n and (not across or across[0][0] == "own"):
            across.append(("ride", 0, 0))
            del ride_due["across"]
            ride_due["out"] = n + 2
        if far and opens[far[0]] <= n:
            c = far.pop(0)
            ins = [("far", c, s) for s in range(cap)]
            arrived.append((n + 2, c))
        else:
            if ride_due.get("in", n + 1) <= n:
                ins = [("ride", 0, 0), ("ride", 0, 1)]
                del ride_due["in"]
                ride_due["across"] = n + 2
            while near and opens[near[0][1]] <= n and len(ins) < cap:
                ins.append(near.pop(0))
        while relayed and relayed[0][0] <= n and len(outs) < cap:
            outs.append(relayed.pop(0)[1])
        if ride_due.get("out", n + 1) <= n and len(outs) < cap:
            outs.append(("ride", 0, 0))
            del ride_due["out"]
        while fresh and opens[fresh[0][1]] <= n and len(outs) < cap:
            outs.append(fresh.pop(0))
        middle.append(across)
        inwards.append(ins)
        outwards.append(outs)
        n += 1
    return middle, inwards, outwards


def link_pairs(chip_pairs, swap_chips=()):
    pairs = []
    for core in range(CORES):
        for a, b in chip_pairs:
            pairs.append((a * CORES + core, b * CORES + core))
        for chip in swap_chips:
            pairs.append((chip * CORES + core, chip * CORES + 1 - core))
    return pairs


EDGES = ((0, 1), (1, 0), (2, 3), (3, 2))


def line_exchange(x_first, quant_rest, dequant, plan, places, routed, shapes, cap):
    experts, blocks, trains, owners = shapes
    features = x_first.shape[-1]
    rows = BLOCK // trains
    shape = (trains, 1, rows, features)
    chunks = [(m, b) for m in range(3) for b in range(blocks)]
    count = len(chunks)
    opens = [(0, 3, 4)[m] for m, _ in chunks]
    ride_from = 8
    middle, inwards, outwards = line_schedule(opens, experts, cap, ride_from)
    rounds = len(outwards)
    edge_pairs = link_pairs(EDGES)
    middle_pairs = link_pairs([(1, 2), (2, 1)], swap_chips=(0, 3))
    swap_pairs = link_pairs([], swap_chips=range(4))
    is_inner, is_outer = (places["inner"], 1), (places["inner"], 0)
    on_core = [(places["core"], core) for core in range(CORES)]
    got_edge, got_middle, where = {}, {}, {}
    last = [x_first]

    xs = [x_first] + [
        lax.all_to_all(quant, "train", split_axis=0, concat_axis=0, tiled=True)
        for quant in quant_rest
    ]

    def local(c, name):
        m, b = chunks[c]
        return xs[m], ("expert", places[name], 0, b)

    def packed(pieces, after=()):
        last[0] = pack(plan, shape, pieces, [last[0]] + list(after))
        return last[0]

    ready = {(c, 0): opens[c] for c in range(count)}

    def note(c, position, n):
        ready[c, position] = max(ready.get((c, position), 0), n)

    from_kind = {"x": 1, "own": 2, "far": 3}
    kind_of = {position: kind for kind, position in from_kind.items()}
    for n in range(rounds):
        for i, piece in enumerate(middle[n]):
            where[("across",) + piece] = (n, i)
            if piece[0] != "ride":
                note(piece[1], 2 if piece[0] == "own" else 3, n)
        for i, piece in enumerate(inwards[n]):
            where[("in",) + piece] = (n, i)
            if piece[0] != "ride":
                note(piece[1], 1, n)
        for i, piece in enumerate(outwards[n]):
            where[("out",) + piece] = (n, i)
            if piece[0] != "ride":
                note(piece[1], from_kind[piece[0]], n)

    def across(kind, c):
        return got_middle[where["across", kind, c, 0][0]]

    def find(c, position, who):
        if position == 0:
            return [((),) + local(c, who)]
        choices = []
        if position == 1:
            for slot in range(experts):
                n, i = where["in", "far" if slot < cap else "near", c, slot]
                test = (places[f"there_{who}"], slot)
                choices.append(((is_inner, test), got_edge[n], ("is", i)))
        else:
            got = across(kind_of[position], c)
            choices.append(((is_inner,), got, ("at", places[f"here_{who}"])))
        for core in range(CORES):
            n, i = where["out", kind_of[position], c, core if who == "own" else 1 - core]
            choices.append(((is_outer, on_core[core]), got_edge[n], ("is", i)))
        return choices

    to_swap = sorted((ready[c, p], c, p) for c in range(count) for p in range(4))
    to_place = []
    outs = [None, None, None]

    def swap(n, by):
        taken = []
        while to_swap and to_swap[0][0] <= by and len(taken) < 3:
            taken.append(to_swap.pop(0))
        if taken:
            got = lax.ppermute(
                packed([find(c, p, "mate") for _, c, p in taken]), "roll", swap_pairs
            )
            to_place.append((n, got, [(c, p) for _, c, p in taken]))
        return bool(taken)

    def place(got, taken):
        for c in sorted({c for c, _ in taken}):
            m, b = chunks[c]
            here = [(i, p) for i, (other, p) in enumerate(taken) if other == c]
            pieces = [find(c, p, "own") for _, p in here]
            pieces += [[((), got, ("is", i))] for i, _ in here]
            sources = [places[f"from_own{p}"] for _, p in here]
            sources += [places[f"from_mate{p}"] for _, p in here]
            outs[m], last[0] = place_pieces(
                plan, shape, owners, pieces, sources, b, blocks, outs[m], (last[0],)
            )

    ride = {}
    tokens, ids, weights = routed
    ups, down = dequant[:-1], dequant[-1]

    def ride_first():
        pre, columns = None, 2 * blocks
        for restored in ups:
            for b in range(restored.shape[1]):
                column = 0 if pre is None else column + 1
                pre = pre_activations(tokens, ids, restored, b, pre, column, columns, (last[0],))
                last[0] = pre
        ride["pre"] = lax.psum(pre, "train")
    def ride_mix():
        ride["keep"], going = mix_experts(
            ride["pre"], ids, weights, down, plan, places, (last[0],)
        )
        last[0] = ride["keep"]
        going = going.reshape((-1,) + shape)
        ride["swapped"] = lax.ppermute(going, "roll", swap_pairs)

    def ride_cores():
        got = ride["swapped"].reshape(-1, features)
        ride["sums"], going = sum_cores(plan, places, ride["keep"], got, (last[0],))
        last[0] = ride["sums"]
        ride["in"] = going.reshape((-1,) + shape)

    def ride_in():
        n, i = where["in", "ride", 0, 0]
        got = got_edge[n].reshape(-1, BLOCK, features)
        ride["inner"], going = sum_inwards(plan, places, ride["sums"], got, i, (last[0],))
        last[0] = ride["inner"]
        ride["across"] = going.reshape((-1,) + shape)

    def ride_across():
        n, i = where["across", "ride", 0, 0]
        got = got_middle[n].reshape(-1, BLOCK, features)
        ride["final"], going = sum_across(
            plan, places, ride["sums"], ride["inner"], got, i, (last[0],)
        )
        last[0] = ride["final"]
        ride["out"] = going.reshape((-1,) + shape)

    def ride_out():
        n, i = where["out", "ride", 0, 0]
        got = got_edge[n].reshape(-1, BLOCK, features)
        ride["mixed"] = sum_outwards(
            plan, places, ride["sums"], ride["final"], got, i, (last[0],)
        )
        last[0] = ride["mixed"]

    spare = local(0, "own")
    for n in range(rounds):
        swap(n, n - 2)
        if middle[n]:
            if where.get(("across", "ride", 0, 0), (-1,))[0] == n:
                ride_in()
            pieces = []
            for kind, c, slot in middle[n]:
                if kind == "own":
                    pieces.append([((),) + local(c, f"send{slot}")])
                elif kind == "ride":
                    pieces.append([((), ride["across"], ("is", 0))])
                else:
                    m, i = where["in", kind, c, slot]
                    pieces.append([((), got_edge[m], ("is", i))])
            after = [got_middle[n - 2]] if n - 2 in got_middle else []
            got_middle[n] = lax.ppermute(packed(pieces, after), "roll", middle_pairs)
        if where["out", "ride", 0, 0][0] == n:
            ride_across()
        pieces = []
        for i in range(max(len(inwards[n]), len(outwards[n]))):
            choices = [((is_inner,),) + spare, ((is_outer,),) + spare]
            if i < len(outwards[n]):
                kind, c, core = outwards[n][i]
                if kind == "x":
                    choices[0] = ((is_inner,),) + local(c, f"out{core}")
                elif kind == "ride":
                    choices[0] = ((is_inner,), ride["out"], ("is", 0))
                else:
                    index = ("at", places[f"here_out{core}"])
                    choices[0] = ((is_inner,), across(kind, c), index)
            if i < len(inwards[n]):
                kind, c, slot = inwards[n][i]
                if kind == "ride":
                    choices[1] = ((is_outer,), ride["in"], ("is", slot))
                else:
                    choices[1] = ((is_outer,),) + local(c, f"send{slot}")
            pieces.append(choices)
        if pieces:
            after = [got_edge[n - 2]] if n - 2 in got_edge else []
            got_edge[n] = lax.ppermute(packed(pieces, after), "roll", edge_pairs)
        if n == 0:
            ride_first()
        if n == ride_from - 3:
            ride_mix()
        if n == ride_from - 1:
            ride_cores()
        if n == where["out", "ride", 0, 0][0] + 2:
            ride_out()
        while to_place and to_place[0][0] <= n - 2:
            place(*to_place.pop(0)[1:])
    while to_swap:
        early = list(to_place)
        del to_place[:]
        swap(rounds, to_swap[0][0])
        for _, got, taken in early:
            place(got, taken)
    if "mixed" not in ride:
        ride_out()
    for _, got, taken in to_place:
        place(got, taken)
    return tuple(outs) + (ride["mixed"],)


def direct_exchange(quants, placement, trains, owners):
    outs = []
    for quant in quants:
        _, experts, blocks, rows, features = quant.shape
        x = lax.all_to_all(quant, "train", split_axis=0, concat_axis=0, tiled=True)
        x = jnp.transpose(x, (1, 2, 3, 0, 4)).reshape(experts, blocks, rows, trains * features)
        picked = jnp.take(x, placement, axis=0)
        got = lax.all_to_all(picked, "roll", split_axis=0, concat_axis=0, tiled=True)
        outs.append(got.reshape(owners * blocks, rows, trains * features))
    return outs


def pre_activation_kernel(experts, top, tok_ref, ids_ref, w_ref, *refs):
    out_ref = refs[-1]
    features = tok_ref.shape[1]
    weights = w_ref[...].reshape(experts * BLOCK, features)
    pre = lax.dot_general(
        tok_ref[...], weights, (((1,), (1,)), ((), ())), preferred_element_type=jnp.float32
    )
    for k in range(top):
        total = jnp.zeros((pre.shape[0], BLOCK), jnp.float32)
        for expert in range(experts):
            part = pre[:, expert * BLOCK : (expert + 1) * BLOCK]
            total = total + jnp.where(ids_ref[:, k : k + 1] == expert, part, 0.0)
        out_ref[:, k * BLOCK : (k + 1) * BLOCK] = total


def pre_activations(tokens, ids, restored, block, out, column, columns, after=()):
    count, features = tokens.shape
    experts, top = restored.shape[0], ids.shape[1]
    tile = min(count, 2 * BLOCK)
    operands = [tokens, ids, restored] + list(after) + ([] if out is None else [out])
    return pl.pallas_call(
        functools.partial(pre_activation_kernel, experts, top),
        grid=(count // tile,),
        in_specs=[
            pl.BlockSpec((tile, features), lambda i: (i, 0)),
            pl.BlockSpec((tile, top), lambda i: (i, 0)),
            pl.BlockSpec((experts, 1, BLOCK, features), lambda i: (0, block, 0, 0)),
        ]
        + [any_spec()] * (len(operands) - 3),
        out_specs=pl.BlockSpec((tile, top * BLOCK), lambda i: (i, column)),
        out_shape=jax.ShapeDtypeStruct((count, columns * top * BLOCK), jnp.float32),
        input_output_aliases={} if out is None else {len(operands) - 1: 0},
        compiler_params=pltpu.CompilerParams(vmem_limit_bytes=VMEM_BYTES),
        cost_estimate=LIGHT,
        name="pre_activations",
    )(*operands)


def mix_rows(experts, top, blocks, pre_ref, ids_ref, weights_ref, down_ref):
    width = top * BLOCK
    count, features = ids_ref.shape[0], down_ref.shape[-1]
    hidden = {}
    for b in range(blocks):
        for k in range(top):
            start = b * width + k * BLOCK
            gate = pre_ref[:, start : start + BLOCK]
            up = pre_ref[:, blocks * width + start : blocks * width + start + BLOCK]
            value = gate / (1.0 + jnp.exp(-gate)) * up
            hidden[b, k] = value.astype(jnp.bfloat16).astype(jnp.float32)
    total = jnp.zeros((count, features), jnp.float32)
    for expert in range(experts):
        weight = jnp.zeros((count, 1), jnp.float32)
        for k in range(top):
            weight = weight + jnp.where(
                ids_ref[:, k : k + 1] == expert, weights_ref[:, k : k + 1], 0.0
            )
        value = jnp.zeros((count, features), jnp.float32)
        for b in range(blocks):
            routed = jnp.zeros((count, BLOCK), jnp.float32)
            for k in range(top):
                routed = routed + jnp.where(ids_ref[:, k : k + 1] == expert, hidden[b, k], 0.0)
            value = value + jnp.dot(
                routed.astype(jnp.bfloat16), down_ref[expert, b], preferred_element_type=jnp.float32
            )
        total = total + weight * value
    return total


def mix_kernel(sizes, pre_ref, ids_ref, weights_ref, down_ref, out_ref):
    out_ref[...] = mix_rows(*sizes, pre_ref, ids_ref, weights_ref, down_ref)


def mix_split_kernel(sizes, core, pre_ref, ids_ref, weights_ref, down_ref, plan_ref, *refs):
    keep_ref, send_ref = refs[-2:]
    total = mix_rows(*sizes, pre_ref, ids_ref, weights_ref, down_ref)
    half = total.shape[0] // CORES
    first = plan_ref[core] == 0
    keep_ref[0] = jnp.where(first, total[:half], total[half:])
    send_ref[...] = jnp.where(first, total[half:], total[:half]).astype(send_ref.dtype)


def mix_specs(pre, ids, down, tile):
    return [
        pl.BlockSpec((tile, pre.shape[1]), lambda i: (i, 0)),
        pl.BlockSpec((tile, ids.shape[1]), lambda i: (i, 0)),
        pl.BlockSpec((tile, ids.shape[1]), lambda i: (i, 0)),
        pl.BlockSpec(down.shape, lambda i: (0, 0, 0, 0)),
    ]


def mix_experts(pre, ids, weights, down, plan=None, places=None, after=()):
    count, top = ids.shape
    experts, blocks, _, features = down.shape
    sizes = (experts, top, blocks)
    tile = min(count, BLOCK)
    params = pltpu.CompilerParams(vmem_limit_bytes=VMEM_BYTES)
    if plan is None:
        return pl.pallas_call(
            functools.partial(mix_kernel, sizes),
            grid=(count // tile,),
            in_specs=mix_specs(pre, ids, down, tile),
            out_specs=pl.BlockSpec((tile, features), lambda i: (i, 0)),
            out_shape=jax.ShapeDtypeStruct((count, features), jnp.float32),
            compiler_params=params,
            cost_estimate=LIGHT,
            name="mix_experts",
        )(pre, ids, weights, down)
    half = tile // CORES
    return pl.pallas_call(
        functools.partial(mix_split_kernel, sizes, places["core"]),
        grid=(count // tile,),
        in_specs=mix_specs(pre, ids, down, tile) + [smem_spec()] + [any_spec()] * len(after),
        out_specs=[
            pl.BlockSpec((1, half, features), lambda i: (i, 0, 0)),
            pl.BlockSpec((half, features), lambda i: (i, 0)),
        ],
        out_shape=[
            jax.ShapeDtypeStruct((count // tile, half, features), jnp.float32),
            jax.ShapeDtypeStruct((count // CORES, features), jnp.bfloat16),
        ],
        compiler_params=params,
        cost_estimate=LIGHT,
        name="mix_experts",
    )(pre, ids, weights, down, plan, *after)


def sum_call(kernel, name, out_shape, plan, arrays, piece, after):
    vmem = pl.BlockSpec(memory_space=pltpu.VMEM)
    operands = [plan] + list(arrays)
    specs = [smem_spec()] + [vmem] * len(arrays)
    if piece is not None:
        array, first, number = piece
        operands += [array] * number
        for n in range(number):
            specs.append(
                pl.BlockSpec((1,) + array.shape[1:], lambda i, n=n: (first + n, 0, 0))
            )
    return pl.pallas_call(
        kernel,
        grid=(1,),
        in_specs=specs + [any_spec()] * len(after),
        out_specs=[vmem] * len(out_shape) if isinstance(out_shape, list) else vmem,
        out_shape=out_shape,
        compiler_params=pltpu.CompilerParams(vmem_limit_bytes=VMEM_BYTES),
        cost_estimate=LIGHT,
        name=name,
    )(*operands, *after)


def sum_cores_kernel(places, plan_ref, keep_ref, got_ref, *refs):
    sums_ref, send_ref = refs[-2:]
    chips, tokens, features = keep_ref.shape
    for chip in range(chips):
        rows = slice(chip * tokens, (chip + 1) * tokens)
        sums_ref[chip] = keep_ref[chip] + got_ref[rows, :].astype(jnp.float32)
    side, chip = plan_ref[places["side"]], plan_ref[places["chip"]]
    for n in range(2):
        send_ref[n * tokens : (n + 1) * tokens, :] = sums_ref[2 * (1 - side) + n].astype(
            send_ref.dtype
        )
    partner = sums_ref[1 + 4 * side - chip].astype(send_ref.dtype)
    for n in range(2, 4):
        send_ref[n * tokens : (n + 1) * tokens, :] = partner


def sum_cores(plan, places, keep, got, after=()):
    _, tokens, features = keep.shape
    out_shape = [
        jax.ShapeDtypeStruct(keep.shape, jnp.float32),
        jax.ShapeDtypeStruct((4 * tokens, features), jnp.bfloat16),
    ]
    kernel = functools.partial(sum_cores_kernel, places)
    return sum_call(kernel, "sum_cores", out_shape, plan, [keep, got], None, after)


def sum_inwards_kernel(places, plan_ref, sums_ref, over_ref, here_ref, *refs):
    inner_ref, send_ref = refs[-2:]
    tokens = inner_ref.shape[0]
    side, chip = plan_ref[places["side"]], plan_ref[places["chip"]]
    for n in range(2):
        rows = slice(n * tokens, (n + 1) * tokens)
        total = sums_ref[2 * (1 - side) + n] + over_ref[0, rows, :].astype(jnp.float32)
        send_ref[rows, :] = total.astype(send_ref.dtype)
    inner_ref[...] = sums_ref[chip] + here_ref[0, :tokens, :].astype(jnp.float32)


def sum_inwards(plan, places, sums, got, first, after=()):
    _, tokens, features = sums.shape
    out_shape = [
        jax.ShapeDtypeStruct((tokens, features), jnp.float32),
        jax.ShapeDtypeStruct((2 * tokens, features), jnp.bfloat16),
    ]
    kernel = functools.partial(sum_inwards_kernel, places)
    return sum_call(kernel, "sum_inwards", out_shape, plan, [sums], (got, first, 2), after)


def sum_across_kernel(places, plan_ref, sums_ref, inner_ref, got_ref, *refs):
    final_ref, send_ref = refs[-2:]
    tokens = inner_ref.shape[0]
    side, chip = plan_ref[places["side"]], plan_ref[places["chip"]]
    place = chip - 2 * side
    low = got_ref[0, :tokens, :].astype(jnp.float32)
    high = got_ref[0, tokens:, :].astype(jnp.float32)
    final_ref[...] = inner_ref[...] + jnp.where(place == 0, low, high)
    total = sums_ref[1 + 4 * side - chip] + jnp.where(place == 0, high, low)
    for n in range(2):
        send_ref[n * tokens : (n + 1) * tokens, :] = total.astype(send_ref.dtype)


def sum_across(plan, places, sums, inner, got, first, after=()):
    _, tokens, features = sums.shape
    out_shape = [
        jax.ShapeDtypeStruct((tokens, features), jnp.float32),
        jax.ShapeDtypeStruct((2 * tokens, features), jnp.bfloat16),
    ]
    kernel = functools.partial(sum_across_kernel, places)
    return sum_call(kernel, "sum_across", out_shape, plan, [sums, inner], (got, first, 1), after)


def sum_outwards_kernel(places, plan_ref, sums_ref, final_ref, got_ref, *refs):
    out_ref = refs[-1]
    tokens = final_ref.shape[0]
    outer = sums_ref[plan_ref[places["chip"]]] + got_ref[0, :tokens, :].astype(jnp.float32)
    out_ref[...] = jnp.where(plan_ref[places["inner"]] == 1, final_ref[...], outer).astype(
        out_ref.dtype
    )


def sum_outwards(plan, places, sums, final, got, first, after=()):
    out_shape = jax.ShapeDtypeStruct(final.shape, jnp.bfloat16)
    kernel = functools.partial(sum_outwards_kernel, places)
    return sum_call(kernel, "sum_outwards", out_shape, plan, [sums, final], (got, first, 1), after)


def gather_tokens(tokens, expert_ids, gate_weights, features):
    mine = lax.dynamic_slice_in_dim(tokens, lax.axis_index("train") * features, features, axis=1)
    top = expert_ids.shape[1]
    high = lax.reduce_precision(gate_weights, 8, 7)
    middle = lax.reduce_precision(gate_weights - high, 8, 7)
    low = gate_weights - high - middle
    beside = jnp.concatenate((expert_ids.astype(jnp.float32), high, middle, low), axis=1)
    beside = jnp.pad(beside, ((0, 0), (0, BLOCK - 4 * top))).astype(jnp.bfloat16)
    every = lax.all_gather(jnp.concatenate((mine, beside), axis=1), "roll", axis=0, tiled=True)
    side = every[:, features : features + 4 * top].astype(jnp.float32)
    ids = side[:, :top].astype(jnp.int32)
    weights = side[:, top : 2 * top] + side[:, 2 * top : 3 * top] + side[:, 3 * top :]
    return every[:, :features], ids, weights


def per_device(master_gate, master_up, master_down, tokens, expert_ids, gate_weights, placement):
    trains = lax.axis_size("train")
    owners = lax.axis_size("roll")
    experts, hidden_rows, features = master_gate.shape
    blocks = hidden_rows // BLOCK
    if owners // CORES == 4 and CORES * tokens.shape[0] == BLOCK:
        quant, gate = quantize(master_gate, 0, blocks, trains, experts)
        x_first = lax.all_to_all(quant, "train", split_axis=0, concat_axis=0, tiled=True)
        plan, places = make_plan(placement, experts, owners, (quant,))
        rest_up, up = quantize(master_up, 0, blocks, trains, experts, 0, None, (plan,))
        rest_down, down = quantize(master_down, 0, blocks, trains, experts, 0, None, (rest_up,))
        rest = (rest_up, rest_down)
        dequant = (gate, up, down)
        routed = gather_tokens(tokens, expert_ids, gate_weights, features)
        most = min(experts, owners // 2)
        shapes = (experts, blocks, trains, owners)

        def branch(cap, x_first, rest, dequant, plan, routed):
            return line_exchange(x_first, rest, dequant, plan, places, routed, shapes, cap)

        outs = lax.cond(
            plan[places["most"]] <= most - 1,
            functools.partial(branch, most - 1),
            functools.partial(branch, most),
            x_first,
            rest,
            dequant,
            plan,
            routed,
        )
    else:
        masters = (master_gate, master_up, master_down)
        quants, dequant = zip(*[quantize(w, 0, blocks, trains, experts) for w in masters])
        every, ids, weights = gather_tokens(tokens, expert_ids, gate_weights, features)
        outs = direct_exchange(quants, placement, trains, owners)
        pre = None
        for n in range(2 * blocks):
            restored = dequant[n // blocks]
            pre = pre_activations(every, ids, restored, n % blocks, pre, n, 2 * blocks)
        mixed = mix_experts(lax.psum(pre, "train"), ids, weights, dequant[2])
        mixed = lax.psum_scatter(mixed, "roll", scatter_dimension=0, tiled=True)
        outs = tuple(outs) + (mixed.astype(jnp.bfloat16),)
    return tuple(out[None] for out in outs[:3]) + (outs[3],)


def solution(mesh):
    in_specs = (
        P(None, "roll", "train"),
        P(None, "roll", "train"),
        P(None, "roll", "train"),
        P("roll", None),
        P("roll", None),
        P("roll", None),
        P(),
    )
    out_specs = (
        P("roll", None, "train", None),
        P("roll", None, "train", None),
        P("roll", None, "train", None),
        P("roll", "train"),
    )
    return jax.shard_map(
        per_device, mesh=mesh, in_specs=in_specs, out_specs=out_specs, check_vma=False
    )
```

```python
import functools

import jax
import jax.numpy as jnp
from jax import lax
from jax.experimental import pallas as pl
from jax.experimental.pallas import tpu as pltpu
from jax.sharding import PartitionSpec as P

BLOCK = 128
CORES = 2
VMEM_BYTES = 48 * 1024 * 1024
LIGHT = pl.CostEstimate(flops=1, bytes_accessed=1, transcendentals=0)


def any_spec():
    return pl.BlockSpec(memory_space=pl.ANY)


def smem_spec():
    return pl.BlockSpec(memory_space=pltpu.SMEM)


def quantize_kernel(trains, x_ref, *refs):
    q_ref, d_ref = refs[-2:]
    rows = BLOCK // trains
    features = x_ref.shape[-1]
    for col in range(features // BLOCK):
        cols = slice(col * BLOCK, (col + 1) * BLOCK)
        block = x_ref[0, :, cols]
        peak = jnp.max(jnp.max(jnp.abs(block), axis=0, keepdims=True), axis=1, keepdims=True)
        scale = peak.astype(jnp.bfloat16).astype(jnp.float32)
        quant = (block * (1.0 / scale)).astype(jnp.bfloat16)
        q_ref[:, 0, 0, :, cols] = quant.reshape(trains, rows, BLOCK)
        d_ref[0, 0, :, cols] = (quant.astype(jnp.float32) * scale).astype(jnp.bfloat16)


def quantize(master, first, blocks, trains, slots, base=0, into=None, after=()):
    experts, _, features = master.shape
    rows = BLOCK // trains
    operands = [master] + list(after) + ([] if into is None else [into])
    return pl.pallas_call(
        functools.partial(quantize_kernel, trains),
        grid=(experts, blocks),
        in_specs=[pl.BlockSpec((1, BLOCK, features), lambda e, b: (e, first + b, 0))]
        + [any_spec()] * (len(operands) - 1),
        out_specs=[
            pl.BlockSpec((trains, 1, 1, rows, features), lambda e, b: (0, base + e, b, 0, 0)),
            pl.BlockSpec((1, 1, BLOCK, features), lambda e, b: (e, b, 0, 0)),
        ],
        out_shape=[
            jax.ShapeDtypeStruct((trains, slots, blocks, rows, features), jnp.bfloat16),
            jax.ShapeDtypeStruct((experts, blocks, BLOCK, features), jnp.bfloat16),
        ],
        input_output_aliases={} if into is None else {len(operands) - 1: 0},
        compiler_params=pltpu.CompilerParams(vmem_limit_bytes=VMEM_BYTES),
        cost_estimate=LIGHT,
        name="quantize",
    )(*operands)


def start_choice(plan_ref, arrays, choice, target, sem):
    tests, array, (kind, n, *more) = choice
    ref = arrays[array]
    if kind == "is":
        view = ref.at[n]
    elif kind == "at":
        view = ref.at[plan_ref[n]]
    else:
        view = ref.at[:, plan_ref[n] + more[0], pl.ds(more[1], 1)]
    hit = None
    for place, value in tests:
        test = plan_ref[place] == value
        hit = test if hit is None else hit & test

    def go():
        pltpu.make_async_copy(view, target, sem).start()

    if hit is None:
        go()
    else:
        pl.when(hit)(go)


def pack_kernel(pieces, n_in, plan_ref, *refs):
    arrays = refs[:n_in]
    out, held, sem_in, sem_out = refs[-4:]
    for n, choices in enumerate(pieces):
        for choice in choices:
            start_choice(plan_ref, arrays, choice, held.at[n], sem_in.at[n])
    for n in range(len(pieces)):
        pltpu.make_async_copy(held.at[n], held.at[n], sem_in.at[n]).wait()
        pltpu.make_async_copy(held.at[n], out.at[n], sem_out.at[n]).start()
    for n in range(len(pieces)):
        pltpu.make_async_copy(held.at[n], out.at[n], sem_out.at[n]).wait()


class Arrays:
    def __init__(self):
        self.items = []

    def add(self, array):
        for n, item in enumerate(self.items):
            if item is array:
                return n
        self.items.append(array)
        return len(self.items) - 1


def number_choices(pieces, arrays):
    return [[(tests, arrays.add(a), index) for tests, a, index in choices] for choices in pieces]


def pack(plan, shape, pieces, after=()):
    arrays = Arrays()
    pieces = number_choices(pieces, arrays)
    n_in = len(arrays.items)
    size = len(pieces)
    for dim in shape:
        size *= dim
    operands = arrays.items + list(after)
    return pl.pallas_call(
        functools.partial(pack_kernel, pieces, n_in),
        in_specs=[smem_spec()] + [any_spec()] * len(operands),
        out_specs=any_spec(),
        out_shape=jax.ShapeDtypeStruct((len(pieces),) + shape, jnp.bfloat16),
        scratch_shapes=[
            pltpu.VMEM((len(pieces),) + shape, jnp.bfloat16),
            pltpu.SemaphoreType.DMA((len(pieces),)),
            pltpu.SemaphoreType.DMA((len(pieces),)),
        ],
        compiler_params=pltpu.CompilerParams(vmem_limit_bytes=VMEM_BYTES),
        cost_estimate=LIGHT,
        name="pack",
    )(plan, *operands)


def place_kernel(pieces, sources, first, blocks, n_in, plan_ref, *refs):
    arrays = refs[:n_in]
    out, mark, held, sem_in, sem_out = refs[-5:]
    trains, count, _, features = held.shape[1:]
    for n, choices in enumerate(pieces):
        for choice in choices:
            start_choice(plan_ref, arrays, choice, held.at[n], sem_in.at[n])
    mark[...] = jnp.zeros_like(mark)
    stores = []
    for n in range(len(pieces)):
        pltpu.make_async_copy(held.at[n], held.at[n], sem_in.at[n]).wait()
        start = plan_ref[sources[n]] * blocks + first
        for part in range(trains):
            store = pltpu.make_async_copy(
                held.at[n, part],
                out.at[pl.ds(start, count), :, pl.ds(part * features, features)],
                sem_out.at[n, part],
            )
            store.start()
            stores.append(store)
    for store in stores:
        store.wait()


def place_pieces(plan, shape, owners, pieces, sources, first, blocks, out, after=()):
    trains, count, rows, features = shape
    arrays = Arrays()
    pieces = number_choices(pieces, arrays)
    n_in = len(arrays.items)
    operands = arrays.items + list(after) + ([] if out is None else [out])
    return pl.pallas_call(
        functools.partial(place_kernel, pieces, sources, first, blocks, n_in),
        in_specs=[smem_spec()] + [any_spec()] * len(operands),
        out_specs=[any_spec(), pl.BlockSpec(memory_space=pltpu.VMEM)],
        out_shape=[
            jax.ShapeDtypeStruct((owners * blocks, rows, trains * features), jnp.bfloat16),
            jax.ShapeDtypeStruct((8, BLOCK), jnp.float32),
        ],
        scratch_shapes=[
            pltpu.VMEM((len(pieces),) + shape, jnp.bfloat16),
            pltpu.SemaphoreType.DMA((len(pieces),)),
            pltpu.SemaphoreType.DMA((len(pieces), trains)),
        ],
        input_output_aliases={} if out is None else {len(operands): 0},
        compiler_params=pltpu.CompilerParams(vmem_limit_bytes=VMEM_BYTES),
        cost_estimate=LIGHT,
        name="place_pieces",
    )(plan, *operands)


def plan_places(experts):
    names = [f"send{slot}" for slot in range(experts)]
    names += ["inner", "core", "chip", "side", "own", "mate", "out0", "out1", "most"]
    names += [f"{list_}_{who}" for list_ in ("here", "there") for who in ("own", "mate", "out0", "out1")]
    names += [f"from_{who}{n}" for who in ("own", "mate") for n in range(4)]
    return {name: n for n, name in enumerate(names)}


def plan_kernel(experts, owners, places, me_ref, placement_ref, out_ref):
    me = me_ref[0]
    chip, core = lax.div(me, CORES), lax.rem(me, CORES)
    side = lax.div(chip, 2)
    half = owners // 2
    needs, ranks = [], []
    for s in range(2):
        need = []
        for e in range(experts):
            found = jnp.int32(0)
            for o in range(s * half, (s + 1) * half):
                found = jnp.where(placement_ref[o] == e, 1, found)
            need.append(found)
        rank = []
        for e in range(experts):
            total = jnp.int32(0)
            for other in range(experts):
                if other != e:
                    ahead = need[other] >= need[e] if other < e else need[other] > need[e]
                    total = total + jnp.where(ahead, 1, 0)
            rank.append(total)
        needs.append(sum(need))
        ranks.append(rank)
    here = [jnp.where(side == 0, a, b) for a, b in zip(*ranks)]
    there = [jnp.where(side == 0, b, a) for a, b in zip(*ranks)]
    outer = 3 * side
    values = {
        "inner": jnp.where((chip == 1) | (chip == 2), 1, 0),
        "core": core,
        "chip": chip,
        "side": side,
        "own": placement_ref[me],
        "mate": placement_ref[chip * CORES + 1 - core],
        "out0": placement_ref[outer * CORES],
        "out1": placement_ref[outer * CORES + 1],
        "most": jnp.maximum(*needs),
    }
    for slot in range(experts):
        values[f"send{slot}"] = sum(jnp.where(there[e] == slot, e, 0) for e in range(experts))
    for who in ("own", "mate", "out0", "out1"):
        for list_, rank in (("here", here), ("there", there)):
            values[f"{list_}_{who}"] = sum(
                jnp.where(values[who] == e, rank[e], 0) for e in range(experts)
            )
    for n, source in enumerate((chip, 1 + 4 * side - chip, 2 - side, 3 - 3 * side)):
        values[f"from_own{n}"] = source * CORES + core
        values[f"from_mate{n}"] = source * CORES + 1 - core
    for name, n in places.items():
        out_ref[n] = values[name]


def make_plan(placement, experts, owners, after=()):
    places = plan_places(experts)
    me = jnp.reshape(lax.axis_index("roll"), (1,)).astype(jnp.int32)
    plan = pl.pallas_call(
        lambda *refs: plan_kernel(experts, owners, places, refs[0], refs[1], refs[-1]),
        in_specs=[smem_spec(), smem_spec()] + [any_spec()] * len(after),
        out_specs=smem_spec(),
        out_shape=jax.ShapeDtypeStruct((len(places),), jnp.int32),
        cost_estimate=LIGHT,
        name="plan",
    )(me, placement, *after)
    return plan, places


def line_schedule(opens, experts, cap, ride_from):
    chunks = range(len(opens))
    own, far = list(chunks), list(chunks)
    fresh = [("x", c, i) for c in chunks for i in range(CORES)]
    near = [("near", c, s) for c in chunks for s in range(cap, experts)]
    middle, inwards, outwards = [], [], []
    arrived, relayed, ride_due = [], [], {"in": ride_from}
    n = 0
    while own or arrived or far or near or fresh or relayed or ride_due:
        across, ins, outs = [], [], []
        if arrived and arrived[0][0] <= n:
            c = arrived.pop(0)[1]
            across = [("far", c, s) for s in range(cap)]
        elif own and opens[own[0]] <= n:
            c = own.pop(0)
            across = [("own", c, s) for s in range(cap)]
        if across:
            relayed += [(n + 2, (across[0][0], c, i)) for i in range(CORES)]
        if ride_due.get("across", n + 1) <= n and (not across or across[0][0] == "own"):
            across.append(("ride", 0, 0))
            del ride_due["across"]
            ride_due["out"] = n + 2
        if far and opens[far[0]] <= n:
            c = far.pop(0)
            ins = [("far", c, s) for s in range(cap)]
            arrived.append((n + 2, c))
        else:
            if ride_due.get("in", n + 1) <= n:
                ins = [("ride", 0, 0), ("ride", 0, 1)]
                del ride_due["in"]
                ride_due["across"] = n + 2
            while near and opens[near[0][1]] <= n and len(ins) < cap:
                ins.append(near.pop(0))
        while relayed and relayed[0][0] <= n and len(outs) < cap:
            outs.append(relayed.pop(0)[1])
        if ride_due.get("out", n + 1) <= n and len(outs) < cap:
            outs.append(("ride", 0, 0))
            del ride_due["out"]
        while fresh and opens[fresh[0][1]] <= n and len(outs) < cap:
            outs.append(fresh.pop(0))
        middle.append(across)
        inwards.append(ins)
        outwards.append(outs)
        n += 1
    return middle, inwards, outwards


def link_pairs(chip_pairs, swap_chips=()):
    pairs = []
    for core in range(CORES):
        for a, b in chip_pairs:
            pairs.append((a * CORES + core, b * CORES + core))
        for chip in swap_chips:
            pairs.append((chip * CORES + core, chip * CORES + 1 - core))
    return pairs


EDGES = ((0, 1), (1, 0), (2, 3), (3, 2))


def line_exchange(x_first, quant_rest, dequant, plan, places, routed, shapes, cap):
    experts, blocks, trains, owners = shapes
    features = x_first.shape[-1]
    rows = BLOCK // trains
    shape = (trains, 1, rows, features)
    chunks = [(m, b) for m in range(3) for b in range(blocks)]
    count = len(chunks)
    opens = [(0, 2, 4)[m] for m, _ in chunks]
    ride_from = 8
    middle, inwards, outwards = line_schedule(opens, experts, cap, ride_from)
    rounds = len(outwards)
    edge_pairs = link_pairs(EDGES)
    middle_pairs = link_pairs([(1, 2), (2, 1)], swap_chips=(0, 3))
    swap_pairs = link_pairs([], swap_chips=range(4))
    is_inner, is_outer = (places["inner"], 1), (places["inner"], 0)
    on_core = [(places["core"], core) for core in range(CORES)]
    got_edge, got_middle, where = {}, {}, {}
    last = [x_first]

    xs = [x_first] + [
        lax.all_to_all(quant, "train", split_axis=0, concat_axis=0, tiled=True)
        for quant in quant_rest
    ]

    def local(c, name):
        m, b = chunks[c]
        return xs[m], ("expert", places[name], 0, b)

    def packed(pieces, after=()):
        last[0] = pack(plan, shape, pieces, [last[0]] + list(after))
        return last[0]

    ready = {(c, 0): opens[c] for c in range(count)}

    def note(c, position, n):
        ready[c, position] = max(ready.get((c, position), 0), n)

    from_kind = {"x": 1, "own": 2, "far": 3}
    kind_of = {position: kind for kind, position in from_kind.items()}
    for n in range(rounds):
        for i, piece in enumerate(middle[n]):
            where[("across",) + piece] = (n, i)
            if piece[0] != "ride":
                note(piece[1], 2 if piece[0] == "own" else 3, n)
        for i, piece in enumerate(inwards[n]):
            where[("in",) + piece] = (n, i)
            if piece[0] != "ride":
                note(piece[1], 1, n)
        for i, piece in enumerate(outwards[n]):
            where[("out",) + piece] = (n, i)
            if piece[0] != "ride":
                note(piece[1], from_kind[piece[0]], n)

    def across(kind, c):
        return got_middle[where["across", kind, c, 0][0]]

    def find(c, position, who):
        if position == 0:
            return [((),) + local(c, who)]
        choices = []
        if position == 1:
            for slot in range(experts):
                n, i = where["in", "far" if slot < cap else "near", c, slot]
                test = (places[f"there_{who}"], slot)
                choices.append(((is_inner, test), got_edge[n], ("is", i)))
        else:
            got = across(kind_of[position], c)
            choices.append(((is_inner,), got, ("at", places[f"here_{who}"])))
        for core in range(CORES):
            n, i = where["out", kind_of[position], c, core if who == "own" else 1 - core]
            choices.append(((is_outer, on_core[core]), got_edge[n], ("is", i)))
        return choices

    to_swap = sorted((ready[c, p], c, p) for c in range(count) for p in range(4))
    to_place = []
    outs = [None, None, None]

    def swap(n, by):
        taken = []
        while to_swap and to_swap[0][0] <= by and len(taken) < 3:
            taken.append(to_swap.pop(0))
        if taken:
            got = lax.ppermute(
                packed([find(c, p, "mate") for _, c, p in taken]), "roll", swap_pairs
            )
            to_place.append((n, got, [(c, p) for _, c, p in taken]))
        return bool(taken)

    def place(got, taken):
        for c in sorted({c for c, _ in taken}):
            m, b = chunks[c]
            here = [(i, p) for i, (other, p) in enumerate(taken) if other == c]
            pieces = [find(c, p, "own") for _, p in here]
            pieces += [[((), got, ("is", i))] for i, _ in here]
            sources = [places[f"from_own{p}"] for _, p in here]
            sources += [places[f"from_mate{p}"] for _, p in here]
            outs[m], last[0] = place_pieces(
                plan, shape, owners, pieces, sources, b, blocks, outs[m], (last[0],)
            )

    ride = {}
    tokens, ids, weights = routed
    ups, down = dequant[:-1], dequant[-1]

    def ride_first():
        pre, columns = None, 2 * blocks
        for restored in ups:
            for b in range(restored.shape[1]):
                column = 0 if pre is None else column + 1
                pre = pre_activations(tokens, ids, restored, b, pre, column, columns, (last[0],))
                last[0] = pre
        ride["pre"] = lax.psum(pre, "train")
    def ride_mix():
        ride["keep"], going = mix_experts(
            ride["pre"], ids, weights, down, plan, places, (last[0],)
        )
        last[0] = ride["keep"]
        going = going.reshape((-1,) + shape)
        ride["swapped"] = lax.ppermute(going, "roll", swap_pairs)

    def ride_cores():
        got = ride["swapped"].reshape(-1, features)
        ride["sums"], going = sum_cores(plan, places, ride["keep"], got, (last[0],))
        last[0] = ride["sums"]
        ride["in"] = going.reshape((-1,) + shape)

    def ride_in():
        n, i = where["in", "ride", 0, 0]
        got = got_edge[n].reshape(-1, BLOCK, features)
        ride["inner"], going = sum_inwards(plan, places, ride["sums"], got, i, (last[0],))
        last[0] = ride["inner"]
        ride["across"] = going.reshape((-1,) + shape)

    def ride_across():
        n, i = where["across", "ride", 0, 0]
        got = got_middle[n].reshape(-1, BLOCK, features)
        ride["final"], going = sum_across(
            plan, places, ride["sums"], ride["inner"], got, i, (last[0],)
        )
        last[0] = ride["final"]
        ride["out"] = going.reshape((-1,) + shape)

    def ride_out():
        n, i = where["out", "ride", 0, 0]
        got = got_edge[n].reshape(-1, BLOCK, features)
        ride["mixed"] = sum_outwards(
            plan, places, ride["sums"], ride["final"], got, i, (last[0],)
        )
        last[0] = ride["mixed"]

    spare = local(0, "own")
    for n in range(rounds):
        swap(n, n - 2)
        if middle[n]:
            if where.get(("across", "ride", 0, 0), (-1,))[0] == n:
                ride_in()
            pieces = []
            for kind, c, slot in middle[n]:
                if kind == "own":
                    pieces.append([((),) + local(c, f"send{slot}")])
                elif kind == "ride":
                    pieces.append([((), ride["across"], ("is", 0))])
                else:
                    m, i = where["in", kind, c, slot]
                    pieces.append([((), got_edge[m], ("is", i))])
            after = [got_middle[n - 2]] if n - 2 in got_middle else []
            got_middle[n] = lax.ppermute(packed(pieces, after), "roll", middle_pairs)
        if where["out", "ride", 0, 0][0] == n:
            ride_across()
        pieces = []
        for i in range(max(len(inwards[n]), len(outwards[n]))):
            choices = [((is_inner,),) + spare, ((is_outer,),) + spare]
            if i < len(outwards[n]):
                kind, c, core = outwards[n][i]
                if kind == "x":
                    choices[0] = ((is_inner,),) + local(c, f"out{core}")
                elif kind == "ride":
                    choices[0] = ((is_inner,), ride["out"], ("is", 0))
                else:
                    index = ("at", places[f"here_out{core}"])
                    choices[0] = ((is_inner,), across(kind, c), index)
            if i < len(inwards[n]):
                kind, c, slot = inwards[n][i]
                if kind == "ride":
                    choices[1] = ((is_outer,), ride["in"], ("is", slot))
                else:
                    choices[1] = ((is_outer,),) + local(c, f"send{slot}")
            pieces.append(choices)
        if pieces:
            after = [got_edge[n - 2]] if n - 2 in got_edge else []
            got_edge[n] = lax.ppermute(packed(pieces, after), "roll", edge_pairs)
        if n == 0:
            ride_first()
        if n == ride_from - 3:
            ride_mix()
        if n == ride_from - 1:
            ride_cores()
        if n == where["out", "ride", 0, 0][0] + 2:
            ride_out()
        while to_place and to_place[0][0] <= n - 2:
            place(*to_place.pop(0)[1:])
    while to_swap:
        early = list(to_place)
        del to_place[:]
        swap(rounds, to_swap[0][0])
        for _, got, taken in early:
            place(got, taken)
    if "mixed" not in ride:
        ride_out()
    for _, got, taken in to_place:
        place(got, taken)
    return tuple(outs) + (ride["mixed"],)


def direct_exchange(quants, placement, trains, owners):
    outs = []
    for quant in quants:
        _, experts, blocks, rows, features = quant.shape
        x = lax.all_to_all(quant, "train", split_axis=0, concat_axis=0, tiled=True)
        x = jnp.transpose(x, (1, 2, 3, 0, 4)).reshape(experts, blocks, rows, trains * features)
        picked = jnp.take(x, placement, axis=0)
        got = lax.all_to_all(picked, "roll", split_axis=0, concat_axis=0, tiled=True)
        outs.append(got.reshape(owners * blocks, rows, trains * features))
    return outs


def pre_activation_kernel(experts, top, tok_ref, ids_ref, w_ref, *refs):
    out_ref = refs[-1]
    features = tok_ref.shape[1]
    weights = w_ref[...].reshape(experts * BLOCK, features)
    pre = lax.dot_general(
        tok_ref[...], weights, (((1,), (1,)), ((), ())), preferred_element_type=jnp.float32
    )
    for k in range(top):
        total = jnp.zeros((pre.shape[0], BLOCK), jnp.float32)
        for expert in range(experts):
            part = pre[:, expert * BLOCK : (expert + 1) * BLOCK]
            total = total + jnp.where(ids_ref[:, k : k + 1] == expert, part, 0.0)
        out_ref[:, k * BLOCK : (k + 1) * BLOCK] = total


def pre_activations(tokens, ids, restored, block, out, column, columns, after=()):
    count, features = tokens.shape
    experts, top = restored.shape[0], ids.shape[1]
    tile = min(count, 2 * BLOCK)
    operands = [tokens, ids, restored] + list(after) + ([] if out is None else [out])
    return pl.pallas_call(
        functools.partial(pre_activation_kernel, experts, top),
        grid=(count // tile,),
        in_specs=[
            pl.BlockSpec((tile, features), lambda i: (i, 0)),
            pl.BlockSpec((tile, top), lambda i: (i, 0)),
            pl.BlockSpec((experts, 1, BLOCK, features), lambda i: (0, block, 0, 0)),
        ]
        + [any_spec()] * (len(operands) - 3),
        out_specs=pl.BlockSpec((tile, top * BLOCK), lambda i: (i, column)),
        out_shape=jax.ShapeDtypeStruct((count, columns * top * BLOCK), jnp.float32),
        input_output_aliases={} if out is None else {len(operands) - 1: 0},
        compiler_params=pltpu.CompilerParams(vmem_limit_bytes=VMEM_BYTES),
        cost_estimate=LIGHT,
        name="pre_activations",
    )(*operands)


def mix_rows(experts, top, blocks, pre_ref, ids_ref, weights_ref, down_ref):
    width = top * BLOCK
    count, features = ids_ref.shape[0], down_ref.shape[-1]
    hidden = {}
    for b in range(blocks):
        for k in range(top):
            start = b * width + k * BLOCK
            gate = pre_ref[:, start : start + BLOCK]
            up = pre_ref[:, blocks * width + start : blocks * width + start + BLOCK]
            value = gate / (1.0 + jnp.exp(-gate)) * up
            hidden[b, k] = value.astype(jnp.bfloat16).astype(jnp.float32)
    total = jnp.zeros((count, features), jnp.float32)
    for expert in range(experts):
        weight = jnp.zeros((count, 1), jnp.float32)
        for k in range(top):
            weight = weight + jnp.where(
                ids_ref[:, k : k + 1] == expert, weights_ref[:, k : k + 1], 0.0
            )
        value = jnp.zeros((count, features), jnp.float32)
        for b in range(blocks):
            routed = jnp.zeros((count, BLOCK), jnp.float32)
            for k in range(top):
                routed = routed + jnp.where(ids_ref[:, k : k + 1] == expert, hidden[b, k], 0.0)
            value = value + jnp.dot(
                routed.astype(jnp.bfloat16), down_ref[expert, b], preferred_element_type=jnp.float32
            )
        total = total + weight * value
    return total


def mix_kernel(sizes, pre_ref, ids_ref, weights_ref, down_ref, out_ref):
    out_ref[...] = mix_rows(*sizes, pre_ref, ids_ref, weights_ref, down_ref)


def mix_split_kernel(sizes, core, pre_ref, ids_ref, weights_ref, down_ref, plan_ref, *refs):
    keep_ref, send_ref = refs[-2:]
    total = mix_rows(*sizes, pre_ref, ids_ref, weights_ref, down_ref)
    half = total.shape[0] // CORES
    first = plan_ref[core] == 0
    keep_ref[0] = jnp.where(first, total[:half], total[half:])
    send_ref[...] = jnp.where(first, total[half:], total[:half]).astype(send_ref.dtype)


def mix_specs(pre, ids, down, tile):
    return [
        pl.BlockSpec((tile, pre.shape[1]), lambda i: (i, 0)),
        pl.BlockSpec((tile, ids.shape[1]), lambda i: (i, 0)),
        pl.BlockSpec((tile, ids.shape[1]), lambda i: (i, 0)),
        pl.BlockSpec(down.shape, lambda i: (0, 0, 0, 0)),
    ]


def mix_experts(pre, ids, weights, down, plan=None, places=None, after=()):
    count, top = ids.shape
    experts, blocks, _, features = down.shape
    sizes = (experts, top, blocks)
    tile = min(count, BLOCK)
    params = pltpu.CompilerParams(vmem_limit_bytes=VMEM_BYTES)
    if plan is None:
        return pl.pallas_call(
            functools.partial(mix_kernel, sizes),
            grid=(count // tile,),
            in_specs=mix_specs(pre, ids, down, tile),
            out_specs=pl.BlockSpec((tile, features), lambda i: (i, 0)),
            out_shape=jax.ShapeDtypeStruct((count, features), jnp.float32),
            compiler_params=params,
            cost_estimate=LIGHT,
            name="mix_experts",
        )(pre, ids, weights, down)
    half = tile // CORES
    return pl.pallas_call(
        functools.partial(mix_split_kernel, sizes, places["core"]),
        grid=(count // tile,),
        in_specs=mix_specs(pre, ids, down, tile) + [smem_spec()] + [any_spec()] * len(after),
        out_specs=[
            pl.BlockSpec((1, half, features), lambda i: (i, 0, 0)),
            pl.BlockSpec((half, features), lambda i: (i, 0)),
        ],
        out_shape=[
            jax.ShapeDtypeStruct((count // tile, half, features), jnp.float32),
            jax.ShapeDtypeStruct((count // CORES, features), jnp.bfloat16),
        ],
        compiler_params=params,
        cost_estimate=LIGHT,
        name="mix_experts",
    )(pre, ids, weights, down, plan, *after)


def sum_call(kernel, name, out_shape, plan, arrays, piece, after):
    vmem = pl.BlockSpec(memory_space=pltpu.VMEM)
    operands = [plan] + list(arrays)
    specs = [smem_spec()] + [vmem] * len(arrays)
    if piece is not None:
        array, first, number = piece
        operands += [array] * number
        for n in range(number):
            specs.append(
                pl.BlockSpec((1,) + array.shape[1:], lambda i, n=n: (first + n, 0, 0))
            )
    return pl.pallas_call(
        kernel,
        grid=(1,),
        in_specs=specs + [any_spec()] * len(after),
        out_specs=[vmem] * len(out_shape) if isinstance(out_shape, list) else vmem,
        out_shape=out_shape,
        compiler_params=pltpu.CompilerParams(vmem_limit_bytes=VMEM_BYTES),
        cost_estimate=LIGHT,
        name=name,
    )(*operands, *after)


def sum_cores_kernel(places, plan_ref, keep_ref, got_ref, *refs):
    sums_ref, send_ref = refs[-2:]
    chips, tokens, features = keep_ref.shape
    for chip in range(chips):
        rows = slice(chip * tokens, (chip + 1) * tokens)
        sums_ref[chip] = keep_ref[chip] + got_ref[rows, :].astype(jnp.float32)
    side, chip = plan_ref[places["side"]], plan_ref[places["chip"]]
    for n in range(2):
        send_ref[n * tokens : (n + 1) * tokens, :] = sums_ref[2 * (1 - side) + n].astype(
            send_ref.dtype
        )
    partner = sums_ref[1 + 4 * side - chip].astype(send_ref.dtype)
    for n in range(2, 4):
        send_ref[n * tokens : (n + 1) * tokens, :] = partner


def sum_cores(plan, places, keep, got, after=()):
    _, tokens, features = keep.shape
    out_shape = [
        jax.ShapeDtypeStruct(keep.shape, jnp.float32),
        jax.ShapeDtypeStruct((4 * tokens, features), jnp.bfloat16),
    ]
    kernel = functools.partial(sum_cores_kernel, places)
    return sum_call(kernel, "sum_cores", out_shape, plan, [keep, got], None, after)


def sum_inwards_kernel(places, plan_ref, sums_ref, over_ref, here_ref, *refs):
    inner_ref, send_ref = refs[-2:]
    tokens = inner_ref.shape[0]
    side, chip = plan_ref[places["side"]], plan_ref[places["chip"]]
    for n in range(2):
        rows = slice(n * tokens, (n + 1) * tokens)
        total = sums_ref[2 * (1 - side) + n] + over_ref[0, rows, :].astype(jnp.float32)
        send_ref[rows, :] = total.astype(send_ref.dtype)
    inner_ref[...] = sums_ref[chip] + here_ref[0, :tokens, :].astype(jnp.float32)


def sum_inwards(plan, places, sums, got, first, after=()):
    _, tokens, features = sums.shape
    out_shape = [
        jax.ShapeDtypeStruct((tokens, features), jnp.float32),
        jax.ShapeDtypeStruct((2 * tokens, features), jnp.bfloat16),
    ]
    kernel = functools.partial(sum_inwards_kernel, places)
    return sum_call(kernel, "sum_inwards", out_shape, plan, [sums], (got, first, 2), after)


def sum_across_kernel(places, plan_ref, sums_ref, inner_ref, got_ref, *refs):
    final_ref, send_ref = refs[-2:]
    tokens = inner_ref.shape[0]
    side, chip = plan_ref[places["side"]], plan_ref[places["chip"]]
    place = chip - 2 * side
    low = got_ref[0, :tokens, :].astype(jnp.float32)
    high = got_ref[0, tokens:, :].astype(jnp.float32)
    final_ref[...] = inner_ref[...] + jnp.where(place == 0, low, high)
    total = sums_ref[1 + 4 * side - chip] + jnp.where(place == 0, high, low)
    for n in range(2):
        send_ref[n * tokens : (n + 1) * tokens, :] = total.astype(send_ref.dtype)


def sum_across(plan, places, sums, inner, got, first, after=()):
    _, tokens, features = sums.shape
    out_shape = [
        jax.ShapeDtypeStruct((tokens, features), jnp.float32),
        jax.ShapeDtypeStruct((2 * tokens, features), jnp.bfloat16),
    ]
    kernel = functools.partial(sum_across_kernel, places)
    return sum_call(kernel, "sum_across", out_shape, plan, [sums, inner], (got, first, 1), after)


def sum_outwards_kernel(places, plan_ref, sums_ref, final_ref, got_ref, *refs):
    out_ref = refs[-1]
    tokens = final_ref.shape[0]
    outer = sums_ref[plan_ref[places["chip"]]] + got_ref[0, :tokens, :].astype(jnp.float32)
    out_ref[...] = jnp.where(plan_ref[places["inner"]] == 1, final_ref[...], outer).astype(
        out_ref.dtype
    )


def sum_outwards(plan, places, sums, final, got, first, after=()):
    out_shape = jax.ShapeDtypeStruct(final.shape, jnp.bfloat16)
    kernel = functools.partial(sum_outwards_kernel, places)
    return sum_call(kernel, "sum_outwards", out_shape, plan, [sums, final], (got, first, 1), after)


def gather_tokens(tokens, expert_ids, gate_weights, features):
    mine = lax.dynamic_slice_in_dim(tokens, lax.axis_index("train") * features, features, axis=1)
    top = expert_ids.shape[1]
    high = lax.reduce_precision(gate_weights, 8, 7)
    middle = lax.reduce_precision(gate_weights - high, 8, 7)
    low = gate_weights - high - middle
    beside = jnp.concatenate((expert_ids.astype(jnp.float32), high, middle, low), axis=1)
    beside = jnp.pad(beside, ((0, 0), (0, BLOCK - 4 * top))).astype(jnp.bfloat16)
    every = lax.all_gather(jnp.concatenate((mine, beside), axis=1), "roll", axis=0, tiled=True)
    side = every[:, features : features + 4 * top].astype(jnp.float32)
    ids = side[:, :top].astype(jnp.int32)
    weights = side[:, top : 2 * top] + side[:, 2 * top : 3 * top] + side[:, 3 * top :]
    return every[:, :features], ids, weights


def per_device(master_gate, master_up, master_down, tokens, expert_ids, gate_weights, placement):
    trains = lax.axis_size("train")
    owners = lax.axis_size("roll")
    experts, hidden_rows, features = master_gate.shape
    blocks = hidden_rows // BLOCK
    if owners // CORES == 4 and CORES * tokens.shape[0] == BLOCK:
        quant, gate = quantize(master_gate, 0, blocks, trains, experts)
        x_first = lax.all_to_all(quant, "train", split_axis=0, concat_axis=0, tiled=True)
        plan, places = make_plan(placement, experts, owners, (quant,))
        rest_up, up = quantize(master_up, 0, blocks, trains, experts, 0, None, (plan,))
        rest_down, down = quantize(master_down, 0, blocks, trains, experts, 0, None, (rest_up,))
        rest = (rest_up, rest_down)
        dequant = (gate, up, down)
        routed = gather_tokens(tokens, expert_ids, gate_weights, features)
        most = min(experts, owners // 2)
        shapes = (experts, blocks, trains, owners)

        def branch(cap, x_first, rest, dequant, plan, routed):
            return line_exchange(x_first, rest, dequant, plan, places, routed, shapes, cap)

        outs = lax.cond(
            plan[places["most"]] <= most - 1,
            functools.partial(branch, most - 1),
            functools.partial(branch, most),
            x_first,
            rest,
            dequant,
            plan,
            routed,
        )
    else:
        masters = (master_gate, master_up, master_down)
        quants, dequant = zip(*[quantize(w, 0, blocks, trains, experts) for w in masters])
        every, ids, weights = gather_tokens(tokens, expert_ids, gate_weights, features)
        outs = direct_exchange(quants, placement, trains, owners)
        pre = None
        for n in range(2 * blocks):
            restored = dequant[n // blocks]
            pre = pre_activations(every, ids, restored, n % blocks, pre, n, 2 * blocks)
        mixed = mix_experts(lax.psum(pre, "train"), ids, weights, dequant[2])
        mixed = lax.psum_scatter(mixed, "roll", scatter_dimension=0, tiled=True)
        outs = tuple(outs) + (mixed.astype(jnp.bfloat16),)
    return tuple(out[None] for out in outs[:3]) + (outs[3],)


def solution(mesh):
    in_specs = (
        P(None, "roll", "train"),
        P(None, "roll", "train"),
        P(None, "roll", "train"),
        P("roll", None),
        P("roll", None),
        P("roll", None),
        P(),
    )
    out_specs = (
        P("roll", None, "train", None),
        P("roll", None, "train", None),
        P("roll", None, "train", None),
        P("roll", "train"),
    )
    return jax.shard_map(
        per_device, mesh=mesh, in_specs=in_specs, out_specs=out_specs, check_vma=False
    )
```

```python
import functools

import jax
import jax.numpy as jnp
from jax import lax
from jax.experimental import pallas as pl
from jax.experimental.pallas import tpu as pltpu
from jax.sharding import PartitionSpec as P

BLOCK = 128
CORES = 2
VMEM_BYTES = 48 * 1024 * 1024
LIGHT = pl.CostEstimate(flops=1, bytes_accessed=1, transcendentals=0)


def any_spec():
    return pl.BlockSpec(memory_space=pl.ANY)


def smem_spec():
    return pl.BlockSpec(memory_space=pltpu.SMEM)


def quantize_kernel(trains, x_ref, *refs):
    q_ref, d_ref = refs[-2:]
    rows = BLOCK // trains
    features = x_ref.shape[-1]
    for col in range(features // BLOCK):
        cols = slice(col * BLOCK, (col + 1) * BLOCK)
        block = x_ref[0, :, cols]
        peak = jnp.max(jnp.max(jnp.abs(block), axis=0, keepdims=True), axis=1, keepdims=True)
        scale = peak.astype(jnp.bfloat16).astype(jnp.float32)
        quant = (block * (1.0 / scale)).astype(jnp.bfloat16)
        q_ref[:, 0, 0, :, cols] = quant.reshape(trains, rows, BLOCK)
        d_ref[0, 0, :, cols] = (quant.astype(jnp.float32) * scale).astype(jnp.bfloat16)


def quantize(master, first, blocks, trains, slots, base=0, into=None, after=()):
    experts, _, features = master.shape
    rows = BLOCK // trains
    operands = [master] + list(after) + ([] if into is None else [into])
    return pl.pallas_call(
        functools.partial(quantize_kernel, trains),
        grid=(experts, blocks),
        in_specs=[pl.BlockSpec((1, BLOCK, features), lambda e, b: (e, first + b, 0))]
        + [any_spec()] * (len(operands) - 1),
        out_specs=[
            pl.BlockSpec((trains, 1, 1, rows, features), lambda e, b: (0, base + e, b, 0, 0)),
            pl.BlockSpec((1, 1, BLOCK, features), lambda e, b: (e, b, 0, 0)),
        ],
        out_shape=[
            jax.ShapeDtypeStruct((trains, slots, blocks, rows, features), jnp.bfloat16),
            jax.ShapeDtypeStruct((experts, blocks, BLOCK, features), jnp.bfloat16),
        ],
        input_output_aliases={} if into is None else {len(operands) - 1: 0},
        compiler_params=pltpu.CompilerParams(vmem_limit_bytes=VMEM_BYTES),
        cost_estimate=LIGHT,
        name="quantize",
    )(*operands)


def start_choice(plan_ref, arrays, choice, target, sem):
    tests, array, (kind, n, *more) = choice
    ref = arrays[array]
    if kind == "is":
        view = ref.at[n]
    elif kind == "at":
        view = ref.at[plan_ref[n]]
    else:
        view = ref.at[:, plan_ref[n] + more[0], pl.ds(more[1], 1)]
    hit = None
    for place, value in tests:
        test = plan_ref[place] == value
        hit = test if hit is None else hit & test

    def go():
        pltpu.make_async_copy(view, target, sem).start()

    if hit is None:
        go()
    else:
        pl.when(hit)(go)


def pack_kernel(pieces, n_in, plan_ref, *refs):
    arrays = refs[:n_in]
    out, held, sem_in, sem_out = refs[-4:]
    for n, choices in enumerate(pieces):
        for choice in choices:
            start_choice(plan_ref, arrays, choice, held.at[n], sem_in.at[n])
    for n in range(len(pieces)):
        pltpu.make_async_copy(held.at[n], held.at[n], sem_in.at[n]).wait()
        pltpu.make_async_copy(held.at[n], out.at[n], sem_out.at[n]).start()
    for n in range(len(pieces)):
        pltpu.make_async_copy(held.at[n], out.at[n], sem_out.at[n]).wait()


class Arrays:
    def __init__(self):
        self.items = []

    def add(self, array):
        for n, item in enumerate(self.items):
            if item is array:
                return n
        self.items.append(array)
        return len(self.items) - 1


def number_choices(pieces, arrays):
    return [[(tests, arrays.add(a), index) for tests, a, index in choices] for choices in pieces]


def pack(plan, shape, pieces, after=()):
    arrays = Arrays()
    pieces = number_choices(pieces, arrays)
    n_in = len(arrays.items)
    size = len(pieces)
    for dim in shape:
        size *= dim
    operands = arrays.items + list(after)
    return pl.pallas_call(
        functools.partial(pack_kernel, pieces, n_in),
        in_specs=[smem_spec()] + [any_spec()] * len(operands),
        out_specs=any_spec(),
        out_shape=jax.ShapeDtypeStruct((len(pieces),) + shape, jnp.bfloat16),
        scratch_shapes=[
            pltpu.VMEM((len(pieces),) + shape, jnp.bfloat16),
            pltpu.SemaphoreType.DMA((len(pieces),)),
            pltpu.SemaphoreType.DMA((len(pieces),)),
        ],
        compiler_params=pltpu.CompilerParams(vmem_limit_bytes=VMEM_BYTES),
        cost_estimate=LIGHT,
        name="pack",
    )(plan, *operands)


def place_kernel(pieces, sources, first, blocks, n_in, plan_ref, *refs):
    arrays = refs[:n_in]
    out, mark, held, sem_in, sem_out = refs[-5:]
    trains, count, _, features = held.shape[1:]
    for n, choices in enumerate(pieces):
        for choice in choices:
            start_choice(plan_ref, arrays, choice, held.at[n], sem_in.at[n])
    mark[...] = jnp.zeros_like(mark)
    stores = []
    for n in range(len(pieces)):
        pltpu.make_async_copy(held.at[n], held.at[n], sem_in.at[n]).wait()
        start = plan_ref[sources[n]] * blocks + first
        for part in range(trains):
            store = pltpu.make_async_copy(
                held.at[n, part],
                out.at[pl.ds(start, count), :, pl.ds(part * features, features)],
                sem_out.at[n, part],
            )
            store.start()
            stores.append(store)
    for store in stores:
        store.wait()


def place_pieces(plan, shape, owners, pieces, sources, first, blocks, out, after=()):
    trains, count, rows, features = shape
    arrays = Arrays()
    pieces = number_choices(pieces, arrays)
    n_in = len(arrays.items)
    operands = arrays.items + list(after) + ([] if out is None else [out])
    return pl.pallas_call(
        functools.partial(place_kernel, pieces, sources, first, blocks, n_in),
        in_specs=[smem_spec()] + [any_spec()] * len(operands),
        out_specs=[any_spec(), pl.BlockSpec(memory_space=pltpu.VMEM)],
        out_shape=[
            jax.ShapeDtypeStruct((owners * blocks, rows, trains * features), jnp.bfloat16),
            jax.ShapeDtypeStruct((8, BLOCK), jnp.float32),
        ],
        scratch_shapes=[
            pltpu.VMEM((len(pieces),) + shape, jnp.bfloat16),
            pltpu.SemaphoreType.DMA((len(pieces),)),
            pltpu.SemaphoreType.DMA((len(pieces), trains)),
        ],
        input_output_aliases={} if out is None else {len(operands): 0},
        compiler_params=pltpu.CompilerParams(vmem_limit_bytes=VMEM_BYTES),
        cost_estimate=LIGHT,
        name="place_pieces",
    )(plan, *operands)


def plan_places(experts):
    names = [f"send{slot}" for slot in range(experts)]
    names += ["inner", "core", "chip", "side", "own", "mate", "out0", "out1", "most"]
    names += [f"{list_}_{who}" for list_ in ("here", "there") for who in ("own", "mate", "out0", "out1")]
    names += [f"from_{who}{n}" for who in ("own", "mate") for n in range(4)]
    return {name: n for n, name in enumerate(names)}


def plan_kernel(experts, owners, places, me_ref, placement_ref, out_ref):
    me = me_ref[0]
    chip, core = lax.div(me, CORES), lax.rem(me, CORES)
    side = lax.div(chip, 2)
    half = owners // 2
    needs, ranks = [], []
    for s in range(2):
        need = []
        for e in range(experts):
            found = jnp.int32(0)
            for o in range(s * half, (s + 1) * half):
                found = jnp.where(placement_ref[o] == e, 1, found)
            need.append(found)
        rank = []
        for e in range(experts):
            total = jnp.int32(0)
            for other in range(experts):
                if other != e:
                    ahead = need[other] >= need[e] if other < e else need[other] > need[e]
                    total = total + jnp.where(ahead, 1, 0)
            rank.append(total)
        needs.append(sum(need))
        ranks.append(rank)
    here = [jnp.where(side == 0, a, b) for a, b in zip(*ranks)]
    there = [jnp.where(side == 0, b, a) for a, b in zip(*ranks)]
    outer = 3 * side
    values = {
        "inner": jnp.where((chip == 1) | (chip == 2), 1, 0),
        "core": core,
        "chip": chip,
        "side": side,
        "own": placement_ref[me],
        "mate": placement_ref[chip * CORES + 1 - core],
        "out0": placement_ref[outer * CORES],
        "out1": placement_ref[outer * CORES + 1],
        "most": jnp.maximum(*needs),
    }
    for slot in range(experts):
        values[f"send{slot}"] = sum(jnp.where(there[e] == slot, e, 0) for e in range(experts))
    for who in ("own", "mate", "out0", "out1"):
        for list_, rank in (("here", here), ("there", there)):
            values[f"{list_}_{who}"] = sum(
                jnp.where(values[who] == e, rank[e], 0) for e in range(experts)
            )
    for n, source in enumerate((chip, 1 + 4 * side - chip, 2 - side, 3 - 3 * side)):
        values[f"from_own{n}"] = source * CORES + core
        values[f"from_mate{n}"] = source * CORES + 1 - core
    for name, n in places.items():
        out_ref[n] = values[name]


def make_plan(placement, experts, owners, after=()):
    places = plan_places(experts)
    me = jnp.reshape(lax.axis_index("roll"), (1,)).astype(jnp.int32)
    plan = pl.pallas_call(
        lambda *refs: plan_kernel(experts, owners, places, refs[0], refs[1], refs[-1]),
        in_specs=[smem_spec(), smem_spec()] + [any_spec()] * len(after),
        out_specs=smem_spec(),
        out_shape=jax.ShapeDtypeStruct((len(places),), jnp.int32),
        cost_estimate=LIGHT,
        name="plan",
    )(me, placement, *after)
    return plan, places


def line_schedule(opens, experts, cap, ride_from):
    chunks = range(len(opens))
    own, far = list(chunks), list(chunks)
    fresh = [("x", c, i) for c in chunks for i in range(CORES)]
    near = [("near", c, s) for c in chunks for s in range(cap, experts)]
    middle, inwards, outwards = [], [], []
    arrived, relayed, ride_due = [], [], {"in": ride_from}
    n = 0
    while own or arrived or far or near or fresh or relayed or ride_due:
        across, ins, outs = [], [], []
        if arrived and arrived[0][0] <= n:
            c = arrived.pop(0)[1]
            across = [("far", c, s) for s in range(cap)]
        elif own and opens[own[0]] <= n:
            c = own.pop(0)
            across = [("own", c, s) for s in range(cap)]
        if across:
            relayed += [(n + 2, (across[0][0], c, i)) for i in range(CORES)]
        if ride_due.get("across", n + 1) <= n and (not across or across[0][0] == "own"):
            across.append(("ride", 0, 0))
            del ride_due["across"]
            ride_due["out"] = n + 2
        if far and opens[far[0]] <= n:
            c = far.pop(0)
            ins = [("far", c, s) for s in range(cap)]
            arrived.append((n + 2, c))
        else:
            if ride_due.get("in", n + 1) <= n:
                ins = [("ride", 0, 0), ("ride", 0, 1)]
                del ride_due["in"]
                ride_due["across"] = n + 2
            while near and opens[near[0][1]] <= n and len(ins) < cap:
                ins.append(near.pop(0))
        while relayed and relayed[0][0] <= n and len(outs) < cap:
            outs.append(relayed.pop(0)[1])
        if ride_due.get("out", n + 1) <= n and len(outs) < cap:
            outs.append(("ride", 0, 0))
            del ride_due["out"]
        while fresh and opens[fresh[0][1]] <= n and len(outs) < cap:
            outs.append(fresh.pop(0))
        middle.append(across)
        inwards.append(ins)
        outwards.append(outs)
        n += 1
    return middle, inwards, outwards


def link_pairs(chip_pairs, swap_chips=()):
    pairs = []
    for core in range(CORES):
        for a, b in chip_pairs:
            pairs.append((a * CORES + core, b * CORES + core))
        for chip in swap_chips:
            pairs.append((chip * CORES + core, chip * CORES + 1 - core))
    return pairs


EDGES = ((0, 1), (1, 0), (2, 3), (3, 2))


def line_exchange(x_first, quant_rest, dequant, plan, places, routed, shapes, cap):
    experts, blocks, trains, owners = shapes
    features = x_first.shape[-1]
    rows = BLOCK // trains
    shape = (trains, 1, rows, features)
    chunks = [(m, b) for m in range(3) for b in range(blocks)]
    count = len(chunks)
    opens = [(0, 2, 5)[m] for m, _ in chunks]
    ride_from = 8
    middle, inwards, outwards = line_schedule(opens, experts, cap, ride_from)
    rounds = len(outwards)
    last_far = max(n for n in range(rounds) if inwards[n] and inwards[n][0][0] == "far")
    edge_pairs = link_pairs(EDGES)
    middle_pairs = link_pairs([(1, 2), (2, 1)], swap_chips=(0, 3))
    swap_pairs = link_pairs([], swap_chips=range(4))
    is_inner, is_outer = (places["inner"], 1), (places["inner"], 0)
    on_core = [(places["core"], core) for core in range(CORES)]
    got_edge, got_middle, where = {}, {}, {}
    last = [x_first]

    xs = [x_first] + [
        lax.all_to_all(quant, "train", split_axis=0, concat_axis=0, tiled=True)
        for quant in quant_rest
    ]

    def local(c, name):
        m, b = chunks[c]
        return xs[m], ("expert", places[name], 0, b)

    def packed(pieces, after=()):
        last[0] = pack(plan, shape, pieces, [last[0]] + list(after))
        return last[0]

    ready = {(c, 0): opens[c] for c in range(count)}

    def note(c, position, n):
        ready[c, position] = max(ready.get((c, position), 0), n)

    from_kind = {"x": 1, "own": 2, "far": 3}
    kind_of = {position: kind for kind, position in from_kind.items()}
    for n in range(rounds):
        for i, piece in enumerate(middle[n]):
            where[("across",) + piece] = (n, i)
            if piece[0] != "ride":
                note(piece[1], 2 if piece[0] == "own" else 3, n)
        for i, piece in enumerate(inwards[n]):
            where[("in",) + piece] = (n, i)
            if piece[0] != "ride":
                note(piece[1], 1, n)
        for i, piece in enumerate(outwards[n]):
            where[("out",) + piece] = (n, i)
            if piece[0] != "ride":
                note(piece[1], from_kind[piece[0]], n)

    def across(kind, c):
        return got_middle[where["across", kind, c, 0][0]]

    def find(c, position, who):
        if position == 0:
            return [((),) + local(c, who)]
        choices = []
        if position == 1:
            for slot in range(experts):
                n, i = where["in", "far" if slot < cap else "near", c, slot]
                test = (places[f"there_{who}"], slot)
                choices.append(((is_inner, test), got_edge[n], ("is", i)))
        else:
            got = across(kind_of[position], c)
            choices.append(((is_inner,), got, ("at", places[f"here_{who}"])))
        for core in range(CORES):
            n, i = where["out", kind_of[position], c, core if who == "own" else 1 - core]
            choices.append(((is_outer, on_core[core]), got_edge[n], ("is", i)))
        return choices

    to_swap = sorted((ready[c, p], c, p) for c in range(count) for p in range(4))
    to_place = []
    outs = [None, None, None]

    def swap(n, by):
        taken = []
        while to_swap and to_swap[0][0] <= by and len(taken) < 3:
            taken.append(to_swap.pop(0))
        if taken:
            got = lax.ppermute(
                packed([find(c, p, "mate") for _, c, p in taken]), "roll", swap_pairs
            )
            to_place.append((n, got, [(c, p) for _, c, p in taken]))
        return bool(taken)

    def place(got, taken):
        for c in sorted({c for c, _ in taken}):
            m, b = chunks[c]
            here = [(i, p) for i, (other, p) in enumerate(taken) if other == c]
            pieces = [find(c, p, "own") for _, p in here]
            pieces += [[((), got, ("is", i))] for i, _ in here]
            sources = [places[f"from_own{p}"] for _, p in here]
            sources += [places[f"from_mate{p}"] for _, p in here]
            outs[m], last[0] = place_pieces(
                plan, shape, owners, pieces, sources, b, blocks, outs[m], (last[0],)
            )

    ride = {}
    tokens, ids, weights = routed
    ups, down = dequant[:-1], dequant[-1]

    def ride_first():
        pre, columns = None, 2 * blocks
        for restored in ups:
            for b in range(restored.shape[1]):
                column = 0 if pre is None else column + 1
                pre = pre_activations(tokens, ids, restored, b, pre, column, columns, (last[0],))
                last[0] = pre
        ride["pre"] = lax.psum(pre, "train")
    def ride_mix():
        ride["keep"], going = mix_experts(
            ride["pre"], ids, weights, down, plan, places, (last[0],)
        )
        last[0] = ride["keep"]
        going = going.reshape((-1,) + shape)
        ride["swapped"] = lax.ppermute(going, "roll", swap_pairs)

    def ride_cores():
        got = ride["swapped"].reshape(-1, features)
        ride["sums"], going = sum_cores(plan, places, ride["keep"], got, (last[0],))
        last[0] = ride["sums"]
        ride["in"] = going.reshape((-1,) + shape)

    def ride_in():
        n, i = where["in", "ride", 0, 0]
        got = got_edge[n].reshape(-1, BLOCK, features)
        ride["inner"], going = sum_inwards(plan, places, ride["sums"], got, i, (last[0],))
        last[0] = ride["inner"]
        ride["across"] = going.reshape((-1,) + shape)

    def ride_across():
        n, i = where["across", "ride", 0, 0]
        got = got_middle[n].reshape(-1, BLOCK, features)
        ride["final"], going = sum_across(
            plan, places, ride["sums"], ride["inner"], got, i, (last[0],)
        )
        last[0] = ride["final"]
        ride["out"] = going.reshape((-1,) + shape)

    def ride_out():
        n, i = where["out", "ride", 0, 0]
        got = got_edge[n].reshape(-1, BLOCK, features)
        ride["mixed"] = sum_outwards(
            plan, places, ride["sums"], ride["final"], got, i, (last[0],)
        )
        last[0] = ride["mixed"]

    spare = local(0, "own")
    for n in range(rounds):
        swap(n, n - 2)
        if middle[n]:
            if where.get(("across", "ride", 0, 0), (-1,))[0] == n:
                ride_in()
            pieces = []
            for kind, c, slot in middle[n]:
                if kind == "own":
                    pieces.append([((),) + local(c, f"send{slot}")])
                elif kind == "ride":
                    pieces.append([((), ride["across"], ("is", 0))])
                else:
                    m, i = where["in", kind, c, slot]
                    pieces.append([((), got_edge[m], ("is", i))])
            after = [got_middle[n - 2]] if n - 2 in got_middle else []
            got_middle[n] = lax.ppermute(packed(pieces, after), "roll", middle_pairs)
        if where["out", "ride", 0, 0][0] == n:
            ride_across()
        pieces = []
        for i in range(max(len(inwards[n]), len(outwards[n]))):
            choices = [((is_inner,),) + spare, ((is_outer,),) + spare]
            if i < len(outwards[n]):
                kind, c, core = outwards[n][i]
                if kind == "x":
                    choices[0] = ((is_inner,),) + local(c, f"out{core}")
                elif kind == "ride":
                    choices[0] = ((is_inner,), ride["out"], ("is", 0))
                else:
                    index = ("at", places[f"here_out{core}"])
                    choices[0] = ((is_inner,), across(kind, c), index)
            if i < len(inwards[n]):
                kind, c, slot = inwards[n][i]
                if kind == "ride":
                    choices[1] = ((is_outer,), ride["in"], ("is", slot))
                else:
                    choices[1] = ((is_outer,),) + local(c, f"send{slot}")
            pieces.append(choices)
        while n < last_far and len(pieces) < cap:
            pieces.append([((),) + spare])
        if pieces:
            after = [got_edge[n - 2]] if n - 2 in got_edge else []
            got_edge[n] = lax.ppermute(packed(pieces, after), "roll", edge_pairs)
        if n == 0:
            ride_first()
        if n == ride_from - 3:
            ride_mix()
        if n == ride_from - 1:
            ride_cores()
        if n == where["out", "ride", 0, 0][0] + 2:
            ride_out()
        while to_place and to_place[0][0] <= n - 2:
            place(*to_place.pop(0)[1:])
    while to_swap:
        early = list(to_place)
        del to_place[:]
        swap(rounds, to_swap[0][0])
        for _, got, taken in early:
            place(got, taken)
    if "mixed" not in ride:
        ride_out()
    for _, got, taken in to_place:
        place(got, taken)
    return tuple(outs) + (ride["mixed"],)


def direct_exchange(quants, placement, trains, owners):
    outs = []
    for quant in quants:
        _, experts, blocks, rows, features = quant.shape
        x = lax.all_to_all(quant, "train", split_axis=0, concat_axis=0, tiled=True)
        x = jnp.transpose(x, (1, 2, 3, 0, 4)).reshape(experts, blocks, rows, trains * features)
        picked = jnp.take(x, placement, axis=0)
        got = lax.all_to_all(picked, "roll", split_axis=0, concat_axis=0, tiled=True)
        outs.append(got.reshape(owners * blocks, rows, trains * features))
    return outs


def pre_activation_kernel(experts, top, tok_ref, ids_ref, w_ref, *refs):
    out_ref = refs[-1]
    features = tok_ref.shape[1]
    weights = w_ref[...].reshape(experts * BLOCK, features)
    pre = lax.dot_general(
        tok_ref[...], weights, (((1,), (1,)), ((), ())), preferred_element_type=jnp.float32
    )
    for k in range(top):
        total = jnp.zeros((pre.shape[0], BLOCK), jnp.float32)
        for expert in range(experts):
            part = pre[:, expert * BLOCK : (expert + 1) * BLOCK]
            total = total + jnp.where(ids_ref[:, k : k + 1] == expert, part, 0.0)
        out_ref[:, k * BLOCK : (k + 1) * BLOCK] = total


def pre_activations(tokens, ids, restored, block, out, column, columns, after=()):
    count, features = tokens.shape
    experts, top = restored.shape[0], ids.shape[1]
    tile = min(count, 2 * BLOCK)
    operands = [tokens, ids, restored] + list(after) + ([] if out is None else [out])
    return pl.pallas_call(
        functools.partial(pre_activation_kernel, experts, top),
        grid=(count // tile,),
        in_specs=[
            pl.BlockSpec((tile, features), lambda i: (i, 0)),
            pl.BlockSpec((tile, top), lambda i: (i, 0)),
            pl.BlockSpec((experts, 1, BLOCK, features), lambda i: (0, block, 0, 0)),
        ]
        + [any_spec()] * (len(operands) - 3),
        out_specs=pl.BlockSpec((tile, top * BLOCK), lambda i: (i, column)),
        out_shape=jax.ShapeDtypeStruct((count, columns * top * BLOCK), jnp.float32),
        input_output_aliases={} if out is None else {len(operands) - 1: 0},
        compiler_params=pltpu.CompilerParams(vmem_limit_bytes=VMEM_BYTES),
        cost_estimate=LIGHT,
        name="pre_activations",
    )(*operands)


def mix_rows(experts, top, blocks, pre_ref, ids_ref, weights_ref, down_ref):
    width = top * BLOCK
    count, features = ids_ref.shape[0], down_ref.shape[-1]
    hidden = {}
    for b in range(blocks):
        for k in range(top):
            start = b * width + k * BLOCK
            gate = pre_ref[:, start : start + BLOCK]
            up = pre_ref[:, blocks * width + start : blocks * width + start + BLOCK]
            value = gate / (1.0 + jnp.exp(-gate)) * up
            hidden[b, k] = value.astype(jnp.bfloat16).astype(jnp.float32)
    total = jnp.zeros((count, features), jnp.float32)
    for expert in range(experts):
        weight = jnp.zeros((count, 1), jnp.float32)
        for k in range(top):
            weight = weight + jnp.where(
                ids_ref[:, k : k + 1] == expert, weights_ref[:, k : k + 1], 0.0
            )
        value = jnp.zeros((count, features), jnp.float32)
        for b in range(blocks):
            routed = jnp.zeros((count, BLOCK), jnp.float32)
            for k in range(top):
                routed = routed + jnp.where(ids_ref[:, k : k + 1] == expert, hidden[b, k], 0.0)
            value = value + jnp.dot(
                routed.astype(jnp.bfloat16), down_ref[expert, b], preferred_element_type=jnp.float32
            )
        total = total + weight * value
    return total


def mix_kernel(sizes, pre_ref, ids_ref, weights_ref, down_ref, out_ref):
    out_ref[...] = mix_rows(*sizes, pre_ref, ids_ref, weights_ref, down_ref)


def mix_split_kernel(sizes, core, pre_ref, ids_ref, weights_ref, down_ref, plan_ref, *refs):
    keep_ref, send_ref = refs[-2:]
    total = mix_rows(*sizes, pre_ref, ids_ref, weights_ref, down_ref)
    half = total.shape[0] // CORES
    first = plan_ref[core] == 0
    keep_ref[0] = jnp.where(first, total[:half], total[half:])
    send_ref[...] = jnp.where(first, total[half:], total[:half]).astype(send_ref.dtype)


def mix_specs(pre, ids, down, tile):
    return [
        pl.BlockSpec((tile, pre.shape[1]), lambda i: (i, 0)),
        pl.BlockSpec((tile, ids.shape[1]), lambda i: (i, 0)),
        pl.BlockSpec((tile, ids.shape[1]), lambda i: (i, 0)),
        pl.BlockSpec(down.shape, lambda i: (0, 0, 0, 0)),
    ]


def mix_experts(pre, ids, weights, down, plan=None, places=None, after=()):
    count, top = ids.shape
    experts, blocks, _, features = down.shape
    sizes = (experts, top, blocks)
    tile = min(count, BLOCK)
    params = pltpu.CompilerParams(vmem_limit_bytes=VMEM_BYTES)
    if plan is None:
        return pl.pallas_call(
            functools.partial(mix_kernel, sizes),
            grid=(count // tile,),
            in_specs=mix_specs(pre, ids, down, tile),
            out_specs=pl.BlockSpec((tile, features), lambda i: (i, 0)),
            out_shape=jax.ShapeDtypeStruct((count, features), jnp.float32),
            compiler_params=params,
            cost_estimate=LIGHT,
            name="mix_experts",
        )(pre, ids, weights, down)
    half = tile // CORES
    return pl.pallas_call(
        functools.partial(mix_split_kernel, sizes, places["core"]),
        grid=(count // tile,),
        in_specs=mix_specs(pre, ids, down, tile) + [smem_spec()] + [any_spec()] * len(after),
        out_specs=[
            pl.BlockSpec((1, half, features), lambda i: (i, 0, 0)),
            pl.BlockSpec((half, features), lambda i: (i, 0)),
        ],
        out_shape=[
            jax.ShapeDtypeStruct((count // tile, half, features), jnp.float32),
            jax.ShapeDtypeStruct((count // CORES, features), jnp.bfloat16),
        ],
        compiler_params=params,
        cost_estimate=LIGHT,
        name="mix_experts",
    )(pre, ids, weights, down, plan, *after)


def sum_call(kernel, name, out_shape, plan, arrays, piece, after):
    vmem = pl.BlockSpec(memory_space=pltpu.VMEM)
    operands = [plan] + list(arrays)
    specs = [smem_spec()] + [vmem] * len(arrays)
    if piece is not None:
        array, first, number = piece
        operands += [array] * number
        for n in range(number):
            specs.append(
                pl.BlockSpec((1,) + array.shape[1:], lambda i, n=n: (first + n, 0, 0))
            )
    return pl.pallas_call(
        kernel,
        grid=(1,),
        in_specs=specs + [any_spec()] * len(after),
        out_specs=[vmem] * len(out_shape) if isinstance(out_shape, list) else vmem,
        out_shape=out_shape,
        compiler_params=pltpu.CompilerParams(vmem_limit_bytes=VMEM_BYTES),
        cost_estimate=LIGHT,
        name=name,
    )(*operands, *after)


def sum_cores_kernel(places, plan_ref, keep_ref, got_ref, *refs):
    sums_ref, send_ref = refs[-2:]
    chips, tokens, features = keep_ref.shape
    for chip in range(chips):
        rows = slice(chip * tokens, (chip + 1) * tokens)
        sums_ref[chip] = keep_ref[chip] + got_ref[rows, :].astype(jnp.float32)
    side, chip = plan_ref[places["side"]], plan_ref[places["chip"]]
    for n in range(2):
        send_ref[n * tokens : (n + 1) * tokens, :] = sums_ref[2 * (1 - side) + n].astype(
            send_ref.dtype
        )
    partner = sums_ref[1 + 4 * side - chip].astype(send_ref.dtype)
    for n in range(2, 4):
        send_ref[n * tokens : (n + 1) * tokens, :] = partner


def sum_cores(plan, places, keep, got, after=()):
    _, tokens, features = keep.shape
    out_shape = [
        jax.ShapeDtypeStruct(keep.shape, jnp.float32),
        jax.ShapeDtypeStruct((4 * tokens, features), jnp.bfloat16),
    ]
    kernel = functools.partial(sum_cores_kernel, places)
    return sum_call(kernel, "sum_cores", out_shape, plan, [keep, got], None, after)


def sum_inwards_kernel(places, plan_ref, sums_ref, over_ref, here_ref, *refs):
    inner_ref, send_ref = refs[-2:]
    tokens = inner_ref.shape[0]
    side, chip = plan_ref[places["side"]], plan_ref[places["chip"]]
    for n in range(2):
        rows = slice(n * tokens, (n + 1) * tokens)
        total = sums_ref[2 * (1 - side) + n] + over_ref[0, rows, :].astype(jnp.float32)
        send_ref[rows, :] = total.astype(send_ref.dtype)
    inner_ref[...] = sums_ref[chip] + here_ref[0, :tokens, :].astype(jnp.float32)


def sum_inwards(plan, places, sums, got, first, after=()):
    _, tokens, features = sums.shape
    out_shape = [
        jax.ShapeDtypeStruct((tokens, features), jnp.float32),
        jax.ShapeDtypeStruct((2 * tokens, features), jnp.bfloat16),
    ]
    kernel = functools.partial(sum_inwards_kernel, places)
    return sum_call(kernel, "sum_inwards", out_shape, plan, [sums], (got, first, 2), after)


def sum_across_kernel(places, plan_ref, sums_ref, inner_ref, got_ref, *refs):
    final_ref, send_ref = refs[-2:]
    tokens = inner_ref.shape[0]
    side, chip = plan_ref[places["side"]], plan_ref[places["chip"]]
    place = chip - 2 * side
    low = got_ref[0, :tokens, :].astype(jnp.float32)
    high = got_ref[0, tokens:, :].astype(jnp.float32)
    final_ref[...] = inner_ref[...] + jnp.where(place == 0, low, high)
    total = sums_ref[1 + 4 * side - chip] + jnp.where(place == 0, high, low)
    for n in range(2):
        send_ref[n * tokens : (n + 1) * tokens, :] = total.astype(send_ref.dtype)


def sum_across(plan, places, sums, inner, got, first, after=()):
    _, tokens, features = sums.shape
    out_shape = [
        jax.ShapeDtypeStruct((tokens, features), jnp.float32),
        jax.ShapeDtypeStruct((2 * tokens, features), jnp.bfloat16),
    ]
    kernel = functools.partial(sum_across_kernel, places)
    return sum_call(kernel, "sum_across", out_shape, plan, [sums, inner], (got, first, 1), after)


def sum_outwards_kernel(places, plan_ref, sums_ref, final_ref, got_ref, *refs):
    out_ref = refs[-1]
    tokens = final_ref.shape[0]
    outer = sums_ref[plan_ref[places["chip"]]] + got_ref[0, :tokens, :].astype(jnp.float32)
    out_ref[...] = jnp.where(plan_ref[places["inner"]] == 1, final_ref[...], outer).astype(
        out_ref.dtype
    )


def sum_outwards(plan, places, sums, final, got, first, after=()):
    out_shape = jax.ShapeDtypeStruct(final.shape, jnp.bfloat16)
    kernel = functools.partial(sum_outwards_kernel, places)
    return sum_call(kernel, "sum_outwards", out_shape, plan, [sums, final], (got, first, 1), after)


def gather_tokens(tokens, expert_ids, gate_weights, features):
    mine = lax.dynamic_slice_in_dim(tokens, lax.axis_index("train") * features, features, axis=1)
    top = expert_ids.shape[1]
    high = lax.reduce_precision(gate_weights, 8, 7)
    middle = lax.reduce_precision(gate_weights - high, 8, 7)
    low = gate_weights - high - middle
    beside = jnp.concatenate((expert_ids.astype(jnp.float32), high, middle, low), axis=1)
    beside = jnp.pad(beside, ((0, 0), (0, BLOCK - 4 * top))).astype(jnp.bfloat16)
    every = lax.all_gather(jnp.concatenate((mine, beside), axis=1), "roll", axis=0, tiled=True)
    side = every[:, features : features + 4 * top].astype(jnp.float32)
    ids = side[:, :top].astype(jnp.int32)
    weights = side[:, top : 2 * top] + side[:, 2 * top : 3 * top] + side[:, 3 * top :]
    return every[:, :features], ids, weights


def per_device(master_gate, master_up, master_down, tokens, expert_ids, gate_weights, placement):
    trains = lax.axis_size("train")
    owners = lax.axis_size("roll")
    experts, hidden_rows, features = master_gate.shape
    blocks = hidden_rows // BLOCK
    if owners // CORES == 4 and CORES * tokens.shape[0] == BLOCK:
        quant, gate = quantize(master_gate, 0, blocks, trains, experts)
        x_first = lax.all_to_all(quant, "train", split_axis=0, concat_axis=0, tiled=True)
        plan, places = make_plan(placement, experts, owners, (quant,))
        rest_up, up = quantize(master_up, 0, blocks, trains, experts, 0, None, (plan,))
        rest_down, down = quantize(master_down, 0, blocks, trains, experts, 0, None, (rest_up,))
        rest = (rest_up, rest_down)
        dequant = (gate, up, down)
        routed = gather_tokens(tokens, expert_ids, gate_weights, features)
        most = min(experts, owners // 2)
        shapes = (experts, blocks, trains, owners)

        def branch(cap, x_first, rest, dequant, plan, routed):
            return line_exchange(x_first, rest, dequant, plan, places, routed, shapes, cap)

        outs = lax.cond(
            plan[places["most"]] <= most - 1,
            functools.partial(branch, most - 1),
            functools.partial(branch, most),
            x_first,
            rest,
            dequant,
            plan,
            routed,
        )
    else:
        masters = (master_gate, master_up, master_down)
        quants, dequant = zip(*[quantize(w, 0, blocks, trains, experts) for w in masters])
        every, ids, weights = gather_tokens(tokens, expert_ids, gate_weights, features)
        outs = direct_exchange(quants, placement, trains, owners)
        pre = None
        for n in range(2 * blocks):
            restored = dequant[n // blocks]
            pre = pre_activations(every, ids, restored, n % blocks, pre, n, 2 * blocks)
        mixed = mix_experts(lax.psum(pre, "train"), ids, weights, dequant[2])
        mixed = lax.psum_scatter(mixed, "roll", scatter_dimension=0, tiled=True)
        outs = tuple(outs) + (mixed.astype(jnp.bfloat16),)
    return tuple(out[None] for out in outs[:3]) + (outs[3],)


def solution(mesh):
    in_specs = (
        P(None, "roll", "train"),
        P(None, "roll", "train"),
        P(None, "roll", "train"),
        P("roll", None),
        P("roll", None),
        P("roll", None),
        P(),
    )
    out_specs = (
        P("roll", None, "train", None),
        P("roll", None, "train", None),
        P("roll", None, "train", None),
        P("roll", "train"),
    )
    return jax.shard_map(
        per_device, mesh=mesh, in_specs=in_specs, out_specs=out_specs, check_vma=False
    )
```

```python
import functools

import jax
import jax.numpy as jnp
from jax import lax
from jax.experimental import pallas as pl
from jax.experimental.pallas import tpu as pltpu
from jax.sharding import PartitionSpec as P

BLOCK = 128
CORES = 2
VMEM_BYTES = 48 * 1024 * 1024
LIGHT = pl.CostEstimate(flops=1, bytes_accessed=1, transcendentals=0)


def any_spec():
    return pl.BlockSpec(memory_space=pl.ANY)


def smem_spec():
    return pl.BlockSpec(memory_space=pltpu.SMEM)


def quantize_kernel(trains, x_ref, *refs):
    q_ref, d_ref = refs[-2:]
    rows = BLOCK // trains
    features = x_ref.shape[-1]
    for col in range(features // BLOCK):
        cols = slice(col * BLOCK, (col + 1) * BLOCK)
        block = x_ref[0, :, cols]
        peak = jnp.max(jnp.max(jnp.abs(block), axis=0, keepdims=True), axis=1, keepdims=True)
        scale = peak.astype(jnp.bfloat16).astype(jnp.float32)
        quant = (block * (1.0 / scale)).astype(jnp.bfloat16)
        q_ref[:, 0, 0, :, cols] = quant.reshape(trains, rows, BLOCK)
        d_ref[0, 0, :, cols] = (quant.astype(jnp.float32) * scale).astype(jnp.bfloat16)


def quantize(master, first, blocks, trains, slots, base=0, into=None, after=()):
    experts, _, features = master.shape
    rows = BLOCK // trains
    operands = [master] + list(after) + ([] if into is None else [into])
    return pl.pallas_call(
        functools.partial(quantize_kernel, trains),
        grid=(experts, blocks),
        in_specs=[pl.BlockSpec((1, BLOCK, features), lambda e, b: (e, first + b, 0))]
        + [any_spec()] * (len(operands) - 1),
        out_specs=[
            pl.BlockSpec((trains, 1, 1, rows, features), lambda e, b: (0, base + e, b, 0, 0)),
            pl.BlockSpec((1, 1, BLOCK, features), lambda e, b: (e, b, 0, 0)),
        ],
        out_shape=[
            jax.ShapeDtypeStruct((trains, slots, blocks, rows, features), jnp.bfloat16),
            jax.ShapeDtypeStruct((experts, blocks, BLOCK, features), jnp.bfloat16),
        ],
        input_output_aliases={} if into is None else {len(operands) - 1: 0},
        compiler_params=pltpu.CompilerParams(vmem_limit_bytes=VMEM_BYTES),
        cost_estimate=LIGHT,
        name="quantize",
    )(*operands)


def start_choice(plan_ref, arrays, choice, target, sem):
    tests, array, (kind, n, *more) = choice
    ref = arrays[array]
    if kind == "is":
        view = ref.at[n]
    elif kind == "at":
        view = ref.at[plan_ref[n]]
    else:
        view = ref.at[:, plan_ref[n] + more[0], pl.ds(more[1], 1)]
    hit = None
    for place, value in tests:
        test = plan_ref[place] == value
        hit = test if hit is None else hit & test

    def go():
        pltpu.make_async_copy(view, target, sem).start()

    if hit is None:
        go()
    else:
        pl.when(hit)(go)


def pack_kernel(pieces, n_in, plan_ref, *refs):
    arrays = refs[:n_in]
    out, held, sem_in, sem_out = refs[-4:]
    for n, choices in enumerate(pieces):
        for choice in choices:
            start_choice(plan_ref, arrays, choice, held.at[n], sem_in.at[n])
    for n in range(len(pieces)):
        pltpu.make_async_copy(held.at[n], held.at[n], sem_in.at[n]).wait()
        pltpu.make_async_copy(held.at[n], out.at[n], sem_out.at[n]).start()
    for n in range(len(pieces)):
        pltpu.make_async_copy(held.at[n], out.at[n], sem_out.at[n]).wait()


class Arrays:
    def __init__(self):
        self.items = []

    def add(self, array):
        for n, item in enumerate(self.items):
            if item is array:
                return n
        self.items.append(array)
        return len(self.items) - 1


def number_choices(pieces, arrays):
    return [[(tests, arrays.add(a), index) for tests, a, index in choices] for choices in pieces]


def pack(plan, shape, pieces, after=()):
    arrays = Arrays()
    pieces = number_choices(pieces, arrays)
    n_in = len(arrays.items)
    size = len(pieces)
    for dim in shape:
        size *= dim
    operands = arrays.items + list(after)
    return pl.pallas_call(
        functools.partial(pack_kernel, pieces, n_in),
        in_specs=[smem_spec()] + [any_spec()] * len(operands),
        out_specs=any_spec(),
        out_shape=jax.ShapeDtypeStruct((len(pieces),) + shape, jnp.bfloat16),
        scratch_shapes=[
            pltpu.VMEM((len(pieces),) + shape, jnp.bfloat16),
            pltpu.SemaphoreType.DMA((len(pieces),)),
            pltpu.SemaphoreType.DMA((len(pieces),)),
        ],
        compiler_params=pltpu.CompilerParams(vmem_limit_bytes=VMEM_BYTES),
        cost_estimate=LIGHT,
        name="pack",
    )(plan, *operands)


def place_kernel(pieces, sources, first, blocks, n_in, plan_ref, *refs):
    arrays = refs[:n_in]
    out, mark, held, sem_in, sem_out = refs[-5:]
    trains, count, _, features = held.shape[1:]
    for n, choices in enumerate(pieces):
        for choice in choices:
            start_choice(plan_ref, arrays, choice, held.at[n], sem_in.at[n])
    mark[...] = jnp.zeros_like(mark)
    stores = []
    for n in range(len(pieces)):
        pltpu.make_async_copy(held.at[n], held.at[n], sem_in.at[n]).wait()
        start = plan_ref[sources[n]] * blocks + first
        for part in range(trains):
            store = pltpu.make_async_copy(
                held.at[n, part],
                out.at[pl.ds(start, count), :, pl.ds(part * features, features)],
                sem_out.at[n, part],
            )
            store.start()
            stores.append(store)
    for store in stores:
        store.wait()


def place_pieces(plan, shape, owners, pieces, sources, first, blocks, out, after=()):
    trains, count, rows, features = shape
    arrays = Arrays()
    pieces = number_choices(pieces, arrays)
    n_in = len(arrays.items)
    operands = arrays.items + list(after) + ([] if out is None else [out])
    return pl.pallas_call(
        functools.partial(place_kernel, pieces, sources, first, blocks, n_in),
        in_specs=[smem_spec()] + [any_spec()] * len(operands),
        out_specs=[any_spec(), pl.BlockSpec(memory_space=pltpu.VMEM)],
        out_shape=[
            jax.ShapeDtypeStruct((owners * blocks, rows, trains * features), jnp.bfloat16),
            jax.ShapeDtypeStruct((8, BLOCK), jnp.float32),
        ],
        scratch_shapes=[
            pltpu.VMEM((len(pieces),) + shape, jnp.bfloat16),
            pltpu.SemaphoreType.DMA((len(pieces),)),
            pltpu.SemaphoreType.DMA((len(pieces), trains)),
        ],
        input_output_aliases={} if out is None else {len(operands): 0},
        compiler_params=pltpu.CompilerParams(vmem_limit_bytes=VMEM_BYTES),
        cost_estimate=LIGHT,
        name="place_pieces",
    )(plan, *operands)


def plan_places(experts):
    names = [f"send{slot}" for slot in range(experts)]
    names += ["inner", "core", "chip", "side", "own", "mate", "out0", "out1", "most"]
    names += [f"{list_}_{who}" for list_ in ("here", "there") for who in ("own", "mate", "out0", "out1")]
    names += [f"from_{who}{n}" for who in ("own", "mate") for n in range(4)]
    return {name: n for n, name in enumerate(names)}


def plan_kernel(experts, owners, places, me_ref, placement_ref, out_ref):
    me = me_ref[0]
    chip, core = lax.div(me, CORES), lax.rem(me, CORES)
    side = lax.div(chip, 2)
    half = owners // 2
    needs, ranks = [], []
    for s in range(2):
        need = []
        for e in range(experts):
            found = jnp.int32(0)
            for o in range(s * half, (s + 1) * half):
                found = jnp.where(placement_ref[o] == e, 1, found)
            need.append(found)
        rank = []
        for e in range(experts):
            total = jnp.int32(0)
            for other in range(experts):
                if other != e:
                    ahead = need[other] >= need[e] if other < e else need[other] > need[e]
                    total = total + jnp.where(ahead, 1, 0)
            rank.append(total)
        needs.append(sum(need))
        ranks.append(rank)
    here = [jnp.where(side == 0, a, b) for a, b in zip(*ranks)]
    there = [jnp.where(side == 0, b, a) for a, b in zip(*ranks)]
    outer = 3 * side
    values = {
        "inner": jnp.where((chip == 1) | (chip == 2), 1, 0),
        "core": core,
        "chip": chip,
        "side": side,
        "own": placement_ref[me],
        "mate": placement_ref[chip * CORES + 1 - core],
        "out0": placement_ref[outer * CORES],
        "out1": placement_ref[outer * CORES + 1],
        "most": jnp.maximum(*needs),
    }
    for slot in range(experts):
        values[f"send{slot}"] = sum(jnp.where(there[e] == slot, e, 0) for e in range(experts))
    for who in ("own", "mate", "out0", "out1"):
        for list_, rank in (("here", here), ("there", there)):
            values[f"{list_}_{who}"] = sum(
                jnp.where(values[who] == e, rank[e], 0) for e in range(experts)
            )
    for n, source in enumerate((chip, 1 + 4 * side - chip, 2 - side, 3 - 3 * side)):
        values[f"from_own{n}"] = source * CORES + core
        values[f"from_mate{n}"] = source * CORES + 1 - core
    for name, n in places.items():
        out_ref[n] = values[name]


def make_plan(placement, experts, owners, after=()):
    places = plan_places(experts)
    me = jnp.reshape(lax.axis_index("roll"), (1,)).astype(jnp.int32)
    plan = pl.pallas_call(
        lambda *refs: plan_kernel(experts, owners, places, refs[0], refs[1], refs[-1]),
        in_specs=[smem_spec(), smem_spec()] + [any_spec()] * len(after),
        out_specs=smem_spec(),
        out_shape=jax.ShapeDtypeStruct((len(places),), jnp.int32),
        cost_estimate=LIGHT,
        name="plan",
    )(me, placement, *after)
    return plan, places


def line_schedule(opens, experts, cap, ride_from):
    chunks = range(len(opens))
    own, far = list(chunks), list(chunks)
    fresh = [("x", c, i) for c in chunks for i in range(CORES)]
    near = [("near", c, s) for c in chunks for s in range(cap, experts)]
    middle, inwards, outwards = [], [], []
    arrived, relayed, ride_due = [], [], {"in": ride_from}
    n = 0
    while own or arrived or far or near or fresh or relayed or ride_due:
        across, ins, outs = [], [], []
        if arrived and arrived[0][0] <= n:
            c = arrived.pop(0)[1]
            across = [("far", c, s) for s in range(cap)]
        elif own and opens[own[0]] <= n:
            c = own.pop(0)
            across = [("own", c, s) for s in range(cap)]
        if across:
            relayed += [(n + (2 if n else 1), (across[0][0], c, i)) for i in range(CORES)]
        if ride_due.get("across", n + 1) <= n and (not across or across[0][0] == "own"):
            across.append(("ride", 0, 0))
            del ride_due["across"]
            ride_due["out"] = n + 2
        if far and opens[far[0]] <= n:
            c = far.pop(0)
            ins = [("far", c, s) for s in range(cap)]
            arrived.append((n + 2, c))
        else:
            if ride_due.get("in", n + 1) <= n:
                ins = [("ride", 0, 0), ("ride", 0, 1)]
                del ride_due["in"]
                ride_due["across"] = n + 2
            while near and opens[near[0][1]] <= n and len(ins) < cap:
                ins.append(near.pop(0))
        while relayed and relayed[0][0] <= n and len(outs) < cap:
            outs.append(relayed.pop(0)[1])
        if ride_due.get("out", n + 1) <= n and len(outs) < cap:
            outs.append(("ride", 0, 0))
            del ride_due["out"]
        while fresh and opens[fresh[0][1]] <= n and len(outs) < cap:
            outs.append(fresh.pop(0))
        middle.append(across)
        inwards.append(ins)
        outwards.append(outs)
        n += 1
    return middle, inwards, outwards


def link_pairs(chip_pairs, swap_chips=()):
    pairs = []
    for core in range(CORES):
        for a, b in chip_pairs:
            pairs.append((a * CORES + core, b * CORES + core))
        for chip in swap_chips:
            pairs.append((chip * CORES + core, chip * CORES + 1 - core))
    return pairs


EDGES = ((0, 1), (1, 0), (2, 3), (3, 2))


def line_exchange(x_first, quant_rest, dequant, plan, places, routed, shapes, cap):
    experts, blocks, trains, owners = shapes
    features = x_first.shape[-1]
    rows = BLOCK // trains
    shape = (trains, 1, rows, features)
    chunks = [(m, b) for m in range(3) for b in range(blocks)]
    count = len(chunks)
    opens = [(0, 2, 5 if cap < experts else 4)[m] for m, _ in chunks]
    ride_from = 8
    middle, inwards, outwards = line_schedule(opens, experts, cap, ride_from)
    rounds = len(outwards)
    last_far = max(n for n in range(rounds) if inwards[n] and inwards[n][0][0] == "far")
    edge_pairs = link_pairs(EDGES)
    middle_pairs = link_pairs([(1, 2), (2, 1)], swap_chips=(0, 3))
    swap_pairs = link_pairs([], swap_chips=range(4))
    is_inner, is_outer = (places["inner"], 1), (places["inner"], 0)
    on_core = [(places["core"], core) for core in range(CORES)]
    got_edge, got_middle, where = {}, {}, {}
    last = [x_first]

    xs = [x_first] + [
        lax.all_to_all(quant, "train", split_axis=0, concat_axis=0, tiled=True)
        for quant in quant_rest
    ]

    def local(c, name):
        m, b = chunks[c]
        return xs[m], ("expert", places[name], 0, b)

    def packed(pieces, after=()):
        last[0] = pack(plan, shape, pieces, [last[0]] + list(after))
        return last[0]

    ready = {(c, 0): opens[c] for c in range(count)}

    def note(c, position, n):
        ready[c, position] = max(ready.get((c, position), 0), n)

    from_kind = {"x": 1, "own": 2, "far": 3}
    kind_of = {position: kind for kind, position in from_kind.items()}
    for n in range(rounds):
        for i, piece in enumerate(middle[n]):
            where[("across",) + piece] = (n, i)
            if piece[0] != "ride":
                note(piece[1], 2 if piece[0] == "own" else 3, n)
        for i, piece in enumerate(inwards[n]):
            where[("in",) + piece] = (n, i)
            if piece[0] != "ride":
                note(piece[1], 1, n)
        for i, piece in enumerate(outwards[n]):
            where[("out",) + piece] = (n, i)
            if piece[0] != "ride":
                note(piece[1], from_kind[piece[0]], n)

    def across(kind, c):
        return got_middle[where["across", kind, c, 0][0]]

    def find(c, position, who):
        if position == 0:
            return [((),) + local(c, who)]
        choices = []
        if position == 1:
            for slot in range(experts):
                n, i = where["in", "far" if slot < cap else "near", c, slot]
                test = (places[f"there_{who}"], slot)
                choices.append(((is_inner, test), got_edge[n], ("is", i)))
        else:
            got = across(kind_of[position], c)
            choices.append(((is_inner,), got, ("at", places[f"here_{who}"])))
        for core in range(CORES):
            n, i = where["out", kind_of[position], c, core if who == "own" else 1 - core]
            choices.append(((is_outer, on_core[core]), got_edge[n], ("is", i)))
        return choices

    to_swap = sorted((ready[c, p], c, p) for c in range(count) for p in range(4))
    to_place = []
    outs = [None, None, None]

    def swap(n, by):
        taken = []
        while to_swap and to_swap[0][0] <= by and len(taken) < 3:
            taken.append(to_swap.pop(0))
        if taken:
            got = lax.ppermute(
                packed([find(c, p, "mate") for _, c, p in taken]), "roll", swap_pairs
            )
            to_place.append((n, got, [(c, p) for _, c, p in taken]))
        return bool(taken)

    def place(got, taken):
        for c in sorted({c for c, _ in taken}):
            m, b = chunks[c]
            here = [(i, p) for i, (other, p) in enumerate(taken) if other == c]
            pieces = [find(c, p, "own") for _, p in here]
            pieces += [[((), got, ("is", i))] for i, _ in here]
            sources = [places[f"from_own{p}"] for _, p in here]
            sources += [places[f"from_mate{p}"] for _, p in here]
            outs[m], last[0] = place_pieces(
                plan, shape, owners, pieces, sources, b, blocks, outs[m], (last[0],)
            )

    ride = {}
    tokens, ids, weights = routed
    ups, down = dequant[:-1], dequant[-1]

    def ride_first():
        pre, columns = None, 2 * blocks
        for restored in ups:
            for b in range(restored.shape[1]):
                column = 0 if pre is None else column + 1
                pre = pre_activations(tokens, ids, restored, b, pre, column, columns, (last[0],))
                last[0] = pre
        ride["pre"] = lax.psum(pre, "train")
    def ride_mix():
        ride["keep"], going = mix_experts(
            ride["pre"], ids, weights, down, plan, places, (last[0],)
        )
        last[0] = ride["keep"]
        going = going.reshape((-1,) + shape)
        ride["swapped"] = lax.ppermute(going, "roll", swap_pairs)

    def ride_cores():
        got = ride["swapped"].reshape(-1, features)
        ride["sums"], going = sum_cores(plan, places, ride["keep"], got, (last[0],))
        last[0] = ride["sums"]
        ride["in"] = going.reshape((-1,) + shape)

    def ride_in():
        n, i = where["in", "ride", 0, 0]
        got = got_edge[n].reshape(-1, BLOCK, features)
        ride["inner"], going = sum_inwards(plan, places, ride["sums"], got, i, (last[0],))
        last[0] = ride["inner"]
        ride["across"] = going.reshape((-1,) + shape)

    def ride_across():
        n, i = where["across", "ride", 0, 0]
        got = got_middle[n].reshape(-1, BLOCK, features)
        ride["final"], going = sum_across(
            plan, places, ride["sums"], ride["inner"], got, i, (last[0],)
        )
        last[0] = ride["final"]
        ride["out"] = going.reshape((-1,) + shape)

    def ride_out():
        n, i = where["out", "ride", 0, 0]
        got = got_edge[n].reshape(-1, BLOCK, features)
        ride["mixed"] = sum_outwards(
            plan, places, ride["sums"], ride["final"], got, i, (last[0],)
        )
        last[0] = ride["mixed"]

    spare = local(0, "own")
    for n in range(rounds):
        swap(n, n - 2)
        if middle[n]:
            if where.get(("across", "ride", 0, 0), (-1,))[0] == n:
                ride_in()
            pieces = []
            for kind, c, slot in middle[n]:
                if kind == "own":
                    pieces.append([((),) + local(c, f"send{slot}")])
                elif kind == "ride":
                    pieces.append([((), ride["across"], ("is", 0))])
                else:
                    m, i = where["in", kind, c, slot]
                    pieces.append([((), got_edge[m], ("is", i))])
            after = [got_middle[n - 2]] if n - 2 in got_middle else []
            got_middle[n] = lax.ppermute(packed(pieces, after), "roll", middle_pairs)
        if where["out", "ride", 0, 0][0] == n:
            ride_across()
        pieces = []
        for i in range(max(len(inwards[n]), len(outwards[n]))):
            choices = [((is_inner,),) + spare, ((is_outer,),) + spare]
            if i < len(outwards[n]):
                kind, c, core = outwards[n][i]
                if kind == "x":
                    choices[0] = ((is_inner,),) + local(c, f"out{core}")
                elif kind == "ride":
                    choices[0] = ((is_inner,), ride["out"], ("is", 0))
                else:
                    index = ("at", places[f"here_out{core}"])
                    choices[0] = ((is_inner,), across(kind, c), index)
            if i < len(inwards[n]):
                kind, c, slot = inwards[n][i]
                if kind == "ride":
                    choices[1] = ((is_outer,), ride["in"], ("is", slot))
                else:
                    choices[1] = ((is_outer,),) + local(c, f"send{slot}")
            pieces.append(choices)
        while n < last_far and len(pieces) < cap:
            pieces.append([((),) + spare])
        if pieces:
            after = [got_edge[n - 2]] if n - 2 in got_edge else []
            got_edge[n] = lax.ppermute(packed(pieces, after), "roll", edge_pairs)
        if n == 0:
            ride_first()
        if n == ride_from - 3:
            ride_mix()
        if n == ride_from - 1:
            ride_cores()
        if n == where["out", "ride", 0, 0][0] + 2:
            ride_out()
        while to_place and to_place[0][0] <= n - 2:
            place(*to_place.pop(0)[1:])
    while to_swap:
        early = list(to_place)
        del to_place[:]
        swap(rounds, to_swap[0][0])
        for _, got, taken in early:
            place(got, taken)
    if "mixed" not in ride:
        ride_out()
    for _, got, taken in to_place:
        place(got, taken)
    return tuple(outs) + (ride["mixed"],)


def direct_exchange(quants, placement, trains, owners):
    outs = []
    for quant in quants:
        _, experts, blocks, rows, features = quant.shape
        x = lax.all_to_all(quant, "train", split_axis=0, concat_axis=0, tiled=True)
        x = jnp.transpose(x, (1, 2, 3, 0, 4)).reshape(experts, blocks, rows, trains * features)
        picked = jnp.take(x, placement, axis=0)
        got = lax.all_to_all(picked, "roll", split_axis=0, concat_axis=0, tiled=True)
        outs.append(got.reshape(owners * blocks, rows, trains * features))
    return outs


def pre_activation_kernel(experts, top, tok_ref, ids_ref, w_ref, *refs):
    out_ref = refs[-1]
    features = tok_ref.shape[1]
    weights = w_ref[...].reshape(experts * BLOCK, features)
    pre = lax.dot_general(
        tok_ref[...], weights, (((1,), (1,)), ((), ())), preferred_element_type=jnp.float32
    )
    for k in range(top):
        total = jnp.zeros((pre.shape[0], BLOCK), jnp.float32)
        for expert in range(experts):
            part = pre[:, expert * BLOCK : (expert + 1) * BLOCK]
            total = total + jnp.where(ids_ref[:, k : k + 1] == expert, part, 0.0)
        out_ref[:, k * BLOCK : (k + 1) * BLOCK] = total


def pre_activations(tokens, ids, restored, block, out, column, columns, after=()):
    count, features = tokens.shape
    experts, top = restored.shape[0], ids.shape[1]
    tile = min(count, 2 * BLOCK)
    operands = [tokens, ids, restored] + list(after) + ([] if out is None else [out])
    return pl.pallas_call(
        functools.partial(pre_activation_kernel, experts, top),
        grid=(count // tile,),
        in_specs=[
            pl.BlockSpec((tile, features), lambda i: (i, 0)),
            pl.BlockSpec((tile, top), lambda i: (i, 0)),
            pl.BlockSpec((experts, 1, BLOCK, features), lambda i: (0, block, 0, 0)),
        ]
        + [any_spec()] * (len(operands) - 3),
        out_specs=pl.BlockSpec((tile, top * BLOCK), lambda i: (i, column)),
        out_shape=jax.ShapeDtypeStruct((count, columns * top * BLOCK), jnp.float32),
        input_output_aliases={} if out is None else {len(operands) - 1: 0},
        compiler_params=pltpu.CompilerParams(vmem_limit_bytes=VMEM_BYTES),
        cost_estimate=LIGHT,
        name="pre_activations",
    )(*operands)


def mix_rows(experts, top, blocks, pre_ref, ids_ref, weights_ref, down_ref):
    width = top * BLOCK
    count, features = ids_ref.shape[0], down_ref.shape[-1]
    hidden = {}
    for b in range(blocks):
        for k in range(top):
            start = b * width + k * BLOCK
            gate = pre_ref[:, start : start + BLOCK]
            up = pre_ref[:, blocks * width + start : blocks * width + start + BLOCK]
            value = gate / (1.0 + jnp.exp(-gate)) * up
            hidden[b, k] = value.astype(jnp.bfloat16).astype(jnp.float32)
    total = jnp.zeros((count, features), jnp.float32)
    for expert in range(experts):
        weight = jnp.zeros((count, 1), jnp.float32)
        for k in range(top):
            weight = weight + jnp.where(
                ids_ref[:, k : k + 1] == expert, weights_ref[:, k : k + 1], 0.0
            )
        value = jnp.zeros((count, features), jnp.float32)
        for b in range(blocks):
            routed = jnp.zeros((count, BLOCK), jnp.float32)
            for k in range(top):
                routed = routed + jnp.where(ids_ref[:, k : k + 1] == expert, hidden[b, k], 0.0)
            value = value + jnp.dot(
                routed.astype(jnp.bfloat16), down_ref[expert, b], preferred_element_type=jnp.float32
            )
        total = total + weight * value
    return total


def mix_kernel(sizes, pre_ref, ids_ref, weights_ref, down_ref, out_ref):
    out_ref[...] = mix_rows(*sizes, pre_ref, ids_ref, weights_ref, down_ref)


def mix_split_kernel(sizes, core, pre_ref, ids_ref, weights_ref, down_ref, plan_ref, *refs):
    keep_ref, send_ref = refs[-2:]
    total = mix_rows(*sizes, pre_ref, ids_ref, weights_ref, down_ref)
    half = total.shape[0] // CORES
    first = plan_ref[core] == 0
    keep_ref[0] = jnp.where(first, total[:half], total[half:])
    send_ref[...] = jnp.where(first, total[half:], total[:half]).astype(send_ref.dtype)


def mix_specs(pre, ids, down, tile):
    return [
        pl.BlockSpec((tile, pre.shape[1]), lambda i: (i, 0)),
        pl.BlockSpec((tile, ids.shape[1]), lambda i: (i, 0)),
        pl.BlockSpec((tile, ids.shape[1]), lambda i: (i, 0)),
        pl.BlockSpec(down.shape, lambda i: (0, 0, 0, 0)),
    ]


def mix_experts(pre, ids, weights, down, plan=None, places=None, after=()):
    count, top = ids.shape
    experts, blocks, _, features = down.shape
    sizes = (experts, top, blocks)
    tile = min(count, BLOCK)
    params = pltpu.CompilerParams(vmem_limit_bytes=VMEM_BYTES)
    if plan is None:
        return pl.pallas_call(
            functools.partial(mix_kernel, sizes),
            grid=(count // tile,),
            in_specs=mix_specs(pre, ids, down, tile),
            out_specs=pl.BlockSpec((tile, features), lambda i: (i, 0)),
            out_shape=jax.ShapeDtypeStruct((count, features), jnp.float32),
            compiler_params=params,
            cost_estimate=LIGHT,
            name="mix_experts",
        )(pre, ids, weights, down)
    half = tile // CORES
    return pl.pallas_call(
        functools.partial(mix_split_kernel, sizes, places["core"]),
        grid=(count // tile,),
        in_specs=mix_specs(pre, ids, down, tile) + [smem_spec()] + [any_spec()] * len(after),
        out_specs=[
            pl.BlockSpec((1, half, features), lambda i: (i, 0, 0)),
            pl.BlockSpec((half, features), lambda i: (i, 0)),
        ],
        out_shape=[
            jax.ShapeDtypeStruct((count // tile, half, features), jnp.float32),
            jax.ShapeDtypeStruct((count // CORES, features), jnp.bfloat16),
        ],
        compiler_params=params,
        cost_estimate=LIGHT,
        name="mix_experts",
    )(pre, ids, weights, down, plan, *after)


def sum_call(kernel, name, out_shape, plan, arrays, piece, after):
    vmem = pl.BlockSpec(memory_space=pltpu.VMEM)
    operands = [plan] + list(arrays)
    specs = [smem_spec()] + [vmem] * len(arrays)
    if piece is not None:
        array, first, number = piece
        operands += [array] * number
        for n in range(number):
            specs.append(
                pl.BlockSpec((1,) + array.shape[1:], lambda i, n=n: (first + n, 0, 0))
            )
    return pl.pallas_call(
        kernel,
        grid=(1,),
        in_specs=specs + [any_spec()] * len(after),
        out_specs=[vmem] * len(out_shape) if isinstance(out_shape, list) else vmem,
        out_shape=out_shape,
        compiler_params=pltpu.CompilerParams(vmem_limit_bytes=VMEM_BYTES),
        cost_estimate=LIGHT,
        name=name,
    )(*operands, *after)


def sum_cores_kernel(places, plan_ref, keep_ref, got_ref, *refs):
    sums_ref, send_ref = refs[-2:]
    chips, tokens, features = keep_ref.shape
    for chip in range(chips):
        rows = slice(chip * tokens, (chip + 1) * tokens)
        sums_ref[chip] = keep_ref[chip] + got_ref[rows, :].astype(jnp.float32)
    side, chip = plan_ref[places["side"]], plan_ref[places["chip"]]
    for n in range(2):
        send_ref[n * tokens : (n + 1) * tokens, :] = sums_ref[2 * (1 - side) + n].astype(
            send_ref.dtype
        )
    partner = sums_ref[1 + 4 * side - chip].astype(send_ref.dtype)
    for n in range(2, 4):
        send_ref[n * tokens : (n + 1) * tokens, :] = partner


def sum_cores(plan, places, keep, got, after=()):
    _, tokens, features = keep.shape
    out_shape = [
        jax.ShapeDtypeStruct(keep.shape, jnp.float32),
        jax.ShapeDtypeStruct((4 * tokens, features), jnp.bfloat16),
    ]
    kernel = functools.partial(sum_cores_kernel, places)
    return sum_call(kernel, "sum_cores", out_shape, plan, [keep, got], None, after)


def sum_inwards_kernel(places, plan_ref, sums_ref, over_ref, here_ref, *refs):
    inner_ref, send_ref = refs[-2:]
    tokens = inner_ref.shape[0]
    side, chip = plan_ref[places["side"]], plan_ref[places["chip"]]
    for n in range(2):
        rows = slice(n * tokens, (n + 1) * tokens)
        total = sums_ref[2 * (1 - side) + n] + over_ref[0, rows, :].astype(jnp.float32)
        send_ref[rows, :] = total.astype(send_ref.dtype)
    inner_ref[...] = sums_ref[chip] + here_ref[0, :tokens, :].astype(jnp.float32)


def sum_inwards(plan, places, sums, got, first, after=()):
    _, tokens, features = sums.shape
    out_shape = [
        jax.ShapeDtypeStruct((tokens, features), jnp.float32),
        jax.ShapeDtypeStruct((2 * tokens, features), jnp.bfloat16),
    ]
    kernel = functools.partial(sum_inwards_kernel, places)
    return sum_call(kernel, "sum_inwards", out_shape, plan, [sums], (got, first, 2), after)


def sum_across_kernel(places, plan_ref, sums_ref, inner_ref, got_ref, *refs):
    final_ref, send_ref = refs[-2:]
    tokens = inner_ref.shape[0]
    side, chip = plan_ref[places["side"]], plan_ref[places["chip"]]
    place = chip - 2 * side
    low = got_ref[0, :tokens, :].astype(jnp.float32)
    high = got_ref[0, tokens:, :].astype(jnp.float32)
    final_ref[...] = inner_ref[...] + jnp.where(place == 0, low, high)
    total = sums_ref[1 + 4 * side - chip] + jnp.where(place == 0, high, low)
    for n in range(2):
        send_ref[n * tokens : (n + 1) * tokens, :] = total.astype(send_ref.dtype)


def sum_across(plan, places, sums, inner, got, first, after=()):
    _, tokens, features = sums.shape
    out_shape = [
        jax.ShapeDtypeStruct((tokens, features), jnp.float32),
        jax.ShapeDtypeStruct((2 * tokens, features), jnp.bfloat16),
    ]
    kernel = functools.partial(sum_across_kernel, places)
    return sum_call(kernel, "sum_across", out_shape, plan, [sums, inner], (got, first, 1), after)


def sum_outwards_kernel(places, plan_ref, sums_ref, final_ref, got_ref, *refs):
    out_ref = refs[-1]
    tokens = final_ref.shape[0]
    outer = sums_ref[plan_ref[places["chip"]]] + got_ref[0, :tokens, :].astype(jnp.float32)
    out_ref[...] = jnp.where(plan_ref[places["inner"]] == 1, final_ref[...], outer).astype(
        out_ref.dtype
    )


def sum_outwards(plan, places, sums, final, got, first, after=()):
    out_shape = jax.ShapeDtypeStruct(final.shape, jnp.bfloat16)
    kernel = functools.partial(sum_outwards_kernel, places)
    return sum_call(kernel, "sum_outwards", out_shape, plan, [sums, final], (got, first, 1), after)


def gather_tokens(tokens, expert_ids, gate_weights, features):
    mine = lax.dynamic_slice_in_dim(tokens, lax.axis_index("train") * features, features, axis=1)
    top = expert_ids.shape[1]
    high = lax.reduce_precision(gate_weights, 8, 7)
    middle = lax.reduce_precision(gate_weights - high, 8, 7)
    low = gate_weights - high - middle
    beside = jnp.concatenate((expert_ids.astype(jnp.float32), high, middle, low), axis=1)
    beside = jnp.pad(beside, ((0, 0), (0, BLOCK - 4 * top))).astype(jnp.bfloat16)
    every = lax.all_gather(jnp.concatenate((mine, beside), axis=1), "roll", axis=0, tiled=True)
    side = every[:, features : features + 4 * top].astype(jnp.float32)
    ids = side[:, :top].astype(jnp.int32)
    weights = side[:, top : 2 * top] + side[:, 2 * top : 3 * top] + side[:, 3 * top :]
    return every[:, :features], ids, weights


def per_device(master_gate, master_up, master_down, tokens, expert_ids, gate_weights, placement):
    trains = lax.axis_size("train")
    owners = lax.axis_size("roll")
    experts, hidden_rows, features = master_gate.shape
    blocks = hidden_rows // BLOCK
    if owners // CORES == 4 and CORES * tokens.shape[0] == BLOCK:
        quant, gate = quantize(master_gate, 0, blocks, trains, experts)
        x_first = lax.all_to_all(quant, "train", split_axis=0, concat_axis=0, tiled=True)
        plan, places = make_plan(placement, experts, owners, (quant,))
        rest_up, up = quantize(master_up, 0, blocks, trains, experts, 0, None, (plan,))
        rest_down, down = quantize(master_down, 0, blocks, trains, experts, 0, None, (rest_up,))
        rest = (rest_up, rest_down)
        dequant = (gate, up, down)
        routed = gather_tokens(tokens, expert_ids, gate_weights, features)
        most = min(experts, owners // 2)
        shapes = (experts, blocks, trains, owners)

        def branch(cap, x_first, rest, dequant, plan, routed):
            return line_exchange(x_first, rest, dequant, plan, places, routed, shapes, cap)

        outs = lax.cond(
            plan[places["most"]] <= most - 1,
            functools.partial(branch, most - 1),
            functools.partial(branch, most),
            x_first,
            rest,
            dequant,
            plan,
            routed,
        )
    else:
        masters = (master_gate, master_up, master_down)
        quants, dequant = zip(*[quantize(w, 0, blocks, trains, experts) for w in masters])
        every, ids, weights = gather_tokens(tokens, expert_ids, gate_weights, features)
        outs = direct_exchange(quants, placement, trains, owners)
        pre = None
        for n in range(2 * blocks):
            restored = dequant[n // blocks]
            pre = pre_activations(every, ids, restored, n % blocks, pre, n, 2 * blocks)
        mixed = mix_experts(lax.psum(pre, "train"), ids, weights, dequant[2])
        mixed = lax.psum_scatter(mixed, "roll", scatter_dimension=0, tiled=True)
        outs = tuple(outs) + (mixed.astype(jnp.bfloat16),)
    return tuple(out[None] for out in outs[:3]) + (outs[3],)


def solution(mesh):
    in_specs = (
        P(None, "roll", "train"),
        P(None, "roll", "train"),
        P(None, "roll", "train"),
        P("roll", None),
        P("roll", None),
        P("roll", None),
        P(),
    )
    out_specs = (
        P("roll", None, "train", None),
        P("roll", None, "train", None),
        P("roll", None, "train", None),
        P("roll", "train"),
    )
    return jax.shard_map(
        per_device, mesh=mesh, in_specs=in_specs, out_specs=out_specs, check_vma=False
    )
```

```python
import functools

import jax
import jax.numpy as jnp
from jax import lax
from jax.experimental import pallas as pl
from jax.experimental.pallas import tpu as pltpu
from jax.sharding import PartitionSpec as P

BLOCK = 128
CORES = 2
VMEM_BYTES = 48 * 1024 * 1024
LIGHT = pl.CostEstimate(flops=1, bytes_accessed=1, transcendentals=0)


def any_spec():
    return pl.BlockSpec(memory_space=pl.ANY)


def smem_spec():
    return pl.BlockSpec(memory_space=pltpu.SMEM)


def quantize_kernel(trains, x_ref, *refs):
    q_ref, d_ref = refs[-2:]
    rows = BLOCK // trains
    features = x_ref.shape[-1]
    for col in range(features // BLOCK):
        cols = slice(col * BLOCK, (col + 1) * BLOCK)
        block = x_ref[0, :, cols]
        peak = jnp.max(jnp.max(jnp.abs(block), axis=0, keepdims=True), axis=1, keepdims=True)
        scale = peak.astype(jnp.bfloat16).astype(jnp.float32)
        quant = (block * (1.0 / scale)).astype(jnp.bfloat16)
        q_ref[:, 0, 0, :, cols] = quant.reshape(trains, rows, BLOCK)
        d_ref[0, 0, :, cols] = (quant.astype(jnp.float32) * scale).astype(jnp.bfloat16)


def quantize(master, first, blocks, trains, slots, base=0, into=None, after=()):
    experts, _, features = master.shape
    rows = BLOCK // trains
    operands = [master] + list(after) + ([] if into is None else [into])
    return pl.pallas_call(
        functools.partial(quantize_kernel, trains),
        grid=(experts, blocks),
        in_specs=[pl.BlockSpec((1, BLOCK, features), lambda e, b: (e, first + b, 0))]
        + [any_spec()] * (len(operands) - 1),
        out_specs=[
            pl.BlockSpec((trains, 1, 1, rows, features), lambda e, b: (0, base + e, b, 0, 0)),
            pl.BlockSpec((1, 1, BLOCK, features), lambda e, b: (e, b, 0, 0)),
        ],
        out_shape=[
            jax.ShapeDtypeStruct((trains, slots, blocks, rows, features), jnp.bfloat16),
            jax.ShapeDtypeStruct((experts, blocks, BLOCK, features), jnp.bfloat16),
        ],
        input_output_aliases={} if into is None else {len(operands) - 1: 0},
        compiler_params=pltpu.CompilerParams(vmem_limit_bytes=VMEM_BYTES),
        cost_estimate=LIGHT,
        name="quantize",
    )(*operands)


def start_choice(plan_ref, arrays, choice, target, sem):
    tests, array, (kind, n, *more) = choice
    ref = arrays[array]
    if kind == "is":
        view = ref.at[n]
    elif kind == "at":
        view = ref.at[plan_ref[n]]
    else:
        view = ref.at[:, plan_ref[n] + more[0], pl.ds(more[1], 1)]
    hit = None
    for place, value in tests:
        test = plan_ref[place] == value
        hit = test if hit is None else hit & test

    def go():
        pltpu.make_async_copy(view, target, sem).start()

    if hit is None:
        go()
    else:
        pl.when(hit)(go)


def pack_kernel(pieces, n_in, plan_ref, *refs):
    arrays = refs[:n_in]
    out, held, sem_in, sem_out = refs[-4:]
    for n, choices in enumerate(pieces):
        for choice in choices:
            start_choice(plan_ref, arrays, choice, held.at[n], sem_in.at[n])
    for n in range(len(pieces)):
        pltpu.make_async_copy(held.at[n], held.at[n], sem_in.at[n]).wait()
        pltpu.make_async_copy(held.at[n], out.at[n], sem_out.at[n]).start()
    for n in range(len(pieces)):
        pltpu.make_async_copy(held.at[n], out.at[n], sem_out.at[n]).wait()


class Arrays:
    def __init__(self):
        self.items = []

    def add(self, array):
        for n, item in enumerate(self.items):
            if item is array:
                return n
        self.items.append(array)
        return len(self.items) - 1


def number_choices(pieces, arrays):
    return [[(tests, arrays.add(a), index) for tests, a, index in choices] for choices in pieces]


def pack(plan, shape, pieces, after=()):
    arrays = Arrays()
    pieces = number_choices(pieces, arrays)
    n_in = len(arrays.items)
    size = len(pieces)
    for dim in shape:
        size *= dim
    operands = arrays.items + list(after)
    return pl.pallas_call(
        functools.partial(pack_kernel, pieces, n_in),
        in_specs=[smem_spec()] + [any_spec()] * len(operands),
        out_specs=any_spec(),
        out_shape=jax.ShapeDtypeStruct((len(pieces),) + shape, jnp.bfloat16),
        scratch_shapes=[
            pltpu.VMEM((len(pieces),) + shape, jnp.bfloat16),
            pltpu.SemaphoreType.DMA((len(pieces),)),
            pltpu.SemaphoreType.DMA((len(pieces),)),
        ],
        compiler_params=pltpu.CompilerParams(vmem_limit_bytes=VMEM_BYTES),
        cost_estimate=LIGHT,
        name="pack",
    )(plan, *operands)


def place_kernel(pieces, sources, first, blocks, n_in, plan_ref, *refs):
    arrays = refs[:n_in]
    out, mark, held, sem_in, sem_out = refs[-5:]
    trains, count, _, features = held.shape[1:]
    for n, choices in enumerate(pieces):
        for choice in choices:
            start_choice(plan_ref, arrays, choice, held.at[n], sem_in.at[n])
    mark[...] = jnp.zeros_like(mark)
    stores = []
    for n in range(len(pieces)):
        pltpu.make_async_copy(held.at[n], held.at[n], sem_in.at[n]).wait()
        start = plan_ref[sources[n]] * blocks + first
        for part in range(trains):
            store = pltpu.make_async_copy(
                held.at[n, part],
                out.at[pl.ds(start, count), :, pl.ds(part * features, features)],
                sem_out.at[n, part],
            )
            store.start()
            stores.append(store)
    for store in stores:
        store.wait()


def place_pieces(plan, shape, owners, pieces, sources, first, blocks, out, after=()):
    trains, count, rows, features = shape
    arrays = Arrays()
    pieces = number_choices(pieces, arrays)
    n_in = len(arrays.items)
    operands = arrays.items + list(after) + ([] if out is None else [out])
    return pl.pallas_call(
        functools.partial(place_kernel, pieces, sources, first, blocks, n_in),
        in_specs=[smem_spec()] + [any_spec()] * len(operands),
        out_specs=[any_spec(), pl.BlockSpec(memory_space=pltpu.VMEM)],
        out_shape=[
            jax.ShapeDtypeStruct((owners * blocks, rows, trains * features), jnp.bfloat16),
            jax.ShapeDtypeStruct((8, BLOCK), jnp.float32),
        ],
        scratch_shapes=[
            pltpu.VMEM((len(pieces),) + shape, jnp.bfloat16),
            pltpu.SemaphoreType.DMA((len(pieces),)),
            pltpu.SemaphoreType.DMA((len(pieces), trains)),
        ],
        input_output_aliases={} if out is None else {len(operands): 0},
        compiler_params=pltpu.CompilerParams(vmem_limit_bytes=VMEM_BYTES),
        cost_estimate=LIGHT,
        name="place_pieces",
    )(plan, *operands)


def plan_places(experts):
    names = [f"send{slot}" for slot in range(experts)]
    names += ["inner", "core", "chip", "side", "own", "mate", "out0", "out1", "most"]
    names += [f"{list_}_{who}" for list_ in ("here", "there") for who in ("own", "mate", "out0", "out1")]
    names += [f"from_{who}{n}" for who in ("own", "mate") for n in range(4)]
    return {name: n for n, name in enumerate(names)}


def plan_kernel(experts, owners, places, me_ref, placement_ref, out_ref):
    me = me_ref[0]
    chip, core = lax.div(me, CORES), lax.rem(me, CORES)
    side = lax.div(chip, 2)
    half = owners // 2
    needs, ranks = [], []
    for s in range(2):
        need = []
        for e in range(experts):
            found = jnp.int32(0)
            for o in range(s * half, (s + 1) * half):
                found = jnp.where(placement_ref[o] == e, 1, found)
            need.append(found)
        rank = []
        for e in range(experts):
            total = jnp.int32(0)
            for other in range(experts):
                if other != e:
                    ahead = need[other] >= need[e] if other < e else need[other] > need[e]
                    total = total + jnp.where(ahead, 1, 0)
            rank.append(total)
        needs.append(sum(need))
        ranks.append(rank)
    here = [jnp.where(side == 0, a, b) for a, b in zip(*ranks)]
    there = [jnp.where(side == 0, b, a) for a, b in zip(*ranks)]
    outer = 3 * side
    values = {
        "inner": jnp.where((chip == 1) | (chip == 2), 1, 0),
        "core": core,
        "chip": chip,
        "side": side,
        "own": placement_ref[me],
        "mate": placement_ref[chip * CORES + 1 - core],
        "out0": placement_ref[outer * CORES],
        "out1": placement_ref[outer * CORES + 1],
        "most": jnp.maximum(*needs),
    }
    for slot in range(experts):
        values[f"send{slot}"] = sum(jnp.where(there[e] == slot, e, 0) for e in range(experts))
    for who in ("own", "mate", "out0", "out1"):
        for list_, rank in (("here", here), ("there", there)):
            values[f"{list_}_{who}"] = sum(
                jnp.where(values[who] == e, rank[e], 0) for e in range(experts)
            )
    for n, source in enumerate((chip, 1 + 4 * side - chip, 2 - side, 3 - 3 * side)):
        values[f"from_own{n}"] = source * CORES + core
        values[f"from_mate{n}"] = source * CORES + 1 - core
    for name, n in places.items():
        out_ref[n] = values[name]


def make_plan(placement, experts, owners, after=()):
    places = plan_places(experts)
    me = jnp.reshape(lax.axis_index("roll"), (1,)).astype(jnp.int32)
    plan = pl.pallas_call(
        lambda *refs: plan_kernel(experts, owners, places, refs[0], refs[1], refs[-1]),
        in_specs=[smem_spec(), smem_spec()] + [any_spec()] * len(after),
        out_specs=smem_spec(),
        out_shape=jax.ShapeDtypeStruct((len(places),), jnp.int32),
        cost_estimate=LIGHT,
        name="plan",
    )(me, placement, *after)
    return plan, places


def line_schedule(opens, experts, cap, ride_from):
    chunks = range(len(opens))
    own, far = list(chunks), list(chunks)
    fresh = [("x", c, i) for c in chunks for i in range(CORES)]
    near = [("near", c, s) for c in chunks for s in range(cap, experts)]
    middle, inwards, outwards = [], [], []
    arrived, relayed, ride_due = [], [], {"in": ride_from}
    n = 0
    while own or arrived or far or near or fresh or relayed or ride_due:
        across, ins, outs = [], [], []
        if arrived and arrived[0][0] <= n:
            c = arrived.pop(0)[1]
            across = [("far", c, s) for s in range(cap)]
        elif own and opens[own[0]] <= n:
            c = own.pop(0)
            across = [("own", c, s) for s in range(cap)]
        if across:
            relayed += [(n + (2 if n else 1), (across[0][0], c, i)) for i in range(CORES)]
        if ride_due.get("across", n + 1) <= n and (not across or across[0][0] == "own"):
            across.append(("ride", 0, 0))
            del ride_due["across"]
            ride_due["out"] = n + 2
        if far and opens[far[0]] <= n:
            c = far.pop(0)
            ins = [("far", c, s) for s in range(cap)]
            arrived.append((n + 2, c))
        else:
            if ride_due.get("in", n + 1) <= n:
                ins = [("ride", 0, 0), ("ride", 0, 1)]
                del ride_due["in"]
                ride_due["across"] = n + 2
            while near and opens[near[0][1]] <= n and len(ins) < cap:
                ins.append(near.pop(0))
        while relayed and relayed[0][0] <= n and len(outs) < cap:
            outs.append(relayed.pop(0)[1])
        if ride_due.get("out", n + 1) <= n and len(outs) < cap:
            outs.append(("ride", 0, 0))
            del ride_due["out"]
        while fresh and opens[fresh[0][1]] + (1 if opens[fresh[0][1]] == 5 else 0) <= n and len(outs) < cap:
            outs.append(fresh.pop(0))
        middle.append(across)
        inwards.append(ins)
        outwards.append(outs)
        n += 1
    return middle, inwards, outwards


def link_pairs(chip_pairs, swap_chips=()):
    pairs = []
    for core in range(CORES):
        for a, b in chip_pairs:
            pairs.append((a * CORES + core, b * CORES + core))
        for chip in swap_chips:
            pairs.append((chip * CORES + core, chip * CORES + 1 - core))
    return pairs


EDGES = ((0, 1), (1, 0), (2, 3), (3, 2))


def line_exchange(x_first, quant_rest, dequant, plan, places, routed, shapes, cap):
    experts, blocks, trains, owners = shapes
    features = x_first.shape[-1]
    rows = BLOCK // trains
    shape = (trains, 1, rows, features)
    chunks = [(m, b) for m in range(3) for b in range(blocks)]
    count = len(chunks)
    opens = [(0, 2, 5 if cap < experts else 4)[m] for m, _ in chunks]
    ride_from = 8
    middle, inwards, outwards = line_schedule(opens, experts, cap, ride_from)
    rounds = len(outwards)
    last_far = max(n for n in range(rounds) if inwards[n] and inwards[n][0][0] == "far")
    edge_pairs = link_pairs(EDGES)
    middle_pairs = link_pairs([(1, 2), (2, 1)], swap_chips=(0, 3))
    swap_pairs = link_pairs([], swap_chips=range(4))
    is_inner, is_outer = (places["inner"], 1), (places["inner"], 0)
    on_core = [(places["core"], core) for core in range(CORES)]
    got_edge, got_middle, where = {}, {}, {}
    last = [x_first]

    xs = [x_first] + [
        lax.all_to_all(quant, "train", split_axis=0, concat_axis=0, tiled=True)
        for quant in quant_rest
    ]

    def local(c, name):
        m, b = chunks[c]
        return xs[m], ("expert", places[name], 0, b)

    def packed(pieces, after=()):
        last[0] = pack(plan, shape, pieces, [last[0]] + list(after))
        return last[0]

    ready = {(c, 0): opens[c] for c in range(count)}

    def note(c, position, n):
        ready[c, position] = max(ready.get((c, position), 0), n)

    from_kind = {"x": 1, "own": 2, "far": 3}
    kind_of = {position: kind for kind, position in from_kind.items()}
    for n in range(rounds):
        for i, piece in enumerate(middle[n]):
            where[("across",) + piece] = (n, i)
            if piece[0] != "ride":
                note(piece[1], 2 if piece[0] == "own" else 3, n)
        for i, piece in enumerate(inwards[n]):
            where[("in",) + piece] = (n, i)
            if piece[0] != "ride":
                note(piece[1], 1, n)
        for i, piece in enumerate(outwards[n]):
            where[("out",) + piece] = (n, i)
            if piece[0] != "ride":
                note(piece[1], from_kind[piece[0]], n)

    def across(kind, c):
        return got_middle[where["across", kind, c, 0][0]]

    def find(c, position, who):
        if position == 0:
            return [((),) + local(c, who)]
        choices = []
        if position == 1:
            for slot in range(experts):
                n, i = where["in", "far" if slot < cap else "near", c, slot]
                test = (places[f"there_{who}"], slot)
                choices.append(((is_inner, test), got_edge[n], ("is", i)))
        else:
            got = across(kind_of[position], c)
            choices.append(((is_inner,), got, ("at", places[f"here_{who}"])))
        for core in range(CORES):
            n, i = where["out", kind_of[position], c, core if who == "own" else 1 - core]
            choices.append(((is_outer, on_core[core]), got_edge[n], ("is", i)))
        return choices

    to_swap = sorted((ready[c, p], c, p) for c in range(count) for p in range(4))
    to_place = []
    outs = [None, None, None]

    def swap(n, by):
        taken = []
        while to_swap and to_swap[0][0] <= by and len(taken) < 3:
            taken.append(to_swap.pop(0))
        if taken:
            got = lax.ppermute(
                packed([find(c, p, "mate") for _, c, p in taken]), "roll", swap_pairs
            )
            to_place.append((n, got, [(c, p) for _, c, p in taken]))
        return bool(taken)

    def place(got, taken):
        for c in sorted({c for c, _ in taken}):
            m, b = chunks[c]
            here = [(i, p) for i, (other, p) in enumerate(taken) if other == c]
            pieces = [find(c, p, "own") for _, p in here]
            pieces += [[((), got, ("is", i))] for i, _ in here]
            sources = [places[f"from_own{p}"] for _, p in here]
            sources += [places[f"from_mate{p}"] for _, p in here]
            outs[m], last[0] = place_pieces(
                plan, shape, owners, pieces, sources, b, blocks, outs[m], (last[0],)
            )

    ride = {}
    tokens, ids, weights = routed
    ups, down = dequant[:-1], dequant[-1]

    def ride_first():
        pre, columns = None, 2 * blocks
        for restored in ups:
            for b in range(restored.shape[1]):
                column = 0 if pre is None else column + 1
                pre = pre_activations(tokens, ids, restored, b, pre, column, columns, (last[0],))
                last[0] = pre
        ride["pre"] = lax.psum(pre, "train")
    def ride_mix():
        ride["keep"], going = mix_experts(
            ride["pre"], ids, weights, down, plan, places, (last[0],)
        )
        last[0] = ride["keep"]
        going = going.reshape((-1,) + shape)
        ride["swapped"] = lax.ppermute(going, "roll", swap_pairs)

    def ride_cores():
        got = ride["swapped"].reshape(-1, features)
        ride["sums"], going = sum_cores(plan, places, ride["keep"], got, (last[0],))
        last[0] = ride["sums"]
        ride["in"] = going.reshape((-1,) + shape)

    def ride_in():
        n, i = where["in", "ride", 0, 0]
        got = got_edge[n].reshape(-1, BLOCK, features)
        ride["inner"], going = sum_inwards(plan, places, ride["sums"], got, i, (last[0],))
        last[0] = ride["inner"]
        ride["across"] = going.reshape((-1,) + shape)

    def ride_across():
        n, i = where["across", "ride", 0, 0]
        got = got_middle[n].reshape(-1, BLOCK, features)
        ride["final"], going = sum_across(
            plan, places, ride["sums"], ride["inner"], got, i, (last[0],)
        )
        last[0] = ride["final"]
        ride["out"] = going.reshape((-1,) + shape)

    def ride_out():
        n, i = where["out", "ride", 0, 0]
        got = got_edge[n].reshape(-1, BLOCK, features)
        ride["mixed"] = sum_outwards(
            plan, places, ride["sums"], ride["final"], got, i, (last[0],)
        )
        last[0] = ride["mixed"]

    spare = local(0, "own")
    for n in range(rounds):
        swap(n, n - 2)
        if middle[n]:
            if where.get(("across", "ride", 0, 0), (-1,))[0] == n:
                ride_in()
            pieces = []
            for kind, c, slot in middle[n]:
                if kind == "own":
                    pieces.append([((),) + local(c, f"send{slot}")])
                elif kind == "ride":
                    pieces.append([((), ride["across"], ("is", 0))])
                else:
                    m, i = where["in", kind, c, slot]
                    pieces.append([((), got_edge[m], ("is", i))])
            after = [got_middle[n - 2]] if n - 2 in got_middle else []
            got_middle[n] = lax.ppermute(packed(pieces, after), "roll", middle_pairs)
        if where["out", "ride", 0, 0][0] == n:
            ride_across()
        pieces = []
        for i in range(max(len(inwards[n]), len(outwards[n]))):
            choices = [((is_inner,),) + spare, ((is_outer,),) + spare]
            if i < len(outwards[n]):
                kind, c, core = outwards[n][i]
                if kind == "x":
                    choices[0] = ((is_inner,),) + local(c, f"out{core}")
                elif kind == "ride":
                    choices[0] = ((is_inner,), ride["out"], ("is", 0))
                else:
                    index = ("at", places[f"here_out{core}"])
                    choices[0] = ((is_inner,), across(kind, c), index)
            if i < len(inwards[n]):
                kind, c, slot = inwards[n][i]
                if kind == "ride":
                    choices[1] = ((is_outer,), ride["in"], ("is", slot))
                else:
                    choices[1] = ((is_outer,),) + local(c, f"send{slot}")
            pieces.append(choices)
        while n < last_far and len(pieces) < cap:
            pieces.append([((),) + spare])
        if pieces:
            after = [got_edge[n - 2]] if n - 2 in got_edge else []
            got_edge[n] = lax.ppermute(packed(pieces, after), "roll", edge_pairs)
        if n == 0:
            ride_first()
        if n == ride_from - 3:
            ride_mix()
        if n == ride_from - 1:
            ride_cores()
        if n == where["out", "ride", 0, 0][0] + 2:
            ride_out()
        while to_place and to_place[0][0] <= n - 2:
            place(*to_place.pop(0)[1:])
    while to_swap:
        early = list(to_place)
        del to_place[:]
        swap(rounds, to_swap[0][0])
        for _, got, taken in early:
            place(got, taken)
    if "mixed" not in ride:
        ride_out()
    for _, got, taken in to_place:
        place(got, taken)
    return tuple(outs) + (ride["mixed"],)


def direct_exchange(quants, placement, trains, owners):
    outs = []
    for quant in quants:
        _, experts, blocks, rows, features = quant.shape
        x = lax.all_to_all(quant, "train", split_axis=0, concat_axis=0, tiled=True)
        x = jnp.transpose(x, (1, 2, 3, 0, 4)).reshape(experts, blocks, rows, trains * features)
        picked = jnp.take(x, placement, axis=0)
        got = lax.all_to_all(picked, "roll", split_axis=0, concat_axis=0, tiled=True)
        outs.append(got.reshape(owners * blocks, rows, trains * features))
    return outs


def pre_activation_kernel(experts, top, tok_ref, ids_ref, w_ref, *refs):
    out_ref = refs[-1]
    features = tok_ref.shape[1]
    weights = w_ref[...].reshape(experts * BLOCK, features)
    pre = lax.dot_general(
        tok_ref[...], weights, (((1,), (1,)), ((), ())), preferred_element_type=jnp.float32
    )
    for k in range(top):
        total = jnp.zeros((pre.shape[0], BLOCK), jnp.float32)
        for expert in range(experts):
            part = pre[:, expert * BLOCK : (expert + 1) * BLOCK]
            total = total + jnp.where(ids_ref[:, k : k + 1] == expert, part, 0.0)
        out_ref[:, k * BLOCK : (k + 1) * BLOCK] = total


def pre_activations(tokens, ids, restored, block, out, column, columns, after=()):
    count, features = tokens.shape
    experts, top = restored.shape[0], ids.shape[1]
    tile = min(count, 2 * BLOCK)
    operands = [tokens, ids, restored] + list(after) + ([] if out is None else [out])
    return pl.pallas_call(
        functools.partial(pre_activation_kernel, experts, top),
        grid=(count // tile,),
        in_specs=[
            pl.BlockSpec((tile, features), lambda i: (i, 0)),
            pl.BlockSpec((tile, top), lambda i: (i, 0)),
            pl.BlockSpec((experts, 1, BLOCK, features), lambda i: (0, block, 0, 0)),
        ]
        + [any_spec()] * (len(operands) - 3),
        out_specs=pl.BlockSpec((tile, top * BLOCK), lambda i: (i, column)),
        out_shape=jax.ShapeDtypeStruct((count, columns * top * BLOCK), jnp.float32),
        input_output_aliases={} if out is None else {len(operands) - 1: 0},
        compiler_params=pltpu.CompilerParams(vmem_limit_bytes=VMEM_BYTES),
        cost_estimate=LIGHT,
        name="pre_activations",
    )(*operands)


def mix_rows(experts, top, blocks, pre_ref, ids_ref, weights_ref, down_ref):
    width = top * BLOCK
    count, features = ids_ref.shape[0], down_ref.shape[-1]
    hidden = {}
    for b in range(blocks):
        for k in range(top):
            start = b * width + k * BLOCK
            gate = pre_ref[:, start : start + BLOCK]
            up = pre_ref[:, blocks * width + start : blocks * width + start + BLOCK]
            value = gate / (1.0 + jnp.exp(-gate)) * up
            hidden[b, k] = value.astype(jnp.bfloat16).astype(jnp.float32)
    total = jnp.zeros((count, features), jnp.float32)
    for expert in range(experts):
        weight = jnp.zeros((count, 1), jnp.float32)
        for k in range(top):
            weight = weight + jnp.where(
                ids_ref[:, k : k + 1] == expert, weights_ref[:, k : k + 1], 0.0
            )
        value = jnp.zeros((count, features), jnp.float32)
        for b in range(blocks):
            routed = jnp.zeros((count, BLOCK), jnp.float32)
            for k in range(top):
                routed = routed + jnp.where(ids_ref[:, k : k + 1] == expert, hidden[b, k], 0.0)
            value = value + jnp.dot(
                routed.astype(jnp.bfloat16), down_ref[expert, b], preferred_element_type=jnp.float32
            )
        total = total + weight * value
    return total


def mix_kernel(sizes, pre_ref, ids_ref, weights_ref, down_ref, out_ref):
    out_ref[...] = mix_rows(*sizes, pre_ref, ids_ref, weights_ref, down_ref)


def mix_split_kernel(sizes, core, pre_ref, ids_ref, weights_ref, down_ref, plan_ref, *refs):
    keep_ref, send_ref = refs[-2:]
    total = mix_rows(*sizes, pre_ref, ids_ref, weights_ref, down_ref)
    half = total.shape[0] // CORES
    first = plan_ref[core] == 0
    keep_ref[0] = jnp.where(first, total[:half], total[half:])
    send_ref[...] = jnp.where(first, total[half:], total[:half]).astype(send_ref.dtype)


def mix_specs(pre, ids, down, tile):
    return [
        pl.BlockSpec((tile, pre.shape[1]), lambda i: (i, 0)),
        pl.BlockSpec((tile, ids.shape[1]), lambda i: (i, 0)),
        pl.BlockSpec((tile, ids.shape[1]), lambda i: (i, 0)),
        pl.BlockSpec(down.shape, lambda i: (0, 0, 0, 0)),
    ]


def mix_experts(pre, ids, weights, down, plan=None, places=None, after=()):
    count, top = ids.shape
    experts, blocks, _, features = down.shape
    sizes = (experts, top, blocks)
    tile = min(count, BLOCK)
    params = pltpu.CompilerParams(vmem_limit_bytes=VMEM_BYTES)
    if plan is None:
        return pl.pallas_call(
            functools.partial(mix_kernel, sizes),
            grid=(count // tile,),
            in_specs=mix_specs(pre, ids, down, tile),
            out_specs=pl.BlockSpec((tile, features), lambda i: (i, 0)),
            out_shape=jax.ShapeDtypeStruct((count, features), jnp.float32),
            compiler_params=params,
            cost_estimate=LIGHT,
            name="mix_experts",
        )(pre, ids, weights, down)
    half = tile // CORES
    return pl.pallas_call(
        functools.partial(mix_split_kernel, sizes, places["core"]),
        grid=(count // tile,),
        in_specs=mix_specs(pre, ids, down, tile) + [smem_spec()] + [any_spec()] * len(after),
        out_specs=[
            pl.BlockSpec((1, half, features), lambda i: (i, 0, 0)),
            pl.BlockSpec((half, features), lambda i: (i, 0)),
        ],
        out_shape=[
            jax.ShapeDtypeStruct((count // tile, half, features), jnp.float32),
            jax.ShapeDtypeStruct((count // CORES, features), jnp.bfloat16),
        ],
        compiler_params=params,
        cost_estimate=LIGHT,
        name="mix_experts",
    )(pre, ids, weights, down, plan, *after)


def sum_call(kernel, name, out_shape, plan, arrays, piece, after):
    vmem = pl.BlockSpec(memory_space=pltpu.VMEM)
    operands = [plan] + list(arrays)
    specs = [smem_spec()] + [vmem] * len(arrays)
    if piece is not None:
        array, first, number = piece
        operands += [array] * number
        for n in range(number):
            specs.append(
                pl.BlockSpec((1,) + array.shape[1:], lambda i, n=n: (first + n, 0, 0))
            )
    return pl.pallas_call(
        kernel,
        grid=(1,),
        in_specs=specs + [any_spec()] * len(after),
        out_specs=[vmem] * len(out_shape) if isinstance(out_shape, list) else vmem,
        out_shape=out_shape,
        compiler_params=pltpu.CompilerParams(vmem_limit_bytes=VMEM_BYTES),
        cost_estimate=LIGHT,
        name=name,
    )(*operands, *after)


def sum_cores_kernel(places, plan_ref, keep_ref, got_ref, *refs):
    sums_ref, send_ref = refs[-2:]
    chips, tokens, features = keep_ref.shape
    for chip in range(chips):
        rows = slice(chip * tokens, (chip + 1) * tokens)
        sums_ref[chip] = keep_ref[chip] + got_ref[rows, :].astype(jnp.float32)
    side, chip = plan_ref[places["side"]], plan_ref[places["chip"]]
    for n in range(2):
        send_ref[n * tokens : (n + 1) * tokens, :] = sums_ref[2 * (1 - side) + n].astype(
            send_ref.dtype
        )
    partner = sums_ref[1 + 4 * side - chip].astype(send_ref.dtype)
    for n in range(2, 4):
        send_ref[n * tokens : (n + 1) * tokens, :] = partner


def sum_cores(plan, places, keep, got, after=()):
    _, tokens, features = keep.shape
    out_shape = [
        jax.ShapeDtypeStruct(keep.shape, jnp.float32),
        jax.ShapeDtypeStruct((4 * tokens, features), jnp.bfloat16),
    ]
    kernel = functools.partial(sum_cores_kernel, places)
    return sum_call(kernel, "sum_cores", out_shape, plan, [keep, got], None, after)


def sum_inwards_kernel(places, plan_ref, sums_ref, over_ref, here_ref, *refs):
    inner_ref, send_ref = refs[-2:]
    tokens = inner_ref.shape[0]
    side, chip = plan_ref[places["side"]], plan_ref[places["chip"]]
    for n in range(2):
        rows = slice(n * tokens, (n + 1) * tokens)
        total = sums_ref[2 * (1 - side) + n] + over_ref[0, rows, :].astype(jnp.float32)
        send_ref[rows, :] = total.astype(send_ref.dtype)
    inner_ref[...] = sums_ref[chip] + here_ref[0, :tokens, :].astype(jnp.float32)


def sum_inwards(plan, places, sums, got, first, after=()):
    _, tokens, features = sums.shape
    out_shape = [
        jax.ShapeDtypeStruct((tokens, features), jnp.float32),
        jax.ShapeDtypeStruct((2 * tokens, features), jnp.bfloat16),
    ]
    kernel = functools.partial(sum_inwards_kernel, places)
    return sum_call(kernel, "sum_inwards", out_shape, plan, [sums], (got, first, 2), after)


def sum_across_kernel(places, plan_ref, sums_ref, inner_ref, got_ref, *refs):
    final_ref, send_ref = refs[-2:]
    tokens = inner_ref.shape[0]
    side, chip = plan_ref[places["side"]], plan_ref[places["chip"]]
    place = chip - 2 * side
    low = got_ref[0, :tokens, :].astype(jnp.float32)
    high = got_ref[0, tokens:, :].astype(jnp.float32)
    final_ref[...] = inner_ref[...] + jnp.where(place == 0, low, high)
    total = sums_ref[1 + 4 * side - chip] + jnp.where(place == 0, high, low)
    for n in range(2):
        send_ref[n * tokens : (n + 1) * tokens, :] = total.astype(send_ref.dtype)


def sum_across(plan, places, sums, inner, got, first, after=()):
    _, tokens, features = sums.shape
    out_shape = [
        jax.ShapeDtypeStruct((tokens, features), jnp.float32),
        jax.ShapeDtypeStruct((2 * tokens, features), jnp.bfloat16),
    ]
    kernel = functools.partial(sum_across_kernel, places)
    return sum_call(kernel, "sum_across", out_shape, plan, [sums, inner], (got, first, 1), after)


def sum_outwards_kernel(places, plan_ref, sums_ref, final_ref, got_ref, *refs):
    out_ref = refs[-1]
    tokens = final_ref.shape[0]
    outer = sums_ref[plan_ref[places["chip"]]] + got_ref[0, :tokens, :].astype(jnp.float32)
    out_ref[...] = jnp.where(plan_ref[places["inner"]] == 1, final_ref[...], outer).astype(
        out_ref.dtype
    )


def sum_outwards(plan, places, sums, final, got, first, after=()):
    out_shape = jax.ShapeDtypeStruct(final.shape, jnp.bfloat16)
    kernel = functools.partial(sum_outwards_kernel, places)
    return sum_call(kernel, "sum_outwards", out_shape, plan, [sums, final], (got, first, 1), after)


def gather_tokens(tokens, expert_ids, gate_weights, features):
    mine = lax.dynamic_slice_in_dim(tokens, lax.axis_index("train") * features, features, axis=1)
    top = expert_ids.shape[1]
    high = lax.reduce_precision(gate_weights, 8, 7)
    middle = lax.reduce_precision(gate_weights - high, 8, 7)
    low = gate_weights - high - middle
    beside = jnp.concatenate((expert_ids.astype(jnp.float32), high, middle, low), axis=1)
    beside = jnp.pad(beside, ((0, 0), (0, BLOCK - 4 * top))).astype(jnp.bfloat16)
    every = lax.all_gather(jnp.concatenate((mine, beside), axis=1), "roll", axis=0, tiled=True)
    side = every[:, features : features + 4 * top].astype(jnp.float32)
    ids = side[:, :top].astype(jnp.int32)
    weights = side[:, top : 2 * top] + side[:, 2 * top : 3 * top] + side[:, 3 * top :]
    return every[:, :features], ids, weights


def per_device(master_gate, master_up, master_down, tokens, expert_ids, gate_weights, placement):
    trains = lax.axis_size("train")
    owners = lax.axis_size("roll")
    experts, hidden_rows, features = master_gate.shape
    blocks = hidden_rows // BLOCK
    if owners // CORES == 4 and CORES * tokens.shape[0] == BLOCK:
        quant, gate = quantize(master_gate, 0, blocks, trains, experts)
        x_first = lax.all_to_all(quant, "train", split_axis=0, concat_axis=0, tiled=True)
        plan, places = make_plan(placement, experts, owners, (quant,))
        rest_up, up = quantize(master_up, 0, blocks, trains, experts, 0, None, (plan,))
        rest_down, down = quantize(master_down, 0, blocks, trains, experts, 0, None, (rest_up,))
        rest = (rest_up, rest_down)
        dequant = (gate, up, down)
        routed = gather_tokens(tokens, expert_ids, gate_weights, features)
        most = min(experts, owners // 2)
        shapes = (experts, blocks, trains, owners)

        def branch(cap, x_first, rest, dequant, plan, routed):
            return line_exchange(x_first, rest, dequant, plan, places, routed, shapes, cap)

        outs = lax.cond(
            plan[places["most"]] <= most - 1,
            functools.partial(branch, most - 1),
            functools.partial(branch, most),
            x_first,
            rest,
            dequant,
            plan,
            routed,
        )
    else:
        masters = (master_gate, master_up, master_down)
        quants, dequant = zip(*[quantize(w, 0, blocks, trains, experts) for w in masters])
        every, ids, weights = gather_tokens(tokens, expert_ids, gate_weights, features)
        outs = direct_exchange(quants, placement, trains, owners)
        pre = None
        for n in range(2 * blocks):
            restored = dequant[n // blocks]
            pre = pre_activations(every, ids, restored, n % blocks, pre, n, 2 * blocks)
        mixed = mix_experts(lax.psum(pre, "train"), ids, weights, dequant[2])
        mixed = lax.psum_scatter(mixed, "roll", scatter_dimension=0, tiled=True)
        outs = tuple(outs) + (mixed.astype(jnp.bfloat16),)
    return tuple(out[None] for out in outs[:3]) + (outs[3],)


def solution(mesh):
    in_specs = (
        P(None, "roll", "train"),
        P(None, "roll", "train"),
        P(None, "roll", "train"),
        P("roll", None),
        P("roll", None),
        P("roll", None),
        P(),
    )
    out_specs = (
        P("roll", None, "train", None),
        P("roll", None, "train", None),
        P("roll", None, "train", None),
        P("roll", "train"),
    )
    return jax.shard_map(
        per_device, mesh=mesh, in_specs=in_specs, out_specs=out_specs, check_vma=False
    )
```
